32 devices in a mesh: dp: 4 (over z), ctx: 2 (over x), mp: 4 (over y, core).
Axes of the slice: x: 2, y: 2, z: 4, core: 2. Of those that a mesh axis runs over, the one named last changes fastest.
Arguments:
- block_input: bfloat16 [16384, 768], P(('dp', 'ctx', 'mp')), may hold values from -6 to 6
- cotangent: bfloat16 [16384, 768], P(('dp', 'ctx', 'mp')), may hold values from -6 to 6
- doc_lengths: int32 [8, 3], P(('dp', 'ctx')), may hold values from 1 to 1024, 1536 in all within a row
- reuse_heads: int32 [6], replicated, may hold values from 0 to 11, as said below
- norm_gain1: bfloat16 [2, 768], replicated, may hold values from 0.099609375 to 1.8984375
- norm_bias1: bfloat16 [2, 768], replicated, may hold values from -4 to 4
- projections1: bfloat16 [3, 768, 768], P(None, None, 'mp'), may hold values from -0.3125 to 0.3125
- front_bias1: bfloat16 [2, 768], P(None, 'mp'), may hold values from -4 to 4
- out_weight1: bfloat16 [768, 768], P('mp'), may hold values from -0.625 to 0.625
- out_bias1: bfloat16 [2, 768], replicated, may hold values from -4 to 4
- up_weight1: bfloat16 [768, 3072], P(None, 'mp'), may hold values from -0.21875 to 0.21875
- up_bias1: bfloat16 [3072], P('mp'), may hold values from -4 to 4
- down_weight1: bfloat16 [3072, 768], P('mp'), may hold values from -0.109375 to 0.109375
- norm_gain2: bfloat16 [2, 768], replicated, may hold values from 0.099609375 to 1.8984375
- norm_bias2: bfloat16 [2, 768], replicated, may hold values from -4 to 4
- query_key2: bfloat16 [2, 768, 768], P(None, None, 'mp'), may hold values from -0.3125 to 0.3125
- query_bias2: bfloat16 [768], P('mp'), may hold values from -4 to 4
- fresh_value2: bfloat16 [768, 384], P(None, 'mp'), may hold values from -0.3125 to 0.3125
- value_bias2: bfloat16 [384], P('mp'), may hold values from -4 to 4
- out_weight2: bfloat16 [768, 768], P('mp'), may hold values from -0.625 to 0.625
- out_bias2: bfloat16 [2, 768], replicated, may hold values from -4 to 4
- up_weight2: bfloat16 [768, 3072], P(None, 'mp'), may hold values from -0.21875 to 0.21875
- up_bias2: bfloat16 [3072], P('mp'), may hold values from -4 to 4
- down_weight2: bfloat16 [3072, 768], P('mp'), may hold values from -0.109375 to 0.109375
Outputs:
- block_output: bfloat16 [16384, 768], P(('dp', 'ctx', 'mp'))
- input_grad: bfloat16 [16384, 768], P(('dp', 'ctx', 'mp'))
- grad_norm_gain1: float32 [2, 768], replicated
- grad_norm_bias1: float32 [2, 768], replicated
- grad_projections1: float32 [3, 768, 768], P(None, None, 'mp')
- grad_front_bias1: float32 [2, 768], P(None, 'mp')
- grad_out_weight1: float32 [768, 768], P('mp')
- grad_out_bias1: float32 [2, 768], replicated
- grad_up_weight1: float32 [768, 3072], P(None, 'mp')
- grad_up_bias1: float32 [3072], P('mp')
- grad_down_weight1: float32 [3072, 768], P('mp')
- grad_norm_gain2: float32 [2, 768], replicated
- grad_norm_bias2: float32 [2, 768], replicated
- grad_query_key2: float32 [2, 768, 768], P(None, None, 'mp')
- grad_query_bias2: float32 [768], P('mp')
- grad_fresh_value2: float32 [768, 384], P(None, 'mp')
- grad_value_bias2: float32 [384], P('mp')
- grad_out_weight2: float32 [768, 768], P('mp')
- grad_out_bias2: float32 [2, 768], replicated
- grad_up_weight2: float32 [768, 3072], P(None, 'mp')
- grad_up_bias2: float32 [3072], P('mp')
- grad_down_weight2: float32 [3072, 768], P('mp')
The draws below stay inside these ranges and needn't reach their ends.
Inputs may be any that keep to these rules, and one draw needn't show every extreme that they name: `doc_lengths`: each row lists the lengths of the 3 documents of one group; they sum to 1536 and the longest is exactly 1024. `reuse_heads`: 6 distinct head numbers.
All inputs are finite; a program needn't handle non-finite values.
Results may differ from the reference program's by a relative error of at most 0.03.
Values may be sent and summed in bfloat16 or wider, within the bound.
A program may use at most 192 MiB of HBM per device.

```python
import math
import jax
import jax.numpy as jnp
import numpy as np
from jax import lax

D = 768
H = 12
HD = 64
FF = 3072
REUSE = 6
DOCS = 3
WIN = 512
SHORT_MOST = 1024
FRESH = 6
SHORT = 1536
TOK_DEV = 2048
GROUPS = 8
TOKENS = 16384
N_DP = 4
N_CTX = 2


def draw_reuse_heads(key, part):
    key = jax.random.fold_in(key, 11)
    return jax.random.permutation(key, H)[:REUSE].astype(jnp.int32)


def steps_of(stream_key, shape, split, smallest, largest):
    def one(axis_at, shards_of):
        draws = jax.random.uniform(jax.random.fold_in(jax.random.fold_in(stream_key, 6), axis_at), (shards_of,), jnp.float32, smallest / len(split), largest / len(split))
        return jnp.repeat(jnp.exp(draws), shape[axis_at] // shards_of).reshape((-1,) + (1,) * (len(shape) - axis_at - 1))

    factor_of = one(*split[0])
    for cut in split[1:]:
        factor_of = factor_of * one(*cut)
    return factor_of


def split_up(number_of, total, limit, skew):
    loads = [(1 << 20) // math.isqrt(grade ** skew) + 1 for grade in range(2, number_of + 1)]
    surplus, given = total - limit - (number_of - 1), [1] * (number_of - 1)
    while surplus > 0:
        candidates = [i for i in range(number_of - 1) if given[i] < limit]
        whole, left = sum([loads[i] for i in candidates]), surplus
        for i in candidates:
            more = min(limit - given[i], max(1, left * loads[i] // whole), surplus)
            given[i] = given[i] + more
            surplus = surplus - more
    return np.array([limit] + given)


def ragged_sizes(rng, amount, total, most, lean):
    if amount == 2:
        one = jax.random.randint(rng, (), max(1, total - most), min(most, total - 1) + 1)
        return jnp.stack([one, total - one])
    sizes = jnp.asarray(split_up(amount, total, most, lean), jnp.int32)
    couples = (amount - 1) // 2
    donor, receiver = sizes[1:1 + 2 * couples:2], sizes[2:2 + 2 * couples:2]
    room = jnp.minimum(donor - 1, most - receiver)
    moved = jax.random.randint(jax.random.fold_in(rng, 1), (couples,), 0, 1 << 20) % (room + 1)
    sizes = sizes.at[1:1 + 2 * couples:2].set(donor - moved).at[2:2 + 2 * couples:2].set(receiver + moved)
    return sizes[jax.random.permutation(jax.random.fold_in(rng, 2), amount)]


def bell_draw(key, shape, scale, bound, cuts=(), kind=jnp.bfloat16):
    level = steps_of(key, shape, cuts, -0.22, 0.18) if cuts else 1.0
    result = jax.random.normal(key, shape, jnp.float32) * scale * level
    return jnp.minimum(jnp.maximum(result, -bound), bound).astype(kind)


def setup_inputs(seed: int = 0) -> dict:
    seeds = jax.random.split(jax.random.key(seed), 25)
    block_input = bell_draw(seeds[0], (TOKENS, D), 1.0, 6.0, ((0, 32),))
    cotangent = bell_draw(seeds[1], (TOKENS, D), 1.0, 6.0, ((0, 32),))
    doc_lengths = jax.vmap(lambda own: ragged_sizes(own, DOCS, SHORT, SHORT_MOST, 2))(jax.random.split(seeds[2], GROUPS)).reshape((GROUPS, DOCS)).astype(jnp.int32)
    reuse_heads = draw_reuse_heads(jax.random.fold_in(seeds[24], 71), 0)
    norm_gain1 = jnp.clip(1.0 + 0.18 * jax.random.normal(seeds[4], (2, D), jnp.float32), 0.099609375, 1.8984375).astype(jnp.bfloat16)
    norm_bias1 = bell_draw(seeds[5], (2, D), 0.3, 4.0)
    projections1 = bell_draw(seeds[6], (3, D, D), (D // 2) ** -0.5, 0.3125, ((2, 4),))
    front_bias1 = bell_draw(seeds[7], (2, D), 0.3, 4.0, ((1, 4),))
    out_weight1 = bell_draw(seeds[8], (D, D), (D // 8) ** -0.5, 0.625, ((0, 4),))
    out_bias1 = bell_draw(seeds[9], (2, D), 0.3, 4.0)
    up_weight1 = bell_draw(seeds[10], (D, FF), D ** -0.5, 0.21875, ((1, 4),))
    up_bias1 = bell_draw(seeds[11], (FF,), 0.3, 4.0, ((0, 4),))
    down_weight1 = bell_draw(seeds[12], (FF, D), FF ** -0.5, 0.109375, ((0, 4),))
    norm_gain2 = jnp.clip(1.0 + 0.18 * jax.random.normal(seeds[13], (2, D), jnp.float32), 0.099609375, 1.8984375).astype(jnp.bfloat16)
    norm_bias2 = bell_draw(seeds[14], (2, D), 0.3, 4.0)
    query_key2 = bell_draw(seeds[15], (2, D, D), (D // 2) ** -0.5, 0.3125, ((2, 4),))
    query_bias2 = bell_draw(seeds[16], (D,), 0.3, 4.0, ((0, 4),))
    fresh_value2 = bell_draw(seeds[17], (D, FRESH * HD), (D // 2) ** -0.5, 0.3125, ((1, 4),))
    value_bias2 = bell_draw(seeds[18], (FRESH * HD,), 0.3, 4.0, ((0, 4),))
    out_weight2 = bell_draw(seeds[19], (D, D), (D // 8) ** -0.5, 0.625, ((0, 4),))
    out_bias2 = bell_draw(seeds[20], (2, D), 0.3, 4.0)
    up_weight2 = bell_draw(seeds[21], (D, FF), D ** -0.5, 0.21875, ((1, 4),))
    up_bias2 = bell_draw(seeds[22], (FF,), 0.3, 4.0, ((0, 4),))
    down_weight2 = bell_draw(seeds[23], (FF, D), FF ** -0.5, 0.109375, ((0, 4),))
    return {"block_input": block_input, "cotangent": cotangent, "doc_lengths": doc_lengths, "reuse_heads": reuse_heads, "norm_gain1": norm_gain1, "norm_bias1": norm_bias1, "projections1": projections1, "front_bias1": front_bias1, "out_weight1": out_weight1, "out_bias1": out_bias1, "up_weight1": up_weight1, "up_bias1": up_bias1, "down_weight1": down_weight1, "norm_gain2": norm_gain2, "norm_bias2": norm_bias2, "query_key2": query_key2, "query_bias2": query_bias2, "fresh_value2": fresh_value2, "value_bias2": value_bias2, "out_weight2": out_weight2, "out_bias2": out_bias2, "up_weight2": up_weight2, "up_bias2": up_bias2, "down_weight2": down_weight2}


@jax.custom_vjp
def low(v):
    return lax.optimization_barrier(v.astype(jnp.bfloat16)).astype(jnp.float32)

@jax.custom_vjp
def low_back(v):
    return v

def low_keep(v):
    return (low(v), None)

def low_pass(kept, grad):
    return (grad,)

def back_keep(v):
    return (v, None)

def back_low(kept, grad):
    return (low(grad),)
low.defvjp(low_keep, low_pass)
low_back.defvjp(back_keep, back_low)
EPS = 1e-05
HIGH = lax.Precision.HIGHEST

def layer_norm(value, gain, shift):
    mean = lax.optimization_barrier(jnp.mean(value, axis=-1, keepdims=True))
    centred = value - mean
    spread = lax.optimization_barrier(jnp.mean(centred * centred, axis=-1, keepdims=True))
    return centred * lax.rsqrt(spread + EPS) * gain + shift

def matmul(left, right):
    return jnp.dot(left, right, precision=HIGH, preferred_element_type=jnp.float32)

def attend(queries, keys, values, allowed):
    scores = low_back(jnp.einsum('qhe,khe->hqk', queries, keys, precision=HIGH) * 0.125)
    scores = jnp.where(allowed[None], scores, -jnp.inf)
    weights = low(jax.nn.softmax(scores, axis=-1))
    return jnp.einsum('hqk,khe->qhe', weights, values, precision=HIGH)

def doc_allowed(lengths):
    ends = jnp.cumsum(lengths)
    place = jnp.arange(SHORT, dtype=jnp.int32)
    docs = lax.optimization_barrier(jnp.sum((place[:, None] >= ends[None, :]).astype(jnp.int32), axis=1))
    return (docs[:, None] == docs[None, :]) & (place[:, None] >= place[None, :])

def attention(queries, keys, values, lengths):

    def regions(tensor):
        grouped = tensor.reshape(N_DP, N_CTX, TOK_DEV, H, HD)
        long_part = grouped[:, :, :WIN].reshape(N_DP, N_CTX * WIN, H, HD)
        short_part = grouped[:, :, WIN:].reshape(N_DP * N_CTX, SHORT, H, HD)
        return (long_part, short_part)
    long_query, short_query = regions(queries)
    long_key, short_key = regions(keys)
    long_value, short_value = regions(values)
    place = jnp.arange(N_CTX * WIN, dtype=jnp.int32)
    causal = place[:, None] >= place[None, :]
    long_out = lax.map(jax.checkpoint(lambda item: attend(item[0], item[1], item[2], causal)), (long_query, long_key, long_value))
    short_out = lax.map(jax.checkpoint(lambda item: attend(item[0], item[1], item[2], doc_allowed(item[3]))), (short_query, short_key, short_value, lengths))
    merged = jnp.concatenate([long_out.reshape(N_DP, N_CTX, WIN, H, HD), short_out.reshape(N_DP, N_CTX, SHORT, H, HD)], axis=2)
    return merged.reshape(N_DP * N_CTX * TOK_DEV, H * HD)

def tail(stream, queries, keys, values, lengths, out_weight, out_bias, norm_gain, norm_bias, up_weight, up_bias, down_weight):
    rows = queries.shape[0]
    heads = low_back(low(attention(queries.reshape(rows, H, HD), keys.reshape(rows, H, HD), values.reshape(rows, H, HD), lengths)))
    stream = stream + low_back(matmul(heads, out_weight)) + out_bias[0]
    normed = low(layer_norm(stream, norm_gain[1], norm_bias[1]))
    hidden = low_back(matmul(normed, up_weight)) + up_bias
    active = low(jax.nn.gelu(hidden, approximate=True))
    return stream + low_back(matmul(active, down_weight)) + out_bias[1]

def forward(stream, norm_gain1, norm_bias1, projections1, front_bias1, out_weight1, out_bias1, up_weight1, up_bias1, down_weight1, norm_gain2, norm_bias2, query_key2, query_bias2, fresh_value2, value_bias2, out_weight2, out_bias2, up_weight2, up_bias2, down_weight2, lengths, reuse_heads):
    rows = stream.shape[0]
    normed = low(layer_norm(stream, norm_gain1[0], norm_bias1[0]))
    queries = low(low_back(matmul(normed, projections1[0])) + front_bias1[0])
    keys = low(low_back(matmul(normed, projections1[1])))
    first_values = low(low_back(matmul(normed, projections1[2])) + front_bias1[1])
    stream = tail(stream, queries, keys, first_values, lengths, out_weight1, out_bias1, norm_gain1, norm_bias1, up_weight1, up_bias1, down_weight1)
    normed = low(layer_norm(stream, norm_gain2[0], norm_bias2[0]))
    queries = low(low_back(matmul(normed, query_key2[0])) + query_bias2)
    keys = low(low_back(matmul(normed, query_key2[1])))
    fresh = low(low_back(matmul(normed, fresh_value2)) + value_bias2)
    source = jnp.concatenate([first_values.reshape(rows, H, HD), fresh.reshape(rows, FRESH, HD)], axis=1)
    chosen = jnp.concatenate([reuse_heads, H + jnp.arange(FRESH, dtype=jnp.int32)])
    values = jnp.take(source, chosen, axis=1).reshape(rows, H * HD)
    return tail(stream, queries, keys, values, lengths, out_weight2, out_bias2, norm_gain2, norm_bias2, up_weight2, up_bias2, down_weight2)

def reference(block_input, cotangent, doc_lengths, reuse_heads, norm_gain1, norm_bias1, projections1, front_bias1, out_weight1, out_bias1, up_weight1, up_bias1, down_weight1, norm_gain2, norm_bias2, query_key2, query_bias2, fresh_value2, value_bias2, out_weight2, out_bias2, up_weight2, up_bias2, down_weight2):
    params = tuple((item.astype(jnp.float32) for item in (norm_gain1, norm_bias1, projections1, front_bias1, out_weight1, out_bias1, up_weight1, up_bias1, down_weight1, norm_gain2, norm_bias2, query_key2, query_bias2, fresh_value2, value_bias2, out_weight2, out_bias2, up_weight2, up_bias2, down_weight2)))

    def run(stream, *weights):
        return forward(stream, *weights, doc_lengths, reuse_heads)
    output, pull = jax.vjp(run, block_input.astype(jnp.float32), *params)
    grads = pull(cotangent.astype(jnp.float32))
    return (output.astype(jnp.bfloat16), grads[0].astype(jnp.bfloat16), grads[1], grads[2], grads[3], grads[4], grads[5], grads[6], grads[7], grads[8], grads[9], grads[10], grads[11], grads[12], grads[13], grads[14], grads[15], grads[16], grads[17], grads[18], grads[19], grads[20])
```

```python
import functools

import jax
import jax.numpy as jnp
from jax import lax
from jax.experimental import pallas as pl
from jax.experimental.pallas import tpu as pltpu
from jax.sharding import PartitionSpec as P

D = 768
HD = 64
REUSE = 6
WIN = 512
GROUP = 3
BAND = GROUP * HD
TILE = 256
TILES = 3 * WIN // TILE
EPS = 1e-05
SCALE = HD**-0.5
F32 = jnp.float32
BF16 = jnp.bfloat16


def swap(value, axis, bit):
    devices = range(lax.axis_size(axis))
    return lax.ppermute(value, axis, [(i, i ^ bit) for i in devices])


def gather_shards(own):
    far = swap(own, "mp", 2)
    near = swap(own, "mp", 1)
    return [own, near, far, swap(far, "mp", 1)]


def in_order(parts):
    me = lax.axis_index("mp")
    result = jnp.zeros((4,) + parts[0].shape, parts[0].dtype)
    for distance, part in enumerate(parts):
        result = lax.dynamic_update_index_in_dim(result, part, me ^ distance, 0)
    return result


def by_distance(stacked):
    me = lax.axis_index("mp")
    return [
        lax.dynamic_index_in_dim(stacked, me ^ distance, 0, keepdims=False)
        for distance in range(4)
    ]


def dot(left, right, left_dim, right_dim):
    return lax.dot_general(
        left, right, (((left_dim,), (right_dim,)), ((), ())), preferred_element_type=F32
    )


def norm_rows(value, gain, shift):
    mean = jnp.mean(value, axis=-1, keepdims=True)
    centred = value - mean
    spread = jnp.mean(centred * centred, axis=-1, keepdims=True)
    scale = lax.rsqrt(spread + EPS)
    unit = centred * scale
    return (unit * gain + shift).astype(BF16), unit, scale


def norm_back(grad, unit, scale, gain):
    scaled = grad * gain
    inner = (
        scaled
        - jnp.mean(scaled, axis=-1, keepdims=True)
        - unit * jnp.mean(scaled * unit, axis=-1, keepdims=True)
    )
    return scale * inner, jnp.sum(grad * unit, axis=0), jnp.sum(grad, axis=0)


def attend_kernel(first_ref, lo_ref, q_ref, k0, k1, k2, v0, v1, v2, out_ref, exact_ref, sum_ref, top, total, acc):
    keys, values = (k2, k1, k0), (v2, v1, v0)
    for t in range(WIN // TILE):
        cols = slice(t * TILE, (t + 1) * TILE)
        low = lo_ref[:, cols]
        place = 2 * WIN + t * TILE + lax.broadcasted_iota(jnp.int32, (1, TILE), 1)
        last = 2 * WIN // TILE + t

        def scores(kt, j):
            rows = slice(j * HD, (j + 1) * HD)
            span = slice(kt % 2 * TILE, (kt % 2 + 1) * TILE)
            return dot(keys[kt // 2][0, rows, span], q_ref[0, rows, cols] * SCALE, 0, 0)

        def tile(kt):
            spot = kt * TILE + lax.broadcasted_iota(jnp.int32, (TILE, TILE), 0)
            keep = spot >= low
            if kt == last:
                keep = keep & (spot <= place)
            span = slice(kt % 2 * TILE, (kt % 2 + 1) * TILE)
            for j in range(GROUP):
                rows = slice(j * HD, (j + 1) * HD)
                raw = jnp.where(keep, scores(kt, j), -jnp.inf)
                peak = jnp.max(raw, axis=0, keepdims=True)
                if kt != last:
                    before = top[j]
                    peak = jnp.maximum(peak, before)
                powers = jnp.exp(raw - peak)
                added = jnp.sum(powers, axis=0, keepdims=True)
                result = dot(values[kt // 2][0, rows, span], powers.astype(BF16), 1, 0)
                if kt != last:
                    shrink = jnp.exp(before - peak)
                    added = added + total[j] * shrink
                    result = result + acc[j] * shrink
                top[j] = peak
                total[j] = added
                acc[j] = result

        tile(last)
        for kt in reversed(range(last)):
            pl.when(kt >= first_ref[t])(functools.partial(tile, kt))
        for j in range(GROUP):
            rows = slice(j * HD, (j + 1) * HD)
            result = acc[j] / total[j]
            out_ref[0, rows, cols] = result.astype(BF16)
            exact_ref[0, rows, cols] = result
            sum_ref[0, j : j + 1, cols] = top[j] + jnp.log(total[j])


def attend_back_kernel(
    first_ref, lo_ref, q_ref, k0, k1, k2, v0, v1, v2, out_ref, grad_ref, sum_ref,
    dq_ref, dk0, dk1, dk2, dv0, dv1, dv2, acc_k, acc_v, acc_q,
):
    keys, values = (k2, k1, k0), (v2, v1, v0)
    acc_k[...] = jnp.zeros_like(acc_k)
    acc_v[...] = jnp.zeros_like(acc_v)
    for t in range(WIN // TILE):
        cols = slice(t * TILE, (t + 1) * TILE)
        low = lo_ref[:, cols]
        place = 2 * WIN + t * TILE + lax.broadcasted_iota(jnp.int32, (1, TILE), 1)
        last = 2 * WIN // TILE + t

        def tile(kt):
            spot = kt * TILE + lax.broadcasted_iota(jnp.int32, (TILE, TILE), 0)
            keep = spot >= low
            if kt == last:
                keep = keep & (spot <= place)
            span = slice(kt % 2 * TILE, (kt % 2 + 1) * TILE)
            for j in range(GROUP):
                rows = slice(j * HD, (j + 1) * HD)
                key = keys[kt // 2][0, rows, span]
                query = q_ref[0, rows, cols] * SCALE
                grad = grad_ref[0, rows, cols]
                inner = jnp.sum(
                    grad.astype(F32) * out_ref[0, rows, cols], axis=0, keepdims=True
                )
                raw = jnp.where(keep, dot(key, query, 0, 0), -jnp.inf)
                weights = jnp.exp(raw - sum_ref[0, j : j + 1, cols])
                grad_weights = dot(values[kt // 2][0, rows, span], grad, 0, 0)
                low_grad = (weights * (grad_weights - inner)).astype(BF16)
                acc_v[kt, rows, :] += dot(grad, weights.astype(BF16), 1, 1)
                acc_k[kt, rows, :] += dot(query, low_grad, 1, 1)
                result = dot(key, low_grad, 1, 0)
                if kt != last:
                    result = result + acc_q[j]
                acc_q[j] = result

        tile(last)
        for kt in reversed(range(last)):
            pl.when(kt >= first_ref[t])(functools.partial(tile, kt))
        for j in range(GROUP):
            rows = slice(j * HD, (j + 1) * HD)
            dq_ref[0, rows, cols] = acc_q[j] * SCALE
    for part, (dk, dv) in enumerate(((dk2, dv2), (dk1, dv1), (dk0, dv0))):
        for half in range(2):
            span = slice(half * TILE, (half + 1) * TILE)
            dk[0, :, span] = acc_k[2 * part + half].astype(dk.dtype)
            dv[0, :, span] = acc_v[2 * part + half].astype(dv.dtype)


def band(place):
    return pl.BlockSpec((1, BAND, WIN), lambda s, *_: (s, place, 0))


LOW = pl.BlockSpec((1, WIN), lambda s, *_: (0, 0))
SUMS = pl.BlockSpec((1, 8, WIN), lambda s, *_: (s, 0, 0))


def attend(first, low, operands, places):
    return pl.pallas_call(
        attend_kernel,
        grid_spec=pltpu.PrefetchScalarGridSpec(
            num_scalar_prefetch=1,
            grid=(4,),
            in_specs=[LOW] + [band(p) for p in places],
            out_specs=[band(0), band(0), SUMS],
            scratch_shapes=[
                pltpu.VMEM((GROUP, 1, TILE), F32),
                pltpu.VMEM((GROUP, 1, TILE), F32),
                pltpu.VMEM((GROUP, HD, TILE), F32),
            ],
        ),
        out_shape=[
            jax.ShapeDtypeStruct((4, BAND, WIN), BF16),
            jax.ShapeDtypeStruct((4, BAND, WIN), F32),
            jax.ShapeDtypeStruct((4, 8, WIN), F32),
        ],
        compiler_params=pltpu.CompilerParams(vmem_limit_bytes=32 * 1024 * 1024),
        name="attend",
    )(first, low, *operands)


def attend_back(first, low, operands, places, heads, grad_heads, sums):
    kinds = (F32, F32, BF16, BF16, F32, BF16, BF16)
    return pl.pallas_call(
        attend_back_kernel,
        grid_spec=pltpu.PrefetchScalarGridSpec(
            num_scalar_prefetch=1,
            grid=(4,),
            in_specs=[LOW] + [band(p) for p in places] + [band(0), band(0), SUMS],
            out_specs=[band(0)] * 7,
            scratch_shapes=[
                pltpu.VMEM((TILES, BAND, TILE), F32),
                pltpu.VMEM((TILES, BAND, TILE), F32),
                pltpu.VMEM((GROUP, HD, TILE), F32),
            ],
        ),
        out_shape=[jax.ShapeDtypeStruct((4, BAND, WIN), kind) for kind in kinds],
        compiler_params=pltpu.CompilerParams(vmem_limit_bytes=32 * 1024 * 1024),
        name="attend_back",
    )(first, low, *operands, heads, grad_heads, sums)


def routes():
    windows, groups = lax.axis_size("ctx"), lax.axis_size("mp")
    onward = [(c * groups + m, c * groups + m + 1) for c in range(windows) for m in (1, 2)]
    onward += [(c * groups, (c + 1) * groups) for c in range(windows - 1)]
    second = [(c * groups + 2, c * groups + 3) for c in range(windows)]
    first_home = [(c * groups + 3, c * groups + 2) for c in range(windows)]
    home = [(c * groups + 2, c * groups + 1) for c in range(windows)]
    home += [((c + 1) * groups, c * groups) for c in range(windows - 1)]
    return onward, second, first_home, home


def pass_on(block):
    onward, second, _, _ = routes()
    before = lax.ppermute(block, ("ctx", "mp"), onward)
    return before, lax.ppermute(before, ("ctx", "mp"), second)


def pass_home(before, earlier):
    _, _, first_home, home = routes()
    near, far = lax.ppermute((before, earlier), ("ctx", "mp"), first_home)
    far = (before.astype(F32) + far.astype(F32)).astype(BF16)
    return near.astype(F32) + lax.ppermute(far, ("ctx", "mp"), home).astype(F32)


def row_starts(lengths):
    part = lax.axis_index("mp")
    place = (part - 1) * WIN + jnp.arange(WIN, dtype=jnp.int32)
    ends = jnp.cumsum(lengths)
    begun = jnp.max(jnp.where(place[:, None] >= ends[None, :], ends[None, :], 0), axis=1)
    document = begun - (part - 1) * WIN + 2 * WIN
    window = jnp.where(lax.axis_index("ctx") > 0, WIN, 2 * WIN)
    low = jnp.where(part == 0, window, document).astype(jnp.int32)
    return low.reshape(1, WIN), low[::TILE] // TILE


def reduce_shards(parts):
    own, near, far, last = parts
    near, last = swap(jnp.stack([near, last]), "mp", 1)
    far = (far.astype(F32) + last.astype(F32)).astype(BF16)
    far = swap(far, "mp", 2)
    total = own.astype(F32) + near.astype(F32) + far.astype(F32)
    return sum_replicas(total.astype(BF16))


def sum_replicas(value):
    steps = [("ctx", 1)]
    bit = 1
    while bit < lax.axis_size("dp"):
        steps.append(("dp", bit))
        bit *= 2
    for axis, bit in steps:
        high = (lax.axis_index(axis) // bit) % 2
        half = value.shape[0] // 2
        kept = lax.dynamic_slice_in_dim(value, high * half, half, 0)
        sent = lax.dynamic_slice_in_dim(value, (1 - high) * half, half, 0)
        value = (kept.astype(F32) + swap(sent, axis, bit).astype(F32)).astype(BF16)
    for axis, bit in reversed(steps):
        high = (lax.axis_index(axis) // bit) % 2
        half = value.shape[0]
        other = swap(value, axis, bit)
        whole = jnp.zeros((2 * half,) + value.shape[1:], BF16)
        whole = lax.dynamic_update_slice_in_dim(whole, value, high * half, 0)
        value = lax.dynamic_update_slice_in_dim(whole, other, (1 - high) * half, 0)
    return value


def sum_all(value):
    for axis in ("mp", "ctx", "dp"):
        bit = 1
        while bit < lax.axis_size(axis):
            value = value + swap(value, axis, bit)
            bit *= 2
    return value


def gelu(hidden):
    return jax.nn.gelu(hidden, approximate=True)


def tail_forward(stream, heads, out_weight, out_bias, gain, shift, ups, up_biases, downs):
    stream = stream + dot(heads, out_weight, 0, 0) + out_bias[0]
    normed, unit, scale = norm_rows(stream, gain[1], shift[1])
    hidden, active, total = [], [], out_bias[1]
    for up, bias, down in zip(ups, up_biases, downs, strict=True):
        hidden.append(dot(normed, up, 1, 0) + bias)
        active.append(gelu(hidden[-1]).astype(BF16))
        total = total + dot(active[-1], down, 1, 0)
    return stream + total, (normed, unit, scale, hidden, active)


def tail_backward(grad, kept, out_weight, gain, ups, downs):
    normed, unit, scale, hidden, active = kept
    bias_mlp = jnp.sum(grad, axis=0)
    rounded = grad.astype(BF16)
    mats, up_biases, normed_grad = [], [], 0.0
    for up, down, before, after in zip(ups, downs, hidden, active, strict=True):
        _, pull = jax.vjp(gelu, before)
        grad_hidden = pull(dot(rounded, down, 1, 1))[0]
        up_biases.append(jnp.sum(grad_hidden, axis=0))
        low = grad_hidden.astype(BF16)
        mats.append(
            jnp.concatenate(
                [dot(normed, low, 0, 0).astype(BF16), dot(after, rounded, 0, 0).astype(BF16)]
            )
        )
        normed_grad = normed_grad + dot(low, up, 1, 1)
    middle, gain_grad, shift_grad = norm_back(normed_grad, unit, scale, gain[1])
    grad = grad + middle
    bias_attn = jnp.sum(grad, axis=0)
    rounded = grad.astype(BF16)
    grad_heads = dot(out_weight, rounded, 1, 1).astype(BF16)
    return grad, rounded, grad_heads, mats, up_biases, (gain_grad, shift_grad, bias_attn, bias_mlp)


def turned(weight):
    return jnp.swapaxes(weight, -1, -2)


def shards(
    block_input, cotangent, doc_lengths, reuse_heads,
    norm_gain1, norm_bias1, projections1, front_bias1, out_weight1, out_bias1,
    up_weight1, up_bias1, down_weight1,
    norm_gain2, norm_bias2, query_key2, query_bias2, fresh_value2, value_bias2,
    out_weight2, out_bias2, up_weight2, up_bias2, down_weight2,
):
    low, first = row_starts(doc_lengths[0])

    front1 = in_order(gather_shards(turned(projections1).reshape(3 * BAND, D)))
    small = jnp.concatenate(
        [front_bias1.reshape(-1), query_bias2, value_bias2, up_bias1, up_bias2]
    )
    filler = (-small.shape[0]) % 1024
    small = gather_shards(jnp.pad(small, (0, filler)).reshape(-1, 128))
    small = [part.reshape(-1) for part in small]
    n_front, n_query, n_value, n_up = 2 * BAND, BAND, BAND // 2, D
    cuts = [n_front, n_front + n_query, n_front + n_query + n_value]
    up_biases1 = [part[cuts[2] : cuts[2] + n_up] for part in small]
    up_biases2 = [part[cuts[2] + n_up : cuts[2] + 2 * n_up] for part in small]
    ordered = in_order([part[: cuts[2]] for part in small])
    none = jnp.zeros((4, BAND), BF16)
    bias1 = jnp.concatenate([ordered[:, :BAND], none, ordered[:, BAND:n_front]], axis=1)
    bias2 = jnp.concatenate(
        [ordered[:, n_front : cuts[1]], none, ordered[:, cuts[1] : cuts[2]]], axis=1
    )
    outs1 = in_order(gather_shards(out_weight1)).reshape(D, D)
    ups1 = gather_shards(up_weight1)
    downs1 = gather_shards(down_weight1)
    front2 = in_order(
        gather_shards(
            jnp.concatenate([turned(query_key2).reshape(2 * BAND, D), turned(fresh_value2)])
        )
    )
    outs2 = in_order(gather_shards(out_weight2)).reshape(D, D)
    ups2 = gather_shards(up_weight2)
    downs2 = gather_shards(down_weight2)

    stream0 = block_input.astype(F32)
    normed1, unit1, scale1 = norm_rows(stream0, norm_gain1[0], norm_bias1[0])
    n_front1, n_front2 = front1.shape[1], front2.shape[1]
    cols1 = dot(front1.reshape(-1, D), normed1, 1, 1).reshape(4, n_front1, WIN)
    cols1 = (cols1 + bias1[:, :, None]).astype(BF16)
    before1, earlier1 = pass_on(cols1[:, BAND:])
    operands1 = (cols1, cols1, before1, earlier1, cols1, before1, earlier1)
    places1 = (0, 1, 0, 0, 2, 1, 1)
    heads1, exact1, sums1 = attend(first, low, operands1, places1)
    stream1, kept1 = tail_forward(
        stream0, heads1.reshape(D, WIN), outs1, out_bias1, norm_gain1, norm_bias1,
        ups1, up_biases1, downs1,
    )

    normed2, unit2, scale2 = norm_rows(stream1, norm_gain2[0], norm_bias2[0])
    cols2 = dot(front2.reshape(-1, D), normed2, 1, 1).reshape(4, n_front2, WIN)
    cols2 = (cols2 + bias2[:, :, None]).astype(BF16)
    before2, earlier2 = pass_on(cols2[:, BAND:])

    def mixed(first_values, fresh):
        first_values = first_values.reshape(-1, HD, WIN)
        reused = [
            lax.dynamic_index_in_dim(first_values, reuse_heads[n], 0, keepdims=True)
            for n in range(REUSE)
        ]
        return jnp.concatenate(reused + [fresh.reshape(-1, HD, WIN)]).reshape(4, BAND, WIN)

    values2 = [
        mixed(cols1[:, 2 * BAND :], cols2[:, 2 * BAND :]),
        mixed(before1[:, BAND:], before2[:, BAND:]),
        mixed(earlier1[:, BAND:], earlier2[:, BAND:]),
    ]
    operands2 = (cols2, cols2, before2, earlier2, *values2)
    places2 = (0, 1, 0, 0, 0, 0, 0)
    heads2, exact2, sums2 = attend(first, low, operands2, places2)
    stream2, kept2 = tail_forward(
        stream1, heads2.reshape(D, WIN), outs2, out_bias2, norm_gain2, norm_bias2,
        ups2, up_biases2, downs2,
    )
    block_output = stream2.astype(BF16)

    grad, rounded, grad_heads, mats2, up_grads2, small2 = tail_backward(
        cotangent.astype(F32), kept2, outs2, norm_gain2, ups2, downs2
    )
    mats2 = reduce_shards(mats2)
    dq2, dk2, dk2_before, dk2_earlier, dv2, dv2_before, dv2_earlier = attend_back(
        first, low, operands2, places2, exact2, grad_heads.reshape(4, BAND, WIN), sums2
    )
    grad_out2 = dot(heads2.reshape(D, WIN), rounded, 1, 0).astype(BF16).reshape(4, BAND, D)

    def fresh_part(grads):
        return grads[2:].reshape(4, BAND // 2, WIN)

    def join2(keys, values):
        return jnp.concatenate([keys, fresh_part(values)], axis=1)

    kv2 = join2(dk2, dv2) + pass_home(
        join2(dk2_before, dv2_before), join2(dk2_earlier, dv2_earlier)
    )
    dcols2 = jnp.concatenate([dq2, kv2], axis=1)
    bias_grad2 = jnp.sum(dcols2, axis=2)
    dcols2 = dcols2.astype(BF16)
    grad_front2 = dot(dcols2.reshape(-1, WIN), normed2, 1, 0).astype(BF16).reshape(4, n_front2, D)
    attn2 = [
        jnp.pad(jnp.concatenate(pair), ((0, D - BAND - n_front2), (0, 0)))
        for pair in zip(by_distance(grad_out2), by_distance(grad_front2), strict=True)
    ]
    attn2 = reduce_shards(attn2)
    normed_grad = dot(dcols2.reshape(-1, WIN), front2.reshape(-1, D), 0, 0)
    middle, gain_front2, shift_front2 = norm_back(normed_grad, unit2, scale2, norm_gain2[0])
    grad = grad + middle

    grad, rounded, grad_heads, mats1, up_grads1, small1 = tail_backward(
        grad, kept1, outs1, norm_gain1, ups1, downs1
    )
    mats1 = reduce_shards(mats1)
    dq1, dk1, dk1_before, dk1_earlier, dv1, dv1_before, dv1_earlier = attend_back(
        first, low, operands1, places1, exact1, grad_heads.reshape(4, BAND, WIN), sums1
    )
    grad_out1 = dot(heads1.reshape(D, WIN), rounded, 1, 0).astype(BF16).reshape(4, BAND, D)

    def reused(values, grads):
        heads = values.astype(F32).reshape(-1, HD, WIN)
        given = grads[:2].astype(F32).reshape(-1, HD, WIN)
        taken = jnp.arange(heads.shape[0])[:, None] == reuse_heads[None, :]
        for n in range(REUSE):
            heads = heads + jnp.where(taken[:, n, None, None], given[n], 0.0)
        return heads.reshape(values.shape)

    def join1(keys, values, grads):
        return jnp.concatenate([keys, reused(values, grads).astype(keys.dtype)], axis=1)

    kv1 = join1(dk1, dv1, dv2) + pass_home(
        join1(dk1_before, dv1_before, dv2_before), join1(dk1_earlier, dv1_earlier, dv2_earlier)
    )
    dcols1 = jnp.concatenate([dq1, kv1], axis=1)
    bias_grad1 = jnp.sum(dcols1, axis=2)
    dcols1 = dcols1.astype(BF16)
    grad_front1 = dot(dcols1.reshape(-1, WIN), normed1, 1, 0).astype(BF16).reshape(4, n_front1, D)
    attn1 = [
        jnp.concatenate(pair)
        for pair in zip(by_distance(grad_out1), by_distance(grad_front1), strict=True)
    ]
    attn1 = reduce_shards(attn1)
    normed_grad = dot(dcols1.reshape(-1, WIN), front1.reshape(-1, D), 0, 0)
    middle, gain_front1, shift_front1 = norm_back(normed_grad, unit1, scale1, norm_gain1[0])
    input_grad = (grad + middle).astype(BF16)

    vectors = [
        gain_front1, small1[0], shift_front1, small1[1], small1[2], small1[3],
        gain_front2, small2[0], shift_front2, small2[1], small2[2], small2[3],
        bias_grad1[:, :BAND].reshape(-1), bias_grad1[:, 2 * BAND :].reshape(-1),
        bias_grad2[:, :BAND].reshape(-1), bias_grad2[:, 2 * BAND :].reshape(-1),
        in_order(up_grads1).reshape(-1), in_order(up_grads2).reshape(-1),
    ]
    lengths = [vector.shape[0] for vector in vectors]
    packed = jnp.concatenate(vectors)
    filler = (-packed.shape[0]) % 1024
    packed = sum_all(jnp.pad(packed, (0, filler)).reshape(-1, 128)).reshape(-1)
    sums, at = [], 0
    for length in lengths:
        sums.append(packed[at : at + length])
        at += length
    me = lax.axis_index("mp")

    def mine(vector):
        return lax.dynamic_index_in_dim(vector.reshape(4, -1), me, 0, keepdims=False)

    def pair(i):
        return jnp.stack([sums[i], sums[i + 1]])

    mats1, attn1 = mats1.astype(F32), attn1.astype(F32)
    mats2, attn2 = mats2.astype(F32), attn2.astype(F32)
    return (
        block_output,
        input_grad,
        pair(0),
        pair(2),
        turned(attn1[BAND : BAND + n_front1].reshape(3, BAND, D)),
        jnp.stack([mine(sums[12]), mine(sums[13])]),
        attn1[:BAND],
        pair(4),
        mats1[:D],
        mine(sums[16]),
        mats1[D:],
        pair(6),
        pair(8),
        turned(attn2[BAND : 3 * BAND].reshape(2, BAND, D)),
        mine(sums[14]),
        turned(attn2[3 * BAND : BAND + n_front2]),
        mine(sums[15]),
        attn2[:BAND],
        pair(10),
        mats2[:D],
        mine(sums[17]),
        mats2[D:],
    )


def solution(mesh):
    rows = P(("dp", "ctx", "mp"), None)
    placed = (
        rows, rows, P(("dp", "ctx"), None), P(),
        P(), P(), P(None, None, "mp"), P(None, "mp"), P("mp", None), P(),
        P(None, "mp"), P("mp"), P("mp", None),
        P(), P(), P(None, None, "mp"), P("mp"), P(None, "mp"), P("mp"),
        P("mp", None), P(), P(None, "mp"), P("mp"), P("mp", None),
    )
    given = (
        rows, rows,
        P(), P(), P(None, None, "mp"), P(None, "mp"), P("mp", None), P(),
        P(None, "mp"), P("mp"), P("mp", None),
        P(), P(), P(None, None, "mp"), P("mp"), P(None, "mp"), P("mp"),
        P("mp", None), P(), P(None, "mp"), P("mp"), P("mp", None),
    )
    return jax.shard_map(shards, mesh=mesh, in_specs=placed, out_specs=given, check_vma=False)
```

```python
import functools

import jax
import jax.numpy as jnp
from jax import lax
from jax.experimental import pallas as pl
from jax.experimental.pallas import tpu as pltpu
from jax.sharding import PartitionSpec as P

D = 768
HD = 64
REUSE = 6
WIN = 512
EARLY = 2
GROUP = 3
BAND = GROUP * HD
TILE = 256
TILES = 3 * WIN // TILE
EPS = 1e-05
SCALE = HD**-0.5
F32 = jnp.float32
BF16 = jnp.bfloat16


def swap(value, axis, bit):
    devices = range(lax.axis_size(axis))
    return lax.ppermute(value, axis, [(i, i ^ bit) for i in devices])


def in_order(parts):
    return jnp.concatenate(by_distance(jnp.stack(parts)))


def by_distance(stacked):
    me = lax.axis_index("mp")
    return [
        lax.dynamic_index_in_dim(stacked, me ^ distance, 0, keepdims=False)
        for distance in range(4)
    ]


def flip(position, bit):
    return position + bit * (1 - 2 * ((position // bit) % 2))


def remote(source, target, sent, received, device):
    return pltpu.make_async_remote_copy(
        src_ref=source, dst_ref=target, send_sem=sent, recv_sem=received,
        device_id=device, device_id_type=pl.DeviceIdType.MESH,
    )


def meet(devices):
    barrier = pltpu.get_barrier_semaphore()
    for device in devices:
        pl.semaphore_signal(barrier, inc=1, device_id=device, device_id_type=pl.DeviceIdType.MESH)
    pl.semaphore_wait(barrier, len(devices))


def dot(left, right, left_dim, right_dim):
    return lax.dot_general(
        left, right, (((left_dim,), (right_dim,)), ((), ())), preferred_element_type=F32
    )


def norm_rows(value, gain, shift):
    mean = jnp.mean(value, axis=-1, keepdims=True)
    centred = value - mean
    spread = jnp.mean(centred * centred, axis=-1, keepdims=True)
    scale = lax.rsqrt(spread + EPS)
    unit = centred * scale
    return (unit * gain + shift).astype(BF16), unit, scale


def norm_back(grad, unit, scale, gain):
    scaled = grad * gain
    inner = (
        scaled
        - jnp.mean(scaled, axis=-1, keepdims=True)
        - unit * jnp.mean(scaled * unit, axis=-1, keepdims=True)
    )
    return scale * inner, jnp.sum(grad * unit, axis=0), jnp.sum(grad, axis=0)


def attend_kernel(first_ref, lo_ref, q_ref, k0, k1, k2, v0, v1, v2, out_ref, exact_ref, sum_ref, top, total, acc):
    keys, values = (k2, k1, k0), (v2, v1, v0)
    for t in range(WIN // TILE):
        cols = slice(t * TILE, (t + 1) * TILE)
        low = lo_ref[:, cols]
        place = 2 * WIN + t * TILE + lax.broadcasted_iota(jnp.int32, (1, TILE), 1)
        last = 2 * WIN // TILE + t

        def scores(kt, j):
            rows = slice(j * HD, (j + 1) * HD)
            span = slice(kt % 2 * TILE, (kt % 2 + 1) * TILE)
            return dot(keys[kt // 2][0, rows, span], q_ref[0, rows, cols] * SCALE, 0, 0)

        def tile(kt):
            spot = kt * TILE + lax.broadcasted_iota(jnp.int32, (TILE, TILE), 0)
            keep = spot >= low
            if kt == last:
                keep = keep & (spot <= place)
            span = slice(kt % 2 * TILE, (kt % 2 + 1) * TILE)
            for j in range(GROUP):
                rows = slice(j * HD, (j + 1) * HD)
                raw = jnp.where(keep, scores(kt, j), -jnp.inf)
                peak = jnp.max(raw, axis=0, keepdims=True)
                if kt != last:
                    before = top[j]
                    peak = jnp.maximum(peak, before)
                powers = jnp.exp(raw - peak)
                added = jnp.sum(powers, axis=0, keepdims=True)
                result = dot(values[kt // 2][0, rows, span], powers.astype(BF16), 1, 0)
                if kt != last:
                    shrink = jnp.exp(before - peak)
                    added = added + total[j] * shrink
                    result = result + acc[j] * shrink
                top[j] = peak
                total[j] = added
                acc[j] = result

        tile(last)
        for kt in reversed(range(last)):
            pl.when(kt >= first_ref[t])(functools.partial(tile, kt))
        for j in range(GROUP):
            rows = slice(j * HD, (j + 1) * HD)
            result = acc[j] / total[j]
            out_ref[0, rows, cols] = result.astype(BF16)
            exact_ref[0, rows, cols] = result
            sum_ref[0, j : j + 1, cols] = top[j] + jnp.log(total[j])


def attend_back_kernel(
    first_ref, lo_ref, q_ref, k0, k1, k2, v0, v1, v2, out_ref, grad_ref, sum_ref,
    dq_ref, dk0, dk1, dk2, dv0, dv1, dv2, acc_k, acc_v, acc_q,
):
    keys, values = (k2, k1, k0), (v2, v1, v0)
    acc_k[...] = jnp.zeros_like(acc_k)
    acc_v[...] = jnp.zeros_like(acc_v)
    for t in range(WIN // TILE):
        cols = slice(t * TILE, (t + 1) * TILE)
        low = lo_ref[:, cols]
        place = 2 * WIN + t * TILE + lax.broadcasted_iota(jnp.int32, (1, TILE), 1)
        last = 2 * WIN // TILE + t

        def tile(kt):
            spot = kt * TILE + lax.broadcasted_iota(jnp.int32, (TILE, TILE), 0)
            keep = spot >= low
            if kt == last:
                keep = keep & (spot <= place)
            span = slice(kt % 2 * TILE, (kt % 2 + 1) * TILE)
            for j in range(GROUP):
                rows = slice(j * HD, (j + 1) * HD)
                key = keys[kt // 2][0, rows, span]
                query = q_ref[0, rows, cols] * SCALE
                grad = grad_ref[0, rows, cols]
                inner = jnp.sum(
                    grad.astype(F32) * out_ref[0, rows, cols], axis=0, keepdims=True
                )
                raw = jnp.where(keep, dot(key, query, 0, 0), -jnp.inf)
                weights = jnp.exp(raw - sum_ref[0, j : j + 1, cols])
                grad_weights = dot(values[kt // 2][0, rows, span], grad, 0, 0)
                low_grad = (weights * (grad_weights - inner)).astype(BF16)
                acc_v[kt, rows, :] += dot(grad, weights.astype(BF16), 1, 1)
                acc_k[kt, rows, :] += dot(query, low_grad, 1, 1)
                result = dot(key, low_grad, 1, 0)
                if kt != last:
                    result = result + acc_q[j]
                acc_q[j] = result

        tile(last)
        for kt in reversed(range(last)):
            pl.when(kt >= first_ref[t])(functools.partial(tile, kt))
        for j in range(GROUP):
            rows = slice(j * HD, (j + 1) * HD)
            dq_ref[0, rows, cols] = acc_q[j] * SCALE
    for part, (dk, dv) in enumerate(((dk2, dv2), (dk1, dv1), (dk0, dv0))):
        for half in range(2):
            span = slice(half * TILE, (half + 1) * TILE)
            dk[0, :, span] = acc_k[2 * part + half].astype(dk.dtype)
            dv[0, :, span] = acc_v[2 * part + half].astype(dv.dtype)


def band(place):
    return pl.BlockSpec((1, BAND, WIN), lambda s, *_: (s, place, 0))


LOW = pl.BlockSpec((1, WIN), lambda s, *_: (0, 0))
SUMS = pl.BlockSpec((1, 8, WIN), lambda s, *_: (s, 0, 0))


def attend(first, low, operands, places):
    return pl.pallas_call(
        attend_kernel,
        grid_spec=pltpu.PrefetchScalarGridSpec(
            num_scalar_prefetch=1,
            grid=(4,),
            in_specs=[LOW] + [band(p) for p in places],
            out_specs=[band(0), band(0), SUMS],
            scratch_shapes=[
                pltpu.VMEM((GROUP, 1, TILE), F32),
                pltpu.VMEM((GROUP, 1, TILE), F32),
                pltpu.VMEM((GROUP, HD, TILE), F32),
            ],
        ),
        out_shape=[
            jax.ShapeDtypeStruct((4, BAND, WIN), BF16),
            jax.ShapeDtypeStruct((4, BAND, WIN), F32),
            jax.ShapeDtypeStruct((4, 8, WIN), F32),
        ],
        compiler_params=pltpu.CompilerParams(vmem_limit_bytes=32 * 1024 * 1024),
        name="attend",
    )(first, low, *operands)


def attend_back(first, low, operands, places, heads, grad_heads, sums):
    kinds = (F32, F32, BF16, BF16, F32, BF16, BF16)
    return pl.pallas_call(
        attend_back_kernel,
        grid_spec=pltpu.PrefetchScalarGridSpec(
            num_scalar_prefetch=1,
            grid=(4,),
            in_specs=[LOW] + [band(p) for p in places] + [band(0), band(0), SUMS],
            out_specs=[band(0)] * 7,
            scratch_shapes=[
                pltpu.VMEM((TILES, BAND, TILE), F32),
                pltpu.VMEM((TILES, BAND, TILE), F32),
                pltpu.VMEM((GROUP, HD, TILE), F32),
            ],
        ),
        out_shape=[jax.ShapeDtypeStruct((4, BAND, WIN), kind) for kind in kinds],
        compiler_params=pltpu.CompilerParams(vmem_limit_bytes=32 * 1024 * 1024),
        name="attend_back",
    )(first, low, *operands, heads, grad_heads, sums)


def front_kernel(n_more, *refs):
    refs = list(refs)

    def take(count):
        taken = refs[:count]
        del refs[:count]
        return taken

    ctx, dp, mp = (lax.axis_index(axis) for axis in ("ctx", "dp", "mp"))
    (normed,) = take(1)
    near, far, last = {"mp": flip(mp, 1)}, {"mp": flip(mp, 2)}, {"mp": 3 - mp}
    window = {"ctx": 1 - ctx}
    order = (mp, flip(mp, 1), flip(mp, 2), 3 - mp)
    if n_more:
        fixed_own = take(3)
        more_own = take(n_more)
        cols, before, earlier = take(3)
        fixed = take(3)
        more = take(n_more)
        kv_out, kv_in, on_out, on_in, f_out, f_in, m_out, m_in = refs
        front, bias, _ = fixed
        meet([near, far, last, window, {"dp": flip(dp, 1)}])
    else:
        front, bias = take(2)
        cols, before, earlier = take(3)
        kv_out, kv_in, on_out, on_in = refs
        meet([near, last, window])

    if n_more:
        def whole(k, way, device):
            return remote(fixed_own[k], fixed[k].at[mp], f_out.at[k, way], f_in.at[k, way], device)

        def onward():
            there = front.at[flip(mp, 2)]
            return remote(there, there, f_out.at[0, 2], f_in.at[0, 2], near)

        whole(0, 1, far).start()
        whole(0, 0, near).start()
        for k in (1, 2):
            for way, device in enumerate((near, far, last)):
                whole(k, way, device).start()

        bit = lax.rem(dp, 2)
        first = [(bit, {"dp": flip(dp, 1)}), (ctx, window)]

        def sizes(a):
            rows = more_own[a].shape[0]
            (low, low_device), (high, high_device) = first if a % 2 else first[::-1]
            return rows, rows // 4, rows // 2, low, low_device, high, high_device

        def beside(a):
            return remote(more_own[a], more[a].at[mp], m_out.at[a, 0], m_in.at[a, 0], near)

        def across(a):
            rows, quarter, half, low, _, high, _ = sizes(a)
            here = pl.ds(pl.multiple_of(high * half + low * quarter, 16), quarter)
            return remote(
                more_own[a].at[here], more[a].at[mp, here], m_out.at[a, 1], m_in.at[a, 1], far
            )

        def widen(a):
            rows, quarter, half, low, device, high, _ = sizes(a)
            here = pl.ds(pl.multiple_of(high * half + low * quarter, 16), quarter)
            there = more[a].at[flip(mp, 2), here]
            return remote(there, there, m_out.at[a, 2], m_in.at[a, 2], device)

        def complete(a):
            rows, quarter, half, low, _, high, device = sizes(a)
            here = pl.ds(pl.multiple_of(high * half, 16), half)
            there = more[a].at[flip(mp, 2), here]
            return remote(there, there, m_out.at[a, 3], m_in.at[a, 3], device)

        def hand_on(a):
            there = more[a].at[flip(mp, 2)]
            return remote(there, there, m_out.at[a, 4], m_in.at[a, 4], near)

        for a in range(EARLY):
            across(a).start()
        for a in range(n_more):
            beside(a).start()
        for k in range(3):
            fixed[k][mp] = fixed_own[k][...]

    kv_rows = before.shape[1]
    from_row = cols.shape[1] - kv_rows
    sends_on = (mp == 1) | (mp == 2)
    sends_window = (mp == 0) & (ctx == 0)
    receives = (mp >= 2) | ((mp == 0) & (ctx == 1))

    def pass_on(slot, device):
        source = cols.at[slot, pl.ds(from_row, kv_rows)]
        return remote(source, before.at[slot], kv_out.at[slot], kv_in.at[slot], device)

    def pass_again(slot):
        return remote(before.at[slot], earlier.at[slot], on_out.at[slot], on_in.at[slot], {"mp": 3})

    for k, slot in enumerate(order):
        if n_more and k == 1:
            for vector in (1, 2):
                for way, device in enumerate((near, far, last)):
                    whole(vector, way, device).wait_recv()
            whole(0, 0, near).wait_recv()
        if n_more and k == 2:
            whole(0, 1, far).wait_recv()
            onward().start()
        if n_more and k == 3:
            onward().wait_recv()
        column = jnp.transpose(bias[slot])[: cols.shape[1], 0:1]
        cols[slot] = (dot(front[slot, : cols.shape[1]], normed[...], 1, 1) + column).astype(BF16)
        pl.when(sends_on)(lambda: pass_on(slot, {"mp": mp + 1}).start())
        pl.when(sends_window)(lambda: pass_on(slot, window).start())

    for a in range(EARLY, n_more):
        across(a).start()
    for a in range(n_more + 2 if n_more else 0):
        if a < n_more:
            across(a).wait_recv()
            widen(a).start()
        if 1 <= a <= n_more:
            widen(a - 1).wait_recv()
            complete(a - 1).start()
        if a >= 2:
            complete(a - 2).wait_recv()
            hand_on(a - 2).start()

    def received():
        for slot in range(4):
            pass_on(slot, window).wait_recv()
            pl.when(mp == 2)(lambda: pass_again(slot).start())

    pl.when(receives)(received)

    def sent(device):
        for slot in range(4):
            pass_on(slot, device).wait_send()

    pl.when(sends_on)(lambda: sent({"mp": mp + 1}))
    pl.when(sends_window)(lambda: sent(window))

    def again_sent():
        for slot in range(4):
            pass_again(slot).wait_send()

    def again_received():
        for slot in range(4):
            pass_again(slot).wait_recv()

    pl.when(mp == 2)(again_sent)
    pl.when(mp == 3)(again_received)
    if n_more:
        for k in range(3):
            for way, device in enumerate((near, far, last)):
                if k or way < 2:
                    whole(k, way, device).wait_send()
        onward().wait_send()
        for a in range(n_more):
            beside(a).wait()
            across(a).wait_send()
            widen(a).wait_send()
            complete(a).wait_send()
            hand_on(a).wait()


def project(normed, front, bias, n_cols, kv_rows, small=None, more=()):
    place = pl.BlockSpec(memory_space=pltpu.VMEM)
    far = pl.BlockSpec(memory_space=pl.ANY)
    dma = pltpu.SemaphoreType.DMA
    fixed = [front, bias] + ([small] if more else [])
    made = [(4, n_cols, WIN), (4, kv_rows, WIN), (4, kv_rows, WIN)]
    made = [jax.ShapeDtypeStruct(shape, BF16) for shape in made]
    scratch = [dma((4,))] * 4
    gathered = []
    if more:
        gathered = [jax.ShapeDtypeStruct((4,) + v.shape, v.dtype) for v in fixed + list(more)]
        scratch += [dma((3, 3))] * 2 + [dma((len(more), 5))] * 2
    return pl.pallas_call(
        functools.partial(front_kernel, len(more)),
        out_shape=made + gathered,
        in_specs=[place] * (1 + len(fixed)) + [far] * len(more),
        out_specs=[place] * (3 + (3 if more else 0)) + [far] * len(more),
        scratch_shapes=scratch,
        compiler_params=pltpu.CompilerParams(
            collective_id=1 if more else 2,
            has_side_effects=True,
            vmem_limit_bytes=48 * 1024 * 1024,
        ),
        name="front_gather" if more else "front",
    )(normed, *fixed, *more)


def routes():
    windows, groups = lax.axis_size("ctx"), lax.axis_size("mp")
    first_home = [(c * groups + 3, c * groups + 2) for c in range(windows)]
    home = [(c * groups + 2, c * groups + 1) for c in range(windows)]
    home += [((c + 1) * groups, c * groups) for c in range(windows - 1)]
    return first_home, home


def pass_home(before, earlier):
    first_home, home = routes()
    near, far = lax.ppermute((before, earlier), ("ctx", "mp"), first_home)
    far = (before.astype(F32) + far.astype(F32)).astype(BF16)
    return near.astype(F32) + lax.ppermute(far, ("ctx", "mp"), home).astype(F32)


def row_starts(lengths):
    part = lax.axis_index("mp")
    place = (part - 1) * WIN + jnp.arange(WIN, dtype=jnp.int32)
    ends = jnp.cumsum(lengths)
    begun = jnp.max(jnp.where(place[:, None] >= ends[None, :], ends[None, :], 0), axis=1)
    document = begun - (part - 1) * WIN + 2 * WIN
    window = jnp.where(lax.axis_index("ctx") > 0, WIN, 2 * WIN)
    low = jnp.where(part == 0, window, document).astype(jnp.int32)
    return low.reshape(1, WIN), low[::TILE] // TILE


def sum_cores(parts):
    own, near, far, last = parts
    near, last = swap(jnp.stack([near, last]), "mp", 1)
    return (
        (own.astype(F32) + near.astype(F32)).astype(BF16),
        (far.astype(F32) + last.astype(F32)).astype(BF16),
    )


def sum_chips(own, far):
    total = own.astype(F32) + swap(far, "mp", 2).astype(F32)
    return lax.psum(total.astype(BF16), ("dp", "ctx"))


def sum_kernel(
    parts, rows, own, far, vec_in, out, vec, from_y, mine, from_x, kept, from_z, from_vec,
    y_out, y_in, x_out, x_in, z_out, z_in, g_out, g_in, h_out, h_in, v_out, v_in,
):
    ctx, dp, mp = (lax.axis_index(axis) for axis in ("ctx", "dp", "mp"))
    n_dp = lax.axis_size("dp")
    half = rows // 2
    piece = half // n_dp
    other_chip, other_window = {"mp": flip(mp, 2)}, {"ctx": 1 - ctx}
    partners = [other_chip, other_window, {"mp": flip(mp, 1)}]
    bit = 1
    while bit < n_dp:
        partners.append({"dp": flip(dp, bit)})
        bit *= 2

    def along(k):
        return {"dp": lax.rem(dp + k, n_dp)}

    def ds(start, size):
        return pl.ds(pl.multiple_of(start, 16), size)

    def span(i, high, at=0, size=half):
        return ds(i * rows + high * half + at * piece, size)

    def to_y(i):
        here = ds(i * rows, rows)
        return remote(far.at[here], from_y.at[here], y_out.at[i], y_in.at[i], other_chip)

    def to_x(i):
        target = from_x.at[ds(i * half, half)]
        return remote(mine.at[span(i, 1 - ctx)], target, x_out.at[i], x_in.at[i], other_window)

    def to_z(i, k):
        other = lax.rem(dp + k, n_dp)
        source = kept.at[ds(i * half + other * piece, piece)]
        target = from_z.at[ds((i * n_dp + k) * piece, piece)]
        return remote(source, target, z_out.at[i, k], z_in.at[i, k], along(k))

    def round_z(i, k):
        here = out.at[span(i, ctx, dp, piece)]
        return remote(here, here, g_out.at[i, k], g_in.at[i, k], along(k))

    def back_x(i):
        here = out.at[span(i, ctx)]
        return remote(here, here, h_out.at[i], h_in.at[i], other_window)

    def each(count, step):
        lax.fori_loop(0, count, lambda i, _: (step(i), 0)[1], 0)

    barrier = pltpu.get_barrier_semaphore()

    def greet(device):
        pl.semaphore_signal(barrier, inc=1, device_id=device, device_id_type=pl.DeviceIdType.MESH)

    for partner in partners[:3]:
        greet(partner)
    each(n_dp - 1, lambda k: greet(along(k + 1)))
    pl.semaphore_wait(barrier, n_dp + 2)

    vec[...] = vec_in[...]
    for hop, partner in enumerate(partners):
        copy = remote(vec, from_vec.at[hop], v_out.at[hop], v_in.at[hop], partner)
        copy.start()
        if hop == 0:
            each(parts, lambda i: to_y(i).start())
        copy.wait()
        vec[...] = vec[...] + from_vec[hop]

    def join(i):
        to_y(i).wait_recv()
        here = ds(i * rows, rows)
        mine[here, :] = (own[here, :].astype(F32) + from_y[here, :].astype(F32)).astype(BF16)
        to_x(i).start()

    def spread(i):
        to_x(i).wait_recv()
        there = ds(i * half, half)
        total = mine[span(i, ctx), :].astype(F32) + from_x[there, :].astype(F32)
        kept[there, :] = total.astype(BF16)
        each(n_dp - 1, lambda k: to_z(i, k + 1).start())

    def gather(i):
        def add(k, total):
            to_z(i, k).wait_recv()
            return total + from_z[ds((i * n_dp + k) * piece, piece), :].astype(F32)

        total = kept[ds(i * half + dp * piece, piece), :].astype(F32)
        out[span(i, ctx, dp, piece), :] = lax.fori_loop(1, n_dp, add, total).astype(BF16)
        each(n_dp - 1, lambda k: round_z(i, k + 1).start())

    def give(i):
        each(n_dp - 1, lambda k: round_z(i, k + 1).wait_recv())
        back_x(i).start()

    def step(i):
        for late, stage in enumerate((join, spread, gather, give)):
            pl.when((i >= late) & (i < parts + late))(functools.partial(stage, i - late))

    each(parts + 3, step)

    def finish(i):
        to_y(i).wait_send()
        to_x(i).wait_send()
        back_x(i).wait()

        def sent(k):
            to_z(i, k + 1).wait_send()
            round_z(i, k + 1).wait_send()

        each(n_dp - 1, sent)

    each(parts, finish)


def sum_replicas(own, far, vectors):
    n_dp = lax.axis_size("dp")
    rows = max(256, 32 * n_dp)
    parts = -(-own.shape[0] // rows)
    total = parts * rows
    hops = 3 + (n_dp - 1).bit_length()
    lanes = own.shape[1]
    own, far = (jnp.pad(v, ((0, total - v.shape[0]), (0, 0))) for v in (own, far))
    place = pl.BlockSpec(memory_space=pltpu.VMEM)
    dma = pltpu.SemaphoreType.DMA
    return pl.pallas_call(
        functools.partial(sum_kernel, parts, rows),
        out_shape=[
            jax.ShapeDtypeStruct((total, lanes), BF16),
            jax.ShapeDtypeStruct(vectors.shape, F32),
        ],
        in_specs=[place, place, place],
        out_specs=[place, place],
        scratch_shapes=[
            pltpu.VMEM((total, lanes), BF16),
            pltpu.VMEM((total, lanes), BF16),
            pltpu.VMEM((total // 2, lanes), BF16),
            pltpu.VMEM((total // 2, lanes), BF16),
            pltpu.VMEM((total // 2, lanes), BF16),
            pltpu.VMEM((hops,) + vectors.shape, F32),
            dma((parts,)), dma((parts,)),
            dma((parts,)), dma((parts,)),
            dma((parts, n_dp)), dma((parts, n_dp)),
            dma((parts, n_dp)), dma((parts, n_dp)),
            dma((parts,)), dma((parts,)),
            dma((hops,)), dma((hops,)),
        ],
        compiler_params=pltpu.CompilerParams(
            collective_id=0, has_side_effects=True, vmem_limit_bytes=56 * 1024 * 1024
        ),
        name="sum_replicas",
    )(own, far, vectors)


def gelu(hidden):
    return jax.nn.gelu(hidden, approximate=True)


def tail_forward(stream, heads, out_weight, out_bias, gain, shift, ups, up_biases, downs):
    stream = stream + dot(heads, out_weight, 0, 0) + out_bias[0]
    normed, unit, scale = norm_rows(stream, gain[1], shift[1])
    hidden, active, total = [], [], out_bias[1]
    for up, bias, down in zip(ups, up_biases, downs, strict=True):
        hidden.append(dot(normed, up, 1, 0) + bias)
        active.append(gelu(hidden[-1]).astype(BF16))
        total = total + dot(active[-1], down, 1, 0)
    return stream + total, (normed, unit, scale, hidden, active)


def tail_backward(grad, kept, out_weight, gain, ups, downs):
    normed, unit, scale, hidden, active = kept
    bias_mlp = jnp.sum(grad, axis=0)
    rounded = grad.astype(BF16)
    mats, up_biases, normed_grad = [], [], 0.0
    for up, down, before, after in zip(ups, downs, hidden, active, strict=True):
        _, pull = jax.vjp(gelu, before)
        grad_hidden = pull(dot(rounded, down, 1, 1))[0]
        up_biases.append(jnp.sum(grad_hidden, axis=0))
        low = grad_hidden.astype(BF16)
        mats.append(
            jnp.concatenate(
                [dot(normed, low, 0, 0).astype(BF16), dot(after, rounded, 0, 0).astype(BF16)]
            )
        )
        normed_grad = normed_grad + dot(low, up, 1, 1)
    middle, gain_grad, shift_grad = norm_back(normed_grad, unit, scale, gain[1])
    grad = grad + middle
    bias_attn = jnp.sum(grad, axis=0)
    rounded = grad.astype(BF16)
    grad_heads = dot(out_weight, rounded, 1, 1).astype(BF16)
    return grad, rounded, grad_heads, mats, up_biases, (gain_grad, shift_grad, bias_attn, bias_mlp)


def turned(weight):
    return jnp.swapaxes(weight, -1, -2)


def shards(
    block_input, cotangent, doc_lengths, reuse_heads,
    norm_gain1, norm_bias1, projections1, front_bias1, out_weight1, out_bias1,
    up_weight1, up_bias1, down_weight1,
    norm_gain2, norm_bias2, query_key2, query_bias2, fresh_value2, value_bias2,
    out_weight2, out_bias2, up_weight2, up_bias2, down_weight2,
):
    low, first = row_starts(doc_lengths[0])

    stream0 = block_input.astype(F32)
    normed1, unit1, scale1 = norm_rows(stream0, norm_gain1[0], norm_bias1[0])
    n_front1, n_front2 = 3 * BAND, 2 * BAND + BAND // 2
    none = jnp.zeros((BAND,), BF16)

    def as_row(pieces):
        row = jnp.concatenate(pieces).astype(F32)
        return jnp.pad(row[None, :], ((0, 7), (0, -row.shape[0] % 128)))

    small = jnp.concatenate([query_bias2, value_bias2, up_bias1, up_bias2])
    small = jnp.pad(small, (0, 16 * 128 - small.shape[0])).reshape(16, 128)
    own_front2 = jnp.concatenate([turned(query_key2).reshape(2 * BAND, D), turned(fresh_value2)])
    own_front2 = jnp.pad(own_front2, ((0, -n_front2 % 64), (0, 0)))
    (
        cols1, before1, earlier1, front1, _, small,
        up1, down1, up2, down2, front2, outs1, outs2,
    ) = project(
        normed1, turned(projections1).reshape(n_front1, D),
        as_row([front_bias1[0], none, front_bias1[1]]), n_front1, 2 * BAND, small,
        (up_weight1, down_weight1, up_weight2, down_weight2, own_front2, out_weight1, out_weight2),
    )
    ups1, downs1, ups2, downs2 = (
        [own] + by_distance(w)[1:]
        for own, w in (
            (up_weight1, up1), (down_weight1, down1), (up_weight2, up2), (down_weight2, down2)
        )
    )
    front2, outs1, outs2 = (
        lax.dynamic_update_index_in_dim(w, own, lax.axis_index("mp"), 0)
        for own, w in ((own_front2, front2), (out_weight1, outs1), (out_weight2, outs2))
    )
    outs1, outs2 = outs1.reshape(D, D), outs2.reshape(D, D)
    small = small.reshape(4, -1)
    at = BAND + BAND // 2
    bias2 = jnp.stack([as_row([small[s, :BAND], none, small[s, BAND:at]]) for s in range(4)])
    up_biases1 = by_distance(small[:, at : at + D])
    up_biases2 = by_distance(small[:, at + D : at + 2 * D])

    operands1 = (cols1, cols1, before1, earlier1, cols1, before1, earlier1)
    places1 = (0, 1, 0, 0, 2, 1, 1)
    heads1, exact1, sums1 = attend(first, low, operands1, places1)
    stream1, kept1 = tail_forward(
        stream0, heads1.reshape(D, WIN), outs1, out_bias1, norm_gain1, norm_bias1,
        ups1, up_biases1, downs1,
    )

    normed2, unit2, scale2 = norm_rows(stream1, norm_gain2[0], norm_bias2[0])
    cols2, before2, earlier2 = project(normed2, front2, bias2, n_front2, n_front2 - BAND)
    front2 = front2[:, :n_front2]

    def mixed(first_values, fresh):
        first_values = first_values.reshape(-1, HD, WIN)
        reused = [
            lax.dynamic_index_in_dim(first_values, reuse_heads[n], 0, keepdims=True)
            for n in range(REUSE)
        ]
        return jnp.concatenate(reused + [fresh.reshape(-1, HD, WIN)]).reshape(4, BAND, WIN)

    values2 = [
        mixed(cols1[:, 2 * BAND :], cols2[:, 2 * BAND :]),
        mixed(before1[:, BAND:], before2[:, BAND:]),
        mixed(earlier1[:, BAND:], earlier2[:, BAND:]),
    ]
    operands2 = (cols2, cols2, before2, earlier2, *values2)
    places2 = (0, 1, 0, 0, 0, 0, 0)
    heads2, exact2, sums2 = attend(first, low, operands2, places2)
    stream2, kept2 = tail_forward(
        stream1, heads2.reshape(D, WIN), outs2, out_bias2, norm_gain2, norm_bias2,
        ups2, up_biases2, downs2,
    )
    block_output = stream2.astype(BF16)

    grad, rounded, grad_heads, mats2, up_grads2, small2 = tail_backward(
        cotangent.astype(F32), kept2, outs2, norm_gain2, ups2, downs2
    )
    mats2 = sum_chips(*sum_cores(mats2))
    dq2, dk2, dk2_before, dk2_earlier, dv2, dv2_before, dv2_earlier = attend_back(
        first, low, operands2, places2, exact2, grad_heads.reshape(4, BAND, WIN), sums2
    )
    grad_out2 = dot(heads2.reshape(D, WIN), rounded, 1, 0).astype(BF16).reshape(4, BAND, D)

    def fresh_part(grads):
        return grads[2:].reshape(4, BAND // 2, WIN)

    def join2(keys, values):
        return jnp.concatenate([keys, fresh_part(values)], axis=1)

    kv2 = join2(dk2, dv2) + pass_home(
        join2(dk2_before, dv2_before), join2(dk2_earlier, dv2_earlier)
    )
    dcols2 = jnp.concatenate([dq2, kv2], axis=1)
    bias_grad2 = jnp.sum(dcols2, axis=2)
    dcols2 = dcols2.astype(BF16)
    grad_front2 = dot(dcols2.reshape(-1, WIN), normed2, 1, 0).astype(BF16).reshape(4, n_front2, D)
    attn2 = [
        jnp.concatenate(pair)
        for pair in zip(by_distance(grad_out2), by_distance(grad_front2), strict=True)
    ]
    attn2 = sum_cores(attn2)
    normed_grad = dot(dcols2.reshape(-1, WIN), front2.reshape(-1, D), 0, 0)
    middle, gain_front2, shift_front2 = norm_back(normed_grad, unit2, scale2, norm_gain2[0])
    grad = grad + middle

    grad, rounded, grad_heads, mats1, up_grads1, small1 = tail_backward(
        grad, kept1, outs1, norm_gain1, ups1, downs1
    )
    mats1 = sum_cores(mats1)
    dq1, dk1, dk1_before, dk1_earlier, dv1, dv1_before, dv1_earlier = attend_back(
        first, low, operands1, places1, exact1, grad_heads.reshape(4, BAND, WIN), sums1
    )
    grad_out1 = dot(heads1.reshape(D, WIN), rounded, 1, 0).astype(BF16).reshape(4, BAND, D)

    def reused(values, grads):
        heads = values.astype(F32).reshape(-1, HD, WIN)
        given = grads[:2].astype(F32).reshape(-1, HD, WIN)
        taken = jnp.arange(heads.shape[0])[:, None] == reuse_heads[None, :]
        for n in range(REUSE):
            heads = heads + jnp.where(taken[:, n, None, None], given[n], 0.0)
        return heads.reshape(values.shape)

    def join1(keys, values, grads):
        return jnp.concatenate([keys, reused(values, grads).astype(keys.dtype)], axis=1)

    kv1 = join1(dk1, dv1, dv2) + pass_home(
        join1(dk1_before, dv1_before, dv2_before), join1(dk1_earlier, dv1_earlier, dv2_earlier)
    )
    dcols1 = jnp.concatenate([dq1, kv1], axis=1)
    bias_grad1 = jnp.sum(dcols1, axis=2)
    dcols1 = dcols1.astype(BF16)
    grad_front1 = dot(dcols1.reshape(-1, WIN), normed1, 1, 0).astype(BF16).reshape(4, n_front1, D)
    attn1 = [
        jnp.concatenate(pair)
        for pair in zip(by_distance(grad_out1), by_distance(grad_front1), strict=True)
    ]
    attn1 = sum_cores(attn1)
    normed_grad = dot(dcols1.reshape(-1, WIN), front1.reshape(-1, D), 0, 0)
    middle, gain_front1, shift_front1 = norm_back(normed_grad, unit1, scale1, norm_gain1[0])
    input_grad = (grad + middle).astype(BF16)

    vectors = [
        gain_front1, small1[0], shift_front1, small1[1], small1[2], small1[3],
        gain_front2, small2[0], shift_front2, small2[1], small2[2], small2[3],
        bias_grad1[:, :BAND].reshape(-1), bias_grad1[:, 2 * BAND :].reshape(-1),
        bias_grad2[:, :BAND].reshape(-1), bias_grad2[:, 2 * BAND :].reshape(-1),
        in_order(up_grads1), in_order(up_grads2),
    ]
    lengths = [vector.shape[0] for vector in vectors]
    packed = jnp.concatenate(vectors)
    filler = (-packed.shape[0]) % 1024
    stack, packed = sum_replicas(
        *(jnp.concatenate(three) for three in zip(attn2, mats1, attn1, strict=True)),
        jnp.pad(packed, (0, filler)).reshape(-1, 128),
    )
    packed = packed.reshape(-1)
    sums, at = [], 0
    for length in lengths:
        sums.append(packed[at : at + length])
        at += length
    me = lax.axis_index("mp")

    def mine(vector):
        return lax.dynamic_index_in_dim(vector.reshape(4, -1), me, 0, keepdims=False)

    def pair(i):
        return jnp.stack([sums[i], sums[i + 1]])

    mats2, stack = mats2.astype(F32), stack.astype(F32)
    rows2, rows1 = BAND + n_front2, BAND + n_front1
    attn2, mats1, attn1 = (
        stack[at : at + size] for at, size in ((0, rows2), (rows2, 2 * D), (rows2 + 2 * D, rows1))
    )
    return (
        block_output,
        input_grad,
        pair(0),
        pair(2),
        turned(attn1[BAND : BAND + n_front1].reshape(3, BAND, D)),
        jnp.stack([mine(sums[12]), mine(sums[13])]),
        attn1[:BAND],
        pair(4),
        mats1[:D],
        mine(sums[16]),
        mats1[D:],
        pair(6),
        pair(8),
        turned(attn2[BAND : 3 * BAND].reshape(2, BAND, D)),
        mine(sums[14]),
        turned(attn2[3 * BAND : BAND + n_front2]),
        mine(sums[15]),
        attn2[:BAND],
        pair(10),
        mats2[:D],
        mine(sums[17]),
        mats2[D:],
    )


def solution(mesh):
    rows = P(("dp", "ctx", "mp"), None)
    placed = (
        rows, rows, P(("dp", "ctx"), None), P(),
        P(), P(), P(None, None, "mp"), P(None, "mp"), P("mp", None), P(),
        P(None, "mp"), P("mp"), P("mp", None),
        P(), P(), P(None, None, "mp"), P("mp"), P(None, "mp"), P("mp"),
        P("mp", None), P(), P(None, "mp"), P("mp"), P("mp", None),
    )
    given = (
        rows, rows,
        P(), P(), P(None, None, "mp"), P(None, "mp"), P("mp", None), P(),
        P(None, "mp"), P("mp"), P("mp", None),
        P(), P(), P(None, None, "mp"), P("mp"), P(None, "mp"), P("mp"),
        P("mp", None), P(), P(None, "mp"), P("mp"), P("mp", None),
    )
    return jax.shard_map(shards, mesh=mesh, in_specs=placed, out_specs=given, check_vma=False)
```

```python
import functools

import jax
import jax.numpy as jnp
from jax import lax
from jax.experimental import pallas as pl
from jax.experimental.pallas import tpu as pltpu
from jax.sharding import PartitionSpec as P

D = 768
HD = 64
REUSE = 6
WIN = 512
EARLY = 2
GROUP = 3
BAND = GROUP * HD
AT_REUSE = 2
AT_FLAG = AT_REUSE + REUSE
AT_GIVEN = AT_FLAG + 4 * GROUP
TILE = 256
TILES = 3 * WIN // TILE
EPS = 1e-05
SCALE = HD**-0.5
F32 = jnp.float32
BF16 = jnp.bfloat16


def swap(value, axis, bit):
    devices = range(lax.axis_size(axis))
    return lax.ppermute(value, axis, [(i, i ^ bit) for i in devices])


def in_order(parts):
    return jnp.concatenate(by_distance(jnp.stack(parts)))


def by_distance(stacked):
    me = lax.axis_index("mp")
    return [
        lax.dynamic_index_in_dim(stacked, me ^ distance, 0, keepdims=False)
        for distance in range(4)
    ]


def flip(position, bit):
    return position + bit * (1 - 2 * ((position // bit) % 2))


def remote(source, target, sent, received, device):
    return pltpu.make_async_remote_copy(
        src_ref=source, dst_ref=target, send_sem=sent, recv_sem=received,
        device_id=device, device_id_type=pl.DeviceIdType.MESH,
    )


def meet(devices):
    barrier = pltpu.get_barrier_semaphore()
    for device in devices:
        pl.semaphore_signal(barrier, inc=1, device_id=device, device_id_type=pl.DeviceIdType.MESH)
    pl.semaphore_wait(barrier, len(devices))


def dot(left, right, left_dim, right_dim):
    return lax.dot_general(
        left, right, (((left_dim,), (right_dim,)), ((), ())), preferred_element_type=F32
    )


def norm_rows(value, gain, shift):
    mean = jnp.mean(value, axis=-1, keepdims=True)
    centred = value - mean
    spread = jnp.mean(centred * centred, axis=-1, keepdims=True)
    scale = lax.rsqrt(spread + EPS)
    unit = centred * scale
    return (unit * gain + shift).astype(BF16), unit, scale


def norm_back(grad, unit, scale, gain):
    scaled = grad * gain
    inner = (
        scaled
        - jnp.mean(scaled, axis=-1, keepdims=True)
        - unit * jnp.mean(scaled * unit, axis=-1, keepdims=True)
    )
    return scale * inner, jnp.sum(grad * unit, axis=0), jnp.sum(grad, axis=0)


def place_values(refs, values):
    if len(refs) == 3:
        for part, ref in enumerate(reversed(refs)):
            values[part] = ref[0]
        return
    group = pl.program_id(0)

    def reused():
        for part in range(3):
            for j in range(GROUP):
                values[part, j * HD : (j + 1) * HD, :] = refs[4 * (2 - part) + j][0]

    def fresh():
        for part in range(3):
            values[part] = refs[4 * (2 - part) + GROUP][0]

    pl.when(group < 2)(reused)
    pl.when(group >= 2)(fresh)


def attend_kernel(n_values, first_ref, lo_ref, q_ref, k0, k1, k2, *refs):
    v_refs = refs[:n_values]
    out_ref, exact_ref, sum_ref, values, raw, top, total, acc = refs[n_values:]
    keys = (k2, k1, k0)
    place_values(v_refs, values)
    for t in range(WIN // TILE):
        cols = slice(t * TILE, (t + 1) * TILE)
        low = lo_ref[:, cols]
        place = 2 * WIN + t * TILE + lax.broadcasted_iota(jnp.int32, (1, TILE), 1)
        last = 2 * WIN // TILE + t

        def score(kt):
            spot = kt * TILE + lax.broadcasted_iota(jnp.int32, (TILE, TILE), 0)
            keep = spot >= low
            if kt == last:
                keep = keep & (spot <= place)
            span = slice(kt % 2 * TILE, (kt % 2 + 1) * TILE)
            for j in range(GROUP):
                rows = slice(j * HD, (j + 1) * HD)
                found = dot(keys[kt // 2][0, rows, span], q_ref[0, rows, cols] * SCALE, 0, 0)
                found = jnp.where(keep, found, -jnp.inf)
                raw[j, kt] = found
                peak = jnp.max(found.reshape(TILE // 8, 8, TILE), axis=0)
                top[j] = peak if kt == last else jnp.maximum(top[j], peak)

        def weigh(kt):
            span = slice(kt % 2 * TILE, (kt % 2 + 1) * TILE)
            for j in range(GROUP):
                rows = slice(j * HD, (j + 1) * HD)
                powers = jnp.exp(raw[j, kt] - top[j, 0:1])
                added = jnp.sum(powers.reshape(TILE // 8, 8, TILE), axis=0)
                result = dot(values[kt // 2, rows, span], powers.astype(BF16), 1, 0)
                total[j] = added if kt == last else total[j] + added
                acc[j] = result if kt == last else acc[j] + result

        for stage in (score, weigh):
            stage(last)
            for kt in reversed(range(last)):
                pl.when(kt >= first_ref[t])(functools.partial(stage, kt))
            if stage is score:
                for j in range(GROUP):
                    top[j] = jnp.broadcast_to(jnp.max(top[j], axis=0, keepdims=True), (8, TILE))
        for j in range(GROUP):
            rows = slice(j * HD, (j + 1) * HD)
            whole = jnp.sum(total[j], axis=0, keepdims=True)
            result = acc[j] / whole
            out_ref[0, rows, cols] = result.astype(BF16)
            exact_ref[0, rows, cols] = result
            sum_ref[0, j : j + 1, cols] = top[j, 0:1] + jnp.log(whole)


def attend_back_kernel(n_values, n_given, first_ref, lo_ref, _, q_ref, k0, k1, k2, *refs):
    v_refs, refs = refs[:n_values], refs[n_values:]
    given, refs = refs[:n_given], refs[n_given:]
    (
        out_ref, grad_ref, sum_ref, dq_ref, dk0, dk1, dk2, dv0, dv1, dv2,
        values, acc_k, acc_v, acc_q,
    ) = refs
    keys = (k2, k1, k0)
    place_values(v_refs, values)
    acc_k[...] = jnp.zeros_like(acc_k)
    acc_v[...] = jnp.zeros_like(acc_v)
    for i, ref in enumerate(given):
        part, j = 2 - i // GROUP, i % GROUP
        head = GROUP * pl.program_id(0) + j

        def add(part=part, j=j, ref=ref):
            for half in range(2):
                span = slice(half * TILE, (half + 1) * TILE)
                acc_v[2 * part + half, j * HD : (j + 1) * HD, :] = ref[0, :, span].astype(F32)

        pl.when(first_ref[AT_FLAG + head] == 1)(add)
    for t in range(WIN // TILE):
        cols = slice(t * TILE, (t + 1) * TILE)
        low = lo_ref[:, cols]
        place = 2 * WIN + t * TILE + lax.broadcasted_iota(jnp.int32, (1, TILE), 1)
        last = 2 * WIN // TILE + t

        def tile(kt):
            spot = kt * TILE + lax.broadcasted_iota(jnp.int32, (TILE, TILE), 0)
            keep = spot >= low
            if kt == last:
                keep = keep & (spot <= place)
            span = slice(kt % 2 * TILE, (kt % 2 + 1) * TILE)
            for j in range(GROUP):
                rows = slice(j * HD, (j + 1) * HD)
                key = keys[kt // 2][0, rows, span]
                query = q_ref[0, rows, cols] * SCALE
                grad = grad_ref[0, rows, cols]
                inner = jnp.sum(
                    grad.astype(F32) * out_ref[0, rows, cols], axis=0, keepdims=True
                )
                raw = jnp.where(keep, dot(key, query, 0, 0), -jnp.inf)
                weights = jnp.exp(raw - sum_ref[0, j : j + 1, cols])
                grad_weights = dot(values[kt // 2, rows, span], grad, 0, 0)
                low_grad = (weights * (grad_weights - inner)).astype(BF16)
                acc_v[kt, rows, :] += dot(grad, weights.astype(BF16), 1, 1)
                acc_k[kt, rows, :] += dot(query, low_grad, 1, 1)
                result = dot(key, low_grad, 1, 0)
                if kt != last:
                    result = result + acc_q[j]
                acc_q[j] = result

        tile(last)
        for kt in reversed(range(last)):
            pl.when(kt >= first_ref[t])(functools.partial(tile, kt))
        for j in range(GROUP):
            rows = slice(j * HD, (j + 1) * HD)
            dq_ref[0, rows, cols] = acc_q[j] * SCALE
    for part, (dk, dv) in enumerate(((dk2, dv2), (dk1, dv1), (dk0, dv0))):
        for half in range(2):
            span = slice(half * TILE, (half + 1) * TILE)
            dk[0, :, span] = acc_k[2 * part + half].astype(dk.dtype)
            dv[0, :, span] = acc_v[2 * part + half].astype(dv.dtype)


def band(place):
    return pl.BlockSpec((1, BAND, WIN), lambda s, *_: (s, place, 0))


LOW = pl.BlockSpec((1, WIN), lambda s, *_: (0, 0))
SUMS = pl.BlockSpec((1, 8, WIN), lambda s, *_: (s, 0, 0))


def head_block(stride, offset, j):
    def at(s, scalars):
        head = scalars[AT_REUSE + jnp.minimum(GROUP * s + j, REUSE - 1)]
        return (head // GROUP * stride + offset + head % GROUP, 0, 0)

    return pl.BlockSpec((1, HD, WIN), at)


def given_block(j):
    return pl.BlockSpec(
        (1, HD, WIN), lambda s, scalars: (scalars[AT_GIVEN + GROUP * s + j], 0, 0)
    )


FRESH = pl.BlockSpec((1, BAND, WIN), lambda s, *_: (jnp.maximum(s - 2, 0), 0, 0))


def values_of(cols, before, earlier):
    return [cols, before, earlier], [band(2), band(1), band(1)]


def values_mixed(firsts, freshes):
    arrays, specs = [], []
    for k, (first, fresh) in enumerate(zip(firsts, freshes, strict=True)):
        stride, offset = (3 * GROUP, 2 * GROUP) if k == 0 else (2 * GROUP, GROUP)
        arrays += [first.reshape(-1, HD, WIN)] * GROUP + [fresh]
        specs += [head_block(stride, offset, j) for j in range(GROUP)] + [FRESH]
    return arrays, specs


def attend(scalars, low, front, values):
    arrays, specs = values
    return pl.pallas_call(
        functools.partial(attend_kernel, len(arrays)),
        grid_spec=pltpu.PrefetchScalarGridSpec(
            num_scalar_prefetch=1,
            grid=(4,),
            in_specs=[LOW, band(0), band(1), band(0), band(0)] + specs,
            out_specs=[band(0), band(0), SUMS],
            scratch_shapes=[
                pltpu.VMEM((3, BAND, WIN), BF16),
                pltpu.VMEM((GROUP, TILES, TILE, TILE), F32),
                pltpu.VMEM((GROUP, 8, TILE), F32),
                pltpu.VMEM((GROUP, 8, TILE), F32),
                pltpu.VMEM((GROUP, HD, TILE), F32),
            ],
        ),
        out_shape=[
            jax.ShapeDtypeStruct((4, BAND, WIN), BF16),
            jax.ShapeDtypeStruct((4, BAND, WIN), F32),
            jax.ShapeDtypeStruct((4, 8, WIN), F32),
        ],
        compiler_params=pltpu.CompilerParams(vmem_limit_bytes=32 * 1024 * 1024),
        name="attend",
    )(scalars, low, front[0], *front, *arrays)


def attend_back(after, scalars, low, front, values, given, heads, grad_heads, sums):
    kinds = (F32, F32, BF16, BF16, F32, BF16, BF16)
    arrays, specs = values
    given_arrays = [v.reshape(-1, HD, WIN) for v in given for _ in range(GROUP)]
    given_specs = [given_block(j) for _ in given for j in range(GROUP)]
    return pl.pallas_call(
        functools.partial(attend_back_kernel, len(arrays), len(given_arrays)),
        grid_spec=pltpu.PrefetchScalarGridSpec(
            num_scalar_prefetch=1,
            grid=(4,),
            in_specs=[LOW, pl.BlockSpec(memory_space=pl.ANY)]
            + [band(0), band(1), band(0), band(0)] + specs + given_specs
            + [band(0), band(0), SUMS],
            out_specs=[band(0)] * 7,
            scratch_shapes=[
                pltpu.VMEM((3, BAND, WIN), BF16),
                pltpu.VMEM((TILES, BAND, TILE), F32),
                pltpu.VMEM((TILES, BAND, TILE), F32),
                pltpu.VMEM((GROUP, HD, TILE), F32),
            ],
        ),
        out_shape=[jax.ShapeDtypeStruct((4, BAND, WIN), kind) for kind in kinds],
        compiler_params=pltpu.CompilerParams(vmem_limit_bytes=32 * 1024 * 1024),
        name="attend_back",
    )(scalars, low, after, front[0], *front, *arrays, *given_arrays, heads, grad_heads, sums)


def front_kernel(n_more, *refs):
    refs = list(refs)

    def take(count):
        taken = refs[:count]
        del refs[:count]
        return taken

    ctx, dp, mp = (lax.axis_index(axis) for axis in ("ctx", "dp", "mp"))
    (normed,) = take(1)
    near, far, last = {"mp": flip(mp, 1)}, {"mp": flip(mp, 2)}, {"mp": 3 - mp}
    window = {"ctx": 1 - ctx}
    order = (mp, flip(mp, 1), flip(mp, 2), 3 - mp)
    if n_more:
        fixed_own = take(3)
        more_own = take(n_more)
        cols, before, earlier = take(3)
        fixed = take(3)
        more = take(n_more)
        kv_out, kv_in, on_out, on_in, f_out, f_in, m_out, m_in = refs
        front, bias, _ = fixed
        meet([near, far, last, window, {"dp": flip(dp, 1)}])
    else:
        front, bias = take(2)
        cols, before, earlier = take(3)
        kv_out, kv_in, on_out, on_in = refs
        meet([near, last, window])

    if n_more:
        def whole(k, way, device):
            return remote(fixed_own[k], fixed[k].at[mp], f_out.at[k, way], f_in.at[k, way], device)

        def onward():
            there = front.at[flip(mp, 2)]
            return remote(there, there, f_out.at[0, 2], f_in.at[0, 2], near)

        whole(0, 1, far).start()
        whole(0, 0, near).start()
        for k in (1, 2):
            for way, device in enumerate((near, far, last)):
                whole(k, way, device).start()

        bit = lax.rem(dp, 2)
        first = [(bit, {"dp": flip(dp, 1)}), (ctx, window)]

        def sizes(a):
            rows = more_own[a].shape[0]
            (low, low_device), (high, high_device) = first if a % 2 else first[::-1]
            return rows, rows // 4, rows // 2, low, low_device, high, high_device

        def beside(a):
            return remote(more_own[a], more[a].at[mp], m_out.at[a, 0], m_in.at[a, 0], near)

        def across(a):
            rows, quarter, half, low, _, high, _ = sizes(a)
            here = pl.ds(pl.multiple_of(high * half + low * quarter, 16), quarter)
            return remote(
                more_own[a].at[here], more[a].at[mp, here], m_out.at[a, 1], m_in.at[a, 1], far
            )

        def widen(a):
            rows, quarter, half, low, device, high, _ = sizes(a)
            here = pl.ds(pl.multiple_of(high * half + low * quarter, 16), quarter)
            there = more[a].at[flip(mp, 2), here]
            return remote(there, there, m_out.at[a, 2], m_in.at[a, 2], device)

        def complete(a):
            rows, quarter, half, low, _, high, device = sizes(a)
            here = pl.ds(pl.multiple_of(high * half, 16), half)
            there = more[a].at[flip(mp, 2), here]
            return remote(there, there, m_out.at[a, 3], m_in.at[a, 3], device)

        def hand_on(a):
            there = more[a].at[flip(mp, 2)]
            return remote(there, there, m_out.at[a, 4], m_in.at[a, 4], near)

        for a in range(EARLY):
            across(a).start()
        for a in range(n_more):
            beside(a).start()
        for k in range(3):
            fixed[k][mp] = fixed_own[k][...]

    kv_rows = before.shape[1]
    from_row = cols.shape[1] - kv_rows
    sends_on = (mp == 1) | (mp == 2)
    sends_window = (mp == 0) & (ctx == 0)
    receives = (mp >= 2) | ((mp == 0) & (ctx == 1))

    def pass_on(slot, device):
        source = cols.at[slot, pl.ds(from_row, kv_rows)]
        return remote(source, before.at[slot], kv_out.at[slot], kv_in.at[slot], device)

    def pass_again(slot):
        return remote(before.at[slot], earlier.at[slot], on_out.at[slot], on_in.at[slot], {"mp": 3})

    for k, slot in enumerate(order):
        if n_more and k == 1:
            for vector in (1, 2):
                for way, device in enumerate((near, far, last)):
                    whole(vector, way, device).wait_recv()
            whole(0, 0, near).wait_recv()
        if n_more and k == 2:
            whole(0, 1, far).wait_recv()
            onward().start()
        if n_more and k == 3:
            onward().wait_recv()
        column = jnp.transpose(bias[slot])[: cols.shape[1], 0:1]
        cols[slot] = (dot(front[slot, : cols.shape[1]], normed[...], 1, 1) + column).astype(BF16)
        pl.when(sends_on)(lambda: pass_on(slot, {"mp": mp + 1}).start())
        pl.when(sends_window)(lambda: pass_on(slot, window).start())

    for a in range(EARLY, n_more):
        across(a).start()
    for a in range(n_more + 2 if n_more else 0):
        if a < n_more:
            across(a).wait_recv()
            widen(a).start()
        if 1 <= a <= n_more:
            widen(a - 1).wait_recv()
            complete(a - 1).start()
        if a >= 2:
            complete(a - 2).wait_recv()
            hand_on(a - 2).start()

    def received():
        for slot in range(4):
            pass_on(slot, window).wait_recv()
            pl.when(mp == 2)(lambda: pass_again(slot).start())

    pl.when(receives)(received)

    def sent(device):
        for slot in range(4):
            pass_on(slot, device).wait_send()

    pl.when(sends_on)(lambda: sent({"mp": mp + 1}))
    pl.when(sends_window)(lambda: sent(window))

    def again_sent():
        for slot in range(4):
            pass_again(slot).wait_send()

    def again_received():
        for slot in range(4):
            pass_again(slot).wait_recv()

    pl.when(mp == 2)(again_sent)
    pl.when(mp == 3)(again_received)
    if n_more:
        for k in range(3):
            for way, device in enumerate((near, far, last)):
                if k or way < 2:
                    whole(k, way, device).wait_send()
        onward().wait_send()
        for a in range(n_more):
            beside(a).wait()
            across(a).wait_send()
            widen(a).wait_send()
            complete(a).wait_send()
            hand_on(a).wait()


def project(normed, front, bias, n_cols, kv_rows, small=None, more=()):
    place = pl.BlockSpec(memory_space=pltpu.VMEM)
    far = pl.BlockSpec(memory_space=pl.ANY)
    dma = pltpu.SemaphoreType.DMA
    fixed = [front, bias] + ([small] if more else [])
    made = [(4, n_cols, WIN), (4, kv_rows, WIN), (4, kv_rows, WIN)]
    made = [jax.ShapeDtypeStruct(shape, BF16) for shape in made]
    scratch = [dma((4,))] * 4
    gathered = []
    if more:
        gathered = [jax.ShapeDtypeStruct((4,) + v.shape, v.dtype) for v in fixed + list(more)]
        scratch += [dma((3, 3))] * 2 + [dma((len(more), 5))] * 2
    return pl.pallas_call(
        functools.partial(front_kernel, len(more)),
        out_shape=made + gathered,
        in_specs=[place] * (1 + len(fixed)) + [far] * len(more),
        out_specs=[place] * (3 + (3 if more else 0)) + [far] * len(more),
        scratch_shapes=scratch,
        compiler_params=pltpu.CompilerParams(
            collective_id=1 if more else 2,
            has_side_effects=True,
            vmem_limit_bytes=48 * 1024 * 1024,
        ),
        name="front_gather" if more else "front",
    )(normed, *fixed, *more)


def routes():
    windows, groups = lax.axis_size("ctx"), lax.axis_size("mp")
    first_home = [(c * groups + 3, c * groups + 2) for c in range(windows)]
    home = [(c * groups + 2, c * groups + 1) for c in range(windows)]
    home += [((c + 1) * groups, c * groups) for c in range(windows - 1)]
    return first_home, home


def pass_home(before, earlier):
    first_home, home = routes()
    near, far = lax.ppermute((before, earlier), ("ctx", "mp"), first_home)
    far = (before.astype(F32) + far.astype(F32)).astype(BF16)
    return near.astype(F32) + lax.ppermute(far, ("ctx", "mp"), home).astype(F32)


def row_starts(lengths):
    part = lax.axis_index("mp")
    place = (part - 1) * WIN + jnp.arange(WIN, dtype=jnp.int32)
    ends = jnp.cumsum(lengths)
    begun = jnp.max(jnp.where(place[:, None] >= ends[None, :], ends[None, :], 0), axis=1)
    document = begun - (part - 1) * WIN + 2 * WIN
    window = jnp.where(lax.axis_index("ctx") > 0, WIN, 2 * WIN)
    low = jnp.where(part == 0, window, document).astype(jnp.int32)
    return low.reshape(1, WIN), low[::TILE] // TILE


def sum_cores(parts):
    own, near, far, last = parts
    near, last = swap(jnp.stack([near, last]), "mp", 1)
    return (
        (own.astype(F32) + near.astype(F32)).astype(BF16),
        (far.astype(F32) + last.astype(F32)).astype(BF16),
    )


def sum_kernel(counts, rows, *refs):
    refs = list(refs)

    def take(count):
        taken = refs[:count]
        del refs[:count]
        return taken

    owns, fars = take(len(counts)), take(len(counts))
    vec_in, out, vec, from_y, mine, from_x, kept, from_z, from_vec = take(9)
    y_out, y_in, x_out, x_in, z_out, z_in, g_out, g_in, h_out, h_in, v_out, v_in = refs
    parts = sum(counts)
    firsts = [sum(counts[:k]) for k in range(len(counts))]
    ctx, dp, mp = (lax.axis_index(axis) for axis in ("ctx", "dp", "mp"))
    half = rows // 2
    bits = [1 << k for k in range((lax.axis_size("dp") - 1).bit_length())]
    highs = [(dp // bit) % 2 for bit in bits]
    other_chip, other_window = {"mp": flip(mp, 2)}, {"ctx": 1 - ctx}
    beside = [{"dp": flip(dp, bit)} for bit in bits]
    partners = [other_chip, other_window, {"mp": flip(mp, 1)}] + beside

    def ds(start, size):
        return pl.ds(pl.multiple_of(start, 16), size)

    def segment(i, k, sent=False):
        start, size = 0, half
        for high in highs[:k]:
            size //= 2
            start = start + high * size
        if sent:
            size //= 2
            start = start + (1 - highs[k]) * size
        return start, size

    def to_y(array, i):
        here = ds((firsts[array] + i) * rows, rows)
        source = fars[array].at[ds(i * rows, rows)]
        place = firsts[array] + i
        return remote(source, from_y.at[here], y_out.at[place], y_in.at[place], other_chip)

    def to_x(i):
        source = mine.at[ds(i * rows + (1 - ctx) * half, half)]
        target = from_x.at[ds(i * half, half)]
        return remote(source, target, x_out.at[i], x_in.at[i], other_window)

    def to_z(i, k):
        start, size = segment(i, k, True)
        target = from_z.at[ds(i * half + half - 2 * size, size)]
        source = kept.at[ds(i * half + start, size)]
        return remote(source, target, z_out.at[i, k], z_in.at[i, k], beside[k])

    def back_z(i, k):
        start, size = segment(i, k + 1)
        here = out.at[ds(i * rows + ctx * half + start, size)]
        return remote(here, here, g_out.at[i, k], g_in.at[i, k], beside[k])

    def back_x(i):
        here = out.at[ds(i * rows + ctx * half, half)]
        return remote(here, here, h_out.at[i], h_in.at[i], other_window)

    def each(count, step):
        lax.fori_loop(0, count, lambda i, _: (step(i), 0)[1], 0)

    meet(partners)
    vec[...] = vec_in[...]
    for hop, partner in enumerate(partners):
        copy = remote(vec, from_vec.at[hop], v_out.at[hop], v_in.at[hop], partner)
        copy.start()
        if hop == 0:
            for array, count in enumerate(counts):
                each(count, lambda i, array=array: to_y(array, i).start())
        copy.wait()
        vec[...] = vec[...] + from_vec[hop]

    def join(i):
        here = ds(i * rows, rows)
        for array, count in enumerate(counts):

            def add(array=array):
                to_y(array, i - firsts[array]).wait_recv()
                term = owns[array][ds((i - firsts[array]) * rows, rows), :]
                mine[here, :] = (term.astype(F32) + from_y[here, :].astype(F32)).astype(BF16)

            pl.when((i >= firsts[array]) & (i < firsts[array] + count))(add)
        to_x(i).start()

    def spread(i):
        to_x(i).wait_recv()
        there = ds(i * half, half)
        total = mine[ds(i * rows + ctx * half, half), :].astype(F32) + from_x[there, :].astype(F32)
        kept[there, :] = total.astype(BF16)
        to_z(i, 0).start()

    def narrow(k, i):
        to_z(i, k).wait_recv()
        start, size = segment(i, k + 1)
        here = ds(i * half + start, size)
        there = ds(i * half + half - 2 * size, size)
        total = (kept[here, :].astype(F32) + from_z[there, :].astype(F32)).astype(BF16)
        if k + 1 < len(bits):
            kept[here, :] = total
            to_z(i, k + 1).start()
        else:
            out[ds(i * rows + ctx * half + start, size), :] = total
            back_z(i, k).start()

    def widen(k, i):
        back_z(i, k).wait_recv()
        if k:
            back_z(i, k - 1).start()
        else:
            back_x(i).start()

    stages = [join, spread]
    stages += [functools.partial(narrow, k) for k in range(len(bits))]
    stages += [functools.partial(widen, k) for k in reversed(range(len(bits)))]

    def step(i):
        for late, stage in enumerate(stages):
            pl.when((i >= late) & (i < parts + late))(functools.partial(stage, i - late))

    each(parts + len(stages) - 1, step)
    for array, count in enumerate(counts):
        each(count, lambda i, array=array: to_y(array, i).wait_send())

    def finish(i):
        to_x(i).wait_send()
        back_x(i).wait()
        for k in range(len(bits)):
            to_z(i, k).wait_send()
            back_z(i, k).wait_send()

    each(parts, finish)


def rows_of_part():
    return max(256, 32 * lax.axis_size("dp"))


def sum_replicas(pairs, vectors):
    rows = rows_of_part()
    bits = (lax.axis_size("dp") - 1).bit_length()
    hops = 3 + bits
    lanes = pairs[0][0].shape[1]
    owns, fars = (
        [jnp.pad(v, ((0, -v.shape[0] % rows), (0, 0))) for v in half] for half in zip(*pairs)
    )
    counts = [v.shape[0] // rows for v in owns]
    parts = sum(counts)
    total = parts * rows
    place = pl.BlockSpec(memory_space=pltpu.VMEM)
    dma = pltpu.SemaphoreType.DMA
    return pl.pallas_call(
        functools.partial(sum_kernel, counts, rows),
        out_shape=[
            jax.ShapeDtypeStruct((total, lanes), BF16),
            jax.ShapeDtypeStruct(vectors.shape, F32),
        ],
        in_specs=[place] * len(counts)
        + [pl.BlockSpec(memory_space=pl.ANY)] * len(counts)
        + [place],
        out_specs=[place, place],
        scratch_shapes=[
            pltpu.VMEM((total, lanes), BF16),
            pltpu.VMEM((total, lanes), BF16),
            pltpu.VMEM((total // 2, lanes), BF16),
            pltpu.VMEM((total // 2, lanes), BF16),
            pltpu.VMEM((total // 2, lanes), BF16),
            pltpu.VMEM((hops,) + vectors.shape, F32),
            dma((parts,)), dma((parts,)),
            dma((parts,)), dma((parts,)),
            dma((parts, bits)), dma((parts, bits)),
            dma((parts, bits)), dma((parts, bits)),
            dma((parts,)), dma((parts,)),
            dma((hops,)), dma((hops,)),
        ],
        compiler_params=pltpu.CompilerParams(
            collective_id=0, has_side_effects=True, vmem_limit_bytes=56 * 1024 * 1024
        ),
        name="sum_replicas",
    )(*owns, *fars, vectors)


def gelu(hidden):
    return jax.nn.gelu(hidden, approximate=True)


def tail_forward(stream, heads, out_weight, out_bias, gain, shift, ups, up_biases, downs):
    stream = stream + dot(heads, out_weight, 0, 0) + out_bias[0]
    normed, unit, scale = norm_rows(stream, gain[1], shift[1])
    hidden, active, total = [], [], out_bias[1]
    for up, bias, down in zip(ups, up_biases, downs, strict=True):
        hidden.append(dot(normed, up, 1, 0) + bias)
        active.append(gelu(hidden[-1]).astype(BF16))
        total = total + dot(active[-1], down, 1, 0)
    return stream + total, (normed, unit, scale, hidden, active)


def tail_backward(grad, kept, out_weight, gain, ups, downs):
    normed, unit, scale, hidden, active = kept
    bias_mlp = jnp.sum(grad, axis=0)
    rounded = grad.astype(BF16)
    mats, up_biases, normed_grad = [], [], 0.0
    for up, down, before, after in zip(ups, downs, hidden, active, strict=True):
        _, pull = jax.vjp(gelu, before)
        grad_hidden = pull(dot(rounded, down, 1, 1))[0]
        up_biases.append(jnp.sum(grad_hidden, axis=0))
        low = grad_hidden.astype(BF16)
        mats.append(
            jnp.concatenate(
                [dot(normed, low, 0, 0).astype(BF16), dot(after, rounded, 0, 0).astype(BF16)]
            )
        )
        normed_grad = normed_grad + dot(low, up, 1, 1)
    middle, gain_grad, shift_grad = norm_back(normed_grad, unit, scale, gain[1])
    grad = grad + middle
    bias_attn = jnp.sum(grad, axis=0)
    rounded = grad.astype(BF16)
    grad_heads = dot(out_weight, rounded, 1, 1).astype(BF16)
    return grad, rounded, grad_heads, mats, up_biases, (gain_grad, shift_grad, bias_attn, bias_mlp)


def turned(weight):
    return jnp.swapaxes(weight, -1, -2)


def shards(
    block_input, cotangent, doc_lengths, reuse_heads,
    norm_gain1, norm_bias1, projections1, front_bias1, out_weight1, out_bias1,
    up_weight1, up_bias1, down_weight1,
    norm_gain2, norm_bias2, query_key2, query_bias2, fresh_value2, value_bias2,
    out_weight2, out_bias2, up_weight2, up_bias2, down_weight2,
):
    low, first = row_starts(doc_lengths[0])
    taken = jnp.arange(4 * GROUP, dtype=jnp.int32)[:, None] == reuse_heads[None, :]
    taker = jnp.sum(jnp.where(taken, jnp.arange(REUSE, dtype=jnp.int32)[None, :], 0), axis=1)
    scalars = jnp.concatenate([first, reuse_heads, jnp.any(taken, axis=1).astype(jnp.int32), taker])

    stream0 = block_input.astype(F32)
    normed1, unit1, scale1 = norm_rows(stream0, norm_gain1[0], norm_bias1[0])
    n_front1, n_front2 = 3 * BAND, 2 * BAND + BAND // 2
    none = jnp.zeros((BAND,), BF16)

    def as_row(pieces):
        row = jnp.concatenate(pieces).astype(F32)
        return jnp.pad(row[None, :], ((0, 7), (0, -row.shape[0] % 128)))

    small = jnp.concatenate([query_bias2, value_bias2, up_bias1, up_bias2])
    small = jnp.pad(small, (0, 16 * 128 - small.shape[0])).reshape(16, 128)
    own_front2 = jnp.concatenate([turned(query_key2).reshape(2 * BAND, D), turned(fresh_value2)])
    own_front2 = jnp.pad(own_front2, ((0, -n_front2 % 64), (0, 0)))
    (
        cols1, before1, earlier1, front1, _, small,
        up1, down1, up2, down2, front2, outs1, outs2,
    ) = project(
        normed1, turned(projections1).reshape(n_front1, D),
        as_row([front_bias1[0], none, front_bias1[1]]), n_front1, 2 * BAND, small,
        (up_weight1, down_weight1, up_weight2, down_weight2, own_front2, out_weight1, out_weight2),
    )
    ups1, downs1, ups2, downs2 = (
        [own] + by_distance(w)[1:]
        for own, w in (
            (up_weight1, up1), (down_weight1, down1), (up_weight2, up2), (down_weight2, down2)
        )
    )
    front2, outs1, outs2 = (
        lax.dynamic_update_index_in_dim(w, own, lax.axis_index("mp"), 0)
        for own, w in ((own_front2, front2), (out_weight1, outs1), (out_weight2, outs2))
    )
    outs1, outs2 = outs1.reshape(D, D), outs2.reshape(D, D)
    small = small.reshape(4, -1)
    at = BAND + BAND // 2
    bias2 = jnp.stack([as_row([small[s, :BAND], none, small[s, BAND:at]]) for s in range(4)])
    up_biases1 = by_distance(small[:, at : at + D])
    up_biases2 = by_distance(small[:, at + D : at + 2 * D])

    front_kv1 = (cols1, before1, earlier1)
    values1 = values_of(cols1, before1, earlier1)
    heads1, exact1, sums1 = attend(scalars, low, front_kv1, values1)
    stream1, kept1 = tail_forward(
        stream0, heads1.reshape(D, WIN), outs1, out_bias1, norm_gain1, norm_bias1,
        ups1, up_biases1, downs1,
    )

    normed2, unit2, scale2 = norm_rows(stream1, norm_gain2[0], norm_bias2[0])
    cols2, before2, earlier2 = project(normed2, front2, bias2, n_front2, n_front2 - BAND)
    front2 = front2[:, :n_front2]

    front_kv2 = (cols2, before2, earlier2)
    fresh2 = [v[:, -(BAND // 2) :].reshape(2, BAND, WIN) for v in front_kv2]
    values2 = values_mixed(front_kv1, fresh2)
    heads2, exact2, sums2 = attend(scalars, low, front_kv2, values2)
    stream2, kept2 = tail_forward(
        stream1, heads2.reshape(D, WIN), outs2, out_bias2, norm_gain2, norm_bias2,
        ups2, up_biases2, downs2,
    )
    block_output = stream2.astype(BF16)

    grad, rounded, grad_heads, mats2, up_grads2, small2 = tail_backward(
        cotangent.astype(F32), kept2, outs2, norm_gain2, ups2, downs2
    )
    own2, far2 = sum_cores(mats2)
    dq2, dk2, dk2_before, dk2_earlier, dv2, dv2_before, dv2_earlier = attend_back(
        far2, scalars, low, front_kv2, values2, (), exact2, grad_heads.reshape(4, BAND, WIN), sums2
    )
    grad_out2 = dot(heads2.reshape(D, WIN), rounded, 1, 0).astype(BF16).reshape(4, BAND, D)

    def fresh_part(grads):
        return grads[2:].reshape(4, BAND // 2, WIN)

    def join2(keys, values):
        return jnp.concatenate([keys, fresh_part(values)], axis=1)

    kv2 = join2(dk2, dv2) + pass_home(
        join2(dk2_before, dv2_before), join2(dk2_earlier, dv2_earlier)
    )
    dcols2 = jnp.concatenate([dq2, kv2], axis=1)
    bias_grad2 = jnp.sum(dcols2, axis=2)
    dcols2 = dcols2.astype(BF16)
    grad_front2 = dot(dcols2.reshape(-1, WIN), normed2, 1, 0).astype(BF16).reshape(4, n_front2, D)
    attn2 = [
        jnp.concatenate(pair)
        for pair in zip(by_distance(grad_out2), by_distance(grad_front2), strict=True)
    ]
    attn2 = sum_cores(attn2)
    normed_grad = dot(dcols2.reshape(-1, WIN), front2.reshape(-1, D), 0, 0)
    middle, gain_front2, shift_front2 = norm_back(normed_grad, unit2, scale2, norm_gain2[0])
    grad = grad + middle

    grad, rounded, grad_heads, mats1, up_grads1, small1 = tail_backward(
        grad, kept1, outs1, norm_gain1, ups1, downs1
    )
    mats1 = sum_cores(mats1)
    dq1, dk1, dk1_before, dk1_earlier, dv1, dv1_before, dv1_earlier = attend_back(
        far2, scalars, low, front_kv1, values1, (dv2, dv2_before, dv2_earlier), exact1,
        grad_heads.reshape(4, BAND, WIN), sums1,
    )
    grad_out1 = dot(heads1.reshape(D, WIN), rounded, 1, 0).astype(BF16).reshape(4, BAND, D)

    def join1(keys, values):
        return jnp.concatenate([keys, values], axis=1)

    kv1 = join1(dk1, dv1) + pass_home(
        join1(dk1_before, dv1_before), join1(dk1_earlier, dv1_earlier)
    )
    dcols1 = jnp.concatenate([dq1, kv1], axis=1)
    bias_grad1 = jnp.sum(dcols1, axis=2)
    dcols1 = dcols1.astype(BF16)
    grad_front1 = dot(dcols1.reshape(-1, WIN), normed1, 1, 0).astype(BF16).reshape(4, n_front1, D)
    attn1 = [
        jnp.concatenate(pair)
        for pair in zip(by_distance(grad_out1), by_distance(grad_front1), strict=True)
    ]
    attn1 = sum_cores(attn1)
    normed_grad = dot(dcols1.reshape(-1, WIN), front1.reshape(-1, D), 0, 0)
    middle, gain_front1, shift_front1 = norm_back(normed_grad, unit1, scale1, norm_gain1[0])
    input_grad = (grad + middle).astype(BF16)

    vectors = [
        gain_front1, small1[0], shift_front1, small1[1], small1[2], small1[3],
        gain_front2, small2[0], shift_front2, small2[1], small2[2], small2[3],
        bias_grad1[:, :BAND].reshape(-1), bias_grad1[:, 2 * BAND :].reshape(-1),
        bias_grad2[:, :BAND].reshape(-1), bias_grad2[:, 2 * BAND :].reshape(-1),
        in_order(up_grads1), in_order(up_grads2),
    ]
    lengths = [vector.shape[0] for vector in vectors]
    packed = jnp.concatenate(vectors)
    filler = (-packed.shape[0]) % 1024
    pairs = ((own2, far2), attn2, mats1, attn1)
    stack, packed = sum_replicas(pairs, jnp.pad(packed, (0, filler)).reshape(-1, 128))
    packed = packed.reshape(-1)
    sums, at = [], 0
    for length in lengths:
        sums.append(packed[at : at + length])
        at += length
    me = lax.axis_index("mp")

    def mine(vector):
        return lax.dynamic_index_in_dim(vector.reshape(4, -1), me, 0, keepdims=False)

    def pair(i):
        return jnp.stack([sums[i], sums[i + 1]])

    shares, at = [], 0
    for own, _ in pairs:
        shares.append(stack[at : at + own.shape[0]])
        at += own.shape[0] + -own.shape[0] % rows_of_part()
    mats2, attn2, mats1, attn1 = shares

    return (
        block_output,
        input_grad,
        pair(0),
        pair(2),
        turned(attn1[BAND : BAND + n_front1].reshape(3, BAND, D)).astype(F32),
        jnp.stack([mine(sums[12]), mine(sums[13])]),
        attn1[:BAND].astype(F32),
        pair(4),
        mats1[:D].astype(F32),
        mine(sums[16]),
        mats1[D:].astype(F32),
        pair(6),
        pair(8),
        turned(attn2[BAND : 3 * BAND].reshape(2, BAND, D)).astype(F32),
        mine(sums[14]),
        turned(attn2[3 * BAND : BAND + n_front2]).astype(F32),
        mine(sums[15]),
        attn2[:BAND].astype(F32),
        pair(10),
        mats2[:D].astype(F32),
        mine(sums[17]),
        mats2[D:].astype(F32),
    )


def solution(mesh):
    rows = P(("dp", "ctx", "mp"), None)
    placed = (
        rows, rows, P(("dp", "ctx"), None), P(),
        P(), P(), P(None, None, "mp"), P(None, "mp"), P("mp", None), P(),
        P(None, "mp"), P("mp"), P("mp", None),
        P(), P(), P(None, None, "mp"), P("mp"), P(None, "mp"), P("mp"),
        P("mp", None), P(), P(None, "mp"), P("mp"), P("mp", None),
    )
    given = (
        rows, rows,
        P(), P(), P(None, None, "mp"), P(None, "mp"), P("mp", None), P(),
        P(None, "mp"), P("mp"), P("mp", None),
        P(), P(), P(None, None, "mp"), P("mp"), P(None, "mp"), P("mp"),
        P("mp", None), P(), P(None, "mp"), P("mp"), P("mp", None),
    )
    return jax.shard_map(shards, mesh=mesh, in_specs=placed, out_specs=given, check_vma=False)
```

```python
import functools

import jax
import jax.numpy as jnp
from jax import lax
from jax.experimental import pallas as pl
from jax.experimental.pallas import tpu as pltpu
from jax.sharding import PartitionSpec as P

D = 768
HD = 64
REUSE = 6
WIN = 512
EARLY = 2
GROUP = 3
BAND = GROUP * HD
AT_REUSE = 2
TILE = 256
TILES = 3 * WIN // TILE
EPS = 1e-05
SCALE = HD**-0.5
F32 = jnp.float32
BF16 = jnp.bfloat16


def swap(value, axis, bit):
    devices = range(lax.axis_size(axis))
    return lax.ppermute(value, axis, [(i, i ^ bit) for i in devices])


def in_order(parts):
    return jnp.concatenate(by_distance(jnp.stack(parts)))


def by_distance(stacked):
    me = lax.axis_index("mp")
    return [
        lax.dynamic_index_in_dim(stacked, me ^ distance, 0, keepdims=False)
        for distance in range(4)
    ]


def flip(position, bit):
    return position + bit * (1 - 2 * ((position // bit) % 2))


def remote(source, target, sent, received, device):
    return pltpu.make_async_remote_copy(
        src_ref=source, dst_ref=target, send_sem=sent, recv_sem=received,
        device_id=device, device_id_type=pl.DeviceIdType.MESH,
    )


def meet(devices):
    barrier = pltpu.get_barrier_semaphore()
    for device in devices:
        pl.semaphore_signal(barrier, inc=1, device_id=device, device_id_type=pl.DeviceIdType.MESH)
    pl.semaphore_wait(barrier, len(devices))


def dot(left, right, left_dim, right_dim):
    return lax.dot_general(
        left, right, (((left_dim,), (right_dim,)), ((), ())), preferred_element_type=F32
    )


def norm_rows(value, gain, shift):
    mean = jnp.mean(value, axis=-1, keepdims=True)
    centred = value - mean
    spread = jnp.mean(centred * centred, axis=-1, keepdims=True)
    scale = lax.rsqrt(spread + EPS)
    unit = centred * scale
    return (unit * gain + shift).astype(BF16), unit, scale


def norm_back(grad, unit, scale, gain):
    scaled = grad * gain
    inner = (
        scaled
        - jnp.mean(scaled, axis=-1, keepdims=True)
        - unit * jnp.mean(scaled * unit, axis=-1, keepdims=True)
    )
    return scale * inner, jnp.sum(grad * unit, axis=0), jnp.sum(grad, axis=0)


def place_values(refs, values):
    if len(refs) == 3:
        for part, ref in enumerate(reversed(refs)):
            values[part] = ref[0]
        return
    group = pl.program_id(0)

    def reused():
        for part in range(3):
            for j in range(GROUP):
                values[part, j * HD : (j + 1) * HD, :] = refs[4 * (2 - part) + j][0]

    def fresh():
        for part in range(3):
            values[part] = refs[4 * (2 - part) + GROUP][0]

    pl.when(group < 2)(reused)
    pl.when(group >= 2)(fresh)


def attend_kernel(n_values, first_ref, lo_ref, q_ref, k0, k1, k2, *refs):
    v_refs = refs[:n_values]
    out_ref, exact_ref, sum_ref, values, raw, top, total, acc = refs[n_values:]
    keys = (k2, k1, k0)
    place_values(v_refs, values)
    for t in range(WIN // TILE):
        cols = slice(t * TILE, (t + 1) * TILE)
        low = lo_ref[:, cols]
        place = 2 * WIN + t * TILE + lax.broadcasted_iota(jnp.int32, (1, TILE), 1)
        last = 2 * WIN // TILE + t

        def score(kt):
            spot = kt * TILE + lax.broadcasted_iota(jnp.int32, (TILE, TILE), 0)
            keep = spot >= low
            if kt == last:
                keep = keep & (spot <= place)
            span = slice(kt % 2 * TILE, (kt % 2 + 1) * TILE)
            for j in range(GROUP):
                rows = slice(j * HD, (j + 1) * HD)
                found = dot(keys[kt // 2][0, rows, span], q_ref[0, rows, cols] * SCALE, 0, 0)
                found = jnp.where(keep, found, -jnp.inf)
                raw[j, kt] = found
                peak = jnp.max(found.reshape(TILE // 8, 8, TILE), axis=0)
                top[j] = peak if kt == last else jnp.maximum(top[j], peak)

        def weigh(kt):
            span = slice(kt % 2 * TILE, (kt % 2 + 1) * TILE)
            for j in range(GROUP):
                rows = slice(j * HD, (j + 1) * HD)
                powers = jnp.exp(raw[j, kt] - top[j, 0:1])
                added = jnp.sum(powers.reshape(TILE // 8, 8, TILE), axis=0)
                result = dot(values[kt // 2, rows, span], powers.astype(BF16), 1, 0)
                total[j] = added if kt == last else total[j] + added
                acc[j] = result if kt == last else acc[j] + result

        for stage in (score, weigh):
            stage(last)
            for kt in reversed(range(last)):
                pl.when(kt >= first_ref[t])(functools.partial(stage, kt))
            if stage is score:
                for j in range(GROUP):
                    top[j] = jnp.broadcast_to(jnp.max(top[j], axis=0, keepdims=True), (8, TILE))
        for j in range(GROUP):
            rows = slice(j * HD, (j + 1) * HD)
            whole = jnp.sum(total[j], axis=0, keepdims=True)
            result = acc[j] / whole
            out_ref[0, rows, cols] = result.astype(BF16)
            exact_ref[0, rows, cols] = result
            sum_ref[0, j : j + 1, cols] = top[j, 0:1] + jnp.log(whole)


def band(place):
    return pl.BlockSpec((1, BAND, WIN), lambda s, *_: (s, place, 0))


LOW = pl.BlockSpec((1, WIN), lambda s, *_: (0, 0))
SUMS = pl.BlockSpec((1, 8, WIN), lambda s, *_: (s, 0, 0))


def head_block(stride, offset, j):
    def at(s, scalars):
        head = scalars[AT_REUSE + jnp.minimum(GROUP * s + j, REUSE - 1)]
        return (head // GROUP * stride + offset + head % GROUP, 0, 0)

    return pl.BlockSpec((1, HD, WIN), at)


FRESH = pl.BlockSpec((1, BAND, WIN), lambda s, *_: (jnp.maximum(s - 2, 0), 0, 0))


def values_of(cols, before, earlier):
    return [cols, before, earlier], [band(2), band(1), band(1)]


def values_mixed(firsts, freshes):
    arrays, specs = [], []
    for k, (first, fresh) in enumerate(zip(firsts, freshes, strict=True)):
        stride, offset = (3 * GROUP, 2 * GROUP) if k == 0 else (2 * GROUP, GROUP)
        arrays += [first.reshape(-1, HD, WIN)] * GROUP + [fresh]
        specs += [head_block(stride, offset, j) for j in range(GROUP)] + [FRESH]
    return arrays, specs


def attend(scalars, low, front, values):
    arrays, specs = values
    return pl.pallas_call(
        functools.partial(attend_kernel, len(arrays)),
        grid_spec=pltpu.PrefetchScalarGridSpec(
            num_scalar_prefetch=1,
            grid=(4,),
            in_specs=[LOW, band(0), band(1), band(0), band(0)] + specs,
            out_specs=[band(0), band(0), SUMS],
            scratch_shapes=[
                pltpu.VMEM((3, BAND, WIN), BF16),
                pltpu.VMEM((GROUP, TILES, TILE, TILE), F32),
                pltpu.VMEM((GROUP, 8, TILE), F32),
                pltpu.VMEM((GROUP, 8, TILE), F32),
                pltpu.VMEM((GROUP, HD, TILE), F32),
            ],
        ),
        out_shape=[
            jax.ShapeDtypeStruct((4, BAND, WIN), BF16),
            jax.ShapeDtypeStruct((4, BAND, WIN), F32),
            jax.ShapeDtypeStruct((4, 8, WIN), F32),
        ],
        compiler_params=pltpu.CompilerParams(vmem_limit_bytes=32 * 1024 * 1024),
        name="attend",
    )(scalars, low, front[0], *front, *arrays)


def front_kernel(n_more, *refs):
    refs = list(refs)

    def take(count):
        taken = refs[:count]
        del refs[:count]
        return taken

    ctx, dp, mp = (lax.axis_index(axis) for axis in ("ctx", "dp", "mp"))
    (normed,) = take(1)
    near, far, last = {"mp": flip(mp, 1)}, {"mp": flip(mp, 2)}, {"mp": 3 - mp}
    window = {"ctx": 1 - ctx}
    order = (mp, flip(mp, 1), flip(mp, 2), 3 - mp)
    if n_more:
        fixed_own = take(3)
        more_own = take(n_more)
        cols, before, earlier = take(3)
        fixed = take(3)
        more = take(n_more)
        kv_out, kv_in, on_out, on_in, f_out, f_in, m_out, m_in = refs
        front, bias, _ = fixed
        meet([near, far, last, window, {"dp": flip(dp, 1)}])
    else:
        front, bias = take(2)
        cols, before, earlier = take(3)
        kv_out, kv_in, on_out, on_in = refs
        meet([near, last, window])

    if n_more:
        def whole(k, way, device):
            return remote(fixed_own[k], fixed[k].at[mp], f_out.at[k, way], f_in.at[k, way], device)

        def onward():
            there = front.at[flip(mp, 2)]
            return remote(there, there, f_out.at[0, 2], f_in.at[0, 2], near)

        whole(0, 1, far).start()
        whole(0, 0, near).start()
        for k in (1, 2):
            for way, device in enumerate((near, far, last)):
                whole(k, way, device).start()

        bit = lax.rem(dp, 2)
        first = [(bit, {"dp": flip(dp, 1)}), (ctx, window)]

        def sizes(a):
            rows = more_own[a].shape[0]
            (low, low_device), (high, high_device) = first if a % 2 else first[::-1]
            return rows, rows // 4, rows // 2, low, low_device, high, high_device

        def beside(a):
            return remote(more_own[a], more[a].at[mp], m_out.at[a, 0], m_in.at[a, 0], near)

        def across(a):
            rows, quarter, half, low, _, high, _ = sizes(a)
            here = pl.ds(pl.multiple_of(high * half + low * quarter, 16), quarter)
            return remote(
                more_own[a].at[here], more[a].at[mp, here], m_out.at[a, 1], m_in.at[a, 1], far
            )

        def widen(a):
            rows, quarter, half, low, device, high, _ = sizes(a)
            here = pl.ds(pl.multiple_of(high * half + low * quarter, 16), quarter)
            there = more[a].at[flip(mp, 2), here]
            return remote(there, there, m_out.at[a, 2], m_in.at[a, 2], device)

        def complete(a):
            rows, quarter, half, low, _, high, device = sizes(a)
            here = pl.ds(pl.multiple_of(high * half, 16), half)
            there = more[a].at[flip(mp, 2), here]
            return remote(there, there, m_out.at[a, 3], m_in.at[a, 3], device)

        def hand_on(a):
            there = more[a].at[flip(mp, 2)]
            return remote(there, there, m_out.at[a, 4], m_in.at[a, 4], near)

        for a in range(EARLY):
            across(a).start()
        for a in range(n_more):
            beside(a).start()
        for k in range(3):
            fixed[k][mp] = fixed_own[k][...]

    kv_rows = before.shape[1]
    from_row = cols.shape[1] - kv_rows
    sends_on = (mp == 1) | (mp == 2)
    sends_window = (mp == 0) & (ctx == 0)
    receives = (mp >= 2) | ((mp == 0) & (ctx == 1))

    def pass_on(slot, device):
        source = cols.at[slot, pl.ds(from_row, kv_rows)]
        return remote(source, before.at[slot], kv_out.at[slot], kv_in.at[slot], device)

    def pass_again(slot):
        return remote(before.at[slot], earlier.at[slot], on_out.at[slot], on_in.at[slot], {"mp": 3})

    for k, slot in enumerate(order):
        if n_more and k == 1:
            for vector in (1, 2):
                for way, device in enumerate((near, far, last)):
                    whole(vector, way, device).wait_recv()
            whole(0, 0, near).wait_recv()
        if n_more and k == 2:
            whole(0, 1, far).wait_recv()
            onward().start()
        if n_more and k == 3:
            onward().wait_recv()
        column = jnp.transpose(bias[slot])[: cols.shape[1], 0:1]
        cols[slot] = (dot(front[slot, : cols.shape[1]], normed[...], 1, 1) + column).astype(BF16)
        pl.when(sends_on)(lambda: pass_on(slot, {"mp": mp + 1}).start())
        pl.when(sends_window)(lambda: pass_on(slot, window).start())

    for a in range(EARLY, n_more):
        across(a).start()
    for a in range(n_more + 2 if n_more else 0):
        if a < n_more:
            across(a).wait_recv()
            widen(a).start()
        if 1 <= a <= n_more:
            widen(a - 1).wait_recv()
            complete(a - 1).start()
        if a >= 2:
            complete(a - 2).wait_recv()
            hand_on(a - 2).start()

    def received():
        for slot in range(4):
            pass_on(slot, window).wait_recv()
            pl.when(mp == 2)(lambda: pass_again(slot).start())

    pl.when(receives)(received)

    def sent(device):
        for slot in range(4):
            pass_on(slot, device).wait_send()

    pl.when(sends_on)(lambda: sent({"mp": mp + 1}))
    pl.when(sends_window)(lambda: sent(window))

    def again_sent():
        for slot in range(4):
            pass_again(slot).wait_send()

    def again_received():
        for slot in range(4):
            pass_again(slot).wait_recv()

    pl.when(mp == 2)(again_sent)
    pl.when(mp == 3)(again_received)
    if n_more:
        for k in range(3):
            for way, device in enumerate((near, far, last)):
                if k or way < 2:
                    whole(k, way, device).wait_send()
        onward().wait_send()
        for a in range(n_more):
            beside(a).wait()
            across(a).wait_send()
            widen(a).wait_send()
            complete(a).wait_send()
            hand_on(a).wait()


def project(normed, front, bias, n_cols, kv_rows, small=None, more=()):
    place = pl.BlockSpec(memory_space=pltpu.VMEM)
    far = pl.BlockSpec(memory_space=pl.ANY)
    dma = pltpu.SemaphoreType.DMA
    fixed = [front, bias] + ([small] if more else [])
    made = [(4, n_cols, WIN), (4, kv_rows, WIN), (4, kv_rows, WIN)]
    made = [jax.ShapeDtypeStruct(shape, BF16) for shape in made]
    scratch = [dma((4,))] * 4
    gathered = []
    if more:
        gathered = [jax.ShapeDtypeStruct((4,) + v.shape, v.dtype) for v in fixed + list(more)]
        scratch += [dma((3, 3))] * 2 + [dma((len(more), 5))] * 2
    return pl.pallas_call(
        functools.partial(front_kernel, len(more)),
        out_shape=made + gathered,
        in_specs=[place] * (1 + len(fixed)) + [far] * len(more),
        out_specs=[place] * (3 + (3 if more else 0)) + [far] * len(more),
        scratch_shapes=scratch,
        compiler_params=pltpu.CompilerParams(
            collective_id=1 if more else 2,
            has_side_effects=True,
            vmem_limit_bytes=48 * 1024 * 1024,
        ),
        name="front_gather" if more else "front",
    )(normed, *fixed, *more)


def row_starts(lengths):
    part = lax.axis_index("mp")
    place = (part - 1) * WIN + jnp.arange(WIN, dtype=jnp.int32)
    ends = jnp.cumsum(lengths)
    begun = jnp.max(jnp.where(place[:, None] >= ends[None, :], ends[None, :], 0), axis=1)
    document = begun - (part - 1) * WIN + 2 * WIN
    window = jnp.where(lax.axis_index("ctx") > 0, WIN, 2 * WIN)
    low = jnp.where(part == 0, window, document).astype(jnp.int32)
    return low.reshape(1, WIN), low[::TILE] // TILE


def sum_cores(parts):
    own, near, far, last = parts
    near, last = swap(jnp.stack([near, last]), "mp", 1)
    return (
        (own.astype(F32) + near.astype(F32)).astype(BF16),
        (far.astype(F32) + last.astype(F32)).astype(BF16),
    )


class Sums:
    def __init__(self, counts, rows, owns, fars, out, refs):
        self.counts, self.rows, self.owns, self.fars, self.out = counts, rows, owns, fars, out
        self.from_y, self.mine, self.from_x, self.kept, self.from_z = refs[:5]
        self.sems = refs[5:]
        self.parts = sum(counts)
        self.firsts = [sum(counts[:k]) for k in range(len(counts))]
        self.ctx, self.dp, mp = (lax.axis_index(axis) for axis in ("ctx", "dp", "mp"))
        self.half = rows // 2
        self.bits = [1 << k for k in range((lax.axis_size("dp") - 1).bit_length())]
        self.highs = [(self.dp // bit) % 2 for bit in self.bits]
        self.other_chip, self.other_window = {"mp": flip(mp, 2)}, {"ctx": 1 - self.ctx}
        self.beside = [{"dp": flip(self.dp, bit)} for bit in self.bits]
        self.partners = [self.other_chip, self.other_window, {"mp": flip(mp, 1)}] + self.beside
        self.stages = [self.join, self.spread]
        self.stages += [functools.partial(self.narrow, k) for k in range(len(self.bits))]
        self.stages += [functools.partial(self.widen, k) for k in reversed(range(len(self.bits)))]
        self.steps = self.parts + len(self.stages) - 1

    @staticmethod
    def scratch(total, parts, bits, lanes):
        dma = pltpu.SemaphoreType.DMA
        return [
            pltpu.VMEM((total, lanes), BF16),
            pltpu.VMEM((total, lanes), BF16),
            pltpu.VMEM((total // 2, lanes), BF16),
            pltpu.VMEM((total // 2, lanes), BF16),
            pltpu.VMEM((total // 2, lanes), BF16),
            dma((parts,)), dma((parts,)),
            dma((parts,)), dma((parts,)),
            dma((parts, bits)), dma((parts, bits)),
            dma((parts, bits)), dma((parts, bits)),
            dma((parts,)), dma((parts,)),
        ]

    def segment(self, k, sent=False):
        start, size = 0, self.half
        for high in self.highs[:k]:
            size //= 2
            start = start + high * size
        if sent:
            size //= 2
            start = start + (1 - self.highs[k]) * size
        return start, size

    def to_y(self, array, i):
        place = self.firsts[array] + i
        source = self.fars[array].at[ds(i * self.rows, self.rows)]
        target = self.from_y.at[ds(place * self.rows, self.rows)]
        return remote(
            source, target, self.sems[0].at[place], self.sems[1].at[place], self.other_chip
        )

    def to_x(self, i):
        source = self.mine.at[ds(i * self.rows + (1 - self.ctx) * self.half, self.half)]
        target = self.from_x.at[ds(i * self.half, self.half)]
        return remote(source, target, self.sems[2].at[i], self.sems[3].at[i], self.other_window)

    def to_z(self, i, k):
        start, size = self.segment(k, True)
        source = self.kept.at[ds(i * self.half + start, size)]
        target = self.from_z.at[ds(i * self.half + self.half - 2 * size, size)]
        return remote(source, target, self.sems[4].at[i, k], self.sems[5].at[i, k], self.beside[k])

    def back_z(self, i, k):
        start, size = self.segment(k + 1)
        here = self.out.at[ds(i * self.rows + self.ctx * self.half + start, size)]
        return remote(here, here, self.sems[6].at[i, k], self.sems[7].at[i, k], self.beside[k])

    def back_x(self, i):
        here = self.out.at[ds(i * self.rows + self.ctx * self.half, self.half)]
        return remote(here, here, self.sems[8].at[i], self.sems[9].at[i], self.other_window)

    def start(self):
        for array, count in enumerate(self.counts):
            each(count, lambda i, array=array: self.to_y(array, i).start())

    def join(self, i):
        here = ds(i * self.rows, self.rows)
        for array, count in enumerate(self.counts):
            first = self.firsts[array]

            def add(array=array, first=first):
                self.to_y(array, i - first).wait_recv()
                term = self.owns[array][ds((i - first) * self.rows, self.rows), :]
                total = term.astype(F32) + self.from_y[here, :].astype(F32)
                self.mine[here, :] = total.astype(BF16)

            pl.when((i >= first) & (i < first + count))(add)
        self.to_x(i).start()

    def spread(self, i):
        self.to_x(i).wait_recv()
        there = ds(i * self.half, self.half)
        term = self.mine[ds(i * self.rows + self.ctx * self.half, self.half), :]
        total = term.astype(F32) + self.from_x[there, :].astype(F32)
        self.kept[there, :] = total.astype(BF16)
        self.to_z(i, 0).start()

    def narrow(self, k, i):
        self.to_z(i, k).wait_recv()
        start, size = self.segment(k + 1)
        here = ds(i * self.half + start, size)
        there = ds(i * self.half + self.half - 2 * size, size)
        total = self.kept[here, :].astype(F32) + self.from_z[there, :].astype(F32)
        if k + 1 < len(self.bits):
            self.kept[here, :] = total.astype(BF16)
            self.to_z(i, k + 1).start()
        else:
            place = ds(i * self.rows + self.ctx * self.half + start, size)
            self.out[place, :] = total.astype(BF16)
            self.back_z(i, k).start()

    def widen(self, k, i):
        self.back_z(i, k).wait_recv()
        if k:
            self.back_z(i, k - 1).start()
        else:
            self.back_x(i).start()

    def step(self, i):
        for late, stage in enumerate(self.stages):
            pl.when((i >= late) & (i < self.parts + late))(functools.partial(stage, i - late))

    def finish(self):
        for array, count in enumerate(self.counts):
            each(count, lambda i, array=array: self.to_y(array, i).wait_send())

        def end(i):
            self.to_x(i).wait_send()
            self.back_x(i).wait()
            for k in range(len(self.bits)):
                self.to_z(i, k).wait_send()
                self.back_z(i, k).wait_send()

        each(self.parts, end)


def ds(start, size):
    return pl.ds(pl.multiple_of(start, 16), size)


def each(count, step):
    lax.fori_loop(0, count, lambda i, _: (step(i), 0)[1], 0)


def sum_kernel(counts, n_vectors, rows, *refs):
    n = len(counts)
    owns, fars, terms = refs[:n], refs[n : 2 * n], refs[2 * n : 2 * n + n_vectors]
    refs = refs[2 * n + n_vectors :]
    out, vec = refs[:2]
    from_vec, v_out, v_in = refs[-3:]
    sums = Sums(counts, rows, owns, fars, out, refs[2:-3])
    meet(sums.partners)
    at = 0
    for term in terms:
        vec[at : at + term.shape[0], : term.shape[1]] = term[...]
        at += term.shape[0]
    for hop, partner in enumerate(sums.partners):
        copy = remote(vec, from_vec.at[hop], v_out.at[hop], v_in.at[hop], partner)
        copy.start()
        if hop == 0:
            sums.start()
        copy.wait()
        vec[...] = vec[...] + from_vec[hop]
    each(sums.steps, sums.step)
    sums.finish()


def rows_of_part():
    return max(256, 32 * lax.axis_size("dp"))


def padded(pairs):
    rows = rows_of_part()
    owns, fars = (
        [jnp.pad(v, ((0, -v.shape[0] % rows), (0, 0))) for v in half] for half in zip(*pairs)
    )
    counts = [v.shape[0] // rows for v in owns]
    bits = (lax.axis_size("dp") - 1).bit_length()
    total = sum(counts) * rows
    shape = jax.ShapeDtypeStruct((total, owns[0].shape[1]), BF16)
    return owns, fars, counts, bits, shape, Sums.scratch(total, sum(counts), bits, shape.shape[1])


def unpadded(stack, pairs):
    shares, at = [], 0
    for own, _ in pairs:
        shares.append(stack[at : at + own.shape[0]])
        at += own.shape[0] + -own.shape[0] % rows_of_part()
    return shares


def sum_replicas(pairs, vectors):
    owns, fars, counts, bits, shape, scratch = padded(pairs)
    place = pl.BlockSpec(memory_space=pltpu.VMEM)
    away = pl.BlockSpec(memory_space=pl.ANY)
    dma = pltpu.SemaphoreType.DMA
    rows = sum(v.shape[0] for v in vectors)
    stack, summed = pl.pallas_call(
        functools.partial(sum_kernel, counts, len(vectors), rows_of_part()),
        out_shape=[shape, jax.ShapeDtypeStruct((rows, D), F32)],
        in_specs=[place] * len(counts) + [away] * len(counts) + [place] * len(vectors),
        out_specs=[place, place],
        scratch_shapes=scratch
        + [pltpu.VMEM((3 + bits, rows, D), F32), dma((3 + bits,)), dma((3 + bits,))],
        compiler_params=pltpu.CompilerParams(
            collective_id=0, has_side_effects=True, vmem_limit_bytes=56 * 1024 * 1024
        ),
        name="sum_replicas",
    )(*owns, *fars, *vectors)
    return unpadded(stack, pairs), summed


def back_kernel(mixed, counts, rows, *refs):
    refs = list(refs)

    def take(count):
        taken = refs[:count]
        del refs[:count]
        return taken

    places, flags, lo_ref, cols, before, earlier = take(6)
    first_values, fresh = (take(3), take(3)) if mixed else ((), ())
    given = () if mixed else take(3)
    exact, grad_ref, sum_ref = take(3)
    owns, fars = take(len(counts)), take(len(counts))
    dq_ref, dk_ref, dv_ref = take(3)
    if mixed:
        dv_before, dv_earlier = take(2)
    (out,) = take(1)
    if not mixed:
        dv_before, dv_earlier = take(2)
    dk_before, dk_earlier = take(2)
    near_k, near_v, far_k, far_v, home_k, home_v = take(6)
    values, acc_k, acc_v, acc_q = take(4)
    kv_out, kv_in = take(2)
    sums = Sums(counts, rows, owns, fars, out, refs)

    ctx, mp = lax.axis_index("ctx"), lax.axis_index("mp")
    sees_one = (mp >= 2) | ((mp == 0) & (ctx == 1))
    sees_two = mp == 3
    meet(sums.partners + [{"mp": 3 - mp}])
    sums.start()
    keys = ((earlier, 0), (before, 0), (cols, BAND))

    def home(which, source, target, g, device):
        return remote(
            source.at[g], target.at[g], kv_out.at[which, g], kv_in.at[which, g], device
        )

    def pair(g, act, step):
        act(step)
        if mixed:
            pl.when(g >= 2)(lambda: act(step + 1))
        else:
            act(step + 1)

    def from_last(g, step):
        source, target = (
            (dk_before, near_k), (dv_before, near_v), (dk_earlier, far_k), (dv_earlier, far_v),
        )[step]
        return home(step, source, target, g, {"mp": 2})

    def from_next(g, step, device):
        source, target = ((dk_before, home_k), (dv_before, home_v))[step]
        return home(4 + step, source, target, g, device)

    def group(g, _):
        if mixed:

            def reused():
                for part in range(3):
                    for j in range(GROUP):
                        at = places[(0 if part == 2 else REUSE) + GROUP * g + j]
                        values[part, j * HD : (j + 1) * HD, :] = first_values[part][at]

            def own():
                for part in range(3):
                    values[part] = fresh[part][g - 2]

            pl.when(g < 2)(reused)
            pl.when(g >= 2)(own)
        else:
            for part, (ref, at) in enumerate(keys):
                values[part] = ref[g, at + BAND : at + 2 * BAND, :]
        acc_k[...] = jnp.zeros_like(acc_k)
        if mixed:
            acc_v[...] = jnp.zeros_like(acc_v)
        else:
            for part in range(3):
                for j in range(GROUP):
                    head = GROUP * g + j
                    term = given[part][places[head]].astype(F32) * flags[head]
                    for side in range(2):
                        acc_v[2 * part + side, j * HD : (j + 1) * HD, :] = term[
                            :, side * TILE : (side + 1) * TILE
                        ]
        for t in range(WIN // TILE):
            tokens = slice(t * TILE, (t + 1) * TILE)
            low = lo_ref[:, tokens]
            place = 2 * WIN + t * TILE + lax.broadcasted_iota(jnp.int32, (1, TILE), 1)
            last = 2 * WIN // TILE + t

            def tile(kt, tokens=tokens, low=low, place=place, last=last):
                spot = kt * TILE + lax.broadcasted_iota(jnp.int32, (TILE, TILE), 0)
                keep = spot >= low
                if kt == last:
                    keep = keep & (spot <= place)
                span = slice(kt % 2 * TILE, (kt % 2 + 1) * TILE)
                key_ref, at = keys[kt // 2]
                for j in range(GROUP):
                    rows_j = slice(j * HD, (j + 1) * HD)
                    key = key_ref[g, at + j * HD : at + (j + 1) * HD, span]
                    query = cols[g, rows_j, tokens] * SCALE
                    grad = grad_ref[g, rows_j, tokens]
                    inner = jnp.sum(
                        grad.astype(F32) * exact[g, rows_j, tokens], axis=0, keepdims=True
                    )
                    raw = jnp.where(keep, dot(key, query, 0, 0), -jnp.inf)
                    weights = jnp.exp(raw - sum_ref[g, j : j + 1, tokens])
                    grad_weights = dot(values[kt // 2, rows_j, span], grad, 0, 0)
                    low_grad = (weights * (grad_weights - inner)).astype(BF16)
                    acc_v[kt, rows_j, :] += dot(grad, weights.astype(BF16), 1, 1)
                    acc_k[kt, rows_j, :] += dot(query, low_grad, 1, 1)
                    result = dot(key, low_grad, 1, 0)
                    acc_q[j] = result if kt == last else result + acc_q[j]

            for kt in reversed(range(last + 1)):
                if kt >= 4:
                    tile(kt)
                else:
                    pl.when(sees_one if kt >= 2 else sees_two)(functools.partial(tile, kt))
            for j in range(GROUP):
                dq_ref[g, j * HD : (j + 1) * HD, tokens] = acc_q[j] * SCALE
            sums.step(2 * g + t)
        results = ((dk_earlier, dv_earlier), (dk_before, dv_before), (dk_ref, dv_ref))
        for part, (dk, dv) in enumerate(results):
            for side in range(2):
                span = slice(side * TILE, (side + 1) * TILE)
                dk[g, :, span] = acc_k[2 * part + side].astype(dk.dtype)
                dv[g, :, span] = acc_v[2 * part + side].astype(dv.dtype)

        def send_last():
            pair(g, lambda step: from_last(g, step).start(), 0)
            pair(g, lambda step: from_last(g, step).start(), 2)

        pl.when(mp == 3)(send_last)
        pl.when((mp == 0) & (ctx == 1))(
            lambda: pair(g, lambda step: from_next(g, step, sums.other_window).start(), 0)
        )
        return 0

    lax.fori_loop(0, 4, group, 0)

    def relay(g):
        def one(step):
            near, far, source, total = (
                (near_k, far_k, dk_before, dk_ref), (near_v, far_v, dv_before, dv_ref),
            )[step]
            from_last(g, step).wait_recv()
            from_last(g, step + 2).wait_recv()
            source[g] = (source[g].astype(F32) + far[g].astype(F32)).astype(BF16)
            from_next(g, step, {"mp": 1}).start()
            total[g] += near[g].astype(F32)

        pair(g, one, 0)

    pl.when(mp == 2)(lambda: each(4, relay))
    for i in range(8, sums.steps):
        sums.step(i)

    def arrive(g):
        def one(step):
            arrived, total = ((home_k, dk_ref), (home_v, dv_ref))[step]
            from_next(g, step, sums.other_window).wait_recv()
            total[g] += arrived[g].astype(F32)

        pair(g, one, 0)

    pl.when((mp == 1) | ((mp == 0) & (ctx == 0)))(lambda: each(4, arrive))

    def sent_last(g):
        pair(g, lambda step: from_last(g, step).wait_send(), 0)
        pair(g, lambda step: from_last(g, step).wait_send(), 2)

    def sent_next(device):
        each(4, lambda g: pair(g, lambda step: from_next(g, step, device).wait_send(), 0))

    pl.when(mp == 3)(lambda: each(4, sent_last))
    pl.when(mp == 2)(lambda: sent_next({"mp": 1}))
    pl.when((mp == 0) & (ctx == 1))(lambda: sent_next(sums.other_window))
    sums.finish()


def attend_back(places, flags, low, front, firsts, freshes, given, exact, grad_heads, lse, pairs):
    mixed = bool(firsts)
    owns, fars, counts, bits, shape, scratch = padded(pairs)
    place = pl.BlockSpec(memory_space=pltpu.VMEM)
    away = pl.BlockSpec(memory_space=pl.ANY)
    scalar = pl.BlockSpec(memory_space=pltpu.SMEM)
    dma = pltpu.SemaphoreType.DMA
    by_head = [v.reshape(-1, HD, WIN) for v in firsts[::-1]] + list(freshes[::-1])
    by_head += [v.reshape(-1, HD, WIN) for v in given[::-1]]
    local = [low, *front, *by_head, exact, grad_heads, lse, *owns]
    wide = jax.ShapeDtypeStruct((4, BAND, WIN), F32)
    slim = jax.ShapeDtypeStruct((4, BAND, WIN), BF16)
    outs = [wide] * 3 + ([slim] * 2 if mixed else []) + [shape]
    block = pltpu.VMEM((4, BAND, WIN), BF16)
    results = pl.pallas_call(
        functools.partial(back_kernel, mixed, counts, rows_of_part()),
        out_shape=outs,
        in_specs=[scalar, scalar] + [place] * len(local) + [away] * len(fars),
        out_specs=[place] * len(outs),
        scratch_shapes=[block] * (8 if mixed else 10)
        + [
            pltpu.VMEM((3, BAND, WIN), BF16),
            pltpu.VMEM((TILES, BAND, TILE), F32),
            pltpu.VMEM((TILES, BAND, TILE), F32),
            pltpu.VMEM((GROUP, HD, TILE), F32),
            dma((6, 4)),
            dma((6, 4)),
        ]
        + scratch,
        compiler_params=pltpu.CompilerParams(
            collective_id=3 if mixed else 4,
            has_side_effects=True,
            vmem_limit_bytes=56 * 1024 * 1024,
        ),
        name="attend_back",
    )(places, flags, *local, *fars)
    return results[:-1], unpadded(results[-1], pairs)


def gelu(hidden):
    return jax.nn.gelu(hidden, approximate=True)


def tail_forward(stream, heads, out_weight, out_bias, gain, shift, ups, up_biases, downs):
    stream = stream + dot(heads, out_weight, 0, 0) + out_bias[0]
    normed, unit, scale = norm_rows(stream, gain[1], shift[1])
    hidden, active, total = [], [], out_bias[1]
    for up, bias, down in zip(ups, up_biases, downs, strict=True):
        hidden.append(dot(normed, up, 1, 0) + bias)
        active.append(gelu(hidden[-1]).astype(BF16))
        total = total + dot(active[-1], down, 1, 0)
    return stream + total, (normed, unit, scale, hidden, active)


def tail_backward(grad, kept, out_weight, gain, ups, downs):
    normed, unit, scale, hidden, active = kept
    bias_mlp = jnp.sum(grad, axis=0)
    rounded = grad.astype(BF16)
    mats, up_biases, normed_grad = [], [], 0.0
    for up, down, before, after in zip(ups, downs, hidden, active, strict=True):
        _, pull = jax.vjp(gelu, before)
        grad_hidden = pull(dot(rounded, down, 1, 1))[0]
        up_biases.append(jnp.sum(grad_hidden, axis=0))
        low = grad_hidden.astype(BF16)
        mats.append(
            jnp.concatenate(
                [dot(normed, low, 0, 0).astype(BF16), dot(after, rounded, 0, 0).astype(BF16)]
            )
        )
        normed_grad = normed_grad + dot(low, up, 1, 1)
    middle, gain_grad, shift_grad = norm_back(normed_grad, unit, scale, gain[1])
    grad = grad + middle
    bias_attn = jnp.sum(grad, axis=0)
    rounded = grad.astype(BF16)
    grad_heads = dot(out_weight, rounded, 1, 1).astype(BF16)
    return grad, rounded, grad_heads, mats, up_biases, (gain_grad, shift_grad, bias_attn, bias_mlp)


def turned(weight):
    return jnp.swapaxes(weight, -1, -2)


def shards(
    block_input, cotangent, doc_lengths, reuse_heads,
    norm_gain1, norm_bias1, projections1, front_bias1, out_weight1, out_bias1,
    up_weight1, up_bias1, down_weight1,
    norm_gain2, norm_bias2, query_key2, query_bias2, fresh_value2, value_bias2,
    out_weight2, out_bias2, up_weight2, up_bias2, down_weight2,
):
    low, first = row_starts(doc_lengths[0])
    taken = jnp.arange(4 * GROUP, dtype=jnp.int32)[:, None] == reuse_heads[None, :]
    taker = jnp.sum(jnp.where(taken, jnp.arange(REUSE, dtype=jnp.int32)[None, :], 0), axis=1)
    flags = jnp.any(taken, axis=1).astype(F32)
    scalars = jnp.concatenate([first, reuse_heads])
    band_of, in_band = reuse_heads // GROUP, reuse_heads % GROUP
    places2 = jnp.concatenate(
        [band_of * 3 * GROUP + 2 * GROUP + in_band, band_of * 2 * GROUP + GROUP + in_band]
    )

    stream0 = block_input.astype(F32)
    normed1, unit1, scale1 = norm_rows(stream0, norm_gain1[0], norm_bias1[0])
    n_front1, n_front2 = 3 * BAND, 2 * BAND + BAND // 2
    none = jnp.zeros((BAND,), BF16)

    def as_row(pieces):
        row = jnp.concatenate(pieces).astype(F32)
        return jnp.pad(row[None, :], ((0, 7), (0, -row.shape[0] % 128)))

    small = jnp.concatenate([query_bias2, value_bias2, up_bias1, up_bias2])
    small = jnp.pad(small, (0, 16 * 128 - small.shape[0])).reshape(16, 128)
    own_front2 = jnp.concatenate([turned(query_key2).reshape(2 * BAND, D), turned(fresh_value2)])
    own_front2 = jnp.pad(own_front2, ((0, -n_front2 % 64), (0, 0)))
    (
        cols1, before1, earlier1, front1, _, small,
        up1, down1, up2, down2, front2, outs1, outs2,
    ) = project(
        normed1, turned(projections1).reshape(n_front1, D),
        as_row([front_bias1[0], none, front_bias1[1]]), n_front1, 2 * BAND, small,
        (up_weight1, down_weight1, up_weight2, down_weight2, own_front2, out_weight1, out_weight2),
    )
    ups1, downs1, ups2, downs2 = (
        [own] + by_distance(w)[1:]
        for own, w in (
            (up_weight1, up1), (down_weight1, down1), (up_weight2, up2), (down_weight2, down2)
        )
    )
    front2, outs1, outs2 = (
        lax.dynamic_update_index_in_dim(w, own, lax.axis_index("mp"), 0)
        for own, w in ((own_front2, front2), (out_weight1, outs1), (out_weight2, outs2))
    )
    outs1, outs2 = outs1.reshape(D, D), outs2.reshape(D, D)
    small = small.reshape(4, -1)
    at = BAND + BAND // 2
    bias2 = jnp.stack([as_row([small[s, :BAND], none, small[s, BAND:at]]) for s in range(4)])
    up_biases1 = by_distance(small[:, at : at + D])
    up_biases2 = by_distance(small[:, at + D : at + 2 * D])

    front_kv1 = (cols1, before1, earlier1)
    values1 = values_of(cols1, before1, earlier1)
    heads1, exact1, sums1 = attend(scalars, low, front_kv1, values1)
    stream1, kept1 = tail_forward(
        stream0, heads1.reshape(D, WIN), outs1, out_bias1, norm_gain1, norm_bias1,
        ups1, up_biases1, downs1,
    )

    normed2, unit2, scale2 = norm_rows(stream1, norm_gain2[0], norm_bias2[0])
    cols2, before2, earlier2 = project(normed2, front2, bias2, n_front2, n_front2 - BAND)
    front2 = front2[:, :n_front2]

    front_kv2 = (cols2, before2, earlier2)
    fresh2 = [v[:, -(BAND // 2) :].reshape(2, BAND, WIN) for v in front_kv2]
    values2 = values_mixed(front_kv1, fresh2)
    heads2, exact2, sums2 = attend(scalars, low, front_kv2, values2)
    stream2, kept2 = tail_forward(
        stream1, heads2.reshape(D, WIN), outs2, out_bias2, norm_gain2, norm_bias2,
        ups2, up_biases2, downs2,
    )
    block_output = stream2.astype(BF16)

    grad, rounded, grad_heads, mats2, up_grads2, small2 = tail_backward(
        cotangent.astype(F32), kept2, outs2, norm_gain2, ups2, downs2
    )
    own2, far2 = sum_cores(mats2)
    (dq2, dk2, dv2, dv2_before, dv2_earlier), (mats2,) = attend_back(
        places2, flags, low, front_kv2, front_kv1, fresh2, (), exact2,
        grad_heads.reshape(4, BAND, WIN), sums2, [(own2, far2)],
    )
    grad_out2 = dot(heads2.reshape(D, WIN), rounded, 1, 0).astype(BF16).reshape(4, BAND, D)

    dcols2 = jnp.concatenate([dq2, dk2, dv2[2:].reshape(4, BAND // 2, WIN)], axis=1)
    bias_grad2 = jnp.sum(dcols2, axis=2)
    dcols2 = dcols2.astype(BF16)
    grad_front2 = dot(dcols2.reshape(-1, WIN), normed2, 1, 0).astype(BF16).reshape(4, n_front2, D)
    attn2 = [
        jnp.concatenate(pair)
        for pair in zip(by_distance(grad_out2), by_distance(grad_front2), strict=True)
    ]
    attn2 = sum_cores(attn2)
    normed_grad = dot(dcols2.reshape(-1, WIN), front2.reshape(-1, D), 0, 0)
    middle, gain_front2, shift_front2 = norm_back(normed_grad, unit2, scale2, norm_gain2[0])
    grad = grad + middle

    grad, rounded, grad_heads, mats1, up_grads1, small1 = tail_backward(
        grad, kept1, outs1, norm_gain1, ups1, downs1
    )
    pairs = [attn2, sum_cores(mats1)]
    (dq1, dk1, dv1), (attn2, mats1) = attend_back(
        taker, flags, low, front_kv1, (), (), (dv2, dv2_before, dv2_earlier), exact1,
        grad_heads.reshape(4, BAND, WIN), sums1, pairs,
    )
    grad_out1 = dot(heads1.reshape(D, WIN), rounded, 1, 0).astype(BF16).reshape(4, BAND, D)

    dcols1 = jnp.concatenate([dq1, dk1, dv1], axis=1)
    bias_grad1 = jnp.sum(dcols1, axis=2)
    dcols1 = dcols1.astype(BF16)
    grad_front1 = dot(dcols1.reshape(-1, WIN), normed1, 1, 0).astype(BF16).reshape(4, n_front1, D)
    attn1 = [
        jnp.concatenate(pair)
        for pair in zip(by_distance(grad_out1), by_distance(grad_front1), strict=True)
    ]
    attn1 = sum_cores(attn1)
    normed_grad = dot(dcols1.reshape(-1, WIN), front1.reshape(-1, D), 0, 0)
    middle, gain_front1, shift_front1 = norm_back(normed_grad, unit1, scale1, norm_gain1[0])
    input_grad = (grad + middle).astype(BF16)

    vectors = [
        gain_front1, small1[0], shift_front1, small1[1], small1[2], small1[3],
        gain_front2, small2[0], shift_front2, small2[1], small2[2], small2[3],
        bias_grad1[:, :BAND].reshape(-1), bias_grad1[:, 2 * BAND :].reshape(-1),
        bias_grad2[:, :BAND].reshape(-1), bias_grad2[:, 2 * BAND :].reshape(-1),
        in_order(up_grads1), in_order(up_grads2),
    ]
    vectors = [vector.reshape(-1, min(D, vector.size)) for vector in vectors]
    (attn1,), packed = sum_replicas([attn1], vectors)
    sums, at = [], 0
    for vector in vectors:
        sums.append(packed[at : at + vector.shape[0]].reshape(-1)[: vector.size])
        at += vector.shape[0]
    me = lax.axis_index("mp")

    def mine(vector):
        return lax.dynamic_index_in_dim(vector.reshape(4, -1), me, 0, keepdims=False)

    def pair(i):
        return jnp.stack([sums[i], sums[i + 1]])

    return (
        block_output,
        input_grad,
        pair(0),
        pair(2),
        turned(attn1[BAND : BAND + n_front1].reshape(3, BAND, D)).astype(F32),
        jnp.stack([mine(sums[12]), mine(sums[13])]),
        attn1[:BAND].astype(F32),
        pair(4),
        mats1[:D].astype(F32),
        mine(sums[16]),
        mats1[D:].astype(F32),
        pair(6),
        pair(8),
        turned(attn2[BAND : 3 * BAND].reshape(2, BAND, D)).astype(F32),
        mine(sums[14]),
        turned(attn2[3 * BAND : BAND + n_front2]).astype(F32),
        mine(sums[15]),
        attn2[:BAND].astype(F32),
        pair(10),
        mats2[:D].astype(F32),
        mine(sums[17]),
        mats2[D:].astype(F32),
    )


def solution(mesh):
    rows = P(("dp", "ctx", "mp"), None)
    placed = (
        rows, rows, P(("dp", "ctx"), None), P(),
        P(), P(), P(None, None, "mp"), P(None, "mp"), P("mp", None), P(),
        P(None, "mp"), P("mp"), P("mp", None),
        P(), P(), P(None, None, "mp"), P("mp"), P(None, "mp"), P("mp"),
        P("mp", None), P(), P(None, "mp"), P("mp"), P("mp", None),
    )
    given = (
        rows, rows,
        P(), P(), P(None, None, "mp"), P(None, "mp"), P("mp", None), P(),
        P(None, "mp"), P("mp"), P("mp", None),
        P(), P(), P(None, None, "mp"), P("mp"), P(None, "mp"), P("mp"),
        P("mp", None), P(), P(None, "mp"), P("mp"), P("mp", None),
    )
    return jax.shard_map(shards, mesh=mesh, in_specs=placed, out_specs=given, check_vma=False)
```

```python
import functools

import jax
import jax.numpy as jnp
from jax import lax
from jax.experimental import pallas as pl
from jax.experimental.pallas import tpu as pltpu
from jax.sharding import PartitionSpec as P

D = 768
HD = 64
REUSE = 6
WIN = 512
EARLY = 4
CHUNK = 256
LAG = 2
HOOK_FIRST, HOOK_SECOND = -3, 0
GROUP = 3
BAND = GROUP * HD
TILE = 256
TILES = 3 * WIN // TILE
EPS = 1e-05
SCALE = HD**-0.5
F32 = jnp.float32
BF16 = jnp.bfloat16


def swap(value, axis, bit):
    devices = range(lax.axis_size(axis))
    return lax.ppermute(value, axis, [(i, i ^ bit) for i in devices])


def in_order(parts):
    return jnp.concatenate(by_distance(jnp.stack(parts)))


def by_distance(stacked):
    me = lax.axis_index("mp")
    return [
        lax.dynamic_index_in_dim(stacked, me ^ distance, 0, keepdims=False)
        for distance in range(4)
    ]


def flip(position, bit):
    return position + bit * (1 - 2 * ((position // bit) % 2))


def remote(source, target, sent, received, device):
    return pltpu.make_async_remote_copy(
        src_ref=source, dst_ref=target, send_sem=sent, recv_sem=received,
        device_id=device, device_id_type=pl.DeviceIdType.MESH,
    )


def meet(devices):
    barrier = pltpu.get_barrier_semaphore()
    for device in devices:
        pl.semaphore_signal(barrier, inc=1, device_id=device, device_id_type=pl.DeviceIdType.MESH)
    pl.semaphore_wait(barrier, len(devices))


def dot(left, right, left_dim, right_dim):
    return lax.dot_general(
        left, right, (((left_dim,), (right_dim,)), ((), ())), preferred_element_type=F32
    )


def norm_rows(value, gain, shift):
    mean = jnp.mean(value, axis=-1, keepdims=True)
    centred = value - mean
    spread = jnp.mean(centred * centred, axis=-1, keepdims=True)
    scale = lax.rsqrt(spread + EPS)
    unit = centred * scale
    return (unit * gain + shift).astype(BF16), unit, scale


def norm_back(grad, unit, scale, gain):
    scaled = grad * gain
    inner = (
        scaled
        - jnp.mean(scaled, axis=-1, keepdims=True)
        - unit * jnp.mean(scaled * unit, axis=-1, keepdims=True)
    )
    return scale * inner, jnp.sum(grad * unit, axis=0), jnp.sum(grad, axis=0)


def front_kernel(more_rows, lead, mixed, *refs):
    refs = list(refs)

    def take(count):
        taken = refs[:count]
        del refs[:count]
        return taken

    ctx, dp, mp = (lax.axis_index(axis) for axis in ("ctx", "dp", "mp"))
    near, far, last = {"mp": flip(mp, 1)}, {"mp": flip(mp, 2)}, {"mp": 3 - mp}
    window = {"ctx": 1 - ctx}
    chunks = chunks_of(lead, more_rows)
    n_chunks, n_more = len(chunks), len(more_rows)
    n_arrays = n_more + lead
    early, offset = (EARLY, HOOK_FIRST) if lead else (2, HOOK_SECOND)
    places, lo_ref, normed = take(3)
    first_values = take(3) if mixed else ()
    front, bias = (None, None) if lead else take(2)
    vectors_own = take(2 * lead)
    arrays_own = take(n_arrays)
    cols, before, earlier, out_ref, exact_ref, sum_ref = take(6)
    vectors = take(2 * lead)
    arrays = take(n_arrays)
    if lead:
        front, bias = arrays[0], vectors[0]
    values, raw, top, total, acc, kv_out, kv_in, on_out, on_in = take(9)
    m_out, m_in = take(2)
    if lead:
        f_out, f_in = take(2)
    meet([near, far, last, window, {"dp": flip(dp, 1)}])
    directions = (near, far, last)
    if True:

        def whole(k, way):
            return remote(
                vectors_own[k], vectors[k].at[mp], f_out.at[k, way], f_in.at[k, way],
                directions[way],
            )

        bit = lax.rem(dp, 2)
        first = [(bit, {"dp": flip(dp, 1)}), (ctx, window)]

        def quarters(c):
            a, start, rows = chunks[c]
            (low, low_device), (high, high_device) = first if c % 2 else first[::-1]
            return a, start, rows // 4, rows // 2, low, low_device, high, high_device

        def copy(c, way, source, target, device):
            return remote(source, target, m_out.at[c, way], m_in.at[c, way], device)

        def beside(c):
            a, start, rows = chunks[c]
            here = pl.ds(start, rows)
            return copy(c, 0, arrays_own[a].at[here], arrays[a].at[mp, here], near)

        def across(c):
            a, start, quarter, half, low, _, high, _ = quarters(c)
            here = ds(start + high * half + low * quarter, quarter)
            return copy(c, 1, arrays_own[a].at[here], arrays[a].at[mp, here], far)

        def widen(c):
            a, start, quarter, half, low, device, high, _ = quarters(c)
            there = arrays[a].at[flip(mp, 2), ds(start + high * half + low * quarter, quarter)]
            return copy(c, 2, there, there, device)

        def complete(c):
            a, start, _, half, _, _, high, device = quarters(c)
            there = arrays[a].at[flip(mp, 2), ds(start + high * half, half)]
            return copy(c, 3, there, there, device)

        def hand_on(c):
            a, start, rows = chunks[c]
            there = arrays[a].at[flip(mp, 2), pl.ds(start, rows)]
            return copy(c, 4, there, there, near)

        across(0).start()
        beside(0).start()
        for k in range(2 * lead):
            for way in range(3):
                whole(k, way).start()
        for c in range(1, early):
            across(c).start()
        for c in range(1, n_chunks):
            beside(c).start()
        if lead:
            arrays[0][mp] = arrays_own[0][...]
        for k in range(2 * lead):
            vectors[k][mp] = vectors_own[k][...]

    def gather(step):
        for late, stage in enumerate(
            ((across, widen), (widen, complete), (complete, hand_on))
        ):
            a = step + lead - LAG * late
            if lead <= a < n_chunks:
                stage[0](a).wait_recv()
                stage[1](a).start()

    kv_rows = before.shape[1]
    from_row = cols.shape[1] - kv_rows
    sends_on = (mp == 1) | (mp == 2)
    sends_window = (mp == 0) & (ctx == 0)
    receives = (mp >= 2) | ((mp == 0) & (ctx == 1))

    def pass_on(slot, device):
        source = cols.at[slot, pl.ds(from_row, kv_rows)]
        return remote(source, before.at[slot], kv_out.at[slot], kv_in.at[slot], device)

    def pass_again(slot):
        return remote(before.at[slot], earlier.at[slot], on_out.at[slot], on_in.at[slot], {"mp": 3})

    order = (mp, flip(mp, 1), flip(mp, 2), 3 - mp) if lead else range(4)
    for k, slot in enumerate(order):
        if lead and k == 1:
            for vector in range(2):
                for way in range(3):
                    whole(vector, way).wait_recv()
            beside(0).wait_recv()
        if lead and k == 2:
            across(0).wait_recv()
            widen(0).start()
            widen(0).wait_recv()
            complete(0).start()
            complete(0).wait_recv()
            hand_on(0).start()
        if lead and k == 3:
            hand_on(0).wait_recv()
        column = jnp.transpose(bias[slot])[: cols.shape[1], 0:1]
        cols[slot] = (dot(front[slot, : cols.shape[1]], normed[...], 1, 1) + column).astype(BF16)
        pl.when(sends_on)(lambda: pass_on(slot, {"mp": mp + 1}).start())
        pl.when(sends_window)(lambda: pass_on(slot, window).start())
    for c in range(early, n_chunks):
        across(c).start()
    steps = n_chunks - lead + 2 * LAG
    for step in range(steps):
        if step + offset < 0:
            gather(step)

    def arrive(slot):
        def from_next():
            pass_on(slot, window).wait_recv()
            pl.when(mp == 2)(lambda: pass_again(slot).start())
            pl.when(mp == 3)(lambda: pass_again(slot).wait_recv())

        pl.when(receives)(from_next)

    keys = ((earlier, 0), (before, 0), (cols, BAND))
    sees_one, sees_two = receives, mp == 3
    sender = lax.max(mp - 1, 0)

    def group(k, _):
        if mixed:
            g = k
            pl.when(k < 2)(lambda: arrive(k))

            def rest():
                arrive(2)
                arrive(3)

            pl.when(k == 2)(rest)
        else:
            g = (sender % 2 + k) % 2 + 2 * ((sender // 2 + k // 2) % 2)
            arrive(g)
        place_values(mixed, g, places, first_values, keys, values)
        for t in range(WIN // TILE):
            tokens = slice(t * TILE, (t + 1) * TILE)
            low = lo_ref[:, tokens]
            place = 2 * WIN + t * TILE + lax.broadcasted_iota(jnp.int32, (1, TILE), 1)
            end = 2 * WIN // TILE + t

            def score(kt, tokens=tokens, low=low, place=place, end=end):
                spot = kt * TILE + lax.broadcasted_iota(jnp.int32, (TILE, TILE), 0)
                keep = spot >= low
                if kt == end:
                    keep = keep & (spot <= place)
                span = slice(kt % 2 * TILE, (kt % 2 + 1) * TILE)
                key_ref, at = keys[kt // 2]
                for j in range(GROUP):
                    rows = slice(j * HD, (j + 1) * HD)
                    key = key_ref[g, at + j * HD : at + (j + 1) * HD, span]
                    found = dot(key, cols[g, rows, tokens] * SCALE, 0, 0)
                    found = jnp.where(keep, found, -jnp.inf)
                    raw[j, kt] = found
                    peak = jnp.max(found.reshape(TILE // 8, 8, TILE), axis=0)
                    top[j] = peak if kt == end else jnp.maximum(top[j], peak)

            def weigh(kt, end=end):
                span = slice(kt % 2 * TILE, (kt % 2 + 1) * TILE)
                for j in range(GROUP):
                    rows = slice(j * HD, (j + 1) * HD)
                    powers = jnp.exp(raw[j, kt] - top[j, 0:1])
                    added = jnp.sum(powers.reshape(TILE // 8, 8, TILE), axis=0)
                    result = dot(values[kt // 2, rows, span], powers.astype(BF16), 1, 0)
                    total[j] = added if kt == end else total[j] + added
                    acc[j] = result if kt == end else acc[j] + result

            for stage in (score, weigh):
                for kt in reversed(range(end + 1)):
                    if kt >= 4:
                        stage(kt)
                    else:
                        pl.when(sees_one if kt >= 2 else sees_two)(functools.partial(stage, kt))
                if stage is score:
                    for j in range(GROUP):
                        top[j] = jnp.broadcast_to(jnp.max(top[j], axis=0, keepdims=True), (8, TILE))
            for j in range(GROUP):
                rows = slice(j * HD, (j + 1) * HD)
                whole_sum = jnp.sum(total[j], axis=0, keepdims=True)
                result = acc[j] / whole_sum
                out_ref[g, rows, tokens] = result.astype(BF16)
                exact_ref[g, rows, tokens] = result
                sum_ref[g, j : j + 1, tokens] = top[j, 0:1] + jnp.log(whole_sum)
            for step in range(steps):
                if (step + offset) % 2 == t and 0 <= step + offset < 8:
                    pl.when(k == (step + offset) // 2)(functools.partial(gather, step))
        return 0

    lax.fori_loop(0, 4, group, 0)
    for step in range(steps):
        if step + offset >= 8:
            gather(step)

    def sent(device):
        each(4, lambda slot: pass_on(slot, device).wait_send())

    pl.when(sends_on)(lambda: sent({"mp": mp + 1}))
    pl.when(sends_window)(lambda: sent(window))
    pl.when(mp == 2)(lambda: each(4, lambda slot: pass_again(slot).wait_send()))
    for k in range(2 * lead):
        for way in range(3):
            whole(k, way).wait_send()
    for a in range(n_chunks):
        beside(a).wait_send()
        if a >= lead:
            beside(a).wait_recv()
            hand_on(a).wait_recv()
        across(a).wait_send()
        widen(a).wait_send()
        complete(a).wait_send()
        hand_on(a).wait_send()


def place_values(mixed, g, places, first_values, keys, values):
    if not mixed:
        for part, (ref, at) in enumerate(keys):
            values[part] = ref[g, at + BAND : at + 2 * BAND, :]
        return

    def reused():
        for part in range(3):
            for j in range(GROUP):
                at = places[(0 if part == 2 else REUSE) + GROUP * g + j]
                values[part, j * HD : (j + 1) * HD, :] = first_values[part][at]

    def own():
        wide = BAND // 2
        for part, (ref, at) in enumerate(keys):
            for side in range(2):
                values[part, side * wide : (side + 1) * wide, :] = ref[
                    2 * (g - 2) + side, at + BAND : at + BAND + wide, :
                ]

    pl.when(g < 2)(reused)
    pl.when(g >= 2)(own)


def chunks_of(lead, more_rows):
    chunks = [(0, 0, 3 * BAND)] * lead
    for array, rows in enumerate(more_rows):
        size = CHUNK if rows % CHUNK == 0 else rows
        chunks += [(array + lead, start, size) for start in range(0, rows, size)]
    return chunks


def project(places, low, normed, front, bias, n_cols, kv_rows, firsts=(), small=None, more=()):
    place = pl.BlockSpec(memory_space=pltpu.VMEM)
    away = pl.BlockSpec(memory_space=pl.ANY)
    dma = pltpu.SemaphoreType.DMA
    given = [low, normed] + [v.reshape(-1, HD, WIN) for v in firsts[::-1]]
    lead = small is not None
    given += [bias, small, front] if lead else [front, bias]
    made = [(4, n_cols, WIN), (4, kv_rows, WIN), (4, kv_rows, WIN), (4, BAND, WIN)]
    made = [jax.ShapeDtypeStruct(shape, BF16) for shape in made]
    made += [jax.ShapeDtypeStruct((4, rows, WIN), F32) for rows in (BAND, 8)]
    scratch = [
        pltpu.VMEM((3, BAND, WIN), BF16),
        pltpu.VMEM((GROUP, TILES, TILE, TILE), F32),
        pltpu.VMEM((GROUP, 8, TILE), F32),
        pltpu.VMEM((GROUP, 8, TILE), F32),
        pltpu.VMEM((GROUP, HD, TILE), F32),
    ] + [dma((4,))] * 4
    gathered = ([bias, small, front] if lead else []) + list(more)
    gathered = [jax.ShapeDtypeStruct((4,) + v.shape, v.dtype) for v in gathered]
    rows = [v.shape[0] for v in more]
    scratch += [dma((len(chunks_of(lead, rows)), 5))] * 2 + ([dma((2, 3))] * 2 if lead else [])
    return pl.pallas_call(
        functools.partial(front_kernel, rows, int(lead), bool(firsts)),
        out_shape=made + gathered,
        in_specs=[pl.BlockSpec(memory_space=pltpu.SMEM)]
        + [place] * len(given) + [away] * len(more),
        out_specs=[place] * (len(made) + 3 * lead) + [away] * len(more),
        scratch_shapes=scratch,
        compiler_params=pltpu.CompilerParams(
            collective_id=1 if lead else 2,
            has_side_effects=True,
            vmem_limit_bytes=48 * 1024 * 1024,
        ),
        name="front_first" if lead else "front_second",
    )(places, *given, *more)


def row_starts(lengths):
    part = lax.axis_index("mp")
    place = (part - 1) * WIN + jnp.arange(WIN, dtype=jnp.int32)
    ends = jnp.cumsum(lengths)
    begun = jnp.max(jnp.where(place[:, None] >= ends[None, :], ends[None, :], 0), axis=1)
    document = begun - (part - 1) * WIN + 2 * WIN
    window = jnp.where(lax.axis_index("ctx") > 0, WIN, 2 * WIN)
    low = jnp.where(part == 0, window, document).astype(jnp.int32)
    return low.reshape(1, WIN)


class Sums:
    def __init__(self, counts, rows, terms, out, refs):
        n = len(counts)
        self.counts, self.rows, self.out = counts, rows, out
        self.owns, self.fars, self.nears, self.lasts = (terms[k * n : k * n + n] for k in range(4))
        self.from_near, self.from_last = refs[:2]
        self.mine = self.from_near
        self.from_y, self.from_x, self.kept, self.from_z = refs[2:6]
        self.sems = refs[6:]
        self.parts = sum(counts)
        self.firsts = [sum(counts[:k]) for k in range(len(counts))]
        self.ctx, self.dp, mp = (lax.axis_index(axis) for axis in ("ctx", "dp", "mp"))
        self.half = rows // 2
        self.bits = [1 << k for k in range((lax.axis_size("dp") - 1).bit_length())]
        self.highs = [(self.dp // bit) % 2 for bit in self.bits]
        self.other_chip, self.other_window = {"mp": flip(mp, 2)}, {"ctx": 1 - self.ctx}
        self.other_core = {"mp": flip(mp, 1)}
        self.beside = [{"dp": flip(self.dp, bit)} for bit in self.bits]
        self.partners = [self.other_chip, self.other_window, self.other_core] + self.beside
        self.stages = [self.join, self.spread]
        self.stages += [functools.partial(self.narrow, k) for k in range(len(self.bits))]
        self.stages += [functools.partial(self.widen, k) for k in reversed(range(len(self.bits)))]
        self.steps = self.parts + len(self.stages) - 1

    @staticmethod
    def scratch(total, parts, bits, lanes):
        dma = pltpu.SemaphoreType.DMA
        return [
            pltpu.VMEM((total, lanes), BF16),
            pltpu.VMEM((total, lanes), BF16),
            pltpu.VMEM((total, lanes), BF16),
            pltpu.VMEM((total // 2, lanes), BF16),
            pltpu.VMEM((total // 2, lanes), BF16),
            pltpu.VMEM((total // 2, lanes), BF16),
            dma((parts,)), dma((parts,)),
            dma((parts,)), dma((parts,)),
            dma((parts, bits)), dma((parts, bits)),
            dma((parts, bits)), dma((parts, bits)),
            dma((parts,)), dma((parts,)),
            dma((parts, 2)), dma((parts, 2)),
        ]

    def segment(self, k, sent=False):
        start, size = 0, self.half
        for high in self.highs[:k]:
            size //= 2
            start = start + high * size
        if sent:
            size //= 2
            start = start + (1 - self.highs[k]) * size
        return start, size

    def to_core(self, array, i, which):
        place = self.firsts[array] + i
        source = (self.nears, self.lasts)[which][array].at[ds(i * self.rows, self.rows)]
        target = (self.from_near, self.from_last)[which].at[ds(place * self.rows, self.rows)]
        sent, received = (sem.at[place, which] for sem in self.sems[10:12])
        return remote(source, target, sent, received, self.other_core)

    def to_y(self, i):
        here = ds(i * self.rows, self.rows)
        source, target = self.from_last.at[here], self.from_y.at[here]
        return remote(source, target, self.sems[0].at[i], self.sems[1].at[i], self.other_chip)

    def to_x(self, i):
        source = self.mine.at[ds(i * self.rows + (1 - self.ctx) * self.half, self.half)]
        target = self.from_x.at[ds(i * self.half, self.half)]
        return remote(source, target, self.sems[2].at[i], self.sems[3].at[i], self.other_window)

    def to_z(self, i, k):
        start, size = self.segment(k, True)
        source = self.kept.at[ds(i * self.half + start, size)]
        target = self.from_z.at[ds(i * self.half + self.half - 2 * size, size)]
        return remote(source, target, self.sems[4].at[i, k], self.sems[5].at[i, k], self.beside[k])

    def back_z(self, i, k):
        start, size = self.segment(k + 1)
        here = self.out.at[ds(i * self.rows + self.ctx * self.half + start, size)]
        return remote(here, here, self.sems[6].at[i, k], self.sems[7].at[i, k], self.beside[k])

    def back_x(self, i):
        here = self.out.at[ds(i * self.rows + self.ctx * self.half, self.half)]
        return remote(here, here, self.sems[8].at[i], self.sems[9].at[i], self.other_window)

    def start(self):
        for array, count in enumerate(self.counts):

            def send(i, array=array):
                self.to_core(array, i, 1).start()
                self.to_core(array, i, 0).start()

            each(count, send)
        for array, count in enumerate(self.counts):

            def fold(i, array=array):
                place = self.firsts[array] + i
                self.to_core(array, i, 1).wait_recv()
                here = ds(place * self.rows, self.rows)
                term = self.fars[array][ds(i * self.rows, self.rows), :]
                total = term.astype(F32) + self.from_last[here, :].astype(F32)
                self.from_last[here, :] = total.astype(BF16)
                self.to_y(place).start()

            each(count, fold)

    def join(self, i):
        here = ds(i * self.rows, self.rows)
        self.to_y(i).wait_recv()
        for array, count in enumerate(self.counts):
            first = self.firsts[array]

            def add(array=array, first=first):
                self.to_core(array, i - first, 0).wait_recv()
                term = self.owns[array][ds((i - first) * self.rows, self.rows), :]
                total = term.astype(F32) + self.from_near[here, :].astype(F32)
                self.mine[here, :] = (total + self.from_y[here, :].astype(F32)).astype(BF16)

            pl.when((i >= first) & (i < first + count))(add)
        self.to_x(i).start()

    def spread(self, i):
        self.to_x(i).wait_recv()
        there = ds(i * self.half, self.half)
        term = self.mine[ds(i * self.rows + self.ctx * self.half, self.half), :]
        total = term.astype(F32) + self.from_x[there, :].astype(F32)
        self.kept[there, :] = total.astype(BF16)
        self.to_z(i, 0).start()

    def narrow(self, k, i):
        self.to_z(i, k).wait_recv()
        start, size = self.segment(k + 1)
        here = ds(i * self.half + start, size)
        there = ds(i * self.half + self.half - 2 * size, size)
        total = self.kept[here, :].astype(F32) + self.from_z[there, :].astype(F32)
        if k + 1 < len(self.bits):
            self.kept[here, :] = total.astype(BF16)
            self.to_z(i, k + 1).start()
        else:
            place = ds(i * self.rows + self.ctx * self.half + start, size)
            self.out[place, :] = total.astype(BF16)
            self.back_z(i, k).start()

    def widen(self, k, i):
        self.back_z(i, k).wait_recv()
        if k:
            self.back_z(i, k - 1).start()
        else:
            self.back_x(i).start()

    def step(self, i):
        for late, stage in enumerate(self.stages):
            pl.when((i >= late) & (i < self.parts + late))(functools.partial(stage, i - late))

    def finish(self):
        for array, count in enumerate(self.counts):

            def sent(i, array=array):
                self.to_core(array, i, 0).wait_send()
                self.to_core(array, i, 1).wait_send()

            each(count, sent)

        def end(i):
            self.to_y(i).wait_send()
            self.to_x(i).wait_send()
            self.back_x(i).wait()
            for k in range(len(self.bits)):
                self.to_z(i, k).wait_send()
                self.back_z(i, k).wait_send()

        each(self.parts, end)


def ds(start, size):
    return pl.ds(pl.multiple_of(start, 16), size)


def each(count, step):
    lax.fori_loop(0, count, lambda i, _: (step(i), 0)[1], 0)


def sum_kernel(counts, n_vectors, rows, *refs):
    n = 4 * len(counts)
    shares, terms = refs[:n], refs[n : n + n_vectors]
    refs = refs[n + n_vectors :]
    out, vec = refs[:2]
    from_vec, v_out, v_in = refs[-3:]
    sums = Sums(counts, rows, shares, out, refs[2:-3])
    meet(sums.partners)
    at = 0
    for term in terms:
        vec[at : at + term.shape[0], : term.shape[1]] = term[...]
        at += term.shape[0]
    for hop, partner in enumerate(sums.partners):
        copy = remote(vec, from_vec.at[hop], v_out.at[hop], v_in.at[hop], partner)
        copy.start()
        if hop == 0:
            sums.start()
        copy.wait()
        vec[...] = vec[...] + from_vec[hop]
    each(sums.steps, sums.step)
    sums.finish()


def rows_of_part():
    return max(128, 32 * lax.axis_size("dp"))


def padded(arrays):
    rows = rows_of_part()
    terms = [
        [jnp.pad(v, ((0, -v.shape[0] % rows), (0, 0))) for v in part]
        for part in zip(*arrays, strict=True)
    ]
    own, near, far, last = terms
    counts = [v.shape[0] // rows for v in own]
    bits = (lax.axis_size("dp") - 1).bit_length()
    total = sum(counts) * rows
    shape = jax.ShapeDtypeStruct((total, own[0].shape[1]), BF16)
    scratch = Sums.scratch(total, sum(counts), bits, shape.shape[1])
    return own + far, near + last, counts, bits, shape, scratch


def unpadded(stack, arrays):
    shares, at = [], 0
    for own, *_ in arrays:
        shares.append(stack[at : at + own.shape[0]])
        at += own.shape[0] + -own.shape[0] % rows_of_part()
    return shares


def sum_replicas(arrays, vectors):
    here, there, counts, bits, shape, scratch = padded(arrays)
    place = pl.BlockSpec(memory_space=pltpu.VMEM)
    away = pl.BlockSpec(memory_space=pl.ANY)
    dma = pltpu.SemaphoreType.DMA
    rows = sum(v.shape[0] for v in vectors)
    stack, summed = pl.pallas_call(
        functools.partial(sum_kernel, counts, len(vectors), rows_of_part()),
        out_shape=[shape, jax.ShapeDtypeStruct((rows, D), F32)],
        in_specs=[place] * len(here) + [away] * len(there) + [place] * len(vectors),
        out_specs=[place, place],
        scratch_shapes=scratch
        + [pltpu.VMEM((3 + bits, rows, D), F32), dma((3 + bits,)), dma((3 + bits,))],
        compiler_params=pltpu.CompilerParams(
            collective_id=0, has_side_effects=True, vmem_limit_bytes=56 * 1024 * 1024
        ),
        name="sum_replicas",
    )(*here, *there, *vectors)
    return unpadded(stack, arrays), summed


def back_kernel(mixed, counts, rows, *refs):
    refs = list(refs)

    def take(count):
        taken = refs[:count]
        del refs[:count]
        return taken

    places, flags, lo_ref = take(3)
    shares, away = take(4 * len(counts)), take(9)
    dq_ref, dk_ref, dv_ref = take(3)
    if mixed:
        dv_before, dv_earlier = take(2)
    (out,) = take(1)
    if not mixed:
        dv_before, dv_earlier = take(2)
    dk_before, dk_earlier = take(2)
    near_k, near_v, far_k, far_v, home_k, home_v = take(6)
    values, acc_k, acc_v, acc_q = take(4)
    kv_out, kv_in = take(2)
    fetched, loaded = take(9), take(1)[0]
    loads = [
        pltpu.make_async_copy(source, target, loaded.at[k])
        for k, (source, target) in enumerate(zip(away, fetched, strict=True))
    ]
    for load in loads:
        load.start()
    cols, before, earlier, *others, exact, grad_ref, sum_ref = fetched
    first_values, given = (others, ()) if mixed else ((), others)
    sums = Sums(counts, rows, shares, out, refs)

    ctx, mp = lax.axis_index("ctx"), lax.axis_index("mp")
    sees_one = (mp >= 2) | ((mp == 0) & (ctx == 1))
    sees_two = mp == 3
    meet(sums.partners + [{"mp": 3 - mp}])
    sums.start()
    keys = ((earlier, 0), (before, 0), (cols, BAND))

    def home(which, source, target, g, device):
        return remote(
            source.at[g], target.at[g], kv_out.at[which, g], kv_in.at[which, g], device
        )

    def pair(g, act, step):
        act(step)
        if mixed:
            pl.when(g >= 2)(lambda: act(step + 1))
        else:
            act(step + 1)

    def from_last(g, step):
        source, target = (
            (dk_before, near_k), (dv_before, near_v), (dk_earlier, far_k), (dv_earlier, far_v),
        )[step]
        return home(step, source, target, g, {"mp": 2})

    def from_next(g, step, device):
        source, target = ((dk_before, home_k), (dv_before, home_v))[step]
        return home(4 + step, source, target, g, device)

    def group(g, _):
        place_values(mixed, g, places, first_values, keys, values)
        acc_k[...] = jnp.zeros_like(acc_k)
        if mixed:
            acc_v[...] = jnp.zeros_like(acc_v)
        else:
            for part in range(3):
                for j in range(GROUP):
                    head = GROUP * g + j
                    term = given[part][places[head]].astype(F32) * flags[head]
                    for side in range(2):
                        acc_v[2 * part + side, j * HD : (j + 1) * HD, :] = term[
                            :, side * TILE : (side + 1) * TILE
                        ]
        for t in range(WIN // TILE):
            tokens = slice(t * TILE, (t + 1) * TILE)
            low = lo_ref[:, tokens]
            place = 2 * WIN + t * TILE + lax.broadcasted_iota(jnp.int32, (1, TILE), 1)
            last = 2 * WIN // TILE + t

            def tile(kt, tokens=tokens, low=low, place=place, last=last):
                spot = kt * TILE + lax.broadcasted_iota(jnp.int32, (TILE, TILE), 0)
                keep = spot >= low
                if kt == last:
                    keep = keep & (spot <= place)
                span = slice(kt % 2 * TILE, (kt % 2 + 1) * TILE)
                key_ref, at = keys[kt // 2]
                for j in range(GROUP):
                    rows_j = slice(j * HD, (j + 1) * HD)
                    key = key_ref[g, at + j * HD : at + (j + 1) * HD, span]
                    query = cols[g, rows_j, tokens] * SCALE
                    grad = grad_ref[g, rows_j, tokens]
                    inner = jnp.sum(
                        grad.astype(F32) * exact[g, rows_j, tokens], axis=0, keepdims=True
                    )
                    raw = jnp.where(keep, dot(key, query, 0, 0), -jnp.inf)
                    weights = jnp.exp(raw - sum_ref[g, j : j + 1, tokens])
                    grad_weights = dot(values[kt // 2, rows_j, span], grad, 0, 0)
                    low_grad = (weights * (grad_weights - inner)).astype(BF16)
                    acc_v[kt, rows_j, :] += dot(grad, weights.astype(BF16), 1, 1)
                    acc_k[kt, rows_j, :] += dot(query, low_grad, 1, 1)
                    result = dot(key, low_grad, 1, 0)
                    acc_q[j] = result if kt == last else result + acc_q[j]

            for kt in reversed(range(last + 1)):
                if kt >= 4:
                    tile(kt)
                else:
                    pl.when(sees_one if kt >= 2 else sees_two)(functools.partial(tile, kt))
            for j in range(GROUP):
                dq_ref[g, j * HD : (j + 1) * HD, tokens] = acc_q[j] * SCALE
            sums.step(2 * g + t)
        results = ((dk_earlier, dv_earlier), (dk_before, dv_before), (dk_ref, dv_ref))
        for part, (dk, dv) in enumerate(results):
            for side in range(2):
                span = slice(side * TILE, (side + 1) * TILE)
                dk[g, :, span] = acc_k[2 * part + side].astype(dk.dtype)
                dv[g, :, span] = acc_v[2 * part + side].astype(dv.dtype)

        def send_last():
            pair(g, lambda step: from_last(g, step).start(), 0)
            pair(g, lambda step: from_last(g, step).start(), 2)

        pl.when(mp == 3)(send_last)
        pl.when((mp == 0) & (ctx == 1))(
            lambda: pair(g, lambda step: from_next(g, step, sums.other_window).start(), 0)
        )
        return 0

    for load in loads:
        load.wait()
    lax.fori_loop(0, 4, group, 0)

    def relay(g):
        def one(step):
            near, far, source, total = (
                (near_k, far_k, dk_before, dk_ref), (near_v, far_v, dv_before, dv_ref),
            )[step]
            from_last(g, step).wait_recv()
            from_last(g, step + 2).wait_recv()
            source[g] = (source[g].astype(F32) + far[g].astype(F32)).astype(BF16)
            from_next(g, step, {"mp": 1}).start()
            total[g] += near[g].astype(F32)

        pair(g, one, 0)

    pl.when(mp == 2)(lambda: each(4, relay))
    for i in range(8, sums.steps):
        sums.step(i)

    def arrive(g):
        def one(step):
            arrived, total = ((home_k, dk_ref), (home_v, dv_ref))[step]
            from_next(g, step, sums.other_window).wait_recv()
            total[g] += arrived[g].astype(F32)

        pair(g, one, 0)

    pl.when((mp == 1) | ((mp == 0) & (ctx == 0)))(lambda: each(4, arrive))

    def sent_last(g):
        pair(g, lambda step: from_last(g, step).wait_send(), 0)
        pair(g, lambda step: from_last(g, step).wait_send(), 2)

    def sent_next(device):
        each(4, lambda g: pair(g, lambda step: from_next(g, step, device).wait_send(), 0))

    pl.when(mp == 3)(lambda: each(4, sent_last))
    pl.when(mp == 2)(lambda: sent_next({"mp": 1}))
    pl.when((mp == 0) & (ctx == 1))(lambda: sent_next(sums.other_window))
    sums.finish()


def attend_back(places, flags, low, front, firsts, given, exact, grad_heads, lse, arrays):
    mixed = bool(firsts)
    here, there, counts, bits, shape, scratch = padded(arrays)
    place = pl.BlockSpec(memory_space=pltpu.VMEM)
    away = pl.BlockSpec(memory_space=pl.ANY)
    scalar = pl.BlockSpec(memory_space=pltpu.SMEM)
    dma = pltpu.SemaphoreType.DMA
    by_head = [v.reshape(-1, HD, WIN) for v in firsts[::-1] + given[::-1]]
    fetched = [*front, *by_head, exact, grad_heads, lse]
    wide = jax.ShapeDtypeStruct((4, BAND, WIN), F32)
    slim = jax.ShapeDtypeStruct((4, BAND, WIN), BF16)
    outs = [wide] * 3 + ([slim] * 2 if mixed else []) + [shape]
    block = pltpu.VMEM((4, BAND, WIN), BF16)
    results = pl.pallas_call(
        functools.partial(back_kernel, mixed, counts, rows_of_part()),
        out_shape=outs,
        in_specs=[scalar, scalar, place]
        + [place] * len(here)
        + [away] * (len(there) + len(fetched)),
        out_specs=[place] * len(outs),
        scratch_shapes=[block] * (8 if mixed else 10)
        + [
            pltpu.VMEM((3, BAND, WIN), BF16),
            pltpu.VMEM((TILES, BAND, TILE), F32),
            pltpu.VMEM((TILES, BAND, TILE), F32),
            pltpu.VMEM((GROUP, HD, TILE), F32),
            dma((6, 4)),
            dma((6, 4)),
        ]
        + [pltpu.VMEM(v.shape, v.dtype) for v in fetched]
        + [dma((len(fetched),))]
        + scratch,
        compiler_params=pltpu.CompilerParams(
            collective_id=3 if mixed else 4,
            has_side_effects=True,
            vmem_limit_bytes=60 * 1024 * 1024,
        ),
        name="attend_back",
    )(places, flags, low, *here, *there, *fetched)
    return results[:-1], unpadded(results[-1], arrays)


def gelu(hidden):
    return jax.nn.gelu(hidden, approximate=True)


def tail_forward(stream, heads, out_weight, out_bias, gain, shift, ups, up_biases, downs):
    stream = stream + dot(heads, out_weight, 0, 0) + out_bias[0]
    normed, unit, scale = norm_rows(stream, gain[1], shift[1])
    hidden, active, total = [], [], out_bias[1]
    for up, bias, down in zip(ups, up_biases, downs, strict=True):
        hidden.append(dot(normed, up, 1, 0) + bias)
        active.append(gelu(hidden[-1]).astype(BF16))
        total = total + dot(active[-1], down, 1, 0)
    return stream + total, (normed, unit, scale, hidden, active)


def tail_backward(grad, kept, out_weight, gain, ups, downs):
    normed, unit, scale, hidden, active = kept
    bias_mlp = jnp.sum(grad, axis=0)
    rounded = grad.astype(BF16)
    mats, up_biases, normed_grad = [], [], 0.0
    for up, down, before, after in zip(ups, downs, hidden, active, strict=True):
        _, pull = jax.vjp(gelu, before)
        grad_hidden = pull(dot(rounded, down, 1, 1))[0]
        up_biases.append(jnp.sum(grad_hidden, axis=0))
        low = grad_hidden.astype(BF16)
        mats.append((dot(normed, low, 0, 0).astype(BF16), dot(after, rounded, 0, 0).astype(BF16)))
        normed_grad = normed_grad + dot(low, up, 1, 1)
    middle, gain_grad, shift_grad = norm_back(normed_grad, unit, scale, gain[1])
    grad = grad + middle
    bias_attn = jnp.sum(grad, axis=0)
    rounded = grad.astype(BF16)
    grad_heads = dot(out_weight, rounded, 1, 1).astype(BF16)
    return grad, rounded, grad_heads, mats, up_biases, (gain_grad, shift_grad, bias_attn, bias_mlp)


def turned(weight):
    return jnp.swapaxes(weight, -1, -2)


def shards(
    block_input, cotangent, doc_lengths, reuse_heads,
    norm_gain1, norm_bias1, projections1, front_bias1, out_weight1, out_bias1,
    up_weight1, up_bias1, down_weight1,
    norm_gain2, norm_bias2, query_key2, query_bias2, fresh_value2, value_bias2,
    out_weight2, out_bias2, up_weight2, up_bias2, down_weight2,
):
    low = row_starts(doc_lengths[0])
    taken = jnp.arange(4 * GROUP, dtype=jnp.int32)[:, None] == reuse_heads[None, :]
    taker = jnp.sum(jnp.where(taken, jnp.arange(REUSE, dtype=jnp.int32)[None, :], 0), axis=1)
    flags = jnp.any(taken, axis=1).astype(F32)
    band_of, in_band = reuse_heads // GROUP, reuse_heads % GROUP
    places2 = jnp.concatenate(
        [band_of * 3 * GROUP + 2 * GROUP + in_band, band_of * 2 * GROUP + GROUP + in_band]
    )

    stream0 = block_input.astype(F32)
    normed1, unit1, scale1 = norm_rows(stream0, norm_gain1[0], norm_bias1[0])
    n_front1, n_front2 = 3 * BAND, 2 * BAND + BAND // 2
    none = jnp.zeros((BAND,), BF16)

    def as_row(pieces):
        row = jnp.concatenate(pieces).astype(F32)
        return jnp.pad(row[None, :], ((0, 7), (0, -row.shape[0] % 128)))

    small = jnp.concatenate([query_bias2, value_bias2, up_bias1, up_bias2])
    small = jnp.pad(small, (0, 16 * 128 - small.shape[0])).reshape(16, 128)
    own_front2 = jnp.concatenate([turned(query_key2).reshape(2 * BAND, D), turned(fresh_value2)])
    own_front2 = jnp.pad(own_front2, ((0, -n_front2 % 64), (0, 0)))
    (
        cols1, before1, earlier1, heads1, exact1, sums1, _, small, front1,
        up1, down1, front2, outs1,
    ) = project(
        places2, low, normed1, turned(projections1).reshape(n_front1, D),
        as_row([front_bias1[0], none, front_bias1[1]]), n_front1, 2 * BAND, (), small,
        (up_weight1, down_weight1, own_front2, out_weight1),
    )
    me = lax.axis_index("mp")
    ups1, downs1 = ([up_weight1] + by_distance(up1)[1:], [down_weight1] + by_distance(down1)[1:])
    front2 = lax.dynamic_update_index_in_dim(front2, own_front2, me, 0)
    outs1 = lax.dynamic_update_index_in_dim(outs1, out_weight1, me, 0).reshape(D, D)
    small = small.reshape(4, -1)
    at = BAND + BAND // 2
    bias2 = jnp.stack([as_row([small[s, :BAND], none, small[s, BAND:at]]) for s in range(4)])
    up_biases1 = by_distance(small[:, at : at + D])
    up_biases2 = by_distance(small[:, at + D : at + 2 * D])

    front_kv1 = (cols1, before1, earlier1)
    stream1, kept1 = tail_forward(
        stream0, heads1.reshape(D, WIN), outs1, out_bias1, norm_gain1, norm_bias1,
        ups1, up_biases1, downs1,
    )

    normed2, unit2, scale2 = norm_rows(stream1, norm_gain2[0], norm_bias2[0])
    front_kv1 = (cols1, before1, earlier1)
    cols2, before2, earlier2, heads2, exact2, sums2, up2, down2, outs2 = project(
        places2, low, normed2, front2, bias2, n_front2, n_front2 - BAND, front_kv1, None,
        (up_weight2, down_weight2, out_weight2),
    )
    ups2, downs2 = ([up_weight2] + by_distance(up2)[1:], [down_weight2] + by_distance(down2)[1:])
    outs2 = lax.dynamic_update_index_in_dim(outs2, out_weight2, me, 0).reshape(D, D)
    front2 = front2[:, :n_front2]

    front_kv2 = (cols2, before2, earlier2)
    stream2, kept2 = tail_forward(
        stream1, heads2.reshape(D, WIN), outs2, out_bias2, norm_gain2, norm_bias2,
        ups2, up_biases2, downs2,
    )
    block_output = stream2.astype(BF16)

    grad, rounded, grad_heads, mats2, up_grads2, small2 = tail_backward(
        cotangent.astype(F32), kept2, outs2, norm_gain2, ups2, downs2
    )
    (dq2, dk2, dv2, dv2_before, dv2_earlier), mats2 = attend_back(
        places2, flags, low, front_kv2, front_kv1, (), exact2,
        grad_heads.reshape(4, BAND, WIN), sums2, list(zip(*mats2, strict=True)),
    )
    grad_out2 = dot(heads2.reshape(D, WIN), rounded, 1, 0).astype(BF16).reshape(4, BAND, D)

    dcols2 = jnp.concatenate([dq2, dk2, dv2[2:].reshape(4, BAND // 2, WIN)], axis=1)
    bias_grad2 = jnp.sum(dcols2, axis=2)
    dcols2 = dcols2.astype(BF16)
    grad_front2 = dot(dcols2.reshape(-1, WIN), normed2, 1, 0).astype(BF16).reshape(4, n_front2, D)
    attn2 = [
        jnp.concatenate(pair)
        for pair in zip(by_distance(grad_out2), by_distance(grad_front2), strict=True)
    ]
    normed_grad = dot(dcols2.reshape(-1, WIN), front2.reshape(-1, D), 0, 0)
    middle, gain_front2, shift_front2 = norm_back(normed_grad, unit2, scale2, norm_gain2[0])
    grad = grad + middle

    grad, rounded, grad_heads, mats1, up_grads1, small1 = tail_backward(
        grad, kept1, outs1, norm_gain1, ups1, downs1
    )
    arrays = [attn2] + list(zip(*mats1, strict=True))
    (dq1, dk1, dv1), (attn2, *mats1) = attend_back(
        taker, flags, low, front_kv1, (), (dv2, dv2_before, dv2_earlier), exact1,
        grad_heads.reshape(4, BAND, WIN), sums1, arrays,
    )
    grad_out1 = dot(heads1.reshape(D, WIN), rounded, 1, 0).astype(BF16).reshape(4, BAND, D)

    dcols1 = jnp.concatenate([dq1, dk1, dv1], axis=1)
    bias_grad1 = jnp.sum(dcols1, axis=2)
    dcols1 = dcols1.astype(BF16)
    grad_front1 = dot(dcols1.reshape(-1, WIN), normed1, 1, 0).astype(BF16).reshape(4, n_front1, D)
    attn1 = [
        jnp.concatenate(pair)
        for pair in zip(by_distance(grad_out1), by_distance(grad_front1), strict=True)
    ]
    normed_grad = dot(dcols1.reshape(-1, WIN), front1.reshape(-1, D), 0, 0)
    middle, gain_front1, shift_front1 = norm_back(normed_grad, unit1, scale1, norm_gain1[0])
    input_grad = (grad + middle).astype(BF16)

    vectors = [
        gain_front1, small1[0], shift_front1, small1[1], small1[2], small1[3],
        gain_front2, small2[0], shift_front2, small2[1], small2[2], small2[3],
        bias_grad1[:, :BAND].reshape(-1), bias_grad1[:, 2 * BAND :].reshape(-1),
        bias_grad2[:, :BAND].reshape(-1), bias_grad2[:, 2 * BAND :].reshape(-1),
        in_order(up_grads1), in_order(up_grads2),
    ]
    vectors = [vector.reshape(-1, min(D, vector.size)) for vector in vectors]
    (attn1,), packed = sum_replicas([attn1], vectors)
    sums, at = [], 0
    for vector in vectors:
        sums.append(packed[at : at + vector.shape[0]].reshape(-1)[: vector.size])
        at += vector.shape[0]
    me = lax.axis_index("mp")

    def mine(vector):
        return lax.dynamic_index_in_dim(vector.reshape(4, -1), me, 0, keepdims=False)

    def pair(i):
        return jnp.stack([sums[i], sums[i + 1]])

    return (
        block_output,
        input_grad,
        pair(0),
        pair(2),
        turned(attn1[BAND : BAND + n_front1].reshape(3, BAND, D)).astype(F32),
        jnp.stack([mine(sums[12]), mine(sums[13])]),
        attn1[:BAND].astype(F32),
        pair(4),
        mats1[0].astype(F32),
        mine(sums[16]),
        mats1[1].astype(F32),
        pair(6),
        pair(8),
        turned(attn2[BAND : 3 * BAND].reshape(2, BAND, D)).astype(F32),
        mine(sums[14]),
        turned(attn2[3 * BAND : BAND + n_front2]).astype(F32),
        mine(sums[15]),
        attn2[:BAND].astype(F32),
        pair(10),
        mats2[0].astype(F32),
        mine(sums[17]),
        mats2[1].astype(F32),
    )


def solution(mesh):
    rows = P(("dp", "ctx", "mp"), None)
    placed = (
        rows, rows, P(("dp", "ctx"), None), P(),
        P(), P(), P(None, None, "mp"), P(None, "mp"), P("mp", None), P(),
        P(None, "mp"), P("mp"), P("mp", None),
        P(), P(), P(None, None, "mp"), P("mp"), P(None, "mp"), P("mp"),
        P("mp", None), P(), P(None, "mp"), P("mp"), P("mp", None),
    )
    given = (
        rows, rows,
        P(), P(), P(None, None, "mp"), P(None, "mp"), P("mp", None), P(),
        P(None, "mp"), P("mp"), P("mp", None),
        P(), P(), P(None, None, "mp"), P("mp"), P(None, "mp"), P("mp"),
        P("mp", None), P(), P(None, "mp"), P("mp"), P("mp", None),
    )
    return jax.shard_map(shards, mesh=mesh, in_specs=placed, out_specs=given, check_vma=False)
```

```python
import functools

import jax
import jax.numpy as jnp
from jax import lax
from jax.experimental import pallas as pl
from jax.experimental.pallas import tpu as pltpu
from jax.sharding import PartitionSpec as P

D = 768
HD = 64
REUSE = 6
WIN = 512
EARLY = 5
CHUNK = 256
LEAD = 3
LAG = 2
HOOK_FIRST, HOOK_SECOND = -3, 0
GROUP = 3
BAND = GROUP * HD
TILE = 256
TILES = 3 * WIN // TILE
EPS = 1e-05
SCALE = HD**-0.5
F32 = jnp.float32
BF16 = jnp.bfloat16


def swap(value, axis, bit):
    devices = range(lax.axis_size(axis))
    return lax.ppermute(value, axis, [(i, i ^ bit) for i in devices])


def in_order(parts):
    return jnp.concatenate(by_distance(jnp.stack(parts)))


def by_distance(stacked):
    me = lax.axis_index("mp")
    return [
        lax.dynamic_index_in_dim(stacked, me ^ distance, 0, keepdims=False)
        for distance in range(4)
    ]


def flip(position, bit):
    return position + bit * (1 - 2 * ((position // bit) % 2))


def remote(source, target, sent, received, device):
    return pltpu.make_async_remote_copy(
        src_ref=source, dst_ref=target, send_sem=sent, recv_sem=received,
        device_id=device, device_id_type=pl.DeviceIdType.MESH,
    )


def meet(devices):
    barrier = pltpu.get_barrier_semaphore()
    for device in devices:
        pl.semaphore_signal(barrier, inc=1, device_id=device, device_id_type=pl.DeviceIdType.MESH)
    pl.semaphore_wait(barrier, len(devices))


def dot(left, right, left_dim, right_dim):
    return lax.dot_general(
        left, right, (((left_dim,), (right_dim,)), ((), ())), preferred_element_type=F32
    )


def norm_rows(value, gain, shift):
    mean = jnp.mean(value, axis=-1, keepdims=True)
    centred = value - mean
    spread = jnp.mean(centred * centred, axis=-1, keepdims=True)
    scale = lax.rsqrt(spread + EPS)
    unit = centred * scale
    return (unit * gain + shift).astype(BF16), unit, scale


def norm_back(grad, unit, scale, gain):
    scaled = grad * gain
    inner = (
        scaled
        - jnp.mean(scaled, axis=-1, keepdims=True)
        - unit * jnp.mean(scaled * unit, axis=-1, keepdims=True)
    )
    return scale * inner, jnp.sum(grad * unit, axis=0), jnp.sum(grad, axis=0)


def front_kernel(more_rows, lead, mixed, *refs):
    refs = list(refs)

    def take(count):
        taken = refs[:count]
        del refs[:count]
        return taken

    ctx, dp, mp = (lax.axis_index(axis) for axis in ("ctx", "dp", "mp"))
    near, far, last = {"mp": flip(mp, 1)}, {"mp": flip(mp, 2)}, {"mp": 3 - mp}
    window = {"ctx": 1 - ctx}
    chunks = chunks_of(lead, more_rows)
    n_chunks, n_more, n_lead = len(chunks), len(more_rows), LEAD * lead
    n_arrays = n_more + lead
    early, offset = (EARLY, HOOK_FIRST) if lead else (4, HOOK_SECOND)
    places, lo_ref, normed = take(3)
    first_values = take(3) if mixed else ()
    front, bias = (None, None) if lead else take(2)
    vectors_own = take(2 * lead)
    arrays_own = take(n_arrays)
    cols, before, earlier, out_ref, exact_ref, sum_ref = take(6)
    vectors = take(2 * lead)
    arrays = take(n_arrays)
    if lead:
        front, bias = arrays[0], vectors[0]
    values, raw, top, total, acc, kv_out, kv_in, on_out, on_in = take(9)
    m_out, m_in = take(2)
    if lead:
        f_out, f_in = take(2)
    meet([near, far, last, window, {"dp": flip(dp, 1)}])
    directions = (near, far, last)
    if True:

        def whole(k, way):
            return remote(
                vectors_own[k], vectors[k].at[mp], f_out.at[k, way], f_in.at[k, way],
                directions[way],
            )

        bit = lax.rem(dp, 2)
        first = [(bit, {"dp": flip(dp, 1)}), (ctx, window)]

        def quarters(c):
            a, start, rows = chunks[c]
            (low, low_device), (high, high_device) = first if c % 2 else first[::-1]
            return a, start, rows // 4, rows // 2, low, low_device, high, high_device

        def copy(c, way, source, target, device):
            return remote(source, target, m_out.at[c, way], m_in.at[c, way], device)

        def beside(c):
            a, start, rows = chunks[c]
            here = pl.ds(start, rows)
            return copy(c, 0, arrays_own[a].at[here], arrays[a].at[mp, here], near)

        def across(c):
            a, start, quarter, half, low, _, high, _ = quarters(c)
            here = ds(start + high * half + low * quarter, quarter)
            return copy(c, 1, arrays_own[a].at[here], arrays[a].at[mp, here], far)

        def widen(c):
            a, start, quarter, half, low, device, high, _ = quarters(c)
            there = arrays[a].at[flip(mp, 2), ds(start + high * half + low * quarter, quarter)]
            return copy(c, 2, there, there, device)

        def complete(c):
            a, start, _, half, _, _, high, device = quarters(c)
            there = arrays[a].at[flip(mp, 2), ds(start + high * half, half)]
            return copy(c, 3, there, there, device)

        def hand_on(c):
            a, start, rows = chunks[c]
            there = arrays[a].at[flip(mp, 2), pl.ds(start, rows)]
            return copy(c, 4, there, there, near)

        for c in range(n_lead):
            across(c).start()
            beside(c).start()
        for k in range(2 * lead):
            for way in range(3):
                whole(k, way).start()
        for c in range(n_lead, early):
            across(c).start()
        for c in range(n_lead, n_chunks):
            beside(c).start()
        if lead:
            arrays[0][mp] = arrays_own[0][...]
        for k in range(2 * lead):
            vectors[k][mp] = vectors_own[k][...]

    def gather(step):
        for late, stage in enumerate(
            ((across, widen), (widen, complete), (complete, hand_on))
        ):
            a = step + n_lead - LAG * late
            if n_lead <= a < n_chunks:
                stage[0](a).wait_recv()
                stage[1](a).start()

    kv_rows = before.shape[1]
    from_row = cols.shape[1] - kv_rows
    sends_on = (mp == 1) | (mp == 2)
    sends_window = (mp == 0) & (ctx == 0)
    receives = (mp >= 2) | ((mp == 0) & (ctx == 1))

    def pass_on(slot, device):
        source = cols.at[slot, pl.ds(from_row, kv_rows)]
        return remote(source, before.at[slot], kv_out.at[slot], kv_in.at[slot], device)

    def pass_again(slot):
        return remote(before.at[slot], earlier.at[slot], on_out.at[slot], on_in.at[slot], {"mp": 3})

    order = (mp, flip(mp, 1), flip(mp, 2), 3 - mp) if lead else range(4)
    for k, slot in enumerate(order):
        if lead and k == 1:
            for vector in range(2):
                for way in range(3):
                    whole(vector, way).wait_recv()
            for c in range(n_lead):
                across(c).wait_recv()
                widen(c).start()
            for c in range(n_lead):
                beside(c).wait_recv()
        if lead and k == 2:
            for c in range(n_lead):
                widen(c).wait_recv()
                complete(c).start()
            for c in range(n_lead):
                complete(c).wait_recv()
                hand_on(c).start()
        if lead and k == 3:
            for c in range(n_lead):
                hand_on(c).wait_recv()
        column = jnp.transpose(bias[slot])[: cols.shape[1], 0:1]
        cols[slot] = (dot(front[slot, : cols.shape[1]], normed[...], 1, 1) + column).astype(BF16)
        pl.when(sends_on)(lambda: pass_on(slot, {"mp": mp + 1}).start())
        pl.when(sends_window)(lambda: pass_on(slot, window).start())
    for c in range(early, n_chunks):
        across(c).start()
    steps = n_chunks - n_lead + 2 * LAG
    for step in range(steps):
        if step + offset < 0:
            gather(step)

    def arrive(slot):
        def from_next():
            pass_on(slot, window).wait_recv()
            pl.when(mp == 2)(lambda: pass_again(slot).start())
            pl.when(mp == 3)(lambda: pass_again(slot).wait_recv())

        pl.when(receives)(from_next)

    keys = ((earlier, 0), (before, 0), (cols, BAND))
    sees_one, sees_two = receives, mp == 3
    sender = lax.max(mp - 1, 0)

    def group(k, _):
        if mixed:
            g = k
            pl.when(k < 2)(lambda: arrive(k))

            def rest():
                arrive(2)
                arrive(3)

            pl.when(k == 2)(rest)
        else:
            g = (sender % 2 + k) % 2 + 2 * ((sender // 2 + k // 2) % 2)
            arrive(g)
        place_values(mixed, g, places, first_values, keys, values)
        for t in range(WIN // TILE):
            tokens = slice(t * TILE, (t + 1) * TILE)
            low = lo_ref[:, tokens]
            place = 2 * WIN + t * TILE + lax.broadcasted_iota(jnp.int32, (1, TILE), 1)
            end = 2 * WIN // TILE + t

            def score(kt, tokens=tokens, low=low, place=place, end=end):
                spot = kt * TILE + lax.broadcasted_iota(jnp.int32, (TILE, TILE), 0)
                keep = spot >= low
                if kt == end:
                    keep = keep & (spot <= place)
                span = slice(kt % 2 * TILE, (kt % 2 + 1) * TILE)
                key_ref, at = keys[kt // 2]
                for j in range(GROUP):
                    rows = slice(j * HD, (j + 1) * HD)
                    key = key_ref[g, at + j * HD : at + (j + 1) * HD, span]
                    found = dot(key, cols[g, rows, tokens] * SCALE, 0, 0)
                    found = jnp.where(keep, found, -jnp.inf)
                    raw[j, kt] = found
                    peak = jnp.max(found.reshape(TILE // 8, 8, TILE), axis=0)
                    top[j] = peak if kt == end else jnp.maximum(top[j], peak)

            def weigh(kt, end=end):
                span = slice(kt % 2 * TILE, (kt % 2 + 1) * TILE)
                for j in range(GROUP):
                    rows = slice(j * HD, (j + 1) * HD)
                    powers = jnp.exp(raw[j, kt] - top[j, 0:1])
                    added = jnp.sum(powers.reshape(TILE // 8, 8, TILE), axis=0)
                    result = dot(values[kt // 2, rows, span], powers.astype(BF16), 1, 0)
                    total[j] = added if kt == end else total[j] + added
                    acc[j] = result if kt == end else acc[j] + result

            for stage in (score, weigh):
                for kt in reversed(range(end + 1)):
                    if kt >= 4:
                        stage(kt)
                    else:
                        pl.when(sees_one if kt >= 2 else sees_two)(functools.partial(stage, kt))
                if stage is score:
                    for j in range(GROUP):
                        top[j] = jnp.broadcast_to(jnp.max(top[j], axis=0, keepdims=True), (8, TILE))
            for j in range(GROUP):
                rows = slice(j * HD, (j + 1) * HD)
                whole_sum = jnp.sum(total[j], axis=0, keepdims=True)
                result = acc[j] / whole_sum
                out_ref[g, rows, tokens] = result.astype(BF16)
                exact_ref[g, rows, tokens] = result
                sum_ref[g, j : j + 1, tokens] = top[j, 0:1] + jnp.log(whole_sum)
            for step in range(steps):
                if (step + offset) % 2 == t and 0 <= step + offset < 8:
                    pl.when(k == (step + offset) // 2)(functools.partial(gather, step))
        return 0

    lax.fori_loop(0, 4, group, 0)
    for step in range(steps):
        if step + offset >= 8:
            gather(step)

    def sent(device):
        each(4, lambda slot: pass_on(slot, device).wait_send())

    pl.when(sends_on)(lambda: sent({"mp": mp + 1}))
    pl.when(sends_window)(lambda: sent(window))
    pl.when(mp == 2)(lambda: each(4, lambda slot: pass_again(slot).wait_send()))
    for k in range(2 * lead):
        for way in range(3):
            whole(k, way).wait_send()
    for a in range(n_chunks):
        beside(a).wait_send()
        if a >= n_lead:
            beside(a).wait_recv()
            hand_on(a).wait_recv()
        across(a).wait_send()
        widen(a).wait_send()
        complete(a).wait_send()
        hand_on(a).wait_send()


def place_values(mixed, g, places, first_values, keys, values):
    if not mixed:
        for part, (ref, at) in enumerate(keys):
            values[part] = ref[g, at + BAND : at + 2 * BAND, :]
        return

    def reused():
        for part in range(3):
            for j in range(GROUP):
                at = places[(0 if part == 2 else REUSE) + GROUP * g + j]
                values[part, j * HD : (j + 1) * HD, :] = first_values[part][at]

    def own():
        wide = BAND // 2
        for part, (ref, at) in enumerate(keys):
            for side in range(2):
                values[part, side * wide : (side + 1) * wide, :] = ref[
                    2 * (g - 2) + side, at + BAND : at + BAND + wide, :
                ]

    pl.when(g < 2)(reused)
    pl.when(g >= 2)(own)


def chunks_of(lead, more_rows):
    chunks = [(0, k * BAND, BAND) for k in range(LEAD)] * lead
    for array, rows in enumerate(more_rows):
        size = CHUNK if rows % CHUNK == 0 else rows
        chunks += [(array + lead, start, size) for start in range(0, rows, size)]
    return chunks


def project(places, low, normed, front, bias, n_cols, kv_rows, firsts=(), small=None, more=()):
    place = pl.BlockSpec(memory_space=pltpu.VMEM)
    away = pl.BlockSpec(memory_space=pl.ANY)
    dma = pltpu.SemaphoreType.DMA
    given = [low, normed] + [v.reshape(-1, HD, WIN) for v in firsts[::-1]]
    lead = small is not None
    given += [bias, small, front] if lead else [front, bias]
    made = [(4, n_cols, WIN), (4, kv_rows, WIN), (4, kv_rows, WIN), (4, BAND, WIN)]
    made = [jax.ShapeDtypeStruct(shape, BF16) for shape in made]
    made += [jax.ShapeDtypeStruct((4, rows, WIN), F32) for rows in (BAND, 8)]
    scratch = [
        pltpu.VMEM((3, BAND, WIN), BF16),
        pltpu.VMEM((GROUP, TILES, TILE, TILE), F32),
        pltpu.VMEM((GROUP, 8, TILE), F32),
        pltpu.VMEM((GROUP, 8, TILE), F32),
        pltpu.VMEM((GROUP, HD, TILE), F32),
    ] + [dma((4,))] * 4
    gathered = ([bias, small, front] if lead else []) + list(more)
    gathered = [jax.ShapeDtypeStruct((4,) + v.shape, v.dtype) for v in gathered]
    rows = [v.shape[0] for v in more]
    scratch += [dma((len(chunks_of(lead, rows)), 5))] * 2 + ([dma((2, 3))] * 2 if lead else [])
    return pl.pallas_call(
        functools.partial(front_kernel, rows, int(lead), bool(firsts)),
        out_shape=made + gathered,
        in_specs=[pl.BlockSpec(memory_space=pltpu.SMEM)]
        + [place] * len(given) + [away] * len(more),
        out_specs=[place] * (len(made) + 3 * lead) + [away] * len(more),
        scratch_shapes=scratch,
        compiler_params=pltpu.CompilerParams(
            collective_id=1 if lead else 2,
            has_side_effects=True,
            vmem_limit_bytes=48 * 1024 * 1024,
        ),
        name="front_first" if lead else "front_second",
    )(places, *given, *more)


def row_starts(lengths):
    part = lax.axis_index("mp")
    place = (part - 1) * WIN + jnp.arange(WIN, dtype=jnp.int32)
    ends = jnp.cumsum(lengths)
    begun = jnp.max(jnp.where(place[:, None] >= ends[None, :], ends[None, :], 0), axis=1)
    document = begun - (part - 1) * WIN + 2 * WIN
    window = jnp.where(lax.axis_index("ctx") > 0, WIN, 2 * WIN)
    low = jnp.where(part == 0, window, document).astype(jnp.int32)
    return low.reshape(1, WIN)


class Sums:
    def __init__(self, counts, rows, terms, out, refs):
        self.counts, self.rows, self.out = counts, rows, out
        self.owns, self.nears, self.fars, self.lasts = zip(*terms)
        self.from_near, self.from_last = refs[:2]
        self.mine, self.from_y = self.from_near, out
        self.from_x, self.kept, self.from_z = refs[2:5]
        self.sems = refs[5:]
        self.parts = sum(counts)
        self.firsts = [sum(counts[:k]) for k in range(len(counts))]
        self.ctx, self.dp, mp = (lax.axis_index(axis) for axis in ("ctx", "dp", "mp"))
        self.half = rows // 2
        self.bits = [1 << k for k in range((lax.axis_size("dp") - 1).bit_length())]
        self.highs = [(self.dp // bit) % 2 for bit in self.bits]
        self.other_chip, self.other_window = {"mp": flip(mp, 2)}, {"ctx": 1 - self.ctx}
        self.other_core = {"mp": flip(mp, 1)}
        self.beside = [{"dp": flip(self.dp, bit)} for bit in self.bits]
        self.partners = [self.other_chip, self.other_window, self.other_core] + self.beside
        self.stages = [self.join, self.spread]
        self.stages += [functools.partial(self.narrow, k) for k in range(len(self.bits))]
        self.stages += [functools.partial(self.widen, k) for k in reversed(range(len(self.bits)))]
        self.steps = self.parts + len(self.stages) - 1

    @staticmethod
    def scratch(total, parts, bits, lanes):
        dma = pltpu.SemaphoreType.DMA
        return [
            pltpu.VMEM((total, lanes), BF16),
            pltpu.VMEM((total, lanes), BF16),
            pltpu.VMEM((total // 2, lanes), BF16),
            pltpu.VMEM((total // 2, lanes), BF16),
            pltpu.VMEM((total // 2, lanes), BF16),
            dma((parts,)), dma((parts,)),
            dma((parts,)), dma((parts,)),
            dma((parts, bits)), dma((parts, bits)),
            dma((parts, bits)), dma((parts, bits)),
            dma((parts,)), dma((parts,)),
            dma((parts, 2)), dma((parts, 2)),
        ]

    def segment(self, k, sent=False):
        start, size = 0, self.half
        for high in self.highs[:k]:
            size //= 2
            start = start + high * size
        if sent:
            size //= 2
            start = start + (1 - self.highs[k]) * size
        return start, size

    def to_core(self, array, i, which):
        place = self.firsts[array] + i
        source = (self.nears, self.lasts)[which][array].at[ds(i * self.rows, self.rows)]
        target = (self.from_near, self.from_last)[which].at[ds(place * self.rows, self.rows)]
        sent, received = (sem.at[place, which] for sem in self.sems[10:12])
        return remote(source, target, sent, received, self.other_core)

    def to_y(self, i):
        here = ds(i * self.rows, self.rows)
        source, target = self.from_last.at[here], self.from_y.at[here]
        return remote(source, target, self.sems[0].at[i], self.sems[1].at[i], self.other_chip)

    def to_x(self, i):
        source = self.mine.at[ds(i * self.rows + (1 - self.ctx) * self.half, self.half)]
        target = self.from_x.at[ds(i * self.half, self.half)]
        return remote(source, target, self.sems[2].at[i], self.sems[3].at[i], self.other_window)

    def to_z(self, i, k):
        start, size = self.segment(k, True)
        source = self.kept.at[ds(i * self.half + start, size)]
        target = self.from_z.at[ds(i * self.half + self.half - 2 * size, size)]
        return remote(source, target, self.sems[4].at[i, k], self.sems[5].at[i, k], self.beside[k])

    def back_z(self, i, k):
        start, size = self.segment(k + 1)
        here = self.out.at[ds(i * self.rows + self.ctx * self.half + start, size)]
        return remote(here, here, self.sems[6].at[i, k], self.sems[7].at[i, k], self.beside[k])

    def back_x(self, i):
        here = self.out.at[ds(i * self.rows + self.ctx * self.half, self.half)]
        return remote(here, here, self.sems[8].at[i], self.sems[9].at[i], self.other_window)

    def start(self):
        for array, count in enumerate(self.counts):

            def send(i, array=array):
                self.to_core(array, i, 1).start()
                self.to_core(array, i, 0).start()

            each(count, send)
        for array, count in enumerate(self.counts):

            def fold(i, array=array):
                place = self.firsts[array] + i
                self.to_core(array, i, 1).wait_recv()
                here = ds(place * self.rows, self.rows)
                term = self.fars[array][ds(i * self.rows, self.rows), :]
                total = term.astype(F32) + self.from_last[here, :].astype(F32)
                self.from_last[here, :] = total.astype(BF16)
                self.to_y(place).start()

            each(count, fold)

    def join(self, i):
        here = ds(i * self.rows, self.rows)
        self.to_y(i).wait_recv()
        for array, count in enumerate(self.counts):
            first = self.firsts[array]

            def add(array=array, first=first):
                self.to_core(array, i - first, 0).wait_recv()
                term = self.owns[array][ds((i - first) * self.rows, self.rows), :]
                total = term.astype(F32) + self.from_near[here, :].astype(F32)
                self.mine[here, :] = (total + self.from_y[here, :].astype(F32)).astype(BF16)

            pl.when((i >= first) & (i < first + count))(add)
        self.to_x(i).start()

    def spread(self, i):
        self.to_x(i).wait_recv()
        there = ds(i * self.half, self.half)
        term = self.mine[ds(i * self.rows + self.ctx * self.half, self.half), :]
        total = term.astype(F32) + self.from_x[there, :].astype(F32)
        self.kept[there, :] = total.astype(BF16)
        self.to_z(i, 0).start()

    def narrow(self, k, i):
        self.to_z(i, k).wait_recv()
        start, size = self.segment(k + 1)
        here = ds(i * self.half + start, size)
        there = ds(i * self.half + self.half - 2 * size, size)
        total = self.kept[here, :].astype(F32) + self.from_z[there, :].astype(F32)
        if k + 1 < len(self.bits):
            self.kept[here, :] = total.astype(BF16)
            self.to_z(i, k + 1).start()
        else:
            place = ds(i * self.rows + self.ctx * self.half + start, size)
            self.out[place, :] = total.astype(BF16)
            self.back_z(i, k).start()

    def widen(self, k, i):
        self.back_z(i, k).wait_recv()
        if k:
            self.back_z(i, k - 1).start()
        else:
            self.back_x(i).start()

    def step(self, i):
        for late, stage in enumerate(self.stages):
            pl.when((i >= late) & (i < self.parts + late))(functools.partial(stage, i - late))

    def finish(self):
        for array, count in enumerate(self.counts):

            def sent(i, array=array):
                self.to_core(array, i, 0).wait_send()
                self.to_core(array, i, 1).wait_send()

            each(count, sent)

        def end(i):
            self.to_y(i).wait_send()
            self.to_x(i).wait_send()
            self.back_x(i).wait()
            for k in range(len(self.bits)):
                self.to_z(i, k).wait_send()
                self.back_z(i, k).wait_send()

        each(self.parts, end)


def ds(start, size):
    return pl.ds(pl.multiple_of(start, 16), size)


def each(count, step):
    lax.fori_loop(0, count, lambda i, _: (step(i), 0)[1], 0)


def sum_kernel(arrays, places, *refs):
    n_here, n_there = len(arrays.here), len(arrays.there)
    here, there, refs = refs[:n_here], refs[n_here : n_here + n_there], refs[n_here + n_there :]
    terms, out, vec = refs[: len(places)], refs[len(places)], refs[len(places) + 1]
    from_vec, v_out, v_in = refs[-3:]
    sums, copies = arrays.open(here, there, out, refs[len(places) + 2 : -3])
    meet(sums.partners)
    mp = lax.axis_index("mp")
    slots = (mp, flip(mp, 1), flip(mp, 2), 3 - mp)
    vec[...] = jnp.zeros_like(vec)
    for term, (row, distance) in zip(terms, places, strict=True):
        at = row if distance is None else row + slots[distance]
        vec[pl.ds(at, 1), : term.shape[0]] = term[...].reshape(1, term.shape[0])
    for hop, partner in enumerate(sums.partners):
        copy = remote(vec, from_vec.at[hop], v_out.at[hop], v_in.at[hop], partner)
        copy.start()
        if hop == 0:
            for own_copy in copies:
                own_copy.wait()
            sums.start()
        copy.wait()
        vec[...] = vec[...] + from_vec[hop]
    each(sums.steps, sums.step)
    sums.finish()


def rows_of_part():
    return max(128, 32 * lax.axis_size("dp"))


class Arrays:
    def __init__(self, arrays):
        self.rows, self.bits = rows_of_part(), (lax.axis_size("dp") - 1).bit_length()
        self.pieces = [(v[0] if isinstance(v, tuple) else v).shape[-2] for v in arrays]
        if self.rows > 512:
            quads = [v if isinstance(v, tuple) else by_distance(v) for v in arrays]
            arrays = [tuple(jnp.concatenate(part) for part in zip(*quads, strict=True))]
        self.stacked = [not isinstance(array, tuple) for array in arrays]
        first = [array if stacked else array[0] for array, stacked in zip(arrays, self.stacked)]
        self.sizes = [v.shape[-2] for v in first]
        self.counts = [-(-size // self.rows) for size in self.sizes]
        filled = [
            tuple(self.fill(v) for v in array) if isinstance(array, tuple) else self.fill(array)
            for array in arrays
        ]
        self.here = [v for array in filled if isinstance(array, tuple) for v in array[::2]]
        self.there = []
        for array in filled:
            self.there += array[1::2] if isinstance(array, tuple) else [array]
        total, lanes = sum(self.counts) * self.rows, first[0].shape[-1]
        self.shape = jax.ShapeDtypeStruct((total, lanes), BF16)
        self.scratch = []
        for count, stacked in zip(self.counts, self.stacked):
            if stacked:
                self.scratch.append(pltpu.VMEM((2, count * self.rows, lanes), BF16))
                self.scratch.append(pltpu.SemaphoreType.DMA((2,)))
        self.scratch += Sums.scratch(total, sum(self.counts), self.bits, lanes)

    def fill(self, value):
        missing = -value.shape[-2] % self.rows
        return jnp.pad(value, [(0, 0)] * (value.ndim - 2) + [(0, missing), (0, 0)])

    def split(self, stack):
        shares, at = [], 0
        merged = len(self.pieces) > len(self.sizes)
        for k, size in enumerate(self.pieces):
            shares.append(stack[at : at + size])
            at += size if merged else self.counts[k] * self.rows
        return shares

    def open(self, here, there, out, refs):
        here, there, refs = list(here), list(there), list(refs)
        mp = lax.axis_index("mp")
        terms, copies = [], []
        for stacked in self.stacked:
            if not stacked:
                own, far = here.pop(0), here.pop(0)
                terms.append((own, there.pop(0), far, there.pop(0)))
                continue
            stack, place, sems = there.pop(0), refs.pop(0), refs.pop(0)
            for k, slot in enumerate((mp, flip(mp, 2))):
                copies.append(pltpu.make_async_copy(stack.at[slot], place.at[k], sems.at[k]))
                copies[-1].start()
            terms.append((place.at[0], stack.at[flip(mp, 1)], place.at[1], stack.at[3 - mp]))
        return Sums(self.counts, self.rows, terms, out, refs), copies


def sum_replicas(arrays, vectors):
    arrays = Arrays(arrays)
    place = pl.BlockSpec(memory_space=pltpu.VMEM)
    away = pl.BlockSpec(memory_space=pl.ANY)
    dma = pltpu.SemaphoreType.DMA
    hops = 3 + arrays.bits
    stack, summed = pl.pallas_call(
        functools.partial(sum_kernel, arrays, [v[1:] for v in vectors]),
        out_shape=[arrays.shape, jax.ShapeDtypeStruct((len(vectors), D), F32)],
        in_specs=[place] * len(arrays.here)
        + [away] * len(arrays.there)
        + [place] * len(vectors),
        out_specs=[place, place],
        scratch_shapes=arrays.scratch
        + [pltpu.VMEM((hops, len(vectors), D), F32), dma((hops,)), dma((hops,))],
        compiler_params=pltpu.CompilerParams(
            collective_id=0, has_side_effects=True, vmem_limit_bytes=56 * 1024 * 1024
        ),
        name="sum_replicas",
    )(*arrays.here, *arrays.there, *(v[0] for v in vectors))
    return arrays.split(stack), summed


def back_kernel(mixed, arrays, *refs):
    refs = list(refs)

    def take(count):
        taken = refs[:count]
        del refs[:count]
        return taken

    places, flags, lo_ref = take(3)
    here, there, away = take(len(arrays.here)), take(len(arrays.there)), take(9)
    (dcols,) = take(1)
    if mixed:
        dv_ref, dv_before, dv_earlier = take(3)
    (out,) = take(1)
    if not mixed:
        dv_ref, dv_before, dv_earlier = take(3)
    dk_ref, dk_before, dk_earlier = take(3)
    near_k, near_v, far_k, far_v, home_k, home_v = take(6)
    values, acc_k, acc_v, acc_q = take(4)
    kv_out, kv_in = take(2)
    fetched, loaded = take(9), take(1)[0]
    loads = [
        pltpu.make_async_copy(source, target, loaded.at[k])
        for k, (source, target) in enumerate(zip(away, fetched, strict=True))
    ]
    for load in loads:
        load.start()
    cols, before, earlier, *others, exact, grad_ref, sum_ref = fetched
    first_values, given = (others, ()) if mixed else ((), others)
    sums, copies = arrays.open(here, there, out, refs)

    ctx, mp = lax.axis_index("ctx"), lax.axis_index("mp")
    sees_one = (mp >= 2) | ((mp == 0) & (ctx == 1))
    sees_two = mp == 3
    meet(sums.partners + [{"mp": 3 - mp}])
    for copy in copies:
        copy.wait()
    sums.start()
    keys = ((earlier, 0), (before, 0), (cols, BAND))

    def home(which, source, target, g, device):
        return remote(
            source.at[g], target.at[g], kv_out.at[which, g], kv_in.at[which, g], device
        )

    def pair(g, act, step):
        act(step)
        if mixed:
            pl.when(g >= 2)(lambda: act(step + 1))
        else:
            act(step + 1)

    def from_last(g, step):
        source, target = (
            (dk_before, near_k), (dv_before, near_v), (dk_earlier, far_k), (dv_earlier, far_v),
        )[step]
        return home(step, source, target, g, {"mp": 2})

    def from_next(g, step, device):
        source, target = ((dk_before, home_k), (dv_before, home_v))[step]
        return home(4 + step, source, target, g, device)

    def group(g, _):
        place_values(mixed, g, places, first_values, keys, values)
        acc_k[...] = jnp.zeros_like(acc_k)
        if mixed:
            acc_v[...] = jnp.zeros_like(acc_v)
        else:
            for part in range(3):
                for j in range(GROUP):
                    head = GROUP * g + j
                    term = given[part][places[head]].astype(F32) * flags[head]
                    for side in range(2):
                        acc_v[2 * part + side, j * HD : (j + 1) * HD, :] = term[
                            :, side * TILE : (side + 1) * TILE
                        ]
        for t in range(WIN // TILE):
            tokens = slice(t * TILE, (t + 1) * TILE)
            low = lo_ref[:, tokens]
            place = 2 * WIN + t * TILE + lax.broadcasted_iota(jnp.int32, (1, TILE), 1)
            last = 2 * WIN // TILE + t

            def tile(kt, tokens=tokens, low=low, place=place, last=last):
                spot = kt * TILE + lax.broadcasted_iota(jnp.int32, (TILE, TILE), 0)
                keep = spot >= low
                if kt == last:
                    keep = keep & (spot <= place)
                span = slice(kt % 2 * TILE, (kt % 2 + 1) * TILE)
                key_ref, at = keys[kt // 2]
                for j in range(GROUP):
                    rows_j = slice(j * HD, (j + 1) * HD)
                    key = key_ref[g, at + j * HD : at + (j + 1) * HD, span]
                    query = cols[g, rows_j, tokens] * SCALE
                    grad = grad_ref[g, rows_j, tokens]
                    inner = jnp.sum(
                        grad.astype(F32) * exact[g, rows_j, tokens], axis=0, keepdims=True
                    )
                    raw = jnp.where(keep, dot(key, query, 0, 0), -jnp.inf)
                    weights = jnp.exp(raw - sum_ref[g, j : j + 1, tokens])
                    grad_weights = dot(values[kt // 2, rows_j, span], grad, 0, 0)
                    low_grad = (weights * (grad_weights - inner)).astype(BF16)
                    acc_v[kt, rows_j, :] += dot(grad, weights.astype(BF16), 1, 1)
                    acc_k[kt, rows_j, :] += dot(query, low_grad, 1, 1)
                    result = dot(key, low_grad, 1, 0)
                    acc_q[j] = result if kt == last else result + acc_q[j]

            for kt in reversed(range(last + 1)):
                if kt >= 4:
                    tile(kt)
                else:
                    pl.when(sees_one if kt >= 2 else sees_two)(functools.partial(tile, kt))
            for j in range(GROUP):
                dcols[g, j * HD : (j + 1) * HD, tokens] = (acc_q[j] * SCALE).astype(BF16)
            sums.step(2 * g + t)
        results = ((dk_earlier, dv_earlier), (dk_before, dv_before), (dk_ref, dv_ref))
        for part, (dk, dv) in enumerate(results):
            for side in range(2):
                span = slice(side * TILE, (side + 1) * TILE)
                dk[g, :, span] = acc_k[2 * part + side].astype(dk.dtype)
                dv[g, :, span] = acc_v[2 * part + side].astype(dv.dtype)

        def send_last():
            pair(g, lambda step: from_last(g, step).start(), 0)
            pair(g, lambda step: from_last(g, step).start(), 2)

        pl.when(mp == 3)(send_last)
        pl.when((mp == 0) & (ctx == 1))(
            lambda: pair(g, lambda step: from_next(g, step, sums.other_window).start(), 0)
        )
        return 0

    for load in loads:
        load.wait()
    lax.fori_loop(0, 4, group, 0)

    def relay(g):
        def one(step):
            near, far, source, total = (
                (near_k, far_k, dk_before, dk_ref), (near_v, far_v, dv_before, dv_ref),
            )[step]
            from_last(g, step).wait_recv()
            from_last(g, step + 2).wait_recv()
            source[g] = (source[g].astype(F32) + far[g].astype(F32)).astype(BF16)
            from_next(g, step, {"mp": 1}).start()
            total[g] += near[g].astype(F32)

        pair(g, one, 0)

    pl.when(mp == 2)(lambda: each(4, relay))
    for i in range(8, sums.steps):
        sums.step(i)

    def arrive(g):
        def one(step):
            arrived, total = ((home_k, dk_ref), (home_v, dv_ref))[step]
            from_next(g, step, sums.other_window).wait_recv()
            total[g] += arrived[g].astype(F32)

        pair(g, one, 0)

    pl.when((mp == 1) | ((mp == 0) & (ctx == 0)))(lambda: each(4, arrive))

    def round_off(g):
        dcols[g, BAND : 2 * BAND, :] = dk_ref[g].astype(BF16)
        if not mixed:
            dcols[g, 2 * BAND : 3 * BAND, :] = dv_ref[g].astype(BF16)

    each(4, round_off)
    wide = BAND // 2 if mixed else BAND
    for slot in range(4):
        if mixed:
            half = slice(slot % 2 * wide, (slot % 2 + 1) * wide)
            dcols[slot, 2 * BAND : 2 * BAND + wide, :] = dv_ref[2 + slot // 2, half, :].astype(BF16)
        rest = dcols.shape[1] - 2 * BAND - wide
        dcols[slot, 2 * BAND + wide :, :] = jnp.zeros((rest, WIN), BF16)

    def sent_last(g):
        pair(g, lambda step: from_last(g, step).wait_send(), 0)
        pair(g, lambda step: from_last(g, step).wait_send(), 2)

    def sent_next(device):
        each(4, lambda g: pair(g, lambda step: from_next(g, step, device).wait_send(), 0))

    pl.when(mp == 3)(lambda: each(4, sent_last))
    pl.when(mp == 2)(lambda: sent_next({"mp": 1}))
    pl.when((mp == 0) & (ctx == 1))(lambda: sent_next(sums.other_window))
    sums.finish()


def attend_back(places, flags, low, front, firsts, given, exact, grad_heads, lse, arrays):
    mixed = bool(firsts)
    arrays = Arrays(arrays)
    place = pl.BlockSpec(memory_space=pltpu.VMEM)
    away = pl.BlockSpec(memory_space=pl.ANY)
    scalar = pl.BlockSpec(memory_space=pltpu.SMEM)
    dma = pltpu.SemaphoreType.DMA
    by_head = [v.reshape(-1, HD, WIN) for v in firsts[::-1] + given[::-1]]
    fetched = [*front, *by_head, exact, grad_heads, lse]
    wide = jax.ShapeDtypeStruct((4, BAND, WIN), F32)
    slim = jax.ShapeDtypeStruct((4, BAND, WIN), BF16)
    n_cols = -(-(5 * BAND // 2 if mixed else 3 * BAND) // 128) * 128
    outs = [jax.ShapeDtypeStruct((4, n_cols, WIN), BF16)]
    outs += ([wide, slim, slim] if mixed else []) + [arrays.shape]
    block, full = pltpu.VMEM((4, BAND, WIN), BF16), pltpu.VMEM((4, BAND, WIN), F32)
    results = pl.pallas_call(
        functools.partial(back_kernel, mixed, arrays),
        out_shape=outs,
        in_specs=[scalar, scalar, place]
        + [place] * len(arrays.here)
        + [away] * (len(arrays.there) + len(fetched)),
        out_specs=[place] * len(outs),
        scratch_shapes=([] if mixed else [full, block, block])
        + [full]
        + [block] * 8
        + [
            pltpu.VMEM((3, BAND, WIN), BF16),
            pltpu.VMEM((TILES, BAND, TILE), F32),
            pltpu.VMEM((TILES, BAND, TILE), F32),
            pltpu.VMEM((GROUP, HD, TILE), F32),
            dma((6, 4)),
            dma((6, 4)),
        ]
        + [pltpu.VMEM(v.shape, v.dtype) for v in fetched]
        + [dma((len(fetched),))]
        + arrays.scratch,
        compiler_params=pltpu.CompilerParams(
            collective_id=3 if mixed else 4,
            has_side_effects=True,
            vmem_limit_bytes=(46 if mixed and arrays.bits < 5 else 60) * 1024 * 1024,
        ),
        name="attend_back",
    )(places, flags, low, *arrays.here, *arrays.there, *fetched)
    return results[:-1], arrays.split(results[-1])


def gelu(hidden):
    return jax.nn.gelu(hidden, approximate=True)


def tail_forward(stream, heads, out_weight, out_bias, gain, shift, ups, up_biases, downs):
    stream = stream + dot(heads, out_weight, 0, 0) + out_bias[0]
    normed, unit, scale = norm_rows(stream, gain[1], shift[1])
    hidden, active, total = [], [], out_bias[1]
    for up, bias, down in zip(ups, up_biases, downs, strict=True):
        hidden.append(dot(normed, up, 1, 0) + bias)
        active.append(gelu(hidden[-1]).astype(BF16))
        total = total + dot(active[-1], down, 1, 0)
    return stream + total, (normed, unit, scale, hidden, active)


def tail_backward(grad, kept, out_weight, gain, ups, downs):
    normed, unit, scale, hidden, active = kept
    bias_mlp = jnp.sum(grad, axis=0)
    rounded = grad.astype(BF16)
    mats, up_biases, normed_grad = [], [], 0.0
    for up, down, before, after in zip(ups, downs, hidden, active, strict=True):
        _, pull = jax.vjp(gelu, before)
        grad_hidden = pull(dot(rounded, down, 1, 1))[0]
        up_biases.append(jnp.sum(grad_hidden, axis=0))
        low = grad_hidden.astype(BF16)
        mats.append((dot(normed, low, 0, 0).astype(BF16), dot(after, rounded, 0, 0).astype(BF16)))
        normed_grad = normed_grad + dot(low, up, 1, 1)
    middle, gain_grad, shift_grad = norm_back(normed_grad, unit, scale, gain[1])
    grad = grad + middle
    bias_attn = jnp.sum(grad, axis=0)
    rounded = grad.astype(BF16)
    grad_heads = dot(out_weight, rounded, 1, 1).astype(BF16)
    return grad, rounded, grad_heads, mats, up_biases, (gain_grad, shift_grad, bias_attn, bias_mlp)


def turned(weight):
    return jnp.swapaxes(weight, -1, -2)


def shards(
    block_input, cotangent, doc_lengths, reuse_heads,
    norm_gain1, norm_bias1, projections1, front_bias1, out_weight1, out_bias1,
    up_weight1, up_bias1, down_weight1,
    norm_gain2, norm_bias2, query_key2, query_bias2, fresh_value2, value_bias2,
    out_weight2, out_bias2, up_weight2, up_bias2, down_weight2,
):
    low = row_starts(doc_lengths[0])
    taken = jnp.arange(4 * GROUP, dtype=jnp.int32)[:, None] == reuse_heads[None, :]
    taker = jnp.sum(jnp.where(taken, jnp.arange(REUSE, dtype=jnp.int32)[None, :], 0), axis=1)
    flags = jnp.any(taken, axis=1).astype(F32)
    band_of, in_band = reuse_heads // GROUP, reuse_heads % GROUP
    places2 = jnp.concatenate(
        [band_of * 3 * GROUP + 2 * GROUP + in_band, band_of * 2 * GROUP + GROUP + in_band]
    )

    stream0 = block_input.astype(F32)
    normed1, unit1, scale1 = norm_rows(stream0, norm_gain1[0], norm_bias1[0])
    n_front1, n_front2 = 3 * BAND, 2 * BAND + BAND // 2
    none = jnp.zeros((BAND,), BF16)

    def as_row(pieces):
        row = jnp.concatenate(pieces).astype(F32)
        return jnp.pad(row[None, :], ((0, 7), (0, -row.shape[0] % 128)))

    small = jnp.concatenate([query_bias2, value_bias2, up_bias1, up_bias2])
    small = jnp.pad(small, (0, 16 * 128 - small.shape[0])).reshape(16, 128)
    own_front2 = jnp.concatenate([turned(query_key2).reshape(2 * BAND, D), turned(fresh_value2)])
    own_front2 = jnp.pad(own_front2, ((0, -n_front2 % 64), (0, 0)))
    (
        cols1, before1, earlier1, heads1, exact1, sums1, _, small, front1,
        up1, down1, front2, outs1,
    ) = project(
        places2, low, normed1, turned(projections1).reshape(n_front1, D),
        as_row([front_bias1[0], none, front_bias1[1]]), n_front1, 2 * BAND, (), small,
        (up_weight1, down_weight1, own_front2, out_weight1),
    )
    me = lax.axis_index("mp")
    ups1, downs1 = ([up_weight1] + by_distance(up1)[1:], [down_weight1] + by_distance(down1)[1:])
    front2 = lax.dynamic_update_index_in_dim(front2, own_front2, me, 0)
    outs1 = lax.dynamic_update_index_in_dim(outs1, out_weight1, me, 0).reshape(D, D)
    small = small.reshape(4, -1)
    at = BAND + BAND // 2
    bias2 = jnp.stack([as_row([small[s, :BAND], none, small[s, BAND:at]]) for s in range(4)])
    up_biases1 = by_distance(small[:, at : at + D])
    up_biases2 = by_distance(small[:, at + D : at + 2 * D])

    front_kv1 = (cols1, before1, earlier1)
    stream1, kept1 = tail_forward(
        stream0, heads1.reshape(D, WIN), outs1, out_bias1, norm_gain1, norm_bias1,
        ups1, up_biases1, downs1,
    )

    normed2, unit2, scale2 = norm_rows(stream1, norm_gain2[0], norm_bias2[0])
    front_kv1 = (cols1, before1, earlier1)
    cols2, before2, earlier2, heads2, exact2, sums2, up2, down2, outs2 = project(
        places2, low, normed2, front2, bias2, n_front2, n_front2 - BAND, front_kv1, None,
        (up_weight2, down_weight2, out_weight2),
    )
    ups2, downs2 = ([up_weight2] + by_distance(up2)[1:], [down_weight2] + by_distance(down2)[1:])
    outs2 = lax.dynamic_update_index_in_dim(outs2, out_weight2, me, 0).reshape(D, D)
    front2 = front2[:, :n_front2]

    front_kv2 = (cols2, before2, earlier2)
    stream2, kept2 = tail_forward(
        stream1, heads2.reshape(D, WIN), outs2, out_bias2, norm_gain2, norm_bias2,
        ups2, up_biases2, downs2,
    )
    block_output = stream2.astype(BF16)

    grad, rounded, grad_heads, mats2, up_grads2, small2 = tail_backward(
        cotangent.astype(F32), kept2, outs2, norm_gain2, ups2, downs2
    )
    (dcols2, dv2, dv2_before, dv2_earlier), mats2 = attend_back(
        places2, flags, low, front_kv2, front_kv1, (), exact2,
        grad_heads.reshape(4, BAND, WIN), sums2, list(zip(*mats2, strict=True)),
    )
    grad_out2 = dot(heads2.reshape(D, WIN), rounded, 1, 0).astype(BF16).reshape(4, BAND, D)
    bias_grad2 = jnp.sum(dcols2.astype(F32), axis=2)
    grad_front2 = dot(dcols2.reshape(-1, WIN), normed2, 1, 0).astype(BF16).reshape(4, -1, D)
    normed_grad = dot(dcols2[:, :n_front2].reshape(-1, WIN), front2.reshape(-1, D), 0, 0)
    middle, gain_front2, shift_front2 = norm_back(normed_grad, unit2, scale2, norm_gain2[0])
    grad = grad + middle

    grad, rounded, grad_heads, mats1, up_grads1, small1 = tail_backward(
        grad, kept1, outs1, norm_gain1, ups1, downs1
    )
    grad_out1 = dot(heads1.reshape(D, WIN), rounded, 1, 0).astype(BF16).reshape(4, BAND, D)
    arrays = [grad_front2, jnp.concatenate([grad_out2, grad_out1], axis=1)]
    (dcols1,), (front_sum2, out_sums, *mats1) = attend_back(
        taker, flags, low, front_kv1, (), (dv2, dv2_before, dv2_earlier), exact1,
        grad_heads.reshape(4, BAND, WIN), sums1, arrays + list(zip(*mats1, strict=True)),
    )
    bias_grad1 = jnp.sum(dcols1.astype(F32), axis=2)
    grad_front1 = dot(dcols1.reshape(-1, WIN), normed1, 1, 0).astype(BF16).reshape(4, -1, D)
    normed_grad = dot(dcols1[:, :n_front1].reshape(-1, WIN), front1.reshape(-1, D), 0, 0)
    middle, gain_front1, shift_front1 = norm_back(normed_grad, unit1, scale1, norm_gain1[0])
    input_grad = (grad + middle).astype(BF16)

    singles = [
        gain_front1, small1[0], shift_front1, small1[1], small1[2], small1[3],
        gain_front2, small2[0], shift_front2, small2[1], small2[2], small2[3],
        bias_grad1[:, :BAND].reshape(-1), bias_grad1[:, 2 * BAND : n_front1].reshape(-1),
        bias_grad2[:, :BAND].reshape(-1), bias_grad2[:, 2 * BAND : n_front2].reshape(-1),
    ]
    vectors = [(vector, row, None) for row, vector in enumerate(singles)]
    for row, shares in ((16, up_grads1), (20, up_grads2)):
        vectors += [(vector, row, distance) for distance, vector in enumerate(shares)]
    (front_sum1,), sums = sum_replicas([grad_front1], vectors)

    def mine(vectors):
        return lax.dynamic_index_in_dim(vectors.reshape(4, -1), me, 0, keepdims=False)

    return (
        block_output,
        input_grad,
        sums[0:2],
        sums[2:4],
        turned(front_sum1[:n_front1].reshape(3, BAND, D)).astype(F32),
        jnp.stack([mine(sums[12]), mine(sums[13])]),
        out_sums[BAND:].astype(F32),
        sums[4:6],
        mats1[0].astype(F32),
        mine(sums[16:20]),
        mats1[1].astype(F32),
        sums[6:8],
        sums[8:10],
        turned(front_sum2[: 2 * BAND].reshape(2, BAND, D)).astype(F32),
        mine(sums[14]),
        turned(front_sum2[2 * BAND : n_front2]).astype(F32),
        mine(sums[15, : D // 2]),
        out_sums[:BAND].astype(F32),
        sums[10:12],
        mats2[0].astype(F32),
        mine(sums[20:24]),
        mats2[1].astype(F32),
    )


def solution(mesh):
    rows = P(("dp", "ctx", "mp"), None)
    placed = (
        rows, rows, P(("dp", "ctx"), None), P(),
        P(), P(), P(None, None, "mp"), P(None, "mp"), P("mp", None), P(),
        P(None, "mp"), P("mp"), P("mp", None),
        P(), P(), P(None, None, "mp"), P("mp"), P(None, "mp"), P("mp"),
        P("mp", None), P(), P(None, "mp"), P("mp"), P("mp", None),
    )
    given = (
        rows, rows,
        P(), P(), P(None, None, "mp"), P(None, "mp"), P("mp", None), P(),
        P(None, "mp"), P("mp"), P("mp", None),
        P(), P(), P(None, None, "mp"), P("mp"), P(None, "mp"), P("mp"),
        P("mp", None), P(), P(None, "mp"), P("mp"), P("mp", None),
    )
    return jax.shard_map(shards, mesh=mesh, in_specs=placed, out_specs=given, check_vma=False)
```

```python
import functools

import jax
import jax.numpy as jnp
from jax import lax
from jax.experimental import pallas as pl
from jax.experimental.pallas import tpu as pltpu
from jax.sharding import PartitionSpec as P

D = 768
HD = 64
REUSE = 6
WIN = 512
EARLY = 5
CHUNK = 256
LEAD = 3
LAG = 2
HOOK_FIRST, HOOK_SECOND = -3, 0
GROUP = 3
BAND = GROUP * HD
TILE = 256
TILES = 3 * WIN // TILE
EPS = 1e-05
SCALE = HD**-0.5
F32 = jnp.float32
BF16 = jnp.bfloat16


def swap(value, axis, bit):
    devices = range(lax.axis_size(axis))
    return lax.ppermute(value, axis, [(i, i ^ bit) for i in devices])


def in_order(parts):
    return jnp.concatenate(by_distance(jnp.stack(parts)))


def by_distance(stacked):
    me = lax.axis_index("mp")
    return [
        lax.dynamic_index_in_dim(stacked, me ^ distance, 0, keepdims=False)
        for distance in range(4)
    ]


def flip(position, bit):
    return position + bit * (1 - 2 * ((position // bit) % 2))


def remote(source, target, sent, received, device):
    return pltpu.make_async_remote_copy(
        src_ref=source, dst_ref=target, send_sem=sent, recv_sem=received,
        device_id=device, device_id_type=pl.DeviceIdType.MESH,
    )


def meet(devices):
    barrier = pltpu.get_barrier_semaphore()
    for device in devices:
        pl.semaphore_signal(barrier, inc=1, device_id=device, device_id_type=pl.DeviceIdType.MESH)
    pl.semaphore_wait(barrier, len(devices))


def dot(left, right, left_dim, right_dim):
    return lax.dot_general(
        left, right, (((left_dim,), (right_dim,)), ((), ())), preferred_element_type=F32
    )


def norm_rows(value, gain, shift):
    mean = jnp.mean(value, axis=-1, keepdims=True)
    centred = value - mean
    spread = jnp.mean(centred * centred, axis=-1, keepdims=True)
    scale = lax.rsqrt(spread + EPS)
    unit = centred * scale
    return (unit * gain + shift).astype(BF16), unit, scale


def norm_back(grad, unit, scale, gain):
    scaled = grad * gain
    inner = (
        scaled
        - jnp.mean(scaled, axis=-1, keepdims=True)
        - unit * jnp.mean(scaled * unit, axis=-1, keepdims=True)
    )
    return scale * inner, jnp.sum(grad * unit, axis=0), jnp.sum(grad, axis=0)


def front_kernel(more_rows, lead, mixed, *refs):
    refs = list(refs)

    def take(count):
        taken = refs[:count]
        del refs[:count]
        return taken

    ctx, dp, mp = (lax.axis_index(axis) for axis in ("ctx", "dp", "mp"))
    near, far, last = {"mp": flip(mp, 1)}, {"mp": flip(mp, 2)}, {"mp": 3 - mp}
    window = {"ctx": 1 - ctx}
    chunks = chunks_of(lead, more_rows)
    n_chunks, n_more, n_lead = len(chunks), len(more_rows), LEAD * lead
    n_arrays = n_more + lead
    early, offset = (EARLY, HOOK_FIRST) if lead else (4, HOOK_SECOND)
    places, lo_ref, normed = take(3)
    first_values = take(3) if mixed else ()
    front, bias = (None, None) if lead else take(2)
    vectors_own = take(2 * lead)
    arrays_own = take(n_arrays)
    cols, before, earlier, out_ref, exact_ref, sum_ref = take(6)
    vectors = take(2 * lead)
    arrays = take(n_arrays)
    if lead:
        front, bias = arrays[0], vectors[0]
    values, raw, top, total, acc, kv_out, kv_in, on_out, on_in = take(9)
    m_out, m_in = take(2)
    if lead:
        f_out, f_in = take(2)
    meet([near, far, last, window, {"dp": flip(dp, 1)}])
    directions = (near, far, last)
    if True:

        def whole(k, way):
            return remote(
                vectors_own[k], vectors[k].at[mp], f_out.at[k, way], f_in.at[k, way],
                directions[way],
            )

        bit = lax.rem(dp, 2)
        first = [(bit, {"dp": flip(dp, 1)}), (ctx, window)]

        def quarters(c):
            a, start, rows = chunks[c]
            (low, low_device), (high, high_device) = first if c % 2 else first[::-1]
            return a, start, rows // 4, rows // 2, low, low_device, high, high_device

        def copy(c, way, source, target, device):
            return remote(source, target, m_out.at[c, way], m_in.at[c, way], device)

        def beside(c):
            a, start, rows = chunks[c]
            here = pl.ds(start, rows)
            return copy(c, 0, arrays_own[a].at[here], arrays[a].at[mp, here], near)

        def across(c):
            a, start, quarter, half, low, _, high, _ = quarters(c)
            here = ds(start + high * half + low * quarter, quarter)
            return copy(c, 1, arrays_own[a].at[here], arrays[a].at[mp, here], far)

        def widen(c):
            a, start, quarter, half, low, device, high, _ = quarters(c)
            there = arrays[a].at[flip(mp, 2), ds(start + high * half + low * quarter, quarter)]
            return copy(c, 2, there, there, device)

        def complete(c):
            a, start, _, half, _, _, high, device = quarters(c)
            there = arrays[a].at[flip(mp, 2), ds(start + high * half, half)]
            return copy(c, 3, there, there, device)

        def hand_on(c):
            a, start, rows = chunks[c]
            there = arrays[a].at[flip(mp, 2), pl.ds(start, rows)]
            return copy(c, 4, there, there, near)

        for c in range(n_lead):
            across(c).start()
            beside(c).start()
        for k in range(2 * lead):
            for way in range(3):
                whole(k, way).start()
        for c in range(n_lead, early):
            across(c).start()
        for c in range(n_lead, n_chunks):
            beside(c).start()
        if lead:
            n_front = arrays_own[0].shape[0]
            arrays[0][mp, :n_front] = arrays_own[0][...]
            arrays[0][:, n_front:] = jnp.zeros((4, arrays[0].shape[1] - n_front, D), BF16)
        for k in range(2 * lead):
            vectors[k][mp] = vectors_own[k][...]

    def gather(step):
        for late, stage in enumerate(
            ((across, widen), (widen, complete), (complete, hand_on))
        ):
            a = step + n_lead - LAG * late
            if n_lead <= a < n_chunks:
                stage[0](a).wait_recv()
                stage[1](a).start()

    kv_rows = before.shape[1]
    from_row = cols.shape[1] - kv_rows
    sends_on = (mp == 1) | (mp == 2)
    sends_window = (mp == 0) & (ctx == 0)
    receives = (mp >= 2) | ((mp == 0) & (ctx == 1))

    def pass_on(slot, device):
        source = cols.at[slot, pl.ds(from_row, kv_rows)]
        return remote(source, before.at[slot], kv_out.at[slot], kv_in.at[slot], device)

    def pass_again(slot):
        return remote(before.at[slot], earlier.at[slot], on_out.at[slot], on_in.at[slot], {"mp": 3})

    order = (mp, flip(mp, 1), flip(mp, 2), 3 - mp) if lead else range(4)
    for k, slot in enumerate(order):
        if lead and k == 1:
            for vector in range(2):
                for way in range(3):
                    whole(vector, way).wait_recv()
            for c in range(n_lead):
                across(c).wait_recv()
                widen(c).start()
            for c in range(n_lead):
                beside(c).wait_recv()
        if lead and k == 2:
            for c in range(n_lead):
                widen(c).wait_recv()
                complete(c).start()
            for c in range(n_lead):
                complete(c).wait_recv()
                hand_on(c).start()
        if lead and k == 3:
            for c in range(n_lead):
                hand_on(c).wait_recv()
        column = jnp.transpose(bias[slot])[: cols.shape[1], 0:1]
        cols[slot] = (dot(front[slot, : cols.shape[1]], normed[...], 1, 1) + column).astype(BF16)
        pl.when(sends_on)(lambda: pass_on(slot, {"mp": mp + 1}).start())
        pl.when(sends_window)(lambda: pass_on(slot, window).start())
    for c in range(early, n_chunks):
        across(c).start()
    steps = n_chunks - n_lead + 2 * LAG
    for step in range(steps):
        if step + offset < 0:
            gather(step)

    def arrive(slot):
        def from_next():
            pass_on(slot, window).wait_recv()
            pl.when(mp == 2)(lambda: pass_again(slot).start())
            pl.when(mp == 3)(lambda: pass_again(slot).wait_recv())

        pl.when(receives)(from_next)

    keys = ((earlier, 0), (before, 0), (cols, BAND))
    sees_one, sees_two = receives, mp == 3
    sender = lax.max(mp - 1, 0)

    def group(k, _):
        if mixed:
            g = k
            pl.when(k < 2)(lambda: arrive(k))

            def rest():
                arrive(2)
                arrive(3)

            pl.when(k == 2)(rest)
        else:
            g = (sender % 2 + k) % 2 + 2 * ((sender // 2 + k // 2) % 2)
            arrive(g)
        place_values(mixed, g, places, first_values, keys, values)
        for t in range(WIN // TILE):
            tokens = slice(t * TILE, (t + 1) * TILE)
            low = lo_ref[:, tokens]
            place = 2 * WIN + t * TILE + lax.broadcasted_iota(jnp.int32, (1, TILE), 1)
            end = 2 * WIN // TILE + t

            def score(kt, tokens=tokens, low=low, place=place, end=end):
                spot = kt * TILE + lax.broadcasted_iota(jnp.int32, (TILE, TILE), 0)
                keep = spot >= low
                if kt == end:
                    keep = keep & (spot <= place)
                span = slice(kt % 2 * TILE, (kt % 2 + 1) * TILE)
                key_ref, at = keys[kt // 2]
                for j in range(GROUP):
                    rows = slice(j * HD, (j + 1) * HD)
                    key = key_ref[g, at + j * HD : at + (j + 1) * HD, span]
                    found = dot(key, cols[g, rows, tokens] * SCALE, 0, 0)
                    found = jnp.where(keep, found, -jnp.inf)
                    raw[j, kt] = found
                    peak = jnp.max(found.reshape(TILE // 8, 8, TILE), axis=0)
                    top[j] = peak if kt == end else jnp.maximum(top[j], peak)

            def weigh(kt, end=end):
                span = slice(kt % 2 * TILE, (kt % 2 + 1) * TILE)
                for j in range(GROUP):
                    rows = slice(j * HD, (j + 1) * HD)
                    powers = jnp.exp(raw[j, kt] - top[j, 0:1])
                    added = jnp.sum(powers.reshape(TILE // 8, 8, TILE), axis=0)
                    result = dot(values[kt // 2, rows, span], powers.astype(BF16), 1, 0)
                    total[j] = added if kt == end else total[j] + added
                    acc[j] = result if kt == end else acc[j] + result

            for stage in (score, weigh):
                for kt in reversed(range(end + 1)):
                    if kt >= 4:
                        stage(kt)
                    else:
                        pl.when(sees_one if kt >= 2 else sees_two)(functools.partial(stage, kt))
                if stage is score:
                    for j in range(GROUP):
                        top[j] = jnp.broadcast_to(jnp.max(top[j], axis=0, keepdims=True), (8, TILE))
            for j in range(GROUP):
                rows = slice(j * HD, (j + 1) * HD)
                whole_sum = jnp.sum(total[j], axis=0, keepdims=True)
                result = acc[j] / whole_sum
                out_ref[g, rows, tokens] = result.astype(BF16)
                exact_ref[g, rows, tokens] = result
                sum_ref[g, j : j + 1, tokens] = top[j, 0:1] + jnp.log(whole_sum)
            for step in range(steps):
                if (step + offset) % 2 == t and 0 <= step + offset < 8:
                    pl.when(k == (step + offset) // 2)(functools.partial(gather, step))
        return 0

    lax.fori_loop(0, 4, group, 0)
    for step in range(steps):
        if step + offset >= 8:
            gather(step)

    def sent(device):
        each(4, lambda slot: pass_on(slot, device).wait_send())

    pl.when(sends_on)(lambda: sent({"mp": mp + 1}))
    pl.when(sends_window)(lambda: sent(window))
    pl.when(mp == 2)(lambda: each(4, lambda slot: pass_again(slot).wait_send()))
    for k in range(2 * lead):
        for way in range(3):
            whole(k, way).wait_send()
    for a in range(n_chunks):
        beside(a).wait_send()
        if a >= n_lead:
            beside(a).wait_recv()
            hand_on(a).wait_recv()
        across(a).wait_send()
        widen(a).wait_send()
        complete(a).wait_send()
        hand_on(a).wait_send()


def place_values(mixed, g, places, first_values, keys, values):
    if not mixed:
        for part, (ref, at) in enumerate(keys):
            values[part] = ref[g, at + BAND : at + 2 * BAND, :]
        return

    def reused():
        for part in range(3):
            for j in range(GROUP):
                at = places[(0 if part == 2 else REUSE) + GROUP * g + j]
                values[part, j * HD : (j + 1) * HD, :] = first_values[part][at]

    def own():
        wide = BAND // 2
        for part, (ref, at) in enumerate(keys):
            for side in range(2):
                values[part, side * wide : (side + 1) * wide, :] = ref[
                    2 * (g - 2) + side, at + BAND : at + BAND + wide, :
                ]

    pl.when(g < 2)(reused)
    pl.when(g >= 2)(own)


def chunks_of(lead, more_rows):
    chunks = [(0, k * BAND, BAND) for k in range(LEAD)] * lead
    for array, rows in enumerate(more_rows):
        size = CHUNK if rows % CHUNK == 0 else rows
        chunks += [(array + lead, start, size) for start in range(0, rows, size)]
    return chunks


def project(places, low, normed, front, bias, n_cols, kv_rows, firsts=(), small=None, more=()):
    place = pl.BlockSpec(memory_space=pltpu.VMEM)
    away = pl.BlockSpec(memory_space=pl.ANY)
    dma = pltpu.SemaphoreType.DMA
    given = [low, normed] + [v.reshape(-1, HD, WIN) for v in firsts[::-1]]
    lead = small is not None
    given += [bias, small, front] if lead else [front, bias]
    made = [(4, n_cols, WIN), (4, kv_rows, WIN), (4, kv_rows, WIN), (4, BAND, WIN)]
    made = [jax.ShapeDtypeStruct(shape, BF16) for shape in made]
    made += [jax.ShapeDtypeStruct((4, rows, WIN), F32) for rows in (BAND, 8)]
    scratch = [
        pltpu.VMEM((3, BAND, WIN), BF16),
        pltpu.VMEM((GROUP, TILES, TILE, TILE), F32),
        pltpu.VMEM((GROUP, 8, TILE), F32),
        pltpu.VMEM((GROUP, 8, TILE), F32),
        pltpu.VMEM((GROUP, HD, TILE), F32),
    ] + [dma((4,))] * 4
    gathered = ([bias, small, front] if lead else []) + list(more)
    gathered = [jax.ShapeDtypeStruct((4,) + v.shape, v.dtype) for v in gathered]
    if lead:
        gathered[2] = jax.ShapeDtypeStruct((4, -(-n_cols // 128) * 128, D), BF16)
    rows = [v.shape[0] for v in more]
    scratch += [dma((len(chunks_of(lead, rows)), 5))] * 2 + ([dma((2, 3))] * 2 if lead else [])
    return pl.pallas_call(
        functools.partial(front_kernel, rows, int(lead), bool(firsts)),
        out_shape=made + gathered,
        in_specs=[pl.BlockSpec(memory_space=pltpu.SMEM)]
        + [place] * len(given) + [away] * len(more),
        out_specs=[place] * (len(made) + 3 * lead) + [away] * len(more),
        scratch_shapes=scratch,
        compiler_params=pltpu.CompilerParams(
            collective_id=1 if lead else 2,
            has_side_effects=True,
            vmem_limit_bytes=(48 if lead else 36) * 1024 * 1024,
        ),
        name="front_first" if lead else "front_second",
    )(places, *given, *more)


def row_starts(lengths):
    part = lax.axis_index("mp")
    place = (part - 1) * WIN + jnp.arange(WIN, dtype=jnp.int32)
    ends = jnp.cumsum(lengths)
    begun = jnp.max(jnp.where(place[:, None] >= ends[None, :], ends[None, :], 0), axis=1)
    document = begun - (part - 1) * WIN + 2 * WIN
    window = jnp.where(lax.axis_index("ctx") > 0, WIN, 2 * WIN)
    low = jnp.where(part == 0, window, document).astype(jnp.int32)
    return low.reshape(1, WIN)


class Sums:
    def __init__(self, counts, rows, terms, out, refs, slack):
        self.counts, self.rows, self.out = counts, rows, out
        self.owns, self.nears, self.fars, self.lasts = zip(*terms)
        self.from_near, self.from_last = refs[:2]
        self.mine, self.from_y = self.from_near, out
        self.from_x, self.kept, self.from_z = refs[2:5]
        self.sems = refs[5:]
        self.parts = sum(counts)
        self.firsts = [sum(counts[:k]) for k in range(len(counts))]
        self.ctx, self.dp, mp = (lax.axis_index(axis) for axis in ("ctx", "dp", "mp"))
        self.half = rows // 2
        self.bits = [1 << k for k in range((lax.axis_size("dp") - 1).bit_length())]
        self.highs = [(self.dp // bit) % 2 for bit in self.bits]
        self.other_chip, self.other_window = {"mp": flip(mp, 2)}, {"ctx": 1 - self.ctx}
        self.other_core = {"mp": flip(mp, 1)}
        self.beside = [{"dp": flip(self.dp, bit)} for bit in self.bits]
        self.partners = [self.other_chip, self.other_window, self.other_core] + self.beside
        self.stages = [self.join, self.spread]
        self.stages += [functools.partial(self.narrow, k) for k in range(len(self.bits))]
        self.stages += [functools.partial(self.widen, k) for k in reversed(range(len(self.bits)))]
        self.lates = [k + slack[min(k, len(slack) - 1)] for k in range(len(self.stages))]
        self.steps = self.parts + self.lates[-1]

    @staticmethod
    def scratch(total, parts, bits, lanes):
        dma = pltpu.SemaphoreType.DMA
        return [
            pltpu.VMEM((total, lanes), BF16),
            pltpu.VMEM((total, lanes), BF16),
            pltpu.VMEM((total // 2, lanes), BF16),
            pltpu.VMEM((total // 2, lanes), BF16),
            pltpu.VMEM((total // 2, lanes), BF16),
            dma((parts,)), dma((parts,)),
            dma((parts,)), dma((parts,)),
            dma((parts, bits)), dma((parts, bits)),
            dma((parts, bits)), dma((parts, bits)),
            dma((parts,)), dma((parts,)),
            dma((parts, 2)), dma((parts, 2)),
        ]

    def segment(self, k, sent=False):
        start, size = 0, self.half
        for high in self.highs[:k]:
            size //= 2
            start = start + high * size
        if sent:
            size //= 2
            start = start + (1 - self.highs[k]) * size
        return start, size

    def to_core(self, array, i, which):
        place = self.firsts[array] + i
        source = (self.nears, self.lasts)[which][array].at[ds(i * self.rows, self.rows)]
        target = (self.from_near, self.from_last)[which].at[ds(place * self.rows, self.rows)]
        sent, received = (sem.at[place, which] for sem in self.sems[10:12])
        return remote(source, target, sent, received, self.other_core)

    def to_y(self, i):
        here = ds(i * self.rows, self.rows)
        source, target = self.from_last.at[here], self.from_y.at[here]
        return remote(source, target, self.sems[0].at[i], self.sems[1].at[i], self.other_chip)

    def to_x(self, i):
        source = self.mine.at[ds(i * self.rows + (1 - self.ctx) * self.half, self.half)]
        target = self.from_x.at[ds(i * self.half, self.half)]
        return remote(source, target, self.sems[2].at[i], self.sems[3].at[i], self.other_window)

    def to_z(self, i, k):
        start, size = self.segment(k, True)
        source = self.kept.at[ds(i * self.half + start, size)]
        target = self.from_z.at[ds(i * self.half + self.half - 2 * size, size)]
        return remote(source, target, self.sems[4].at[i, k], self.sems[5].at[i, k], self.beside[k])

    def back_z(self, i, k):
        start, size = self.segment(k + 1)
        here = self.out.at[ds(i * self.rows + self.ctx * self.half + start, size)]
        return remote(here, here, self.sems[6].at[i, k], self.sems[7].at[i, k], self.beside[k])

    def back_x(self, i):
        here = self.out.at[ds(i * self.rows + self.ctx * self.half, self.half)]
        return remote(here, here, self.sems[8].at[i], self.sems[9].at[i], self.other_window)

    def start(self):
        for array, count in enumerate(self.counts):

            def send(i, array=array):
                self.to_core(array, i, 1).start()
                self.to_core(array, i, 0).start()

            each(count, send)
        for array, count in enumerate(self.counts):

            def fold(i, array=array):
                place = self.firsts[array] + i
                self.to_core(array, i, 1).wait_recv()
                here = ds(place * self.rows, self.rows)
                term = self.fars[array][ds(i * self.rows, self.rows), :]
                total = term.astype(F32) + self.from_last[here, :].astype(F32)
                self.from_last[here, :] = total.astype(BF16)
                self.to_y(place).start()

            each(count, fold)

    def join(self, i):
        here = ds(i * self.rows, self.rows)
        self.to_y(i).wait_recv()
        for array, count in enumerate(self.counts):
            first = self.firsts[array]

            def add(array=array, first=first):
                self.to_core(array, i - first, 0).wait_recv()
                term = self.owns[array][ds((i - first) * self.rows, self.rows), :]
                total = term.astype(F32) + self.from_near[here, :].astype(F32)
                self.mine[here, :] = (total + self.from_y[here, :].astype(F32)).astype(BF16)

            pl.when((i >= first) & (i < first + count))(add)
        self.to_x(i).start()

    def spread(self, i):
        self.to_x(i).wait_recv()
        there = ds(i * self.half, self.half)
        term = self.mine[ds(i * self.rows + self.ctx * self.half, self.half), :]
        total = term.astype(F32) + self.from_x[there, :].astype(F32)
        self.kept[there, :] = total.astype(BF16)
        self.to_z(i, 0).start()

    def narrow(self, k, i):
        self.to_z(i, k).wait_recv()
        start, size = self.segment(k + 1)
        here = ds(i * self.half + start, size)
        there = ds(i * self.half + self.half - 2 * size, size)
        total = self.kept[here, :].astype(F32) + self.from_z[there, :].astype(F32)
        if k + 1 < len(self.bits):
            self.kept[here, :] = total.astype(BF16)
            self.to_z(i, k + 1).start()
        else:
            place = ds(i * self.rows + self.ctx * self.half + start, size)
            self.out[place, :] = total.astype(BF16)
            self.back_z(i, k).start()

    def widen(self, k, i):
        self.back_z(i, k).wait_recv()
        if k:
            self.back_z(i, k - 1).start()
        else:
            self.back_x(i).start()

    def step(self, i):
        for late, stage in zip(self.lates, self.stages, strict=True):
            pl.when((i >= late) & (i < self.parts + late))(functools.partial(stage, i - late))

    def finish(self):
        for array, count in enumerate(self.counts):

            def sent(i, array=array):
                self.to_core(array, i, 0).wait_send()
                self.to_core(array, i, 1).wait_send()

            each(count, sent)

        def end(i):
            self.to_y(i).wait_send()
            self.to_x(i).wait_send()
            self.back_x(i).wait()
            for k in range(len(self.bits)):
                self.to_z(i, k).wait_send()
                self.back_z(i, k).wait_send()

        each(self.parts, end)


def ds(start, size):
    return pl.ds(pl.multiple_of(start, 16), size)


def each(count, step):
    lax.fori_loop(0, count, lambda i, _: (step(i), 0)[1], 0)


def sum_kernel(arrays, places, *refs):
    n_here, n_there = len(arrays.here), len(arrays.there)
    here, there, refs = refs[:n_here], refs[n_here : n_here + n_there], refs[n_here + n_there :]
    terms, out, vec = refs[: len(places)], refs[len(places)], refs[len(places) + 1]
    from_vec, v_out, v_in = refs[-3:]
    sums, copies = arrays.open(here, there, out, refs[len(places) + 2 : -3])
    meet(sums.partners)
    mp = lax.axis_index("mp")
    slots = (mp, flip(mp, 1), flip(mp, 2), 3 - mp)
    vec[...] = jnp.zeros_like(vec)
    for term, (row, distance) in zip(terms, places, strict=True):
        at = row if distance is None else row + slots[distance]
        vec[pl.ds(at, 1), : term.shape[0]] = term[...].reshape(1, term.shape[0])
    for hop, partner in enumerate(sums.partners):
        copy = remote(vec, from_vec.at[hop], v_out.at[hop], v_in.at[hop], partner)
        copy.start()
        if hop == 0:
            for own_copy in copies:
                own_copy.wait()
            sums.start()
        copy.wait()
        vec[...] = vec[...] + from_vec[hop]
    each(sums.steps, sums.step)
    sums.finish()


def rows_of_part():
    return max(128, 32 * lax.axis_size("dp"))


class Arrays:
    def __init__(self, arrays):
        self.rows, self.bits = rows_of_part(), (lax.axis_size("dp") - 1).bit_length()
        self.pieces = [(v[0] if isinstance(v, tuple) else v).shape[-2] for v in arrays]
        if self.rows > 512:
            quads = [v if isinstance(v, tuple) else by_distance(v) for v in arrays]
            arrays = [tuple(jnp.concatenate(part) for part in zip(*quads, strict=True))]
        self.stacked = [not isinstance(array, tuple) for array in arrays]
        first = [array if stacked else array[0] for array, stacked in zip(arrays, self.stacked)]
        self.sizes = [v.shape[-2] for v in first]
        self.counts = [-(-size // self.rows) for size in self.sizes]
        filled = [
            tuple(self.fill(v) for v in array) if isinstance(array, tuple) else self.fill(array)
            for array in arrays
        ]
        self.here = [v for array in filled if isinstance(array, tuple) for v in array[::2]]
        self.there = []
        for array in filled:
            self.there += array[1::2] if isinstance(array, tuple) else [array]
        total, lanes = sum(self.counts) * self.rows, first[0].shape[-1]
        self.shape = jax.ShapeDtypeStruct((total, lanes), BF16)
        self.scratch = []
        for count, stacked in zip(self.counts, self.stacked):
            if stacked:
                self.scratch.append(pltpu.VMEM((2, count * self.rows, lanes), BF16))
                self.scratch.append(pltpu.SemaphoreType.DMA((2,)))
        self.scratch += Sums.scratch(total, sum(self.counts), self.bits, lanes)

    def fill(self, value):
        missing = -value.shape[-2] % self.rows
        return jnp.pad(value, [(0, 0)] * (value.ndim - 2) + [(0, missing), (0, 0)])

    def split(self, stack):
        shares, at = [], 0
        merged = len(self.pieces) > len(self.sizes)
        for k, size in enumerate(self.pieces):
            shares.append(stack[at : at + size])
            at += size if merged else self.counts[k] * self.rows
        return shares

    def open(self, here, there, out, refs, slack=(0,)):
        here, there, refs = list(here), list(there), list(refs)
        mp = lax.axis_index("mp")
        terms, copies = [], []
        for stacked in self.stacked:
            if not stacked:
                own, far = here.pop(0), here.pop(0)
                terms.append((own, there.pop(0), far, there.pop(0)))
                continue
            stack, place, sems = there.pop(0), refs.pop(0), refs.pop(0)
            for k, slot in enumerate((mp, flip(mp, 2))):
                copies.append(pltpu.make_async_copy(stack.at[slot], place.at[k], sems.at[k]))
                copies[-1].start()
            terms.append((place.at[0], stack.at[flip(mp, 1)], place.at[1], stack.at[3 - mp]))
        return Sums(self.counts, self.rows, terms, out, refs, slack), copies


def sum_replicas(arrays, vectors):
    arrays = Arrays(arrays)
    place = pl.BlockSpec(memory_space=pltpu.VMEM)
    away = pl.BlockSpec(memory_space=pl.ANY)
    dma = pltpu.SemaphoreType.DMA
    hops = 3 + arrays.bits
    stack, summed = pl.pallas_call(
        functools.partial(sum_kernel, arrays, [v[1:] for v in vectors]),
        out_shape=[arrays.shape, jax.ShapeDtypeStruct((len(vectors), D), F32)],
        in_specs=[place] * len(arrays.here)
        + [away] * len(arrays.there)
        + [place] * len(vectors),
        out_specs=[place, place],
        scratch_shapes=arrays.scratch
        + [pltpu.VMEM((hops, len(vectors), D), F32), dma((hops,)), dma((hops,))],
        compiler_params=pltpu.CompilerParams(
            collective_id=0, has_side_effects=True, vmem_limit_bytes=(32 if arrays.bits > 4 else 16) * 1024 * 1024
        ),
        name="sum_replicas",
    )(*arrays.here, *arrays.there, *(v[0] for v in vectors))
    return arrays.split(stack), summed


def back_kernel(mixed, arrays, *refs):
    refs = list(refs)

    def take(count):
        taken = refs[:count]
        del refs[:count]
        return taken

    places, flags, lo_ref = take(3)
    here, there, away = take(len(arrays.here)), take(len(arrays.there)), take(9)
    (dcols,) = take(1)
    if mixed:
        dv_ref, dv_before, dv_earlier = take(3)
    (out,) = take(1)
    if not mixed:
        dv_ref, dv_before, dv_earlier = take(3)
    dk_ref, dk_before, dk_earlier = take(3)
    near_k, near_v, far_k, far_v, home_k, home_v = take(6)
    values, acc_k, acc_v, acc_q = take(4)
    kv_out, kv_in = take(2)
    fetched, loaded = take(9), take(1)[0]
    loads = [
        pltpu.make_async_copy(source, target, loaded.at[k])
        for k, (source, target) in enumerate(zip(away, fetched, strict=True))
    ]
    for load in loads:
        load.start()
    cols, before, earlier, *others, exact, grad_ref, sum_ref = fetched
    first_values, given = (others, ()) if mixed else ((), others)
    slack = (0, 1, 1, 1, 1, 2) if mixed else (0, 2)
    sums, copies = arrays.open(here, there, out, refs, slack)

    ctx, mp = lax.axis_index("ctx"), lax.axis_index("mp")
    sees_one = (mp >= 2) | ((mp == 0) & (ctx == 1))
    sees_two = mp == 3
    meet(sums.partners + [{"mp": 3 - mp}])
    for copy in copies:
        copy.wait()
    sums.start()
    keys = ((earlier, 0), (before, 0), (cols, BAND))

    def home(which, source, target, g, device):
        return remote(
            source.at[g], target.at[g], kv_out.at[which, g], kv_in.at[which, g], device
        )

    def pair(g, act, step):
        act(step)
        if mixed:
            pl.when(g >= 2)(lambda: act(step + 1))
        else:
            act(step + 1)

    def from_last(g, step):
        source, target = (
            (dk_before, near_k), (dv_before, near_v), (dk_earlier, far_k), (dv_earlier, far_v),
        )[step]
        return home(step, source, target, g, {"mp": 2})

    def from_next(g, step, device):
        source, target = ((dk_before, home_k), (dv_before, home_v))[step]
        return home(4 + step, source, target, g, device)

    def group(g, _):
        place_values(mixed, g, places, first_values, keys, values)
        acc_k[...] = jnp.zeros_like(acc_k)
        if mixed:
            acc_v[...] = jnp.zeros_like(acc_v)
        else:
            for part in range(3):
                for j in range(GROUP):
                    head = GROUP * g + j
                    term = given[part][places[head]].astype(F32) * flags[head]
                    for side in range(2):
                        acc_v[2 * part + side, j * HD : (j + 1) * HD, :] = term[
                            :, side * TILE : (side + 1) * TILE
                        ]
        for t in range(WIN // TILE):
            tokens = slice(t * TILE, (t + 1) * TILE)
            low = lo_ref[:, tokens]
            place = 2 * WIN + t * TILE + lax.broadcasted_iota(jnp.int32, (1, TILE), 1)
            last = 2 * WIN // TILE + t

            def tile(kt, tokens=tokens, low=low, place=place, last=last):
                spot = kt * TILE + lax.broadcasted_iota(jnp.int32, (TILE, TILE), 0)
                keep = spot >= low
                if kt == last:
                    keep = keep & (spot <= place)
                span = slice(kt % 2 * TILE, (kt % 2 + 1) * TILE)
                key_ref, at = keys[kt // 2]
                for j in range(GROUP):
                    rows_j = slice(j * HD, (j + 1) * HD)
                    key = key_ref[g, at + j * HD : at + (j + 1) * HD, span]
                    query = cols[g, rows_j, tokens] * SCALE
                    grad = grad_ref[g, rows_j, tokens]
                    inner = jnp.sum(
                        grad.astype(F32) * exact[g, rows_j, tokens], axis=0, keepdims=True
                    )
                    raw = jnp.where(keep, dot(key, query, 0, 0), -jnp.inf)
                    weights = jnp.exp(raw - sum_ref[g, j : j + 1, tokens])
                    grad_weights = dot(values[kt // 2, rows_j, span], grad, 0, 0)
                    low_grad = (weights * (grad_weights - inner)).astype(BF16)
                    acc_v[kt, rows_j, :] += dot(grad, weights.astype(BF16), 1, 1)
                    acc_k[kt, rows_j, :] += dot(query, low_grad, 1, 1)
                    result = dot(key, low_grad, 1, 0)
                    acc_q[j] = result if kt == last else result + acc_q[j]

            for kt in reversed(range(last + 1)):
                if kt >= 4:
                    tile(kt)
                else:
                    pl.when(sees_one if kt >= 2 else sees_two)(functools.partial(tile, kt))
            for j in range(GROUP):
                dcols[g, j * HD : (j + 1) * HD, tokens] = (acc_q[j] * SCALE).astype(BF16)
            sums.step(2 * g + t)
        results = ((dk_earlier, dv_earlier), (dk_before, dv_before), (dk_ref, dv_ref))
        for part, (dk, dv) in enumerate(results):
            for side in range(2):
                span = slice(side * TILE, (side + 1) * TILE)
                dk[g, :, span] = acc_k[2 * part + side].astype(dk.dtype)
                dv[g, :, span] = acc_v[2 * part + side].astype(dv.dtype)

        def send_last():
            pair(g, lambda step: from_last(g, step).start(), 0)
            pair(g, lambda step: from_last(g, step).start(), 2)

        pl.when(mp == 3)(send_last)
        pl.when((mp == 0) & (ctx == 1))(
            lambda: pair(g, lambda step: from_next(g, step, sums.other_window).start(), 0)
        )
        return 0

    for load in loads:
        load.wait()
    lax.fori_loop(0, 4, group, 0)

    def relay(g):
        def one(step):
            near, far, source, total = (
                (near_k, far_k, dk_before, dk_ref), (near_v, far_v, dv_before, dv_ref),
            )[step]
            from_last(g, step).wait_recv()
            from_last(g, step + 2).wait_recv()
            source[g] = (source[g].astype(F32) + far[g].astype(F32)).astype(BF16)
            from_next(g, step, {"mp": 1}).start()
            total[g] += near[g].astype(F32)

        pair(g, one, 0)

    pl.when(mp == 2)(lambda: each(4, relay))
    for i in range(8, sums.steps):
        sums.step(i)

    def arrive(g):
        def one(step):
            arrived, total = ((home_k, dk_ref), (home_v, dv_ref))[step]
            from_next(g, step, sums.other_window).wait_recv()
            total[g] += arrived[g].astype(F32)

        pair(g, one, 0)

    pl.when((mp == 1) | ((mp == 0) & (ctx == 0)))(lambda: each(4, arrive))

    def round_off(g):
        dcols[g, BAND : 2 * BAND, :] = dk_ref[g].astype(BF16)
        if not mixed:
            dcols[g, 2 * BAND : 3 * BAND, :] = dv_ref[g].astype(BF16)

    each(4, round_off)
    wide = BAND // 2 if mixed else BAND
    for slot in range(4):
        if mixed:
            half = slice(slot % 2 * wide, (slot % 2 + 1) * wide)
            dcols[slot, 2 * BAND : 2 * BAND + wide, :] = dv_ref[2 + slot // 2, half, :].astype(BF16)
        rest = dcols.shape[1] - 2 * BAND - wide
        dcols[slot, 2 * BAND + wide :, :] = jnp.zeros((rest, WIN), BF16)

    def sent_last(g):
        pair(g, lambda step: from_last(g, step).wait_send(), 0)
        pair(g, lambda step: from_last(g, step).wait_send(), 2)

    def sent_next(device):
        each(4, lambda g: pair(g, lambda step: from_next(g, step, device).wait_send(), 0))

    pl.when(mp == 3)(lambda: each(4, sent_last))
    pl.when(mp == 2)(lambda: sent_next({"mp": 1}))
    pl.when((mp == 0) & (ctx == 1))(lambda: sent_next(sums.other_window))
    sums.finish()


def attend_back(places, flags, low, front, firsts, given, exact, grad_heads, lse, arrays):
    mixed = bool(firsts)
    arrays = Arrays(arrays)
    place = pl.BlockSpec(memory_space=pltpu.VMEM)
    away = pl.BlockSpec(memory_space=pl.ANY)
    scalar = pl.BlockSpec(memory_space=pltpu.SMEM)
    dma = pltpu.SemaphoreType.DMA
    by_head = [v.reshape(-1, HD, WIN) for v in firsts[::-1] + given[::-1]]
    fetched = [*front, *by_head, exact, grad_heads, lse]
    wide = jax.ShapeDtypeStruct((4, BAND, WIN), F32)
    slim = jax.ShapeDtypeStruct((4, BAND, WIN), BF16)
    n_cols = -(-(5 * BAND // 2 if mixed else 3 * BAND) // 128) * 128
    outs = [jax.ShapeDtypeStruct((4, n_cols, WIN), BF16)]
    outs += ([wide, slim, slim] if mixed else []) + [arrays.shape]
    block, full = pltpu.VMEM((4, BAND, WIN), BF16), pltpu.VMEM((4, BAND, WIN), F32)
    results = pl.pallas_call(
        functools.partial(back_kernel, mixed, arrays),
        out_shape=outs,
        in_specs=[scalar, scalar, place]
        + [place] * len(arrays.here)
        + [away] * (len(arrays.there) + len(fetched)),
        out_specs=[place] * len(outs),
        scratch_shapes=([] if mixed else [full, block, block])
        + [full]
        + [block] * 8
        + [
            pltpu.VMEM((3, BAND, WIN), BF16),
            pltpu.VMEM((TILES, BAND, TILE), F32),
            pltpu.VMEM((TILES, BAND, TILE), F32),
            pltpu.VMEM((GROUP, HD, TILE), F32),
            dma((6, 4)),
            dma((6, 4)),
        ]
        + [pltpu.VMEM(v.shape, v.dtype) for v in fetched]
        + [dma((len(fetched),))]
        + arrays.scratch,
        compiler_params=pltpu.CompilerParams(
            collective_id=3 if mixed else 4,
            has_side_effects=True,
            vmem_limit_bytes=(60 if arrays.bits > 4 else 38 if mixed else 48) * 1024 * 1024,
        ),
        name="attend_back",
    )(places, flags, low, *arrays.here, *arrays.there, *fetched)
    return results[:-1], arrays.split(results[-1])


def gelu(hidden):
    return jax.nn.gelu(hidden, approximate=True)


def tail_forward(stream, heads, out_weight, out_bias, gain, shift, ups, up_biases, downs):
    stream = stream + dot(heads, out_weight, 0, 0) + out_bias[0]
    normed, unit, scale = norm_rows(stream, gain[1], shift[1])
    hidden, active, total = [], [], out_bias[1]
    for up, bias, down in zip(ups, up_biases, downs, strict=True):
        hidden.append(dot(normed, up, 1, 0) + bias)
        active.append(gelu(hidden[-1]).astype(BF16))
        total = total + dot(active[-1], down, 1, 0)
    return stream + total, (normed, unit, scale, hidden, active)


def tail_backward(grad, kept, out_weight, gain, ups, downs):
    normed, unit, scale, hidden, active = kept
    bias_mlp = jnp.sum(grad, axis=0)
    rounded = grad.astype(BF16)
    mats, up_biases, normed_grad = [], [], 0.0
    for up, down, before, after in zip(ups, downs, hidden, active, strict=True):
        _, pull = jax.vjp(gelu, before)
        grad_hidden = pull(dot(rounded, down, 1, 1))[0]
        up_biases.append(jnp.sum(grad_hidden, axis=0))
        low = grad_hidden.astype(BF16)
        mats.append((dot(normed, low, 0, 0).astype(BF16), dot(after, rounded, 0, 0).astype(BF16)))
        normed_grad = normed_grad + dot(low, up, 1, 1)
    middle, gain_grad, shift_grad = norm_back(normed_grad, unit, scale, gain[1])
    grad = grad + middle
    bias_attn = jnp.sum(grad, axis=0)
    rounded = grad.astype(BF16)
    grad_heads = dot(out_weight, rounded, 1, 1).astype(BF16)
    return grad, rounded, grad_heads, mats, up_biases, (gain_grad, shift_grad, bias_attn, bias_mlp)


def turned(weight):
    return jnp.swapaxes(weight, -1, -2)


def shards(
    block_input, cotangent, doc_lengths, reuse_heads,
    norm_gain1, norm_bias1, projections1, front_bias1, out_weight1, out_bias1,
    up_weight1, up_bias1, down_weight1,
    norm_gain2, norm_bias2, query_key2, query_bias2, fresh_value2, value_bias2,
    out_weight2, out_bias2, up_weight2, up_bias2, down_weight2,
):
    low = row_starts(doc_lengths[0])
    taken = jnp.arange(4 * GROUP, dtype=jnp.int32)[:, None] == reuse_heads[None, :]
    taker = jnp.sum(jnp.where(taken, jnp.arange(REUSE, dtype=jnp.int32)[None, :], 0), axis=1)
    flags = jnp.any(taken, axis=1).astype(F32)
    band_of, in_band = reuse_heads // GROUP, reuse_heads % GROUP
    places2 = jnp.concatenate(
        [band_of * 3 * GROUP + 2 * GROUP + in_band, band_of * 2 * GROUP + GROUP + in_band]
    )

    stream0 = block_input.astype(F32)
    normed1, unit1, scale1 = norm_rows(stream0, norm_gain1[0], norm_bias1[0])
    n_front1, n_front2 = 3 * BAND, 2 * BAND + BAND // 2
    none = jnp.zeros((BAND,), BF16)

    def as_row(pieces):
        row = jnp.concatenate(pieces).astype(F32)
        return jnp.pad(row[None, :], ((0, 7), (0, -row.shape[0] % 128)))

    small = jnp.concatenate([query_bias2, value_bias2, up_bias1, up_bias2])
    small = jnp.pad(small, (0, 16 * 128 - small.shape[0])).reshape(16, 128)
    own_front2 = jnp.concatenate([turned(query_key2).reshape(2 * BAND, D), turned(fresh_value2)])
    own_front2 = jnp.pad(own_front2, ((0, -n_front2 % 64), (0, 0)))
    (
        cols1, before1, earlier1, heads1, exact1, sums1, _, small, front1,
        up1, down1, front2, outs1,
    ) = project(
        places2, low, normed1, turned(projections1).reshape(n_front1, D),
        as_row([front_bias1[0], none, front_bias1[1]]), n_front1, 2 * BAND, (), small,
        (up_weight1, down_weight1, own_front2, out_weight1),
    )
    me = lax.axis_index("mp")
    ups1, downs1 = ([up_weight1] + by_distance(up1)[1:], [down_weight1] + by_distance(down1)[1:])
    front2 = lax.dynamic_update_index_in_dim(front2, own_front2, me, 0)
    outs1 = lax.dynamic_update_index_in_dim(outs1, out_weight1, me, 0).reshape(D, D)
    small = small.reshape(4, -1)
    at = BAND + BAND // 2
    bias2 = jnp.stack([as_row([small[s, :BAND], none, small[s, BAND:at]]) for s in range(4)])
    up_biases1 = by_distance(small[:, at : at + D])
    up_biases2 = by_distance(small[:, at + D : at + 2 * D])

    front_kv1 = (cols1, before1, earlier1)
    stream1, kept1 = tail_forward(
        stream0, heads1.reshape(D, WIN), outs1, out_bias1, norm_gain1, norm_bias1,
        ups1, up_biases1, downs1,
    )

    normed2, unit2, scale2 = norm_rows(stream1, norm_gain2[0], norm_bias2[0])
    front_kv1 = (cols1, before1, earlier1)
    cols2, before2, earlier2, heads2, exact2, sums2, up2, down2, outs2 = project(
        places2, low, normed2, front2, bias2, n_front2, n_front2 - BAND, front_kv1, None,
        (up_weight2, down_weight2, out_weight2),
    )
    ups2, downs2 = ([up_weight2] + by_distance(up2)[1:], [down_weight2] + by_distance(down2)[1:])
    outs2 = lax.dynamic_update_index_in_dim(outs2, out_weight2, me, 0).reshape(D, D)

    front_kv2 = (cols2, before2, earlier2)
    stream2, kept2 = tail_forward(
        stream1, heads2.reshape(D, WIN), outs2, out_bias2, norm_gain2, norm_bias2,
        ups2, up_biases2, downs2,
    )
    block_output = stream2.astype(BF16)

    grad, rounded, grad_heads, mats2, up_grads2, small2 = tail_backward(
        cotangent.astype(F32), kept2, outs2, norm_gain2, ups2, downs2
    )
    (dcols2, dv2, dv2_before, dv2_earlier), mats2 = attend_back(
        places2, flags, low, front_kv2, front_kv1, (), exact2,
        grad_heads.reshape(4, BAND, WIN), sums2, list(zip(*mats2, strict=True)),
    )
    grad_out2 = dot(heads2.reshape(D, WIN), rounded, 1, 0).astype(BF16).reshape(4, BAND, D)
    bias_grad2 = jnp.sum(dcols2.astype(F32), axis=2)
    grad_front2 = dot(dcols2.reshape(-1, WIN), normed2, 1, 0).astype(BF16).reshape(4, -1, D)
    normed_grad = dot(dcols2.reshape(-1, WIN), front2.reshape(-1, D), 0, 0)
    middle, gain_front2, shift_front2 = norm_back(normed_grad, unit2, scale2, norm_gain2[0])
    grad = grad + middle

    grad, rounded, grad_heads, mats1, up_grads1, small1 = tail_backward(
        grad, kept1, outs1, norm_gain1, ups1, downs1
    )
    grad_out1 = dot(heads1.reshape(D, WIN), rounded, 1, 0).astype(BF16).reshape(4, BAND, D)
    arrays = [grad_front2, jnp.concatenate([grad_out2, grad_out1], axis=1)]
    (dcols1,), (front_sum2, out_sums, *mats1) = attend_back(
        taker, flags, low, front_kv1, (), (dv2, dv2_before, dv2_earlier), exact1,
        grad_heads.reshape(4, BAND, WIN), sums1, arrays + list(zip(*mats1, strict=True)),
    )
    bias_grad1 = jnp.sum(dcols1.astype(F32), axis=2)
    grad_front1 = dot(dcols1.reshape(-1, WIN), normed1, 1, 0).astype(BF16).reshape(4, -1, D)
    normed_grad = dot(dcols1.reshape(-1, WIN), front1.reshape(-1, D), 0, 0)
    middle, gain_front1, shift_front1 = norm_back(normed_grad, unit1, scale1, norm_gain1[0])
    input_grad = (grad + middle).astype(BF16)

    singles = [
        gain_front1, small1[0], shift_front1, small1[1], small1[2], small1[3],
        gain_front2, small2[0], shift_front2, small2[1], small2[2], small2[3],
        bias_grad1[:, :BAND].reshape(-1), bias_grad1[:, 2 * BAND : n_front1].reshape(-1),
        bias_grad2[:, :BAND].reshape(-1), bias_grad2[:, 2 * BAND : n_front2].reshape(-1),
    ]
    vectors = [(vector, row, None) for row, vector in enumerate(singles)]
    for row, shares in ((16, up_grads1), (20, up_grads2)):
        vectors += [(vector, row, distance) for distance, vector in enumerate(shares)]
    (front_sum1,), sums = sum_replicas([grad_front1], vectors)

    def mine(vectors):
        return lax.dynamic_index_in_dim(vectors.reshape(4, -1), me, 0, keepdims=False)

    return (
        block_output,
        input_grad,
        sums[0:2],
        sums[2:4],
        turned(front_sum1[:n_front1].reshape(3, BAND, D)).astype(F32),
        jnp.stack([mine(sums[12]), mine(sums[13])]),
        out_sums[BAND:].astype(F32),
        sums[4:6],
        mats1[0].astype(F32),
        mine(sums[16:20]),
        mats1[1].astype(F32),
        sums[6:8],
        sums[8:10],
        turned(front_sum2[: 2 * BAND].reshape(2, BAND, D)).astype(F32),
        mine(sums[14]),
        turned(front_sum2[2 * BAND : n_front2]).astype(F32),
        mine(sums[15, : D // 2]),
        out_sums[:BAND].astype(F32),
        sums[10:12],
        mats2[0].astype(F32),
        mine(sums[20:24]),
        mats2[1].astype(F32),
    )


def solution(mesh):
    rows = P(("dp", "ctx", "mp"), None)
    placed = (
        rows, rows, P(("dp", "ctx"), None), P(),
        P(), P(), P(None, None, "mp"), P(None, "mp"), P("mp", None), P(),
        P(None, "mp"), P("mp"), P("mp", None),
        P(), P(), P(None, None, "mp"), P("mp"), P(None, "mp"), P("mp"),
        P("mp", None), P(), P(None, "mp"), P("mp"), P("mp", None),
    )
    given = (
        rows, rows,
        P(), P(), P(None, None, "mp"), P(None, "mp"), P("mp", None), P(),
        P(None, "mp"), P("mp"), P("mp", None),
        P(), P(), P(None, None, "mp"), P("mp"), P(None, "mp"), P("mp"),
        P("mp", None), P(), P(None, "mp"), P("mp"), P("mp", None),
    )
    return jax.shard_map(shards, mesh=mesh, in_specs=placed, out_specs=given, check_vma=False)
```

```python
import functools

import jax
import jax.numpy as jnp
from jax import lax
from jax.experimental import pallas as pl
from jax.experimental.pallas import tpu as pltpu
from jax.sharding import PartitionSpec as P

D = 768
HD = 64
REUSE = 6
WIN = 512
EARLY = 5
CHUNK = 256
LEAD = 3
LAG_FIRST, LAG_SECOND = 3, 2
HOOK_FIRST, HOOK_SECOND = -2, 0
GROUP = 3
BAND = GROUP * HD
TILE = 256
TILES = 3 * WIN // TILE
EPS = 1e-05
SCALE = HD**-0.5
F32 = jnp.float32
BF16 = jnp.bfloat16


def swap(value, axis, bit):
    devices = range(lax.axis_size(axis))
    return lax.ppermute(value, axis, [(i, i ^ bit) for i in devices])


def in_order(parts):
    return jnp.concatenate(by_distance(jnp.stack(parts)))


def by_distance(stacked):
    me = lax.axis_index("mp")
    return [
        lax.dynamic_index_in_dim(stacked, me ^ distance, 0, keepdims=False)
        for distance in range(4)
    ]


def flip(position, bit):
    return position + bit * (1 - 2 * ((position // bit) % 2))


def remote(source, target, sent, received, device):
    return pltpu.make_async_remote_copy(
        src_ref=source, dst_ref=target, send_sem=sent, recv_sem=received,
        device_id=device, device_id_type=pl.DeviceIdType.MESH,
    )


def meet(devices):
    barrier = pltpu.get_barrier_semaphore()
    for device in devices:
        pl.semaphore_signal(barrier, inc=1, device_id=device, device_id_type=pl.DeviceIdType.MESH)
    pl.semaphore_wait(barrier, len(devices))


def dot(left, right, left_dim, right_dim):
    return lax.dot_general(
        left, right, (((left_dim,), (right_dim,)), ((), ())), preferred_element_type=F32
    )


def norm_rows(value, gain, shift):
    mean = jnp.mean(value, axis=-1, keepdims=True)
    centred = value - mean
    spread = jnp.mean(centred * centred, axis=-1, keepdims=True)
    scale = lax.rsqrt(spread + EPS)
    unit = centred * scale
    return (unit * gain + shift).astype(BF16), unit, scale


def norm_back(grad, unit, scale, gain):
    scaled = grad * gain
    inner = (
        scaled
        - jnp.mean(scaled, axis=-1, keepdims=True)
        - unit * jnp.mean(scaled * unit, axis=-1, keepdims=True)
    )
    return scale * inner, jnp.sum(grad * unit, axis=0), jnp.sum(grad, axis=0)


def front_kernel(more_rows, lead, mixed, *refs):
    refs = list(refs)

    def take(count):
        taken = refs[:count]
        del refs[:count]
        return taken

    ctx, dp, mp = (lax.axis_index(axis) for axis in ("ctx", "dp", "mp"))
    near, far, last = {"mp": flip(mp, 1)}, {"mp": flip(mp, 2)}, {"mp": 3 - mp}
    window = {"ctx": 1 - ctx}
    chunks = chunks_of(lead, more_rows)
    n_chunks, n_more, n_lead = len(chunks), len(more_rows), LEAD * lead
    n_arrays = n_more + lead
    early, offset = (EARLY, HOOK_FIRST) if lead else (4, HOOK_SECOND)
    lag = LAG_FIRST if lead else LAG_SECOND
    places, lo_ref, normed = take(3)
    first_values = take(3) if mixed else ()
    front, bias = (None, None) if lead else take(2)
    vectors_own = take(2 * lead)
    arrays_own = take(n_arrays)
    cols, before, earlier, out_ref, exact_ref, sum_ref = take(6)
    vectors = take(2 * lead)
    arrays = take(n_arrays)
    if lead:
        front, bias = arrays[0], vectors[0]
    values, raw, top, total, acc, kv_out, kv_in, on_out, on_in = take(9)
    m_out, m_in = take(2)
    if lead:
        f_out, f_in = take(2)
    meet([near, far, last, window, {"dp": flip(dp, 1)}])
    directions = (near, far, last)
    if True:

        def whole(k, way):
            return remote(
                vectors_own[k], vectors[k].at[mp], f_out.at[k, way], f_in.at[k, way],
                directions[way],
            )

        bit = lax.rem(dp, 2)
        first = [(bit, {"dp": flip(dp, 1)}), (ctx, window)]

        def quarters(c):
            a, start, rows = chunks[c]
            (low, low_device), (high, high_device) = first if c % 2 else first[::-1]
            return a, start, rows // 4, rows // 2, low, low_device, high, high_device

        def copy(c, way, source, target, device):
            return remote(source, target, m_out.at[c, way], m_in.at[c, way], device)

        def beside(c):
            a, start, rows = chunks[c]
            here = pl.ds(start, rows)
            return copy(c, 0, arrays_own[a].at[here], arrays[a].at[mp, here], near)

        def across(c):
            a, start, quarter, half, low, _, high, _ = quarters(c)
            here = ds(start + high * half + low * quarter, quarter)
            return copy(c, 1, arrays_own[a].at[here], arrays[a].at[mp, here], far)

        def widen(c):
            a, start, quarter, half, low, device, high, _ = quarters(c)
            there = arrays[a].at[flip(mp, 2), ds(start + high * half + low * quarter, quarter)]
            return copy(c, 2, there, there, device)

        def complete(c):
            a, start, _, half, _, _, high, device = quarters(c)
            there = arrays[a].at[flip(mp, 2), ds(start + high * half, half)]
            return copy(c, 3, there, there, device)

        def hand_on(c):
            a, start, rows = chunks[c]
            there = arrays[a].at[flip(mp, 2), pl.ds(start, rows)]
            return copy(c, 4, there, there, near)

        for c in range(n_lead):
            across(c).start()
            beside(c).start()
        for k in range(2 * lead):
            for way in range(3):
                whole(k, way).start()
        for c in range(n_lead, early):
            across(c).start()
        for c in range(n_lead, n_chunks):
            beside(c).start()
        if lead:
            n_front = arrays_own[0].shape[0]
            arrays[0][mp, :n_front] = arrays_own[0][...]
            arrays[0][:, n_front:] = jnp.zeros((4, arrays[0].shape[1] - n_front, D), BF16)
        for k in range(2 * lead):
            vectors[k][mp] = vectors_own[k][...]

    def gather(step):
        for late, stage in enumerate(
            ((across, widen), (widen, complete), (complete, hand_on))
        ):
            a = step + n_lead - lag * late
            if n_lead <= a < n_chunks:
                stage[0](a).wait_recv()
                stage[1](a).start()

    kv_rows = before.shape[1]
    from_row = cols.shape[1] - kv_rows
    sends_on = (mp == 1) | (mp == 2)
    sends_window = (mp == 0) & (ctx == 0)
    receives = (mp >= 2) | ((mp == 0) & (ctx == 1))

    def pass_on(slot, device):
        source = cols.at[slot, pl.ds(from_row, kv_rows)]
        return remote(source, before.at[slot], kv_out.at[slot], kv_in.at[slot], device)

    def pass_again(slot):
        return remote(before.at[slot], earlier.at[slot], on_out.at[slot], on_in.at[slot], {"mp": 3})

    order = (mp, flip(mp, 1), flip(mp, 2), 3 - mp) if lead else range(4)
    for k, slot in enumerate(order):
        if lead and k == 1:
            for vector in range(2):
                for way in range(3):
                    whole(vector, way).wait_recv()
            for c in range(n_lead):
                across(c).wait_recv()
                widen(c).start()
            for c in range(n_lead):
                beside(c).wait_recv()
        if lead and k == 2:
            for c in range(n_lead):
                widen(c).wait_recv()
                complete(c).start()
            for c in range(n_lead):
                complete(c).wait_recv()
                hand_on(c).start()
        if lead and k == 3:
            for c in range(n_lead):
                hand_on(c).wait_recv()
        column = jnp.transpose(bias[slot])[: cols.shape[1], 0:1]
        cols[slot] = (dot(front[slot, : cols.shape[1]], normed[...], 1, 1) + column).astype(BF16)
        pl.when(sends_on)(lambda: pass_on(slot, {"mp": mp + 1}).start())
        pl.when(sends_window)(lambda: pass_on(slot, window).start())
    for c in range(early, n_chunks):
        across(c).start()
    steps = n_chunks - n_lead + 2 * lag
    for step in range(steps):
        if step + offset < 0:
            gather(step)

    def arrive(slot):
        def from_next():
            pass_on(slot, window).wait_recv()
            pl.when(mp == 2)(lambda: pass_again(slot).start())
            pl.when(mp == 3)(lambda: pass_again(slot).wait_recv())

        pl.when(receives)(from_next)

    keys = ((earlier, 0), (before, 0), (cols, BAND))
    sees_one, sees_two = receives, mp == 3
    sender = lax.max(mp - 1, 0)

    def group(k, _):
        if mixed:
            g = k
            pl.when(k < 2)(lambda: arrive(k))

            def rest():
                arrive(2)
                arrive(3)

            pl.when(k == 2)(rest)
        else:
            g = (sender % 2 + k) % 2 + 2 * ((sender // 2 + k // 2) % 2)
            arrive(g)
        place_values(mixed, g, places, first_values, keys, values)
        for t in range(WIN // TILE):
            tokens = slice(t * TILE, (t + 1) * TILE)
            low = lo_ref[:, tokens]
            place = 2 * WIN + t * TILE + lax.broadcasted_iota(jnp.int32, (1, TILE), 1)
            end = 2 * WIN // TILE + t

            def score(kt, tokens=tokens, low=low, place=place, end=end):
                spot = kt * TILE + lax.broadcasted_iota(jnp.int32, (TILE, TILE), 0)
                keep = spot >= low
                if kt == end:
                    keep = keep & (spot <= place)
                span = slice(kt % 2 * TILE, (kt % 2 + 1) * TILE)
                key_ref, at = keys[kt // 2]
                for j in range(GROUP):
                    rows = slice(j * HD, (j + 1) * HD)
                    key = key_ref[g, at + j * HD : at + (j + 1) * HD, span]
                    found = dot(key, cols[g, rows, tokens] * SCALE, 0, 0)
                    found = jnp.where(keep, found, -jnp.inf)
                    raw[j, kt] = found
                    peak = jnp.max(found.reshape(TILE // 8, 8, TILE), axis=0)
                    top[j] = peak if kt == end else jnp.maximum(top[j], peak)

            def weigh(kt, end=end):
                span = slice(kt % 2 * TILE, (kt % 2 + 1) * TILE)
                for j in range(GROUP):
                    rows = slice(j * HD, (j + 1) * HD)
                    powers = jnp.exp(raw[j, kt] - top[j, 0:1])
                    added = jnp.sum(powers.reshape(TILE // 8, 8, TILE), axis=0)
                    result = dot(values[kt // 2, rows, span], powers.astype(BF16), 1, 0)
                    total[j] = added if kt == end else total[j] + added
                    acc[j] = result if kt == end else acc[j] + result

            for stage in (score, weigh):
                for kt in reversed(range(end + 1)):
                    if kt >= 4:
                        stage(kt)
                    else:
                        pl.when(sees_one if kt >= 2 else sees_two)(functools.partial(stage, kt))
                if stage is score:
                    for j in range(GROUP):
                        top[j] = jnp.broadcast_to(jnp.max(top[j], axis=0, keepdims=True), (8, TILE))
            for j in range(GROUP):
                rows = slice(j * HD, (j + 1) * HD)
                whole_sum = jnp.sum(total[j], axis=0, keepdims=True)
                result = acc[j] / whole_sum
                out_ref[g, rows, tokens] = result.astype(BF16)
                exact_ref[g, rows, tokens] = result
                sum_ref[g, j : j + 1, tokens] = top[j, 0:1] + jnp.log(whole_sum)
            for step in range(steps):
                if (step + offset) % 2 == t and 0 <= step + offset < 8:
                    pl.when(k == (step + offset) // 2)(functools.partial(gather, step))
        return 0

    lax.fori_loop(0, 4, group, 0)
    for step in range(steps):
        if step + offset >= 8:
            gather(step)

    def sent(device):
        each(4, lambda slot: pass_on(slot, device).wait_send())

    pl.when(sends_on)(lambda: sent({"mp": mp + 1}))
    pl.when(sends_window)(lambda: sent(window))
    pl.when(mp == 2)(lambda: each(4, lambda slot: pass_again(slot).wait_send()))
    for k in range(2 * lead):
        for way in range(3):
            whole(k, way).wait_send()
    for a in range(n_chunks):
        beside(a).wait_send()
        if a >= n_lead:
            beside(a).wait_recv()
            hand_on(a).wait_recv()
        across(a).wait_send()
        widen(a).wait_send()
        complete(a).wait_send()
        hand_on(a).wait_send()


def place_values(mixed, g, places, first_values, keys, values):
    if not mixed:
        for part, (ref, at) in enumerate(keys):
            values[part] = ref[g, at + BAND : at + 2 * BAND, :]
        return

    def reused():
        for part in range(3):
            for j in range(GROUP):
                at = places[(0 if part == 2 else REUSE) + GROUP * g + j]
                values[part, j * HD : (j + 1) * HD, :] = first_values[part][at]

    def own():
        wide = BAND // 2
        for part, (ref, at) in enumerate(keys):
            for side in range(2):
                values[part, side * wide : (side + 1) * wide, :] = ref[
                    2 * (g - 2) + side, at + BAND : at + BAND + wide, :
                ]

    pl.when(g < 2)(reused)
    pl.when(g >= 2)(own)


def chunks_of(lead, more_rows):
    chunks = [(0, k * BAND, BAND) for k in range(LEAD)] * lead
    for array, rows in enumerate(more_rows):
        size = CHUNK if rows % CHUNK == 0 else rows
        chunks += [(array + lead, start, size) for start in range(0, rows, size)]
    return chunks


def project(places, low, normed, front, bias, n_cols, kv_rows, firsts=(), small=None, more=()):
    place = pl.BlockSpec(memory_space=pltpu.VMEM)
    away = pl.BlockSpec(memory_space=pl.ANY)
    dma = pltpu.SemaphoreType.DMA
    given = [low, normed] + [v.reshape(-1, HD, WIN) for v in firsts[::-1]]
    lead = small is not None
    given += [bias, small, front] if lead else [front, bias]
    made = [(4, n_cols, WIN), (4, kv_rows, WIN), (4, kv_rows, WIN), (4, BAND, WIN)]
    made = [jax.ShapeDtypeStruct(shape, BF16) for shape in made]
    made += [jax.ShapeDtypeStruct((4, rows, WIN), F32) for rows in (BAND, 8)]
    scratch = [
        pltpu.VMEM((3, BAND, WIN), BF16),
        pltpu.VMEM((GROUP, TILES, TILE, TILE), F32),
        pltpu.VMEM((GROUP, 8, TILE), F32),
        pltpu.VMEM((GROUP, 8, TILE), F32),
        pltpu.VMEM((GROUP, HD, TILE), F32),
    ] + [dma((4,))] * 4
    gathered = ([bias, small, front] if lead else []) + list(more)
    gathered = [jax.ShapeDtypeStruct((4,) + v.shape, v.dtype) for v in gathered]
    if lead:
        gathered[2] = jax.ShapeDtypeStruct((4, -(-n_cols // 128) * 128, D), BF16)
    rows = [v.shape[0] for v in more]
    scratch += [dma((len(chunks_of(lead, rows)), 5))] * 2 + ([dma((2, 3))] * 2 if lead else [])
    return pl.pallas_call(
        functools.partial(front_kernel, rows, int(lead), bool(firsts)),
        out_shape=made + gathered,
        in_specs=[pl.BlockSpec(memory_space=pltpu.SMEM)]
        + [place] * len(given) + [away] * len(more),
        out_specs=[place] * (len(made) + 3 * lead) + [away] * len(more),
        scratch_shapes=scratch,
        compiler_params=pltpu.CompilerParams(
            collective_id=1 if lead else 2,
            has_side_effects=True,
            vmem_limit_bytes=(48 if lead else 36) * 1024 * 1024,
        ),
        name="front_first" if lead else "front_second",
    )(places, *given, *more)


def row_starts(lengths):
    part = lax.axis_index("mp")
    place = (part - 1) * WIN + jnp.arange(WIN, dtype=jnp.int32)
    ends = jnp.cumsum(lengths)
    begun = jnp.max(jnp.where(place[:, None] >= ends[None, :], ends[None, :], 0), axis=1)
    document = begun - (part - 1) * WIN + 2 * WIN
    window = jnp.where(lax.axis_index("ctx") > 0, WIN, 2 * WIN)
    low = jnp.where(part == 0, window, document).astype(jnp.int32)
    return low.reshape(1, WIN)


class Sums:
    def __init__(self, counts, rows, terms, out, refs, slack):
        self.counts, self.rows, self.out = counts, rows, out
        self.owns, self.nears, self.fars, self.lasts = zip(*terms)
        self.from_near, self.from_last = refs[:2]
        self.mine, self.from_y = self.from_near, out
        self.from_x, self.kept, self.from_z = refs[2:5]
        self.sems = refs[5:]
        self.parts = sum(counts)
        self.firsts = [sum(counts[:k]) for k in range(len(counts))]
        self.ctx, self.dp, mp = (lax.axis_index(axis) for axis in ("ctx", "dp", "mp"))
        self.half = rows // 2
        self.bits = [1 << k for k in range((lax.axis_size("dp") - 1).bit_length())]
        self.highs = [(self.dp // bit) % 2 for bit in self.bits]
        self.other_chip, self.other_window = {"mp": flip(mp, 2)}, {"ctx": 1 - self.ctx}
        self.other_core = {"mp": flip(mp, 1)}
        self.beside = [{"dp": flip(self.dp, bit)} for bit in self.bits]
        self.partners = [self.other_chip, self.other_window, self.other_core] + self.beside
        self.stages = [self.join, self.spread]
        self.stages += [functools.partial(self.narrow, k) for k in range(len(self.bits))]
        self.stages += [functools.partial(self.widen, k) for k in reversed(range(len(self.bits)))]
        self.lates = [k + slack[min(k, len(slack) - 1)] for k in range(len(self.stages))]
        self.steps = self.parts + self.lates[-1]

    @staticmethod
    def scratch(total, parts, bits, lanes):
        dma = pltpu.SemaphoreType.DMA
        return [
            pltpu.VMEM((total, lanes), BF16),
            pltpu.VMEM((total, lanes), BF16),
            pltpu.VMEM((total // 2, lanes), BF16),
            pltpu.VMEM((total // 2, lanes), BF16),
            pltpu.VMEM((total // 2, lanes), BF16),
            dma((parts,)), dma((parts,)),
            dma((parts,)), dma((parts,)),
            dma((parts, bits)), dma((parts, bits)),
            dma((parts, bits)), dma((parts, bits)),
            dma((parts,)), dma((parts,)),
            dma((parts, 2)), dma((parts, 2)),
        ]

    def segment(self, k, sent=False):
        start, size = 0, self.half
        for high in self.highs[:k]:
            size //= 2
            start = start + high * size
        if sent:
            size //= 2
            start = start + (1 - self.highs[k]) * size
        return start, size

    def to_core(self, array, i, which):
        place = self.firsts[array] + i
        source = (self.nears, self.lasts)[which][array].at[ds(i * self.rows, self.rows)]
        target = (self.from_near, self.from_last)[which].at[ds(place * self.rows, self.rows)]
        sent, received = (sem.at[place, which] for sem in self.sems[10:12])
        return remote(source, target, sent, received, self.other_core)

    def to_y(self, i):
        here = ds(i * self.rows, self.rows)
        source, target = self.from_last.at[here], self.from_y.at[here]
        return remote(source, target, self.sems[0].at[i], self.sems[1].at[i], self.other_chip)

    def to_x(self, i):
        source = self.mine.at[ds(i * self.rows + (1 - self.ctx) * self.half, self.half)]
        target = self.from_x.at[ds(i * self.half, self.half)]
        return remote(source, target, self.sems[2].at[i], self.sems[3].at[i], self.other_window)

    def to_z(self, i, k):
        start, size = self.segment(k, True)
        source = self.kept.at[ds(i * self.half + start, size)]
        target = self.from_z.at[ds(i * self.half + self.half - 2 * size, size)]
        return remote(source, target, self.sems[4].at[i, k], self.sems[5].at[i, k], self.beside[k])

    def back_z(self, i, k):
        start, size = self.segment(k + 1)
        here = self.out.at[ds(i * self.rows + self.ctx * self.half + start, size)]
        return remote(here, here, self.sems[6].at[i, k], self.sems[7].at[i, k], self.beside[k])

    def back_x(self, i):
        here = self.out.at[ds(i * self.rows + self.ctx * self.half, self.half)]
        return remote(here, here, self.sems[8].at[i], self.sems[9].at[i], self.other_window)

    def start(self):
        for array, count in enumerate(self.counts):

            def send(i, array=array):
                self.to_core(array, i, 1).start()
                self.to_core(array, i, 0).start()

            each(count, send)
        for array, count in enumerate(self.counts):

            def fold(i, array=array):
                place = self.firsts[array] + i
                self.to_core(array, i, 1).wait_recv()
                here = ds(place * self.rows, self.rows)
                term = self.fars[array][ds(i * self.rows, self.rows), :]
                total = term.astype(F32) + self.from_last[here, :].astype(F32)
                self.from_last[here, :] = total.astype(BF16)
                self.to_y(place).start()

            each(count, fold)

    def join(self, i):
        here = ds(i * self.rows, self.rows)
        self.to_y(i).wait_recv()
        for array, count in enumerate(self.counts):
            first = self.firsts[array]

            def add(array=array, first=first):
                self.to_core(array, i - first, 0).wait_recv()
                term = self.owns[array][ds((i - first) * self.rows, self.rows), :]
                total = term.astype(F32) + self.from_near[here, :].astype(F32)
                self.mine[here, :] = (total + self.from_y[here, :].astype(F32)).astype(BF16)

            pl.when((i >= first) & (i < first + count))(add)
        self.to_x(i).start()

    def spread(self, i):
        self.to_x(i).wait_recv()
        there = ds(i * self.half, self.half)
        term = self.mine[ds(i * self.rows + self.ctx * self.half, self.half), :]
        total = term.astype(F32) + self.from_x[there, :].astype(F32)
        self.kept[there, :] = total.astype(BF16)
        self.to_z(i, 0).start()

    def narrow(self, k, i):
        self.to_z(i, k).wait_recv()
        start, size = self.segment(k + 1)
        here = ds(i * self.half + start, size)
        there = ds(i * self.half + self.half - 2 * size, size)
        total = self.kept[here, :].astype(F32) + self.from_z[there, :].astype(F32)
        if k + 1 < len(self.bits):
            self.kept[here, :] = total.astype(BF16)
            self.to_z(i, k + 1).start()
        else:
            place = ds(i * self.rows + self.ctx * self.half + start, size)
            self.out[place, :] = total.astype(BF16)
            self.back_z(i, k).start()

    def widen(self, k, i):
        self.back_z(i, k).wait_recv()
        if k:
            self.back_z(i, k - 1).start()
        else:
            self.back_x(i).start()

    def step(self, i):
        for late, stage in zip(self.lates, self.stages, strict=True):
            pl.when((i >= late) & (i < self.parts + late))(functools.partial(stage, i - late))

    def finish(self):
        for array, count in enumerate(self.counts):

            def sent(i, array=array):
                self.to_core(array, i, 0).wait_send()
                self.to_core(array, i, 1).wait_send()

            each(count, sent)

        def end(i):
            self.to_y(i).wait_send()
            self.to_x(i).wait_send()
            self.back_x(i).wait()
            for k in range(len(self.bits)):
                self.to_z(i, k).wait_send()
                self.back_z(i, k).wait_send()

        each(self.parts, end)


def ds(start, size):
    return pl.ds(pl.multiple_of(start, 16), size)


def each(count, step):
    lax.fori_loop(0, count, lambda i, _: (step(i), 0)[1], 0)


def sum_kernel(arrays, places, *refs):
    n_here, n_there = len(arrays.here), len(arrays.there)
    here, there, refs = refs[:n_here], refs[n_here : n_here + n_there], refs[n_here + n_there :]
    terms, out, vec = refs[: len(places)], refs[len(places)], refs[len(places) + 1]
    from_vec, v_out, v_in = refs[-3:]
    sums, copies = arrays.open(here, there, out, refs[len(places) + 2 : -3])
    meet(sums.partners)
    mp = lax.axis_index("mp")
    slots = (mp, flip(mp, 1), flip(mp, 2), 3 - mp)
    vec[...] = jnp.zeros_like(vec)
    for term, (row, distance) in zip(terms, places, strict=True):
        at = row if distance is None else row + slots[distance]
        vec[pl.ds(at, 1), : term.shape[0]] = term[...].reshape(1, term.shape[0])
    hops = [
        remote(vec, from_vec.at[hop], v_out.at[hop], v_in.at[hop], partner)
        for hop, partner in enumerate(sums.partners)
    ]
    hops[0].start()
    for own_copy in copies:
        own_copy.wait()
    sums.start()
    for i in range(max(sums.steps, len(hops))):
        sums.step(i)
        if i < len(hops):
            hops[i].wait()
            vec[...] = vec[...] + from_vec[i]
        if i + 1 < len(hops):
            hops[i + 1].start()
    sums.finish()


def rows_of_part():
    return max(128, 32 * lax.axis_size("dp"))


class Arrays:
    def __init__(self, arrays):
        self.rows, self.bits = rows_of_part(), (lax.axis_size("dp") - 1).bit_length()
        self.pieces = [(v[0] if isinstance(v, tuple) else v).shape[-2] for v in arrays]
        if self.rows > 512:
            quads = [v if isinstance(v, tuple) else by_distance(v) for v in arrays]
            arrays = [tuple(jnp.concatenate(part) for part in zip(*quads, strict=True))]
        self.stacked = [not isinstance(array, tuple) for array in arrays]
        first = [array if stacked else array[0] for array, stacked in zip(arrays, self.stacked)]
        self.sizes = [v.shape[-2] for v in first]
        self.counts = [-(-size // self.rows) for size in self.sizes]
        filled = [
            tuple(self.fill(v) for v in array) if isinstance(array, tuple) else self.fill(array)
            for array in arrays
        ]
        self.here = [v for array in filled if isinstance(array, tuple) for v in array[::2]]
        self.there = []
        for array in filled:
            self.there += array[1::2] if isinstance(array, tuple) else [array]
        total, lanes = sum(self.counts) * self.rows, first[0].shape[-1]
        self.shape = jax.ShapeDtypeStruct((total, lanes), BF16)
        self.scratch = []
        for count, stacked in zip(self.counts, self.stacked):
            if stacked:
                self.scratch.append(pltpu.VMEM((2, count * self.rows, lanes), BF16))
                self.scratch.append(pltpu.SemaphoreType.DMA((2,)))
        self.scratch += Sums.scratch(total, sum(self.counts), self.bits, lanes)

    def fill(self, value):
        missing = -value.shape[-2] % self.rows
        return jnp.pad(value, [(0, 0)] * (value.ndim - 2) + [(0, missing), (0, 0)])

    def split(self, stack):
        shares, at = [], 0
        merged = len(self.pieces) > len(self.sizes)
        for k, size in enumerate(self.pieces):
            shares.append(stack[at : at + size])
            at += size if merged else self.counts[k] * self.rows
        return shares

    def open(self, here, there, out, refs, slack=(0,)):
        here, there, refs = list(here), list(there), list(refs)
        mp = lax.axis_index("mp")
        terms, copies = [], []
        for stacked in self.stacked:
            if not stacked:
                own, far = here.pop(0), here.pop(0)
                terms.append((own, there.pop(0), far, there.pop(0)))
                continue
            stack, place, sems = there.pop(0), refs.pop(0), refs.pop(0)
            for k, slot in enumerate((mp, flip(mp, 2))):
                copies.append(pltpu.make_async_copy(stack.at[slot], place.at[k], sems.at[k]))
                copies[-1].start()
            terms.append((place.at[0], stack.at[flip(mp, 1)], place.at[1], stack.at[3 - mp]))
        return Sums(self.counts, self.rows, terms, out, refs, slack), copies


def sum_replicas(arrays, vectors):
    arrays = Arrays(arrays)
    place = pl.BlockSpec(memory_space=pltpu.VMEM)
    away = pl.BlockSpec(memory_space=pl.ANY)
    dma = pltpu.SemaphoreType.DMA
    hops = 3 + arrays.bits
    stack, summed = pl.pallas_call(
        functools.partial(sum_kernel, arrays, [v[1:] for v in vectors]),
        out_shape=[arrays.shape, jax.ShapeDtypeStruct((len(vectors), D), F32)],
        in_specs=[place] * len(arrays.here)
        + [away] * len(arrays.there)
        + [place] * len(vectors),
        out_specs=[place, place],
        scratch_shapes=arrays.scratch
        + [pltpu.VMEM((hops, len(vectors), D), F32), dma((hops,)), dma((hops,))],
        compiler_params=pltpu.CompilerParams(
            collective_id=0, has_side_effects=True, vmem_limit_bytes=(32 if arrays.bits > 4 else 16) * 1024 * 1024
        ),
        name="sum_replicas",
    )(*arrays.here, *arrays.there, *(v[0] for v in vectors))
    return arrays.split(stack), summed


def back_kernel(mixed, arrays, *refs):
    refs = list(refs)

    def take(count):
        taken = refs[:count]
        del refs[:count]
        return taken

    places, flags, lo_ref = take(3)
    here, there, away = take(len(arrays.here)), take(len(arrays.there)), take(9)
    (dcols,) = take(1)
    if mixed:
        dv_ref, dv_before, dv_earlier = take(3)
    (out,) = take(1)
    if not mixed:
        dv_ref, dv_before, dv_earlier = take(3)
    dk_ref, dk_before, dk_earlier = take(3)
    near_k, near_v, far_k, far_v, home_k, home_v = take(6)
    values, acc_k, acc_v, acc_q = take(4)
    kv_out, kv_in = take(2)
    fetched, loaded = take(9), take(1)[0]
    loads = [
        pltpu.make_async_copy(source, target, loaded.at[k])
        for k, (source, target) in enumerate(zip(away, fetched, strict=True))
    ]
    for load in loads:
        load.start()
    cols, before, earlier, *others, exact, grad_ref, sum_ref = fetched
    first_values, given = (others, ()) if mixed else ((), others)
    slack = (0, 1, 1, 1, 1, 2) if mixed else (0, 2)
    sums, copies = arrays.open(here, there, out, refs, slack)

    ctx, mp = lax.axis_index("ctx"), lax.axis_index("mp")
    sees_one = (mp >= 2) | ((mp == 0) & (ctx == 1))
    sees_two = mp == 3
    meet(sums.partners + [{"mp": 3 - mp}])
    for copy in copies:
        copy.wait()
    sums.start()
    keys = ((earlier, 0), (before, 0), (cols, BAND))

    def home(which, source, target, g, device):
        return remote(
            source.at[g], target.at[g], kv_out.at[which, g], kv_in.at[which, g], device
        )

    def pair(g, act, step):
        act(step)
        if mixed:
            pl.when(g >= 2)(lambda: act(step + 1))
        else:
            act(step + 1)

    def from_last(g, step):
        source, target = (
            (dk_before, near_k), (dv_before, near_v), (dk_earlier, far_k), (dv_earlier, far_v),
        )[step]
        return home(step, source, target, g, {"mp": 2})

    def from_next(g, step, device):
        source, target = ((dk_before, home_k), (dv_before, home_v))[step]
        return home(4 + step, source, target, g, device)

    def group(g, _):
        place_values(mixed, g, places, first_values, keys, values)
        acc_k[...] = jnp.zeros_like(acc_k)
        if mixed:
            acc_v[...] = jnp.zeros_like(acc_v)
        else:
            for part in range(3):
                for j in range(GROUP):
                    head = GROUP * g + j
                    term = given[part][places[head]].astype(F32) * flags[head]
                    for side in range(2):
                        acc_v[2 * part + side, j * HD : (j + 1) * HD, :] = term[
                            :, side * TILE : (side + 1) * TILE
                        ]
        for t in range(WIN // TILE):
            tokens = slice(t * TILE, (t + 1) * TILE)
            low = lo_ref[:, tokens]
            place = 2 * WIN + t * TILE + lax.broadcasted_iota(jnp.int32, (1, TILE), 1)
            last = 2 * WIN // TILE + t

            def tile(kt, tokens=tokens, low=low, place=place, last=last):
                spot = kt * TILE + lax.broadcasted_iota(jnp.int32, (TILE, TILE), 0)
                keep = spot >= low
                if kt == last:
                    keep = keep & (spot <= place)
                span = slice(kt % 2 * TILE, (kt % 2 + 1) * TILE)
                key_ref, at = keys[kt // 2]
                for j in range(GROUP):
                    rows_j = slice(j * HD, (j + 1) * HD)
                    key = key_ref[g, at + j * HD : at + (j + 1) * HD, span]
                    query = cols[g, rows_j, tokens] * SCALE
                    grad = grad_ref[g, rows_j, tokens]
                    inner = jnp.sum(
                        grad.astype(F32) * exact[g, rows_j, tokens], axis=0, keepdims=True
                    )
                    raw = jnp.where(keep, dot(key, query, 0, 0), -jnp.inf)
                    weights = jnp.exp(raw - sum_ref[g, j : j + 1, tokens])
                    grad_weights = dot(values[kt // 2, rows_j, span], grad, 0, 0)
                    low_grad = (weights * (grad_weights - inner)).astype(BF16)
                    acc_v[kt, rows_j, :] += dot(grad, weights.astype(BF16), 1, 1)
                    acc_k[kt, rows_j, :] += dot(query, low_grad, 1, 1)
                    result = dot(key, low_grad, 1, 0)
                    acc_q[j] = result if kt == last else result + acc_q[j]

            for kt in reversed(range(last + 1)):
                if kt >= 4:
                    tile(kt)
                else:
                    pl.when(sees_one if kt >= 2 else sees_two)(functools.partial(tile, kt))
            for j in range(GROUP):
                dcols[g, j * HD : (j + 1) * HD, tokens] = (acc_q[j] * SCALE).astype(BF16)
            sums.step(2 * g + t)
        results = ((dk_earlier, dv_earlier), (dk_before, dv_before), (dk_ref, dv_ref))
        for part, (dk, dv) in enumerate(results):
            for side in range(2):
                span = slice(side * TILE, (side + 1) * TILE)
                dk[g, :, span] = acc_k[2 * part + side].astype(dk.dtype)
                dv[g, :, span] = acc_v[2 * part + side].astype(dv.dtype)

        def send_last():
            pair(g, lambda step: from_last(g, step).start(), 0)
            pair(g, lambda step: from_last(g, step).start(), 2)

        pl.when(mp == 3)(send_last)
        pl.when((mp == 0) & (ctx == 1))(
            lambda: pair(g, lambda step: from_next(g, step, sums.other_window).start(), 0)
        )
        return 0

    for load in loads:
        load.wait()
    lax.fori_loop(0, 4, group, 0)

    def relay(g):
        def one(step):
            near, far, source, total = (
                (near_k, far_k, dk_before, dk_ref), (near_v, far_v, dv_before, dv_ref),
            )[step]
            from_last(g, step).wait_recv()
            from_last(g, step + 2).wait_recv()
            source[g] = (source[g].astype(F32) + far[g].astype(F32)).astype(BF16)
            from_next(g, step, {"mp": 1}).start()
            total[g] += near[g].astype(F32)

        pair(g, one, 0)

    pl.when(mp == 2)(lambda: each(4, relay))
    for i in range(8, sums.steps):
        sums.step(i)

    def arrive(g):
        def one(step):
            arrived, total = ((home_k, dk_ref), (home_v, dv_ref))[step]
            from_next(g, step, sums.other_window).wait_recv()
            total[g] += arrived[g].astype(F32)

        pair(g, one, 0)

    pl.when((mp == 1) | ((mp == 0) & (ctx == 0)))(lambda: each(4, arrive))

    def round_off(g):
        dcols[g, BAND : 2 * BAND, :] = dk_ref[g].astype(BF16)
        if not mixed:
            dcols[g, 2 * BAND : 3 * BAND, :] = dv_ref[g].astype(BF16)

    each(4, round_off)
    wide = BAND // 2 if mixed else BAND
    for slot in range(4):
        if mixed:
            half = slice(slot % 2 * wide, (slot % 2 + 1) * wide)
            dcols[slot, 2 * BAND : 2 * BAND + wide, :] = dv_ref[2 + slot // 2, half, :].astype(BF16)
        rest = dcols.shape[1] - 2 * BAND - wide
        dcols[slot, 2 * BAND + wide :, :] = jnp.zeros((rest, WIN), BF16)

    def sent_last(g):
        pair(g, lambda step: from_last(g, step).wait_send(), 0)
        pair(g, lambda step: from_last(g, step).wait_send(), 2)

    def sent_next(device):
        each(4, lambda g: pair(g, lambda step: from_next(g, step, device).wait_send(), 0))

    pl.when(mp == 3)(lambda: each(4, sent_last))
    pl.when(mp == 2)(lambda: sent_next({"mp": 1}))
    pl.when((mp == 0) & (ctx == 1))(lambda: sent_next(sums.other_window))
    sums.finish()


def attend_back(places, flags, low, front, firsts, given, exact, grad_heads, lse, arrays):
    mixed = bool(firsts)
    arrays = Arrays(arrays)
    place = pl.BlockSpec(memory_space=pltpu.VMEM)
    away = pl.BlockSpec(memory_space=pl.ANY)
    scalar = pl.BlockSpec(memory_space=pltpu.SMEM)
    dma = pltpu.SemaphoreType.DMA
    by_head = [v.reshape(-1, HD, WIN) for v in firsts[::-1] + given[::-1]]
    fetched = [*front, *by_head, exact, grad_heads, lse]
    wide = jax.ShapeDtypeStruct((4, BAND, WIN), F32)
    slim = jax.ShapeDtypeStruct((4, BAND, WIN), BF16)
    n_cols = -(-(5 * BAND // 2 if mixed else 3 * BAND) // 128) * 128
    outs = [jax.ShapeDtypeStruct((4, n_cols, WIN), BF16)]
    outs += ([wide, slim, slim] if mixed else []) + [arrays.shape]
    block, full = pltpu.VMEM((4, BAND, WIN), BF16), pltpu.VMEM((4, BAND, WIN), F32)
    results = pl.pallas_call(
        functools.partial(back_kernel, mixed, arrays),
        out_shape=outs,
        in_specs=[scalar, scalar, place]
        + [place] * len(arrays.here)
        + [away] * (len(arrays.there) + len(fetched)),
        out_specs=[place] * len(outs),
        scratch_shapes=([] if mixed else [full, block, block])
        + [full]
        + [block] * 8
        + [
            pltpu.VMEM((3, BAND, WIN), BF16),
            pltpu.VMEM((TILES, BAND, TILE), F32),
            pltpu.VMEM((TILES, BAND, TILE), F32),
            pltpu.VMEM((GROUP, HD, TILE), F32),
            dma((6, 4)),
            dma((6, 4)),
        ]
        + [pltpu.VMEM(v.shape, v.dtype) for v in fetched]
        + [dma((len(fetched),))]
        + arrays.scratch,
        compiler_params=pltpu.CompilerParams(
            collective_id=3 if mixed else 4,
            has_side_effects=True,
            vmem_limit_bytes=(60 if arrays.bits > 4 else 38 if mixed else 43) * 1024 * 1024,
        ),
        name="attend_back",
    )(places, flags, low, *arrays.here, *arrays.there, *fetched)
    return results[:-1], arrays.split(results[-1])


def gelu(hidden):
    return jax.nn.gelu(hidden, approximate=True)


def tail_forward(stream, heads, out_weight, out_bias, gain, shift, ups, up_biases, downs):
    stream = stream + dot(heads, out_weight, 0, 0) + out_bias[0]
    normed, unit, scale = norm_rows(stream, gain[1], shift[1])
    hidden, active, total = [], [], out_bias[1]
    for up, bias, down in zip(ups, up_biases, downs, strict=True):
        hidden.append(dot(normed, up, 1, 0) + bias)
        active.append(gelu(hidden[-1]).astype(BF16))
        total = total + dot(active[-1], down, 1, 0)
    return stream + total, (normed, unit, scale, hidden, active)


def tail_backward(grad, kept, out_weight, gain, ups, downs):
    normed, unit, scale, hidden, active = kept
    bias_mlp = jnp.sum(grad, axis=0)
    rounded = grad.astype(BF16)
    mats, up_biases, normed_grad = [], [], 0.0
    for up, down, before, after in zip(ups, downs, hidden, active, strict=True):
        _, pull = jax.vjp(gelu, before)
        grad_hidden = pull(dot(rounded, down, 1, 1))[0]
        up_biases.append(jnp.sum(grad_hidden, axis=0))
        low = grad_hidden.astype(BF16)
        mats.append((dot(normed, low, 0, 0).astype(BF16), dot(after, rounded, 0, 0).astype(BF16)))
        normed_grad = normed_grad + dot(low, up, 1, 1)
    middle, gain_grad, shift_grad = norm_back(normed_grad, unit, scale, gain[1])
    grad = grad + middle
    bias_attn = jnp.sum(grad, axis=0)
    rounded = grad.astype(BF16)
    grad_heads = dot(out_weight, rounded, 1, 1).astype(BF16)
    return grad, rounded, grad_heads, mats, up_biases, (gain_grad, shift_grad, bias_attn, bias_mlp)


def turned(weight):
    return jnp.swapaxes(weight, -1, -2)


def shards(
    block_input, cotangent, doc_lengths, reuse_heads,
    norm_gain1, norm_bias1, projections1, front_bias1, out_weight1, out_bias1,
    up_weight1, up_bias1, down_weight1,
    norm_gain2, norm_bias2, query_key2, query_bias2, fresh_value2, value_bias2,
    out_weight2, out_bias2, up_weight2, up_bias2, down_weight2,
):
    low = row_starts(doc_lengths[0])
    taken = jnp.arange(4 * GROUP, dtype=jnp.int32)[:, None] == reuse_heads[None, :]
    taker = jnp.sum(jnp.where(taken, jnp.arange(REUSE, dtype=jnp.int32)[None, :], 0), axis=1)
    flags = jnp.any(taken, axis=1).astype(F32)
    band_of, in_band = reuse_heads // GROUP, reuse_heads % GROUP
    places2 = jnp.concatenate(
        [band_of * 3 * GROUP + 2 * GROUP + in_band, band_of * 2 * GROUP + GROUP + in_band]
    )

    stream0 = block_input.astype(F32)
    normed1, unit1, scale1 = norm_rows(stream0, norm_gain1[0], norm_bias1[0])
    n_front1, n_front2 = 3 * BAND, 2 * BAND + BAND // 2
    none = jnp.zeros((BAND,), BF16)

    def as_row(pieces):
        row = jnp.concatenate(pieces).astype(F32)
        return jnp.pad(row[None, :], ((0, 7), (0, -row.shape[0] % 128)))

    small = jnp.concatenate([query_bias2, value_bias2, up_bias1, up_bias2])
    small = jnp.pad(small, (0, 16 * 128 - small.shape[0])).reshape(16, 128)
    own_front2 = jnp.concatenate([turned(query_key2).reshape(2 * BAND, D), turned(fresh_value2)])
    own_front2 = jnp.pad(own_front2, ((0, -n_front2 % 64), (0, 0)))
    (
        cols1, before1, earlier1, heads1, exact1, sums1, _, small, front1,
        up1, down1, front2, outs1,
    ) = project(
        places2, low, normed1, turned(projections1).reshape(n_front1, D),
        as_row([front_bias1[0], none, front_bias1[1]]), n_front1, 2 * BAND, (), small,
        (up_weight1, down_weight1, own_front2, out_weight1),
    )
    me = lax.axis_index("mp")
    ups1, downs1 = ([up_weight1] + by_distance(up1)[1:], [down_weight1] + by_distance(down1)[1:])
    front2 = lax.dynamic_update_index_in_dim(front2, own_front2, me, 0)
    outs1 = lax.dynamic_update_index_in_dim(outs1, out_weight1, me, 0).reshape(D, D)
    small = small.reshape(4, -1)
    at = BAND + BAND // 2
    bias2 = jnp.stack([as_row([small[s, :BAND], none, small[s, BAND:at]]) for s in range(4)])
    up_biases1 = by_distance(small[:, at : at + D])
    up_biases2 = by_distance(small[:, at + D : at + 2 * D])

    front_kv1 = (cols1, before1, earlier1)
    stream1, kept1 = tail_forward(
        stream0, heads1.reshape(D, WIN), outs1, out_bias1, norm_gain1, norm_bias1,
        ups1, up_biases1, downs1,
    )

    normed2, unit2, scale2 = norm_rows(stream1, norm_gain2[0], norm_bias2[0])
    front_kv1 = (cols1, before1, earlier1)
    cols2, before2, earlier2, heads2, exact2, sums2, up2, down2, outs2 = project(
        places2, low, normed2, front2, bias2, n_front2, n_front2 - BAND, front_kv1, None,
        (up_weight2, down_weight2, out_weight2),
    )
    ups2, downs2 = ([up_weight2] + by_distance(up2)[1:], [down_weight2] + by_distance(down2)[1:])
    outs2 = lax.dynamic_update_index_in_dim(outs2, out_weight2, me, 0).reshape(D, D)

    front_kv2 = (cols2, before2, earlier2)
    stream2, kept2 = tail_forward(
        stream1, heads2.reshape(D, WIN), outs2, out_bias2, norm_gain2, norm_bias2,
        ups2, up_biases2, downs2,
    )
    block_output = stream2.astype(BF16)

    grad, rounded, grad_heads, mats2, up_grads2, small2 = tail_backward(
        cotangent.astype(F32), kept2, outs2, norm_gain2, ups2, downs2
    )
    (dcols2, dv2, dv2_before, dv2_earlier), mats2 = attend_back(
        places2, flags, low, front_kv2, front_kv1, (), exact2,
        grad_heads.reshape(4, BAND, WIN), sums2, list(zip(*mats2, strict=True)),
    )
    grad_out2 = dot(heads2.reshape(D, WIN), rounded, 1, 0).astype(BF16).reshape(4, BAND, D)
    bias_grad2 = jnp.sum(dcols2.astype(F32), axis=2)
    grad_front2 = dot(dcols2.reshape(-1, WIN), normed2, 1, 0).astype(BF16).reshape(4, -1, D)
    normed_grad = dot(dcols2.reshape(-1, WIN), front2.reshape(-1, D), 0, 0)
    middle, gain_front2, shift_front2 = norm_back(normed_grad, unit2, scale2, norm_gain2[0])
    grad = grad + middle

    grad, rounded, grad_heads, mats1, up_grads1, small1 = tail_backward(
        grad, kept1, outs1, norm_gain1, ups1, downs1
    )
    grad_out1 = dot(heads1.reshape(D, WIN), rounded, 1, 0).astype(BF16).reshape(4, BAND, D)
    arrays = [grad_front2]
    (dcols1,), (front_sum2, *mats1) = attend_back(
        taker, flags, low, front_kv1, (), (dv2, dv2_before, dv2_earlier), exact1,
        grad_heads.reshape(4, BAND, WIN), sums1, arrays + list(zip(*mats1, strict=True)),
    )
    bias_grad1 = jnp.sum(dcols1.astype(F32), axis=2)
    grad_front1 = dot(dcols1.reshape(-1, WIN), normed1, 1, 0).astype(BF16).reshape(4, -1, D)
    normed_grad = dot(dcols1.reshape(-1, WIN), front1.reshape(-1, D), 0, 0)
    middle, gain_front1, shift_front1 = norm_back(normed_grad, unit1, scale1, norm_gain1[0])
    input_grad = (grad + middle).astype(BF16)

    singles = [
        gain_front1, small1[0], shift_front1, small1[1], small1[2], small1[3],
        gain_front2, small2[0], shift_front2, small2[1], small2[2], small2[3],
        bias_grad1[:, :BAND].reshape(-1), bias_grad1[:, 2 * BAND : n_front1].reshape(-1),
        bias_grad2[:, :BAND].reshape(-1), bias_grad2[:, 2 * BAND : n_front2].reshape(-1),
    ]
    vectors = [(vector, row, None) for row, vector in enumerate(singles)]
    for row, shares in ((16, up_grads1), (20, up_grads2)):
        vectors += [(vector, row, distance) for distance, vector in enumerate(shares)]
    grad_outs = jnp.concatenate([grad_out2, grad_out1], axis=1)
    (out_sums, front_sum1), sums = sum_replicas([grad_outs, grad_front1], vectors)

    def mine(vectors):
        return lax.dynamic_index_in_dim(vectors.reshape(4, -1), me, 0, keepdims=False)

    return (
        block_output,
        input_grad,
        sums[0:2],
        sums[2:4],
        turned(front_sum1[:n_front1].reshape(3, BAND, D)).astype(F32),
        jnp.stack([mine(sums[12]), mine(sums[13])]),
        out_sums[BAND:].astype(F32),
        sums[4:6],
        mats1[0].astype(F32),
        mine(sums[16:20]),
        mats1[1].astype(F32),
        sums[6:8],
        sums[8:10],
        turned(front_sum2[: 2 * BAND].reshape(2, BAND, D)).astype(F32),
        mine(sums[14]),
        turned(front_sum2[2 * BAND : n_front2]).astype(F32),
        mine(sums[15, : D // 2]),
        out_sums[:BAND].astype(F32),
        sums[10:12],
        mats2[0].astype(F32),
        mine(sums[20:24]),
        mats2[1].astype(F32),
    )


def solution(mesh):
    rows = P(("dp", "ctx", "mp"), None)
    placed = (
        rows, rows, P(("dp", "ctx"), None), P(),
        P(), P(), P(None, None, "mp"), P(None, "mp"), P("mp", None), P(),
        P(None, "mp"), P("mp"), P("mp", None),
        P(), P(), P(None, None, "mp"), P("mp"), P(None, "mp"), P("mp"),
        P("mp", None), P(), P(None, "mp"), P("mp"), P("mp", None),
    )
    given = (
        rows, rows,
        P(), P(), P(None, None, "mp"), P(None, "mp"), P("mp", None), P(),
        P(None, "mp"), P("mp"), P("mp", None),
        P(), P(), P(None, None, "mp"), P("mp"), P(None, "mp"), P("mp"),
        P("mp", None), P(), P(None, "mp"), P("mp"), P("mp", None),
    )
    return jax.shard_map(shards, mesh=mesh, in_specs=placed, out_specs=given, check_vma=False)
```

```python
import functools

import jax
import jax.numpy as jnp
from jax import lax
from jax.experimental import pallas as pl
from jax.experimental.pallas import tpu as pltpu
from jax.sharding import PartitionSpec as P

D = 768
HD = 64
REUSE = 6
WIN = 512
EARLY = 5
CHUNK = 256
LEAD = 3
LAG_FIRST, LAG_SECOND = 3, 2
HOOK_FIRST, HOOK_SECOND = -2, 0
GROUP = 3
BAND = GROUP * HD
TILE = 256
TILES = 3 * WIN // TILE
EPS = 1e-05
SCALE = HD**-0.5
F32 = jnp.float32
BF16 = jnp.bfloat16


def swap(value, axis, bit):
    devices = range(lax.axis_size(axis))
    return lax.ppermute(value, axis, [(i, i ^ bit) for i in devices])


def in_order(parts):
    return jnp.concatenate(by_distance(jnp.stack(parts)))


def by_distance(stacked):
    me = lax.axis_index("mp")
    return [
        lax.dynamic_index_in_dim(stacked, me ^ distance, 0, keepdims=False)
        for distance in range(4)
    ]


def flip(position, bit):
    return position + bit * (1 - 2 * ((position // bit) % 2))


def remote(source, target, sent, received, device):
    return pltpu.make_async_remote_copy(
        src_ref=source, dst_ref=target, send_sem=sent, recv_sem=received,
        device_id=device, device_id_type=pl.DeviceIdType.MESH,
    )


def meet(devices):
    barrier = pltpu.get_barrier_semaphore()
    for device in devices:
        pl.semaphore_signal(barrier, inc=1, device_id=device, device_id_type=pl.DeviceIdType.MESH)
    pl.semaphore_wait(barrier, len(devices))


def dot(left, right, left_dim, right_dim):
    return lax.dot_general(
        left, right, (((left_dim,), (right_dim,)), ((), ())), preferred_element_type=F32
    )


def norm_rows(value, gain, shift):
    mean = jnp.mean(value, axis=-1, keepdims=True)
    centred = value - mean
    spread = jnp.mean(centred * centred, axis=-1, keepdims=True)
    scale = lax.rsqrt(spread + EPS)
    unit = centred * scale
    return (unit * gain + shift).astype(BF16), unit, scale


def norm_back(grad, unit, scale, gain):
    scaled = grad * gain
    inner = (
        scaled
        - jnp.mean(scaled, axis=-1, keepdims=True)
        - unit * jnp.mean(scaled * unit, axis=-1, keepdims=True)
    )
    return scale * inner, jnp.sum(grad * unit, axis=0), jnp.sum(grad, axis=0)


def front_kernel(more_rows, lead, mixed, *refs):
    refs = list(refs)

    def take(count):
        taken = refs[:count]
        del refs[:count]
        return taken

    ctx, dp, mp = (lax.axis_index(axis) for axis in ("ctx", "dp", "mp"))
    near, far, last = {"mp": flip(mp, 1)}, {"mp": flip(mp, 2)}, {"mp": 3 - mp}
    window = {"ctx": 1 - ctx}
    chunks = chunks_of(lead, more_rows)
    n_chunks, n_more, n_lead = len(chunks), len(more_rows), LEAD * lead
    n_arrays = n_more + lead
    early, offset = (EARLY, HOOK_FIRST) if lead else (4, HOOK_SECOND)
    lag = LAG_FIRST if lead else LAG_SECOND
    places, lo_ref, normed = take(3)
    first_values = take(3) if mixed else ()
    front, bias = (None, None) if lead else take(2)
    vectors_own = take(2 * lead)
    arrays_own = take(n_arrays)
    cols, before, earlier, out_ref, exact_ref, sum_ref = take(6)
    vectors = take(2 * lead)
    arrays = take(n_arrays)
    if lead:
        front, bias = arrays[0], vectors[0]
    values, raw, top, total, acc, kv_out, kv_in, on_out, on_in = take(9)
    m_out, m_in = take(2)
    if lead:
        f_out, f_in = take(2)
    meet([near, far, last, window, {"dp": flip(dp, 1)}])
    directions = (near, far, last)
    if True:

        def whole(k, way):
            return remote(
                vectors_own[k], vectors[k].at[mp], f_out.at[k, way], f_in.at[k, way],
                directions[way],
            )

        bit = lax.rem(dp, 2)
        first = [(bit, {"dp": flip(dp, 1)}), (ctx, window)]

        def quarters(c):
            a, start, rows = chunks[c]
            (low, low_device), (high, high_device) = first if c % 2 else first[::-1]
            return a, start, rows // 4, rows // 2, low, low_device, high, high_device

        def copy(c, way, source, target, device):
            return remote(source, target, m_out.at[c, way], m_in.at[c, way], device)

        def beside(c):
            a, start, rows = chunks[c]
            here = pl.ds(start, rows)
            return copy(c, 0, arrays_own[a].at[here], arrays[a].at[mp, here], near)

        def across(c):
            a, start, quarter, half, low, _, high, _ = quarters(c)
            here = ds(start + high * half + low * quarter, quarter)
            return copy(c, 1, arrays_own[a].at[here], arrays[a].at[mp, here], far)

        def widen(c):
            a, start, quarter, half, low, device, high, _ = quarters(c)
            there = arrays[a].at[flip(mp, 2), ds(start + high * half + low * quarter, quarter)]
            return copy(c, 2, there, there, device)

        def complete(c):
            a, start, _, half, _, _, high, device = quarters(c)
            there = arrays[a].at[flip(mp, 2), ds(start + high * half, half)]
            return copy(c, 3, there, there, device)

        def hand_on(c):
            a, start, rows = chunks[c]
            there = arrays[a].at[flip(mp, 2), pl.ds(start, rows)]
            return copy(c, 4, there, there, near)

        for c in range(n_lead):
            across(c).start()
            beside(c).start()
        for k in range(2 * lead):
            for way in range(3):
                whole(k, way).start()
        for c in range(n_lead, early):
            across(c).start()
        for c in range(n_lead, n_chunks):
            beside(c).start()
        if lead:
            n_front = arrays_own[0].shape[0]
            arrays[0][mp, :n_front] = arrays_own[0][...]
            arrays[0][:, n_front:] = jnp.zeros((4, arrays[0].shape[1] - n_front, D), BF16)
        for k in range(2 * lead):
            vectors[k][mp] = vectors_own[k][...]

    def gather(step):
        for late, stage in enumerate(
            ((across, widen), (widen, complete), (complete, hand_on))
        ):
            a = step + n_lead - lag * late
            if n_lead <= a < n_chunks:
                stage[0](a).wait_recv()
                stage[1](a).start()

    kv_rows = before.shape[1]
    from_row = cols.shape[1] - kv_rows
    sends_on = (mp == 1) | (mp == 2)
    sends_window = (mp == 0) & (ctx == 0)
    receives = (mp >= 2) | ((mp == 0) & (ctx == 1))

    def pass_on(slot, device):
        source = cols.at[slot, pl.ds(from_row, kv_rows)]
        return remote(source, before.at[slot], kv_out.at[slot], kv_in.at[slot], device)

    def pass_again(slot):
        return remote(before.at[slot], earlier.at[slot], on_out.at[slot], on_in.at[slot], {"mp": 3})

    order = (mp, flip(mp, 1), flip(mp, 2), 3 - mp) if lead else range(4)
    for k, slot in enumerate(order):
        if lead and k == 1:
            for vector in range(2):
                for way in range(3):
                    whole(vector, way).wait_recv()
            for c in range(n_lead):
                across(c).wait_recv()
                widen(c).start()
            for c in range(n_lead):
                beside(c).wait_recv()
        if lead and k == 2:
            for c in range(n_lead):
                widen(c).wait_recv()
                complete(c).start()
            for c in range(n_lead):
                complete(c).wait_recv()
                hand_on(c).start()
        if lead and k == 3:
            for c in range(n_lead):
                hand_on(c).wait_recv()
        column = jnp.transpose(bias[slot])[: cols.shape[1], 0:1]
        cols[slot] = (dot(front[slot, : cols.shape[1]], normed[...], 1, 1) + column).astype(BF16)
        pl.when(sends_on)(lambda: pass_on(slot, {"mp": mp + 1}).start())
        pl.when(sends_window)(lambda: pass_on(slot, window).start())
    for c in range(early, n_chunks):
        across(c).start()
    steps = n_chunks - n_lead + 2 * lag
    for step in range(steps):
        if step + offset < 0:
            gather(step)

    def arrive(slot):
        def from_next():
            pass_on(slot, window).wait_recv()
            pl.when(mp == 2)(lambda: pass_again(slot).start())
            pl.when(mp == 3)(lambda: pass_again(slot).wait_recv())

        pl.when(receives)(from_next)

    keys = ((earlier, 0), (before, 0), (cols, BAND))
    sees_one, sees_two = receives, mp == 3
    sender = lax.max(mp - 1, 0)

    def group(k, _):
        if mixed:
            g = k
            pl.when(k < 2)(lambda: arrive(k))

            def rest():
                arrive(2)
                arrive(3)

            pl.when(k == 2)(rest)
        else:
            g = (sender % 2 + k) % 2 + 2 * ((sender // 2 + k // 2) % 2)
            arrive(g)
        place_values(mixed, g, places, first_values, keys, values)
        for t in range(WIN // TILE):
            tokens = slice(t * TILE, (t + 1) * TILE)
            low = lo_ref[:, tokens]
            place = 2 * WIN + t * TILE + lax.broadcasted_iota(jnp.int32, (1, TILE), 1)
            end = 2 * WIN // TILE + t

            def score(kt, tokens=tokens, low=low, place=place, end=end):
                spot = kt * TILE + lax.broadcasted_iota(jnp.int32, (TILE, TILE), 0)
                keep = spot >= low
                if kt == end:
                    keep = keep & (spot <= place)
                span = slice(kt % 2 * TILE, (kt % 2 + 1) * TILE)
                key_ref, at = keys[kt // 2]
                for j in range(GROUP):
                    rows = slice(j * HD, (j + 1) * HD)
                    key = key_ref[g, at + j * HD : at + (j + 1) * HD, span]
                    found = dot(key, cols[g, rows, tokens] * SCALE, 0, 0)
                    found = jnp.where(keep, found, -jnp.inf)
                    raw[j, kt] = found
                    peak = jnp.max(found.reshape(TILE // 8, 8, TILE), axis=0)
                    top[j] = peak if kt == end else jnp.maximum(top[j], peak)

            def weigh(kt, end=end):
                span = slice(kt % 2 * TILE, (kt % 2 + 1) * TILE)
                for j in range(GROUP):
                    rows = slice(j * HD, (j + 1) * HD)
                    powers = jnp.exp(raw[j, kt] - top[j, 0:1])
                    added = jnp.sum(powers.reshape(TILE // 8, 8, TILE), axis=0)
                    result = dot(values[kt // 2, rows, span], powers.astype(BF16), 1, 0)
                    total[j] = added if kt == end else total[j] + added
                    acc[j] = result if kt == end else acc[j] + result

            for stage in (score, weigh):
                for kt in reversed(range(end + 1)):
                    if kt >= 4:
                        stage(kt)
                    else:
                        pl.when(sees_one if kt >= 2 else sees_two)(functools.partial(stage, kt))
                if stage is score:
                    for j in range(GROUP):
                        top[j] = jnp.broadcast_to(jnp.max(top[j], axis=0, keepdims=True), (8, TILE))
            for j in range(GROUP):
                rows = slice(j * HD, (j + 1) * HD)
                whole_sum = jnp.sum(total[j], axis=0, keepdims=True)
                result = acc[j] / whole_sum
                out_ref[g, rows, tokens] = result.astype(BF16)
                exact_ref[g, rows, tokens] = result
                sum_ref[g, j : j + 1, tokens] = top[j, 0:1] + jnp.log(whole_sum)
            for step in range(steps):
                if (step + offset) % 2 == t and 0 <= step + offset < 8:
                    pl.when(k == (step + offset) // 2)(functools.partial(gather, step))
        return 0

    lax.fori_loop(0, 4, group, 0)
    for step in range(steps):
        if step + offset >= 8:
            gather(step)

    def sent(device):
        each(4, lambda slot: pass_on(slot, device).wait_send())

    pl.when(sends_on)(lambda: sent({"mp": mp + 1}))
    pl.when(sends_window)(lambda: sent(window))
    pl.when(mp == 2)(lambda: each(4, lambda slot: pass_again(slot).wait_send()))
    for k in range(2 * lead):
        for way in range(3):
            whole(k, way).wait_send()
    for a in range(n_chunks):
        beside(a).wait_send()
        if a >= n_lead:
            beside(a).wait_recv()
            hand_on(a).wait_recv()
        across(a).wait_send()
        widen(a).wait_send()
        complete(a).wait_send()
        hand_on(a).wait_send()


def place_values(mixed, g, places, first_values, keys, values):
    if not mixed:
        for part, (ref, at) in enumerate(keys):
            values[part] = ref[g, at + BAND : at + 2 * BAND, :]
        return

    def reused():
        for part in range(3):
            for j in range(GROUP):
                at = places[(0 if part == 2 else REUSE) + GROUP * g + j]
                values[part, j * HD : (j + 1) * HD, :] = first_values[part][at]

    def own():
        wide = BAND // 2
        for part, (ref, at) in enumerate(keys):
            for side in range(2):
                values[part, side * wide : (side + 1) * wide, :] = ref[
                    2 * (g - 2) + side, at + BAND : at + BAND + wide, :
                ]

    pl.when(g < 2)(reused)
    pl.when(g >= 2)(own)


def chunks_of(lead, more_rows):
    chunks = [(0, k * BAND, BAND) for k in range(LEAD)] * lead
    for array, rows in enumerate(more_rows):
        size = CHUNK if rows % CHUNK == 0 else rows
        chunks += [(array + lead, start, size) for start in range(0, rows, size)]
    return chunks


def project(places, low, normed, front, bias, n_cols, kv_rows, firsts=(), small=None, more=()):
    place = pl.BlockSpec(memory_space=pltpu.VMEM)
    away = pl.BlockSpec(memory_space=pl.ANY)
    dma = pltpu.SemaphoreType.DMA
    given = [low, normed] + [v.reshape(-1, HD, WIN) for v in firsts[::-1]]
    lead = small is not None
    given += [bias, small, front] if lead else [front, bias]
    made = [(4, n_cols, WIN), (4, kv_rows, WIN), (4, kv_rows, WIN), (4, BAND, WIN)]
    made = [jax.ShapeDtypeStruct(shape, BF16) for shape in made]
    made += [jax.ShapeDtypeStruct((4, rows, WIN), F32) for rows in (BAND, 8)]
    scratch = [
        pltpu.VMEM((3, BAND, WIN), BF16),
        pltpu.VMEM((GROUP, TILES, TILE, TILE), F32),
        pltpu.VMEM((GROUP, 8, TILE), F32),
        pltpu.VMEM((GROUP, 8, TILE), F32),
        pltpu.VMEM((GROUP, HD, TILE), F32),
    ] + [dma((4,))] * 4
    gathered = ([bias, small, front] if lead else []) + list(more)
    gathered = [jax.ShapeDtypeStruct((4,) + v.shape, v.dtype) for v in gathered]
    if lead:
        gathered[2] = jax.ShapeDtypeStruct((4, -(-n_cols // 128) * 128, D), BF16)
    rows = [v.shape[0] for v in more]
    scratch += [dma((len(chunks_of(lead, rows)), 5))] * 2 + ([dma((2, 3))] * 2 if lead else [])
    return pl.pallas_call(
        functools.partial(front_kernel, rows, int(lead), bool(firsts)),
        out_shape=made + gathered,
        in_specs=[pl.BlockSpec(memory_space=pltpu.SMEM)]
        + [place] * len(given) + [away] * len(more),
        out_specs=[place] * (len(made) + 3 * lead) + [away] * len(more),
        scratch_shapes=scratch,
        compiler_params=pltpu.CompilerParams(
            collective_id=1 if lead else 2,
            has_side_effects=True,
            vmem_limit_bytes=(48 if lead else 28) * 1024 * 1024,
        ),
        name="front_first" if lead else "front_second",
    )(places, *given, *more)


def row_starts(lengths):
    part = lax.axis_index("mp")
    place = (part - 1) * WIN + jnp.arange(WIN, dtype=jnp.int32)
    ends = jnp.cumsum(lengths)
    begun = jnp.max(jnp.where(place[:, None] >= ends[None, :], ends[None, :], 0), axis=1)
    document = begun - (part - 1) * WIN + 2 * WIN
    window = jnp.where(lax.axis_index("ctx") > 0, WIN, 2 * WIN)
    low = jnp.where(part == 0, window, document).astype(jnp.int32)
    return low.reshape(1, WIN)


class Sums:
    def __init__(self, counts, rows, terms, out, refs, slack):
        self.counts, self.rows, self.out = counts, rows, out
        self.owns, self.nears, self.fars, self.lasts = zip(*terms)
        self.from_near, self.from_last = refs[:2]
        self.mine, self.from_y = self.from_near, out
        self.from_x, self.kept, self.from_z = refs[2:5]
        self.sems = refs[5:]
        self.parts = sum(counts)
        self.firsts = [sum(counts[:k]) for k in range(len(counts))]
        self.ctx, self.dp, mp = (lax.axis_index(axis) for axis in ("ctx", "dp", "mp"))
        self.half = rows // 2
        self.bits = [1 << k for k in range((lax.axis_size("dp") - 1).bit_length())]
        self.highs = [(self.dp // bit) % 2 for bit in self.bits]
        self.other_chip, self.other_window = {"mp": flip(mp, 2)}, {"ctx": 1 - self.ctx}
        self.other_core = {"mp": flip(mp, 1)}
        self.beside = [{"dp": flip(self.dp, bit)} for bit in self.bits]
        self.partners = [self.other_chip, self.other_window, self.other_core] + self.beside
        self.stages = [self.join, self.spread]
        self.stages += [functools.partial(self.narrow, k) for k in range(len(self.bits))]
        self.stages += [functools.partial(self.widen, k) for k in reversed(range(len(self.bits)))]
        self.lates = [k + slack[min(k, len(slack) - 1)] for k in range(len(self.stages))]
        self.steps = self.parts + self.lates[-1]

    @staticmethod
    def scratch(total, parts, bits, lanes):
        dma = pltpu.SemaphoreType.DMA
        return [
            pltpu.VMEM((total, lanes), BF16),
            pltpu.VMEM((total, lanes), BF16),
            pltpu.VMEM((total // 2, lanes), BF16),
            pltpu.VMEM((total // 2, lanes), BF16),
            pltpu.VMEM((total // 2, lanes), BF16),
            dma((parts,)), dma((parts,)),
            dma((parts,)), dma((parts,)),
            dma((parts, bits)), dma((parts, bits)),
            dma((parts, bits)), dma((parts, bits)),
            dma((parts,)), dma((parts,)),
            dma((parts, 2)), dma((parts, 2)),
        ]

    def segment(self, k, sent=False):
        start, size = 0, self.half
        for high in self.highs[:k]:
            size //= 2
            start = start + high * size
        if sent:
            size //= 2
            start = start + (1 - self.highs[k]) * size
        return start, size

    def to_core(self, array, i, which):
        place = self.firsts[array] + i
        source = (self.nears, self.lasts)[which][array].at[ds(i * self.rows, self.rows)]
        target = (self.from_near, self.from_last)[which].at[ds(place * self.rows, self.rows)]
        sent, received = (sem.at[place, which] for sem in self.sems[10:12])
        return remote(source, target, sent, received, self.other_core)

    def to_y(self, i):
        here = ds(i * self.rows, self.rows)
        source, target = self.from_last.at[here], self.from_y.at[here]
        return remote(source, target, self.sems[0].at[i], self.sems[1].at[i], self.other_chip)

    def to_x(self, i):
        source = self.mine.at[ds(i * self.rows + (1 - self.ctx) * self.half, self.half)]
        target = self.from_x.at[ds(i * self.half, self.half)]
        return remote(source, target, self.sems[2].at[i], self.sems[3].at[i], self.other_window)

    def to_z(self, i, k):
        start, size = self.segment(k, True)
        source = self.kept.at[ds(i * self.half + start, size)]
        target = self.from_z.at[ds(i * self.half + self.half - 2 * size, size)]
        return remote(source, target, self.sems[4].at[i, k], self.sems[5].at[i, k], self.beside[k])

    def back_z(self, i, k):
        start, size = self.segment(k + 1)
        here = self.out.at[ds(i * self.rows + self.ctx * self.half + start, size)]
        return remote(here, here, self.sems[6].at[i, k], self.sems[7].at[i, k], self.beside[k])

    def back_x(self, i):
        here = self.out.at[ds(i * self.rows + self.ctx * self.half, self.half)]
        return remote(here, here, self.sems[8].at[i], self.sems[9].at[i], self.other_window)

    def start(self):
        for array, count in enumerate(self.counts):

            def send(i, array=array):
                self.to_core(array, i, 1).start()
                self.to_core(array, i, 0).start()

            each(count, send)
        for array, count in enumerate(self.counts):

            def fold(i, array=array):
                place = self.firsts[array] + i
                self.to_core(array, i, 1).wait_recv()
                here = ds(place * self.rows, self.rows)
                term = self.fars[array][ds(i * self.rows, self.rows), :]
                total = term.astype(F32) + self.from_last[here, :].astype(F32)
                self.from_last[here, :] = total.astype(BF16)
                self.to_y(place).start()

            each(count, fold)

    def join(self, i):
        here = ds(i * self.rows, self.rows)
        self.to_y(i).wait_recv()
        for array, count in enumerate(self.counts):
            first = self.firsts[array]

            def add(array=array, first=first):
                self.to_core(array, i - first, 0).wait_recv()
                term = self.owns[array][ds((i - first) * self.rows, self.rows), :]
                total = term.astype(F32) + self.from_near[here, :].astype(F32)
                self.mine[here, :] = (total + self.from_y[here, :].astype(F32)).astype(BF16)

            pl.when((i >= first) & (i < first + count))(add)
        self.to_x(i).start()

    def spread(self, i):
        self.to_x(i).wait_recv()
        there = ds(i * self.half, self.half)
        term = self.mine[ds(i * self.rows + self.ctx * self.half, self.half), :]
        total = term.astype(F32) + self.from_x[there, :].astype(F32)
        self.kept[there, :] = total.astype(BF16)
        self.to_z(i, 0).start()

    def narrow(self, k, i):
        self.to_z(i, k).wait_recv()
        start, size = self.segment(k + 1)
        here = ds(i * self.half + start, size)
        there = ds(i * self.half + self.half - 2 * size, size)
        total = self.kept[here, :].astype(F32) + self.from_z[there, :].astype(F32)
        if k + 1 < len(self.bits):
            self.kept[here, :] = total.astype(BF16)
            self.to_z(i, k + 1).start()
        else:
            place = ds(i * self.rows + self.ctx * self.half + start, size)
            self.out[place, :] = total.astype(BF16)
            self.back_z(i, k).start()

    def widen(self, k, i):
        self.back_z(i, k).wait_recv()
        if k:
            self.back_z(i, k - 1).start()
        else:
            self.back_x(i).start()

    def step(self, i):
        for late, stage in zip(self.lates, self.stages, strict=True):
            pl.when((i >= late) & (i < self.parts + late))(functools.partial(stage, i - late))

    def finish(self):
        for array, count in enumerate(self.counts):

            def sent(i, array=array):
                self.to_core(array, i, 0).wait_send()
                self.to_core(array, i, 1).wait_send()

            each(count, sent)

        def end(i):
            self.to_y(i).wait_send()
            self.to_x(i).wait_send()
            self.back_x(i).wait()
            for k in range(len(self.bits)):
                self.to_z(i, k).wait_send()
                self.back_z(i, k).wait_send()

        each(self.parts, end)


def ds(start, size):
    return pl.ds(pl.multiple_of(start, 16), size)


def each(count, step):
    lax.fori_loop(0, count, lambda i, _: (step(i), 0)[1], 0)


def sum_kernel(arrays, places, *refs):
    n_here, n_there = len(arrays.here), len(arrays.there)
    here, there, refs = refs[:n_here], refs[n_here : n_here + n_there], refs[n_here + n_there :]
    terms, out, vec = refs[: len(places)], refs[len(places)], refs[len(places) + 1]
    from_vec, v_out, v_in = refs[-3:]
    sums, copies = arrays.open(here, there, out, refs[len(places) + 2 : -3])
    meet(sums.partners)
    mp = lax.axis_index("mp")
    slots = (mp, flip(mp, 1), flip(mp, 2), 3 - mp)
    vec[...] = jnp.zeros_like(vec)
    for term, (row, distance) in zip(terms, places, strict=True):
        at = row if distance is None else row + slots[distance]
        vec[pl.ds(at, 1), : term.shape[0]] = term[...].reshape(1, term.shape[0])
    hops = [
        remote(vec, from_vec.at[hop], v_out.at[hop], v_in.at[hop], partner)
        for hop, partner in enumerate(sums.partners)
    ]
    hops[0].start()
    for own_copy in copies:
        own_copy.wait()
    sums.start()
    for i in range(max(sums.steps, len(hops))):
        sums.step(i)
        if i < len(hops):
            hops[i].wait()
            vec[...] = vec[...] + from_vec[i]
        if i + 1 < len(hops):
            hops[i + 1].start()
    sums.finish()


def rows_of_part():
    return max(128, 32 * lax.axis_size("dp"))


class Arrays:
    def __init__(self, arrays):
        self.rows, self.bits = rows_of_part(), (lax.axis_size("dp") - 1).bit_length()
        self.pieces = [(v[0] if isinstance(v, tuple) else v).shape[-2] for v in arrays]
        if self.rows > 512:
            quads = [v if isinstance(v, tuple) else by_distance(v) for v in arrays]
            arrays = [tuple(jnp.concatenate(part) for part in zip(*quads, strict=True))]
        self.stacked = [not isinstance(array, tuple) for array in arrays]
        first = [array if stacked else array[0] for array, stacked in zip(arrays, self.stacked)]
        self.sizes = [v.shape[-2] for v in first]
        self.counts = [-(-size // self.rows) for size in self.sizes]
        filled = [
            tuple(self.fill(v) for v in array) if isinstance(array, tuple) else self.fill(array)
            for array in arrays
        ]
        self.here = [v for array in filled if isinstance(array, tuple) for v in array[::2]]
        self.there = []
        for array in filled:
            self.there += array[1::2] if isinstance(array, tuple) else [array]
        total, lanes = sum(self.counts) * self.rows, first[0].shape[-1]
        self.shape = jax.ShapeDtypeStruct((total, lanes), BF16)
        self.scratch = []
        for count, stacked in zip(self.counts, self.stacked):
            if stacked:
                self.scratch.append(pltpu.VMEM((2, count * self.rows, lanes), BF16))
                self.scratch.append(pltpu.SemaphoreType.DMA((2,)))
        self.scratch += Sums.scratch(total, sum(self.counts), self.bits, lanes)

    def fill(self, value):
        missing = -value.shape[-2] % self.rows
        return jnp.pad(value, [(0, 0)] * (value.ndim - 2) + [(0, missing), (0, 0)])

    def split(self, stack):
        shares, at = [], 0
        merged = len(self.pieces) > len(self.sizes)
        for k, size in enumerate(self.pieces):
            shares.append(stack[at : at + size])
            at += size if merged else self.counts[k] * self.rows
        return shares

    def open(self, here, there, out, refs, slack=(0,)):
        here, there, refs = list(here), list(there), list(refs)
        mp = lax.axis_index("mp")
        terms, copies = [], []
        for stacked in self.stacked:
            if not stacked:
                own, far = here.pop(0), here.pop(0)
                terms.append((own, there.pop(0), far, there.pop(0)))
                continue
            stack, place, sems = there.pop(0), refs.pop(0), refs.pop(0)
            for k, slot in enumerate((mp, flip(mp, 2))):
                copies.append(pltpu.make_async_copy(stack.at[slot], place.at[k], sems.at[k]))
                copies[-1].start()
            terms.append((place.at[0], stack.at[flip(mp, 1)], place.at[1], stack.at[3 - mp]))
        return Sums(self.counts, self.rows, terms, out, refs, slack), copies


def sum_replicas(arrays, vectors):
    arrays = Arrays(arrays)
    place = pl.BlockSpec(memory_space=pltpu.VMEM)
    away = pl.BlockSpec(memory_space=pl.ANY)
    dma = pltpu.SemaphoreType.DMA
    hops = 3 + arrays.bits
    stack, summed = pl.pallas_call(
        functools.partial(sum_kernel, arrays, [v[1:] for v in vectors]),
        out_shape=[arrays.shape, jax.ShapeDtypeStruct((len(vectors), D), F32)],
        in_specs=[place] * len(arrays.here)
        + [away] * len(arrays.there)
        + [place] * len(vectors),
        out_specs=[place, place],
        scratch_shapes=arrays.scratch
        + [pltpu.VMEM((hops, len(vectors), D), F32), dma((hops,)), dma((hops,))],
        compiler_params=pltpu.CompilerParams(
            collective_id=0, has_side_effects=True, vmem_limit_bytes=(32 if arrays.bits > 4 else 16) * 1024 * 1024
        ),
        name="sum_replicas",
    )(*arrays.here, *arrays.there, *(v[0] for v in vectors))
    return arrays.split(stack), summed


def back_kernel(mixed, arrays, *refs):
    refs = list(refs)

    def take(count):
        taken = refs[:count]
        del refs[:count]
        return taken

    places, flags, lo_ref = take(3)
    here, there, away = take(len(arrays.here)), take(len(arrays.there)), take(9)
    (dcols,) = take(1)
    if mixed:
        dv_ref, dv_before, dv_earlier = take(3)
    (out,) = take(1)
    if not mixed:
        dv_ref, dv_before, dv_earlier = take(3)
    dk_ref, dk_before, dk_earlier = take(3)
    near_k, near_v, far_k, far_v, home_k, home_v = take(6)
    values, acc_k, acc_v, acc_q = take(4)
    kv_out, kv_in = take(2)
    fetched, loaded = take(9), take(1)[0]
    loads = [
        pltpu.make_async_copy(source, target, loaded.at[k])
        for k, (source, target) in enumerate(zip(away, fetched, strict=True))
    ]
    for load in loads:
        load.start()
    cols, before, earlier, *others, exact, grad_ref, sum_ref = fetched
    first_values, given = (others, ()) if mixed else ((), others)
    slack = (0, 1, 1, 1, 1, 2) if mixed else (0, 2)
    sums, copies = arrays.open(here, there, out, refs, slack)

    ctx, mp = lax.axis_index("ctx"), lax.axis_index("mp")
    sees_one = (mp >= 2) | ((mp == 0) & (ctx == 1))
    sees_two = mp == 3
    meet(sums.partners + [{"mp": 3 - mp}])
    for copy in copies:
        copy.wait()
    sums.start()
    keys = ((earlier, 0), (before, 0), (cols, BAND))

    def home(which, source, target, g, device):
        return remote(
            source.at[g], target.at[g], kv_out.at[which, g], kv_in.at[which, g], device
        )

    def pair(g, act, step):
        act(step)
        if mixed:
            pl.when(g >= 2)(lambda: act(step + 1))
        else:
            act(step + 1)

    def from_last(g, step):
        source, target = (
            (dk_before, near_k), (dv_before, near_v), (dk_earlier, far_k), (dv_earlier, far_v),
        )[step]
        return home(step, source, target, g, {"mp": 2})

    def from_next(g, step, device):
        source, target = ((dk_before, home_k), (dv_before, home_v))[step]
        return home(4 + step, source, target, g, device)

    def group(g, _):
        place_values(mixed, g, places, first_values, keys, values)
        acc_k[...] = jnp.zeros_like(acc_k)
        if mixed:
            acc_v[...] = jnp.zeros_like(acc_v)
        else:
            for part in range(3):
                for j in range(GROUP):
                    head = GROUP * g + j
                    term = given[part][places[head]].astype(F32) * flags[head]
                    for side in range(2):
                        acc_v[2 * part + side, j * HD : (j + 1) * HD, :] = term[
                            :, side * TILE : (side + 1) * TILE
                        ]
        for t in range(WIN // TILE):
            tokens = slice(t * TILE, (t + 1) * TILE)
            low = lo_ref[:, tokens]
            place = 2 * WIN + t * TILE + lax.broadcasted_iota(jnp.int32, (1, TILE), 1)
            last = 2 * WIN // TILE + t

            def tile(kt, tokens=tokens, low=low, place=place, last=last):
                spot = kt * TILE + lax.broadcasted_iota(jnp.int32, (TILE, TILE), 0)
                keep = spot >= low
                if kt == last:
                    keep = keep & (spot <= place)
                span = slice(kt % 2 * TILE, (kt % 2 + 1) * TILE)
                key_ref, at = keys[kt // 2]
                for j in range(GROUP):
                    rows_j = slice(j * HD, (j + 1) * HD)
                    key = key_ref[g, at + j * HD : at + (j + 1) * HD, span]
                    query = cols[g, rows_j, tokens] * SCALE
                    grad = grad_ref[g, rows_j, tokens]
                    inner = jnp.sum(
                        grad.astype(F32) * exact[g, rows_j, tokens], axis=0, keepdims=True
                    )
                    raw = jnp.where(keep, dot(key, query, 0, 0), -jnp.inf)
                    weights = jnp.exp(raw - sum_ref[g, j : j + 1, tokens])
                    grad_weights = dot(values[kt // 2, rows_j, span], grad, 0, 0)
                    low_grad = (weights * (grad_weights - inner)).astype(BF16)
                    acc_v[kt, rows_j, :] += dot(grad, weights.astype(BF16), 1, 1)
                    acc_k[kt, rows_j, :] += dot(query, low_grad, 1, 1)
                    result = dot(key, low_grad, 1, 0)
                    acc_q[j] = result if kt == last else result + acc_q[j]

            for kt in reversed(range(last + 1)):
                if kt >= 4:
                    tile(kt)
                else:
                    pl.when(sees_one if kt >= 2 else sees_two)(functools.partial(tile, kt))
            for j in range(GROUP):
                dcols[g, j * HD : (j + 1) * HD, tokens] = (acc_q[j] * SCALE).astype(BF16)
            sums.step(2 * g + t)
        results = ((dk_earlier, dv_earlier), (dk_before, dv_before), (dk_ref, dv_ref))
        for part, (dk, dv) in enumerate(results):
            for side in range(2):
                span = slice(side * TILE, (side + 1) * TILE)
                dk[g, :, span] = acc_k[2 * part + side].astype(dk.dtype)
                dv[g, :, span] = acc_v[2 * part + side].astype(dv.dtype)

        def send_last():
            pair(g, lambda step: from_last(g, step).start(), 0)
            pair(g, lambda step: from_last(g, step).start(), 2)

        pl.when(mp == 3)(send_last)
        pl.when((mp == 0) & (ctx == 1))(
            lambda: pair(g, lambda step: from_next(g, step, sums.other_window).start(), 0)
        )
        return 0

    for load in loads:
        load.wait()
    lax.fori_loop(0, 4, group, 0)

    def relay(g):
        def one(step):
            near, far, source, total = (
                (near_k, far_k, dk_before, dk_ref), (near_v, far_v, dv_before, dv_ref),
            )[step]
            from_last(g, step).wait_recv()
            from_last(g, step + 2).wait_recv()
            source[g] = (source[g].astype(F32) + far[g].astype(F32)).astype(BF16)
            from_next(g, step, {"mp": 1}).start()
            total[g] += near[g].astype(F32)

        pair(g, one, 0)

    pl.when(mp == 2)(lambda: each(4, relay))
    for i in range(8, sums.steps):
        sums.step(i)

    def arrive(g):
        def one(step):
            arrived, total = ((home_k, dk_ref), (home_v, dv_ref))[step]
            from_next(g, step, sums.other_window).wait_recv()
            total[g] += arrived[g].astype(F32)

        pair(g, one, 0)

    pl.when((mp == 1) | ((mp == 0) & (ctx == 0)))(lambda: each(4, arrive))

    def round_off(g):
        dcols[g, BAND : 2 * BAND, :] = dk_ref[g].astype(BF16)
        if not mixed:
            dcols[g, 2 * BAND : 3 * BAND, :] = dv_ref[g].astype(BF16)

    each(4, round_off)
    wide = BAND // 2 if mixed else BAND
    for slot in range(4):
        if mixed:
            half = slice(slot % 2 * wide, (slot % 2 + 1) * wide)
            dcols[slot, 2 * BAND : 2 * BAND + wide, :] = dv_ref[2 + slot // 2, half, :].astype(BF16)
        rest = dcols.shape[1] - 2 * BAND - wide
        dcols[slot, 2 * BAND + wide :, :] = jnp.zeros((rest, WIN), BF16)

    def sent_last(g):
        pair(g, lambda step: from_last(g, step).wait_send(), 0)
        pair(g, lambda step: from_last(g, step).wait_send(), 2)

    def sent_next(device):
        each(4, lambda g: pair(g, lambda step: from_next(g, step, device).wait_send(), 0))

    pl.when(mp == 3)(lambda: each(4, sent_last))
    pl.when(mp == 2)(lambda: sent_next({"mp": 1}))
    pl.when((mp == 0) & (ctx == 1))(lambda: sent_next(sums.other_window))
    sums.finish()


def attend_back(places, flags, low, front, firsts, given, exact, grad_heads, lse, arrays):
    mixed = bool(firsts)
    arrays = Arrays(arrays)
    place = pl.BlockSpec(memory_space=pltpu.VMEM)
    away = pl.BlockSpec(memory_space=pl.ANY)
    scalar = pl.BlockSpec(memory_space=pltpu.SMEM)
    dma = pltpu.SemaphoreType.DMA
    by_head = [v.reshape(-1, HD, WIN) for v in firsts[::-1] + given[::-1]]
    fetched = [*front, *by_head, exact, grad_heads, lse]
    wide = jax.ShapeDtypeStruct((4, BAND, WIN), F32)
    slim = jax.ShapeDtypeStruct((4, BAND, WIN), BF16)
    n_cols = -(-(5 * BAND // 2 if mixed else 3 * BAND) // 128) * 128
    outs = [jax.ShapeDtypeStruct((4, n_cols, WIN), BF16)]
    outs += ([wide, slim, slim] if mixed else []) + [arrays.shape]
    block, full = pltpu.VMEM((4, BAND, WIN), BF16), pltpu.VMEM((4, BAND, WIN), F32)
    results = pl.pallas_call(
        functools.partial(back_kernel, mixed, arrays),
        out_shape=outs,
        in_specs=[scalar, scalar, place]
        + [place] * len(arrays.here)
        + [away] * (len(arrays.there) + len(fetched)),
        out_specs=[place] * len(outs),
        scratch_shapes=([] if mixed else [full, block, block])
        + [full]
        + [block] * 8
        + [
            pltpu.VMEM((3, BAND, WIN), BF16),
            pltpu.VMEM((TILES, BAND, TILE), F32),
            pltpu.VMEM((TILES, BAND, TILE), F32),
            pltpu.VMEM((GROUP, HD, TILE), F32),
            dma((6, 4)),
            dma((6, 4)),
        ]
        + [pltpu.VMEM(v.shape, v.dtype) for v in fetched]
        + [dma((len(fetched),))]
        + arrays.scratch,
        compiler_params=pltpu.CompilerParams(
            collective_id=3 if mixed else 4,
            has_side_effects=True,
            vmem_limit_bytes=(60 if arrays.bits > 4 else 36 if mixed else 43) * 1024 * 1024,
        ),
        name="attend_back",
    )(places, flags, low, *arrays.here, *arrays.there, *fetched)
    return results[:-1], arrays.split(results[-1])


def gelu(hidden):
    return jax.nn.gelu(hidden, approximate=True)


def tail_forward(stream, heads, out_weight, out_bias, gain, shift, ups, up_biases, downs):
    stream = stream + dot(heads, out_weight, 0, 0) + out_bias[0]
    normed, unit, scale = norm_rows(stream, gain[1], shift[1])
    hidden, active, total = [], [], out_bias[1]
    for up, bias, down in zip(ups, up_biases, downs, strict=True):
        hidden.append(dot(normed, up, 1, 0) + bias)
        active.append(gelu(hidden[-1]).astype(BF16))
        total = total + dot(active[-1], down, 1, 0)
    return stream + total, (normed, unit, scale, hidden, active)


def tail_backward(grad, kept, out_weight, gain, ups, downs):
    normed, unit, scale, hidden, active = kept
    bias_mlp = jnp.sum(grad, axis=0)
    rounded = grad.astype(BF16)
    mats, up_biases, normed_grad = [], [], 0.0
    for up, down, before, after in zip(ups, downs, hidden, active, strict=True):
        _, pull = jax.vjp(gelu, before)
        grad_hidden = pull(dot(rounded, down, 1, 1))[0]
        up_biases.append(jnp.sum(grad_hidden, axis=0))
        low = grad_hidden.astype(BF16)
        mats.append((dot(normed, low, 0, 0).astype(BF16), dot(after, rounded, 0, 0).astype(BF16)))
        normed_grad = normed_grad + dot(low, up, 1, 1)
    middle, gain_grad, shift_grad = norm_back(normed_grad, unit, scale, gain[1])
    grad = grad + middle
    bias_attn = jnp.sum(grad, axis=0)
    rounded = grad.astype(BF16)
    grad_heads = dot(out_weight, rounded, 1, 1).astype(BF16)
    return grad, rounded, grad_heads, mats, up_biases, (gain_grad, shift_grad, bias_attn, bias_mlp)


def turned(weight):
    return jnp.swapaxes(weight, -1, -2)


def shards(
    block_input, cotangent, doc_lengths, reuse_heads,
    norm_gain1, norm_bias1, projections1, front_bias1, out_weight1, out_bias1,
    up_weight1, up_bias1, down_weight1,
    norm_gain2, norm_bias2, query_key2, query_bias2, fresh_value2, value_bias2,
    out_weight2, out_bias2, up_weight2, up_bias2, down_weight2,
):
    low = row_starts(doc_lengths[0])
    taken = jnp.arange(4 * GROUP, dtype=jnp.int32)[:, None] == reuse_heads[None, :]
    taker = jnp.sum(jnp.where(taken, jnp.arange(REUSE, dtype=jnp.int32)[None, :], 0), axis=1)
    flags = jnp.any(taken, axis=1).astype(F32)
    band_of, in_band = reuse_heads // GROUP, reuse_heads % GROUP
    places2 = jnp.concatenate(
        [band_of * 3 * GROUP + 2 * GROUP + in_band, band_of * 2 * GROUP + GROUP + in_band]
    )

    stream0 = block_input.astype(F32)
    normed1, unit1, scale1 = norm_rows(stream0, norm_gain1[0], norm_bias1[0])
    n_front1, n_front2 = 3 * BAND, 2 * BAND + BAND // 2
    none = jnp.zeros((BAND,), BF16)

    def as_row(pieces):
        row = jnp.concatenate(pieces).astype(F32)
        return jnp.pad(row[None, :], ((0, 7), (0, -row.shape[0] % 128)))

    small = jnp.concatenate([query_bias2, value_bias2, up_bias1, up_bias2])
    small = jnp.pad(small, (0, 16 * 128 - small.shape[0])).reshape(16, 128)
    own_front2 = jnp.concatenate([turned(query_key2).reshape(2 * BAND, D), turned(fresh_value2)])
    own_front2 = jnp.pad(own_front2, ((0, -n_front2 % 64), (0, 0)))
    (
        cols1, before1, earlier1, heads1, exact1, sums1, _, small, front1,
        up1, down1, front2, outs1,
    ) = project(
        places2, low, normed1, turned(projections1).reshape(n_front1, D),
        as_row([front_bias1[0], none, front_bias1[1]]), n_front1, 2 * BAND, (), small,
        (up_weight1, down_weight1, own_front2, out_weight1),
    )
    me = lax.axis_index("mp")
    ups1, downs1 = ([up_weight1] + by_distance(up1)[1:], [down_weight1] + by_distance(down1)[1:])
    front2 = lax.dynamic_update_index_in_dim(front2, own_front2, me, 0)
    outs1 = lax.dynamic_update_index_in_dim(outs1, out_weight1, me, 0).reshape(D, D)
    small = small.reshape(4, -1)
    at = BAND + BAND // 2
    bias2 = jnp.stack([as_row([small[s, :BAND], none, small[s, BAND:at]]) for s in range(4)])
    up_biases1 = by_distance(small[:, at : at + D])
    up_biases2 = by_distance(small[:, at + D : at + 2 * D])

    front_kv1 = (cols1, before1, earlier1)
    stream1, kept1 = tail_forward(
        stream0, heads1.reshape(D, WIN), outs1, out_bias1, norm_gain1, norm_bias1,
        ups1, up_biases1, downs1,
    )

    normed2, unit2, scale2 = norm_rows(stream1, norm_gain2[0], norm_bias2[0])
    front_kv1 = (cols1, before1, earlier1)
    cols2, before2, earlier2, heads2, exact2, sums2, up2, down2, outs2 = project(
        places2, low, normed2, front2, bias2, n_front2, n_front2 - BAND, front_kv1, None,
        (up_weight2, down_weight2, out_weight2),
    )
    ups2, downs2 = ([up_weight2] + by_distance(up2)[1:], [down_weight2] + by_distance(down2)[1:])
    outs2 = lax.dynamic_update_index_in_dim(outs2, out_weight2, me, 0).reshape(D, D)

    front_kv2 = (cols2, before2, earlier2)
    stream2, kept2 = tail_forward(
        stream1, heads2.reshape(D, WIN), outs2, out_bias2, norm_gain2, norm_bias2,
        ups2, up_biases2, downs2,
    )
    block_output = stream2.astype(BF16)

    grad, rounded, grad_heads, mats2, up_grads2, small2 = tail_backward(
        cotangent.astype(F32), kept2, outs2, norm_gain2, ups2, downs2
    )
    (dcols2, dv2, dv2_before, dv2_earlier), mats2 = attend_back(
        places2, flags, low, front_kv2, front_kv1, (), exact2,
        grad_heads.reshape(4, BAND, WIN), sums2, list(zip(*mats2, strict=True)),
    )
    grad_out2 = dot(heads2.reshape(D, WIN), rounded, 1, 0).astype(BF16).reshape(4, BAND, D)
    bias_grad2 = jnp.sum(dcols2.astype(F32), axis=2)
    grad_front2 = dot(dcols2.reshape(-1, WIN), normed2, 1, 0).astype(BF16).reshape(4, -1, D)
    normed_grad = dot(dcols2.reshape(-1, WIN), front2.reshape(-1, D), 0, 0)
    middle, gain_front2, shift_front2 = norm_back(normed_grad, unit2, scale2, norm_gain2[0])
    grad = grad + middle

    grad, rounded, grad_heads, mats1, up_grads1, small1 = tail_backward(
        grad, kept1, outs1, norm_gain1, ups1, downs1
    )
    grad_out1 = dot(heads1.reshape(D, WIN), rounded, 1, 0).astype(BF16).reshape(4, BAND, D)
    arrays = [grad_front2]
    (dcols1,), (front_sum2, *mats1) = attend_back(
        taker, flags, low, front_kv1, (), (dv2, dv2_before, dv2_earlier), exact1,
        grad_heads.reshape(4, BAND, WIN), sums1, arrays + list(zip(*mats1, strict=True)),
    )
    bias_grad1 = jnp.sum(dcols1.astype(F32), axis=2)
    grad_front1 = dot(dcols1.reshape(-1, WIN), normed1, 1, 0).astype(BF16).reshape(4, -1, D)
    normed_grad = dot(dcols1.reshape(-1, WIN), front1.reshape(-1, D), 0, 0)
    middle, gain_front1, shift_front1 = norm_back(normed_grad, unit1, scale1, norm_gain1[0])
    input_grad = (grad + middle).astype(BF16)

    singles = [
        gain_front1, small1[0], shift_front1, small1[1], small1[2], small1[3],
        gain_front2, small2[0], shift_front2, small2[1], small2[2], small2[3],
        bias_grad1[:, :BAND].reshape(-1), bias_grad1[:, 2 * BAND : n_front1].reshape(-1),
        bias_grad2[:, :BAND].reshape(-1), bias_grad2[:, 2 * BAND : n_front2].reshape(-1),
    ]
    vectors = [(vector, row, None) for row, vector in enumerate(singles)]
    for row, shares in ((16, up_grads1), (20, up_grads2)):
        vectors += [(vector, row, distance) for distance, vector in enumerate(shares)]
    grad_outs = jnp.concatenate([grad_out2, grad_out1], axis=1)
    (out_sums, front_sum1), sums = sum_replicas([grad_outs, grad_front1], vectors)

    def mine(vectors):
        return lax.dynamic_index_in_dim(vectors.reshape(4, -1), me, 0, keepdims=False)

    return (
        block_output,
        input_grad,
        sums[0:2],
        sums[2:4],
        turned(front_sum1[:n_front1].reshape(3, BAND, D)).astype(F32),
        jnp.stack([mine(sums[12]), mine(sums[13])]),
        out_sums[BAND:].astype(F32),
        sums[4:6],
        mats1[0].astype(F32),
        mine(sums[16:20]),
        mats1[1].astype(F32),
        sums[6:8],
        sums[8:10],
        turned(front_sum2[: 2 * BAND].reshape(2, BAND, D)).astype(F32),
        mine(sums[14]),
        turned(front_sum2[2 * BAND : n_front2]).astype(F32),
        mine(sums[15, : D // 2]),
        out_sums[:BAND].astype(F32),
        sums[10:12],
        mats2[0].astype(F32),
        mine(sums[20:24]),
        mats2[1].astype(F32),
    )


def solution(mesh):
    rows = P(("dp", "ctx", "mp"), None)
    placed = (
        rows, rows, P(("dp", "ctx"), None), P(),
        P(), P(), P(None, None, "mp"), P(None, "mp"), P("mp", None), P(),
        P(None, "mp"), P("mp"), P("mp", None),
        P(), P(), P(None, None, "mp"), P("mp"), P(None, "mp"), P("mp"),
        P("mp", None), P(), P(None, "mp"), P("mp"), P("mp", None),
    )
    given = (
        rows, rows,
        P(), P(), P(None, None, "mp"), P(None, "mp"), P("mp", None), P(),
        P(None, "mp"), P("mp"), P("mp", None),
        P(), P(), P(None, None, "mp"), P("mp"), P(None, "mp"), P("mp"),
        P("mp", None), P(), P(None, "mp"), P("mp"), P("mp", None),
    )
    return jax.shard_map(shards, mesh=mesh, in_specs=placed, out_specs=given, check_vma=False)
```
